32 devices in a mesh: pipe: 2 (over x), seq: 4 (over z), dp: 4 (over y, core).
Axes of the slice: x: 2, y: 2, z: 4, core: 2. Of those that a mesh axis runs over, the one named last changes fastest.
Arguments:
- embedded_families: bfloat16 [8, 4, 128, 768], P('dp', 'seq'), may hold values from -6 to 6
- order: int32 [4, 2], P('dp'), may hold values from 0 to 1, each once within a row
- token_quarter_factor: int32 [8, 4, 128], P('dp', 'seq'), may hold values from 0 to 4
- genuine_residue_tally: int32 [8], P('dp'), may hold values from 64 to 128
- standardizer_scales: float32 [2, 3, 768], P('pipe', None, 'seq'), may hold values from 0.5 to 1.5
- standardizer_offsets: float32 [2, 3, 768], P('pipe', None, 'seq'), may hold values from -1.5 to 1.5
- row_qkv: bfloat16 [2, 768, 2304], P('pipe', 'seq'), may hold values from -0.21875 to 0.21875
- row_out: bfloat16 [2, 768, 768], P('pipe', 'seq'), may hold values from -1.75 to 1.75
- col_qkv: bfloat16 [2, 768, 2304], P('pipe', 'seq'), may hold values from -0.21875 to 0.21875
- col_out: bfloat16 [2, 768, 768], P('pipe', 'seq'), may hold values from -1.75 to 1.75
- ffn_up: bfloat16 [2, 768, 3072], P('pipe', 'seq'), may hold values from -0.21875 to 0.21875
- ffn_down: bfloat16 [2, 3072, 768], P('pipe', 'seq'), may hold values from -0.109375 to 0.109375
- upstream_sensitivity: bfloat16 [8, 4, 128, 768], P('dp', 'seq'), may hold values from -6 to 6
Outputs:
- activations: bfloat16 [2, 8, 4, 128, 768], P('pipe', 'dp', 'seq')
- block_entry_derivs: bfloat16 [2, 8, 4, 128, 768], P('pipe', 'dp', 'seq')
- disorder_cost: float32 [2, 8], P('pipe', 'dp')
- grad_row_qkv: float32 [2, 768, 2304], P('pipe', 'seq')
- grad_row_out: float32 [2, 768, 768], P('pipe', 'seq')
- grad_col_qkv: float32 [2, 768, 2304], P('pipe', 'seq')
- grad_col_out: float32 [2, 768, 768], P('pipe', 'seq')
- grad_ffn_up: float32 [2, 768, 3072], P('pipe', 'seq')
- grad_ffn_down: float32 [2, 3072, 768], P('pipe', 'seq')
- grad_ln_gain: float32 [2, 3, 768], P('pipe', None, 'seq')
- grad_ln_bias: float32 [2, 3, 768], P('pipe', None, 'seq')
The draws below stay inside these ranges and needn't reach their ends.
Inputs may be any that keep to these rules, and one draw needn't show every extreme that they name: Each row of order is a permutation of 0 to 1.
All inputs are finite; a program needn't handle non-finite values.
Results may differ from the reference program's by a relative error of at most 0.04.
Values may be sent and summed in bfloat16 or wider, within the bound.
A program may use at most 320 MiB of HBM per device.

```python
import math
import jax
import jax.numpy as jnp
from jax import lax

EMBED_WIDTH = 768
HEAD_TALLY = 12
FF = 3072
PER_HEAD_WIDTH = 64
RESIDUE_TALLY = 128
MB = 2
RELATIVE_TALLY = 4
FAMILY_TOTAL = 8
N_DP = 4


def plant(drawn, stream_key, low, top_value):
    place = [jax.random.randint(jax.random.fold_in(stream_key, axis), (), 0, length) for axis, length in enumerate(drawn.shape)]
    widest = drawn.shape.index(max(drawn.shape))
    next_to = place[:widest] + [(place[widest] + 1) % drawn.shape[widest]] + place[widest + 1:]
    return drawn.at[tuple(place)].set(low).at[tuple(next_to)].set(top_value)


def level_of(rng, dims, cuts, low, top_value):
    factor_of = 1.0
    for axis_at, blocks in cuts:
        draws = jax.random.uniform(jax.random.fold_in(jax.random.fold_in(rng, 6), axis_at), (blocks,), jnp.float32, low / len(cuts), top_value / len(cuts))
        factor_of = factor_of * jnp.repeat(jnp.exp(draws), dims[axis_at] // blocks).reshape((-1,) + (1,) * (len(dims) - 1 - axis_at))
    return factor_of


def gaussian(key, shape, deviation, bound, pieces=(), kind=jnp.bfloat16):
    entries = jax.random.normal(key, shape, jnp.float32) * deviation
    if len(pieces) > 0:
        entries = level_of(key, shape, pieces, -0.22, 0.18) * entries
    return jnp.clip(entries, min=-bound, max=bound).astype(kind)


def setup_inputs(seed: int = 0) -> dict:
    splits = jax.random.split(jax.random.key(seed), 14)
    return {
        "embedded_families": gaussian(splits[0], (FAMILY_TOTAL, RELATIVE_TALLY, RESIDUE_TALLY, EMBED_WIDTH), 1.0, 6.0, ((0, 4), (1, 4))),
        "order": jax.vmap(lambda own: jax.random.permutation(own, MB))(jax.random.split(splits[1], N_DP)).reshape((N_DP, MB)).astype(jnp.int32),
        "token_quarter_factor": plant(jax.random.randint(splits[2], (FAMILY_TOTAL, RELATIVE_TALLY, RESIDUE_TALLY), 0, 5), jax.random.fold_in(splits[2], 1), 0, 4).astype(jnp.int32),
        "genuine_residue_tally": plant(jax.random.randint(splits[3], (FAMILY_TOTAL,), RESIDUE_TALLY // 2, RESIDUE_TALLY + 1), jax.random.fold_in(splits[3], 1), RESIDUE_TALLY // 2, RESIDUE_TALLY).astype(jnp.int32),
        "standardizer_scales": jnp.clip(1.0 + 0.1 * jax.random.normal(splits[4], (2, 3, EMBED_WIDTH), jnp.float32), 0.5, 1.5),
        "standardizer_offsets": gaussian(splits[5], (2, 3, EMBED_WIDTH), 0.3, 1.5, ((0, 2), (2, 4)), jnp.float32),
        "row_qkv": gaussian(splits[6], (2, EMBED_WIDTH, 3 * EMBED_WIDTH), EMBED_WIDTH ** -0.5, 0.21875, ((0, 2), (1, 4))),
        "row_out": gaussian(splits[7], (2, EMBED_WIDTH, EMBED_WIDTH), (EMBED_WIDTH // 64) ** -0.5, 1.75, ((0, 2), (1, 4))),
        "col_qkv": gaussian(splits[8], (2, EMBED_WIDTH, 3 * EMBED_WIDTH), EMBED_WIDTH ** -0.5, 0.21875, ((0, 2), (1, 4))),
        "col_out": gaussian(splits[9], (2, EMBED_WIDTH, EMBED_WIDTH), (EMBED_WIDTH // 64) ** -0.5, 1.75, ((0, 2), (1, 4))),
        "ffn_up": gaussian(splits[10], (2, EMBED_WIDTH, FF), EMBED_WIDTH ** -0.5, 0.21875, ((0, 2), (1, 4))),
        "ffn_down": gaussian(splits[11], (2, FF, EMBED_WIDTH), FF ** -0.5, 0.109375, ((0, 2), (1, 4))),
        "upstream_sensitivity": gaussian(splits[12], (FAMILY_TOTAL, RELATIVE_TALLY, RESIDUE_TALLY, EMBED_WIDTH), 1.0, 6.0, ((0, 4), (1, 4))),
    }


@jax.custom_vjp
def low(v):
    return lax.optimization_barrier(v.astype(jnp.bfloat16)).astype(jnp.float32)

@jax.custom_vjp
def low_back(v):
    return v

def low_keep(v):
    return (low(v), None)

def low_pass(kept, grad):
    return (grad,)

def back_keep(v):
    return (v, None)

def back_low(kept, grad):
    return (low(grad),)
low.defvjp(low_keep, low_pass)
low_back.defvjp(back_keep, back_low)
norm_epsilon = 1e-05

def truncated_value(values):
    return low_back(low(values))

def normed(values, gain_row, bias_row):
    average = lax.optimization_barrier(jnp.mean(values, axis=-1, keepdims=True))
    centered = values - average
    variance = lax.optimization_barrier(jnp.mean(centered * centered, axis=-1, keepdims=True))
    return centered * lax.rsqrt(variance + norm_epsilon) * gain_row + bias_row

def linear_product(left, weight):
    return jnp.einsum('rcd,df->rcf', left, weight, precision=lax.Precision.HIGHEST)

def alignment_layer(source_rows, family_residues, parameters):
    horizontal_coefficients, w_row_out, vertical_coefficients, w_col_out, w_up, w_down, gain_rows, bias_rows = parameters
    source_rows = low_back(source_rows)
    layernorm_first = low(normed(source_rows, gain_rows[0], bias_rows[0]))
    horizontal_mixer = truncated_value(linear_product(layernorm_first, horizontal_coefficients)).reshape(RELATIVE_TALLY, RESIDUE_TALLY, 3, HEAD_TALLY, PER_HEAD_WIDTH)
    queries, key_rows, content_lines = (horizontal_mixer[:, :, 0], horizontal_mixer[:, :, 1], horizontal_mixer[:, :, 2])
    logit_factor = 1.0 / (math.sqrt(PER_HEAD_WIDTH) * math.sqrt(RELATIVE_TALLY))
    logits = low_back(logit_factor * jnp.einsum('rihe,rjhe->hij', queries, key_rows, precision=lax.Precision.HIGHEST))
    softmax_share = jax.nn.softmax(logits, axis=-1)
    log_probs = jax.nn.log_softmax(logits, axis=-1)
    entropy = -lax.optimization_barrier(jnp.sum(softmax_share * log_probs, axis=-1))
    valid_residues = (jnp.arange(RESIDUE_TALLY, dtype=jnp.int32) < family_residues).astype(jnp.float32)
    disorder_cost = jnp.sum(entropy * valid_residues[None, :]) / float(HEAD_TALLY * RESIDUE_TALLY)
    blended_lines = truncated_value(jnp.einsum('vyp,opvl->oyvl', low(softmax_share), content_lines, precision=lax.Precision.HIGHEST)).reshape(RELATIVE_TALLY, RESIDUE_TALLY, EMBED_WIDTH)
    after_row = source_rows + low_back(linear_product(blended_lines, w_row_out))
    layernorm_second = low(normed(after_row, gain_rows[1], bias_rows[1]))
    vertical_mixer = truncated_value(linear_product(layernorm_second, vertical_coefficients)).reshape(RELATIVE_TALLY, RESIDUE_TALLY, 3, HEAD_TALLY, PER_HEAD_WIDTH)
    scores = low_back(jnp.einsum('rche,sche->chrs', vertical_mixer[:, :, 0], vertical_mixer[:, :, 1], precision=lax.Precision.HIGHEST) / math.sqrt(PER_HEAD_WIDTH))
    vertical_factors = jax.nn.softmax(scores, axis=-1)
    mixed_values = truncated_value(jnp.einsum('gmqi,igmu->qgmu', low(vertical_factors), vertical_mixer[:, :, 2], precision=lax.Precision.HIGHEST)).reshape(RELATIVE_TALLY, RESIDUE_TALLY, EMBED_WIDTH)
    after_col = after_row + low_back(linear_product(mixed_values, w_col_out))
    normal_c = low(normed(after_col, gain_rows[2], bias_rows[2]))
    hidden = low(jax.nn.gelu(low_back(linear_product(normal_c, w_up)), approximate=False))
    result = after_col + low_back(linear_product(hidden, w_down))
    return (low(result), disorder_cost)

def reference(embedded_families, order, token_quarter_factor, genuine_residue_tally, standardizer_scales, standardizer_offsets, row_qkv, row_out, col_qkv, col_out, ffn_up, ffn_down, upstream_sensitivity):
    slot_order = (jnp.arange(N_DP, dtype=jnp.int32)[:, None] * MB + order).reshape(-1).astype(jnp.int32)
    projection_tables = tuple((piece.astype(jnp.float32) for piece in (row_qkv, row_out, col_qkv, col_out, ffn_up, ffn_down)))
    starting_homologs = embedded_families.astype(jnp.float32)[slot_order]
    counts = genuine_residue_tally[slot_order]
    handoff_hidden = jnp.zeros_like(starting_homologs)

    def finished_answer(starting_homologs, handoff_hidden, projection_tables, gain_all, bias_all):
        parameters = [tuple((piece[layer_index] for piece in projection_tables)) + (gain_all[layer_index], bias_all[layer_index]) for layer_index in range(2)]

        def per_alignment(element):
            source_rows, added_zero, family_residues = element
            midway_state, penalty_primary = alignment_layer(source_rows, family_residues, parameters[0])
            midway_state = midway_state + added_zero
            closing_rows, penalty_secondary = alignment_layer(midway_state, family_residues, parameters[1])
            return (midway_state, closing_rows, penalty_primary, penalty_secondary)
        midway_state, closing_rows, penalty_primary, penalty_secondary = lax.map(jax.checkpoint(per_alignment), (starting_homologs, handoff_hidden, counts))
        return (jnp.stack([midway_state, closing_rows]), jnp.stack([penalty_primary, penalty_secondary]))
    (block_products, focus_spread_levies), backward_cotangent_map = jax.vjp(finished_answer, starting_homologs, handoff_hidden, projection_tables, standardizer_scales, standardizer_offsets)
    outgrad = upstream_sensitivity.astype(jnp.float32) * token_quarter_factor[slot_order].astype(jnp.float32)[..., None] * 0.25
    output_grad = jnp.stack([jnp.zeros_like(outgrad), outgrad])
    spread_levy_slope = jnp.full(focus_spread_levies.shape, float(RELATIVE_TALLY * RESIDUE_TALLY), jnp.float32)
    grad_entry, grad_between, projection_derivs, scale_derivative, offset_derivative = backward_cotangent_map((output_grad, spread_levy_slope))
    block_entry_derivs = jnp.stack([grad_entry, grad_between]).astype(jnp.bfloat16)
    return (block_products.astype(jnp.bfloat16), block_entry_derivs, focus_spread_levies, projection_derivs[0], projection_derivs[1], projection_derivs[2], projection_derivs[3], projection_derivs[4], projection_derivs[5], scale_derivative, offset_derivative)
```

```python
import functools
import math

import jax
import jax.numpy as jnp
from jax import lax
from jax.experimental import pallas as pl
from jax.experimental.pallas import tpu as pltpu
from jax.sharding import PartitionSpec as P

HEAD_TALLY = 12
LINE = 4
MESH = pl.DeviceIdType.MESH


norm_epsilon = 1e-05


def shifted(value, axis, steps):
    count = lax.axis_size(axis)
    initial, last = (max(0, -steps), min(count, count - steps))
    return lax.ppermute(value, axis, [(source, source + steps) for source in range(initial, last)])


def normed(values, gain_row, bias_row):
    average = jnp.mean(values, axis=-1, keepdims=True)
    centered = values - average
    variance = jnp.mean(centered * centered, axis=-1, keepdims=True)
    return centered * lax.rsqrt(variance + norm_epsilon) * gain_row + bias_row


def gelu_exact(values):
    return jax.nn.gelu(values, approximate=False)


def product(left, weight):
    return lax.dot_general(
        left, weight, (((left.ndim - 1,), (0,)), ((), ())), preferred_element_type=jnp.float32
    )


def product_back(left, weight):
    return lax.dot_general(
        left, weight, (((left.ndim - 1,), (1,)), ((), ())), preferred_element_type=jnp.float32
    )


def weight_term(left, right):
    return lax.dot_general(
        left, right, (((0, 1), (0, 1)), ((), ())), preferred_element_type=jnp.float32
    )


def split_heads(values, head_count):
    return values.reshape(values.shape[:-1] + (head_count, values.shape[-1] // head_count))


def choose(flag, first_tree, second_tree):
    return jax.tree.map(lambda early, later: jnp.where(flag, early, later), first_tree, second_tree)


def column_scores(queries, key_rows, head_count):
    query_heads = split_heads(queries, head_count)
    raw = jnp.einsum(
        "rche,sche->chrs",
        query_heads,
        split_heads(key_rows, head_count),
        preferred_element_type=jnp.float32,
    )
    return raw / math.sqrt(query_heads.shape[-1])


def column_forward(queries, key_rows, content_lines, head_count):
    scores = column_scores(queries, key_rows, head_count)
    log_total = jax.nn.logsumexp(scores, axis=-1)
    vertical_factors = jnp.exp(scores - log_total[..., None]).astype(jnp.bfloat16)
    mixed_cols = jnp.einsum(
        "gmqi,igmu->qgmu",
        vertical_factors,
        split_heads(content_lines, head_count),
        preferred_element_type=jnp.float32,
    )
    return (mixed_cols.reshape(queries.shape).astype(jnp.bfloat16), log_total)


def column_backward(queries, key_rows, content_lines, log_total, grad_mixed, head_count):
    scores = column_scores(queries, key_rows, head_count)
    softmax_share = jnp.exp(scores - log_total[..., None])
    grad_heads = split_heads(grad_mixed, head_count)
    grad_probs = jnp.einsum(
        "rche,sche->chrs",
        grad_heads,
        split_heads(content_lines, head_count),
        preferred_element_type=jnp.float32,
    )
    grad_values = jnp.einsum(
        "chrs,rche->sche",
        softmax_share.astype(jnp.bfloat16),
        grad_heads,
        preferred_element_type=jnp.float32,
    )
    grad_scores = (
        softmax_share * (grad_probs - jnp.sum(softmax_share * grad_probs, axis=-1, keepdims=True))
    ).astype(jnp.bfloat16)
    root_size = math.sqrt(queries.shape[-1] // head_count)
    grad_queries = (
        jnp.einsum(
            "gmqi,igmu->qgmu",
            grad_scores,
            split_heads(key_rows, head_count),
            preferred_element_type=jnp.float32,
        )
        / root_size
    )
    grad_keys = (
        jnp.einsum(
            "chrs,rche->sche",
            grad_scores,
            split_heads(queries, head_count),
            preferred_element_type=jnp.float32,
        )
        / root_size
    )
    return (
        grad_queries.reshape(queries.shape),
        grad_keys.reshape(key_rows.shape),
        grad_values.reshape(content_lines.shape),
    )


def row_split(horizontal_mixer, model_width, head_count):
    queries = split_heads(horizontal_mixer[..., :model_width], head_count)
    key_rows = split_heads(horizontal_mixer[..., model_width : 2 * model_width], head_count)
    content_lines = split_heads(horizontal_mixer[..., 2 * model_width :], head_count)
    return (queries, key_rows, content_lines)


def layer_forward(source_rows, family_residues, projection_tables, head_count):
    (
        horizontal_coefficients,
        w_row_out,
        vertical_coefficients,
        w_col_out,
        w_up,
        w_down,
        gain_rows,
        bias_rows,
    ) = projection_tables
    row_count, columns, model_width = source_rows.shape
    total_rows = row_count * lax.axis_size("seq")
    start = source_rows.astype(jnp.float32)
    layernorm_first = normed(start, gain_rows[0], bias_rows[0]).astype(jnp.bfloat16)
    horizontal_mixer = product(layernorm_first, horizontal_coefficients).astype(jnp.bfloat16)
    queries, key_rows, content_lines = row_split(horizontal_mixer, model_width, head_count)
    logit_factor = 1.0 / (math.sqrt(model_width // head_count) * math.sqrt(total_rows))
    partial_value = logit_factor * jnp.einsum(
        "rihe,rjhe->hij", queries, key_rows, preferred_element_type=jnp.float32
    )
    logits = lax.psum(partial_value.astype(jnp.bfloat16), "seq").astype(jnp.float32)
    softmax_share = jax.nn.softmax(logits, axis=-1)
    log_probs = jax.nn.log_softmax(logits, axis=-1)
    entropy = -jnp.sum(softmax_share * log_probs, axis=-1)
    valid_residues = (jnp.arange(columns, dtype=jnp.int32) < family_residues).astype(jnp.float32)
    disorder_cost = jnp.sum(entropy * valid_residues[None, :]) / float(head_count * columns)
    blended_lines = jnp.einsum(
        "vyp,opvl->oyvl",
        softmax_share.astype(jnp.bfloat16),
        content_lines,
        preferred_element_type=jnp.float32,
    )
    blended_lines = blended_lines.reshape(row_count, columns, model_width).astype(jnp.bfloat16)
    after_row = start + product(blended_lines, w_row_out)
    layernorm_second = normed(after_row, gain_rows[1], bias_rows[1]).astype(jnp.bfloat16)
    vertical_mixer = product(layernorm_second, vertical_coefficients).astype(jnp.bfloat16)
    everyone = lax.all_gather(vertical_mixer[..., model_width:], "seq", axis=0, tiled=True)
    mixed_values, log_total = column_forward(
        vertical_mixer[..., :model_width],
        everyone[..., :model_width],
        everyone[..., model_width:],
        head_count,
    )
    column_state = (everyone, log_total)
    after_col = after_row + product(mixed_values, w_col_out)
    normal_c = normed(after_col, gain_rows[2], bias_rows[2]).astype(jnp.bfloat16)
    upward = product(normal_c, w_up)
    hidden = gelu_exact(upward).astype(jnp.bfloat16)
    result = after_col + product(hidden, w_down)
    kept_state = (
        source_rows,
        layernorm_first,
        horizontal_mixer,
        logits,
        blended_lines,
        after_row,
        layernorm_second,
        vertical_mixer,
        column_state,
        mixed_values,
        after_col,
        normal_c,
        upward,
        hidden,
    )
    return (result.astype(jnp.bfloat16), disorder_cost, kept_state)


def layer_backward(kept_state, family_residues, grad_result, projection_tables, head_count):
    (
        horizontal_coefficients,
        w_row_out,
        vertical_coefficients,
        w_col_out,
        w_up,
        w_down,
        gain_rows,
        bias_rows,
    ) = projection_tables
    (
        source_rows,
        layernorm_first,
        horizontal_mixer,
        logits,
        blended_lines,
        after_row,
        layernorm_second,
        vertical_mixer,
        column_state,
        mixed_values,
        after_col,
        normal_c,
        upward,
        hidden,
    ) = kept_state
    row_count, columns, model_width = source_rows.shape
    total_rows = row_count * lax.axis_size("seq")
    grad_branch_ffn = grad_result.astype(jnp.bfloat16)
    grad_hidden = product_back(grad_branch_ffn, w_down)
    grad_upward = jax.vjp(gelu_exact, upward)[1](grad_hidden)[0].astype(jnp.bfloat16)
    grad_normal_c = product_back(grad_upward, w_up)
    from_norm, gain_last, bias_last = jax.vjp(normed, after_col, gain_rows[2], bias_rows[2])[1](
        grad_normal_c
    )
    grad_col = grad_result + from_norm
    grad_branch_col = grad_col.astype(jnp.bfloat16)
    grad_attended = product_back(grad_branch_col, w_col_out).astype(jnp.bfloat16)
    everyone, log_total = column_state
    grad_query_col, grad_key_col, grad_value_col = column_backward(
        vertical_mixer[..., :model_width],
        everyone[..., :model_width],
        everyone[..., model_width:],
        log_total,
        grad_attended,
        head_count,
    )
    grad_kv_rows = lax.psum_scatter(
        jnp.concatenate([grad_key_col, grad_value_col], axis=-1).astype(jnp.bfloat16),
        "seq",
        scatter_dimension=0,
        tiled=True,
    ).astype(jnp.float32)
    grad_col_proj = jnp.concatenate([grad_query_col, grad_kv_rows], axis=-1).astype(jnp.bfloat16)
    grad_normal_b = product_back(grad_col_proj, vertical_coefficients)
    from_norm, gain_middle, bias_middle = jax.vjp(normed, after_row, gain_rows[1], bias_rows[1])[1](
        grad_normal_b
    )
    grad_row = grad_col + from_norm
    grad_branch_row = grad_row.astype(jnp.bfloat16)
    grad_mixed = split_heads(
        product_back(grad_branch_row, w_row_out).astype(jnp.bfloat16), head_count
    )
    queries, key_rows, content_lines = row_split(horizontal_mixer, model_width, head_count)
    softmax_share = jax.nn.softmax(logits, axis=-1)
    log_probs = jax.nn.log_softmax(logits, axis=-1)
    entropy = -jnp.sum(softmax_share * log_probs, axis=-1)
    partial_value = jnp.einsum(
        "rihe,rjhe->hij", grad_mixed, content_lines, preferred_element_type=jnp.float32
    )
    grad_probs = lax.psum(partial_value.astype(jnp.bfloat16), "seq").astype(jnp.float32)
    grad_values = jnp.einsum(
        "hij,rihe->rjhe",
        softmax_share.astype(jnp.bfloat16),
        grad_mixed,
        preferred_element_type=jnp.float32,
    )
    valid_residues = (jnp.arange(columns, dtype=jnp.int32) < family_residues).astype(jnp.float32)
    column_weight = float(total_rows * columns) * valid_residues / float(head_count * columns)
    grad_logits = softmax_share * (
        grad_probs - jnp.sum(softmax_share * grad_probs, axis=-1, keepdims=True)
    )
    grad_logits = grad_logits - column_weight[None, :, None] * softmax_share * (
        log_probs + entropy[..., None]
    )
    grad_logits = grad_logits.astype(jnp.bfloat16)
    logit_factor = 1.0 / (math.sqrt(model_width // head_count) * math.sqrt(total_rows))
    grad_queries = logit_factor * jnp.einsum(
        "vyp,opvl->oyvl", grad_logits, key_rows, preferred_element_type=jnp.float32
    )
    grad_keys = logit_factor * jnp.einsum(
        "hij,rihe->rjhe", grad_logits, queries, preferred_element_type=jnp.float32
    )
    grad_row_proj = jnp.concatenate(
        [
            grad_queries.reshape(row_count, columns, model_width),
            grad_keys.reshape(row_count, columns, model_width),
            grad_values.reshape(row_count, columns, model_width),
        ],
        axis=-1,
    ).astype(jnp.bfloat16)
    grad_normal_a = product_back(grad_row_proj, horizontal_coefficients)
    from_norm, gain_first, bias_first = jax.vjp(
        normed, source_rows.astype(jnp.float32), gain_rows[0], bias_rows[0]
    )[1](grad_normal_a)
    grad_source = (grad_row + from_norm).astype(jnp.bfloat16)
    operand_pairs = (
        (layernorm_first, grad_row_proj),
        (blended_lines, grad_branch_row),
        (layernorm_second, grad_col_proj),
        (mixed_values, grad_branch_col),
        (normal_c, grad_upward),
        (hidden, grad_branch_ffn),
    )
    norm_grads = (
        jnp.stack([gain_first, gain_middle, gain_last]),
        jnp.stack([bias_first, bias_middle, bias_last]),
    )
    return (grad_source, operand_pairs, norm_grads)


def on_device(
    embedded_families,
    order,
    token_quarter_factor,
    genuine_residue_tally,
    standardizer_scales,
    standardizer_offsets,
    row_qkv,
    row_out,
    col_qkv,
    col_out,
    ffn_up,
    ffn_down,
    upstream_sensitivity,
):
    head_count = HEAD_TALLY
    segment_place = lax.axis_index("pipe")
    gathered = (
        lax.all_gather(row_qkv, "seq", axis=1, tiled=True),
        lax.all_gather(row_out, "seq", axis=1, tiled=True),
        lax.all_gather(col_qkv, "seq", axis=1, tiled=True),
        lax.all_gather(col_out, "seq", axis=1, tiled=True),
        lax.all_gather(ffn_up, "seq", axis=1, tiled=True),
        lax.all_gather(ffn_down, "seq", axis=1, tiled=True),
        lax.all_gather(standardizer_scales.astype(jnp.bfloat16), "seq", axis=2, tiled=True).astype(
            standardizer_scales.dtype
        ),
        lax.all_gather(standardizer_offsets.astype(jnp.bfloat16), "seq", axis=2, tiled=True).astype(
            standardizer_offsets.dtype
        ),
    )
    projection_tables = tuple((gathered_piece[0] for gathered_piece in gathered))
    small_batch_number = embedded_families.shape[0]
    sequence = order[0]
    received = jnp.zeros(embedded_families.shape[1:], jnp.bfloat16)
    results = []
    focus_spread_levies = []
    kept_list = []
    for period in range(small_batch_number + 1):
        slot_here = jnp.clip(period - segment_place, 0, small_batch_number - 1)
        align_here = sequence[slot_here]
        source_rows = jnp.where(segment_place == 0, embedded_families[align_here], received)
        result, disorder_cost, kept_state = layer_forward(
            source_rows, genuine_residue_tally[align_here], projection_tables, head_count
        )
        results.append(result)
        focus_spread_levies.append(disorder_cost)
        kept_list.append(kept_state)
        if period < small_batch_number:
            received = shifted(result, "pipe", 1)
    activations = lax.dynamic_slice_in_dim(jnp.stack(results), segment_place, small_batch_number, 0)
    penalty_output = lax.dynamic_slice_in_dim(
        jnp.stack(focus_spread_levies), segment_place, small_batch_number, 0
    )
    grad_received = jnp.zeros(embedded_families.shape[1:], jnp.bfloat16)
    left_lists = [[] for index in range(6)]
    right_lists = [[] for index in range(6)]
    gain_total = None
    bias_total = None
    grad_sources = []
    for period in range(small_batch_number + 1):
        slot_raw = period - 1 + segment_place
        in_range = jnp.logical_and(slot_raw >= 0, slot_raw < small_batch_number)
        slot_here = jnp.clip(slot_raw, 0, small_batch_number - 1)
        align_here = sequence[slot_here]
        kept_state = choose(
            segment_place == 0,
            kept_list[max(period - 1, 0)],
            kept_list[min(period + 1, small_batch_number)],
        )
        outgrad = (
            upstream_sensitivity[slot_here].astype(jnp.float32)
            * token_quarter_factor[align_here].astype(jnp.float32)[..., None]
            * 0.25
        )
        incoming_grad = jnp.where(segment_place == 1, outgrad, grad_received.astype(jnp.float32))
        grad_source, operand_pairs, norm_grads = layer_backward(
            kept_state,
            genuine_residue_tally[align_here],
            incoming_grad,
            projection_tables,
            head_count,
        )
        for index in range(6):
            left_lists[index].append(operand_pairs[index][0])
            right_lists[index].append(
                jnp.where(
                    in_range, operand_pairs[index][1], jnp.zeros_like(operand_pairs[index][1])
                )
            )
        gain_term = jnp.where(in_range, norm_grads[0], jnp.zeros_like(norm_grads[0]))
        bias_term = jnp.where(in_range, norm_grads[1], jnp.zeros_like(norm_grads[1]))
        gain_total = gain_term if gain_total is None else gain_total + gain_term
        bias_total = bias_term if bias_total is None else bias_total + bias_term
        grad_sources.append(grad_source)
        if period < small_batch_number:
            grad_received = shifted(grad_source, "pipe", -1)
    block_entry_derivs = lax.dynamic_slice_in_dim(
        jnp.stack(grad_sources), 1 - segment_place, small_batch_number, 0
    )
    weight_totals = [
        weight_term(
            jnp.concatenate(left_lists[index], axis=0), jnp.concatenate(right_lists[index], axis=0)
        )
        for index in range(6)
    ]
    shared = (
        lax.psum_scatter(
            weight_totals[0].astype(jnp.bfloat16), "seq", scatter_dimension=0, tiled=True
        ).astype(jnp.float32),
        lax.psum_scatter(
            weight_totals[1].astype(jnp.bfloat16), "seq", scatter_dimension=0, tiled=True
        ).astype(jnp.float32),
        lax.psum_scatter(
            weight_totals[2].astype(jnp.bfloat16), "seq", scatter_dimension=0, tiled=True
        ).astype(jnp.float32),
        lax.psum_scatter(
            weight_totals[3].astype(jnp.bfloat16), "seq", scatter_dimension=0, tiled=True
        ).astype(jnp.float32),
        lax.psum_scatter(
            weight_totals[4].astype(jnp.bfloat16), "seq", scatter_dimension=0, tiled=True
        ).astype(jnp.float32),
        lax.psum_scatter(
            weight_totals[5].astype(jnp.bfloat16), "seq", scatter_dimension=0, tiled=True
        ).astype(jnp.float32),
        lax.psum_scatter(
            gain_total.astype(jnp.bfloat16), "seq", scatter_dimension=1, tiled=True
        ).astype(jnp.float32),
        lax.psum_scatter(
            bias_total.astype(jnp.bfloat16), "seq", scatter_dimension=1, tiled=True
        ).astype(jnp.float32),
    )
    (
        shared_row_qkv,
        shared_row_out,
        shared_col_qkv,
        shared_col_out,
        shared_up,
        shared_down,
        shared_gain,
        shared_bias,
    ) = shared
    summed = (
        lax.psum(shared_row_qkv.astype(jnp.bfloat16), "dp").astype(jnp.float32),
        lax.psum(shared_row_out.astype(jnp.bfloat16), "dp").astype(jnp.float32),
        lax.psum(shared_col_qkv.astype(jnp.bfloat16), "dp").astype(jnp.float32),
        lax.psum(shared_col_out.astype(jnp.bfloat16), "dp").astype(jnp.float32),
        lax.psum(shared_up.astype(jnp.bfloat16), "dp").astype(jnp.float32),
        lax.psum(shared_down.astype(jnp.bfloat16), "dp").astype(jnp.float32),
        lax.psum(shared_gain.astype(jnp.bfloat16), "dp").astype(jnp.float32),
        lax.psum(shared_bias.astype(jnp.bfloat16), "dp").astype(jnp.float32),
    )
    return (
        activations[None],
        block_entry_derivs[None],
        penalty_output[None],
        summed[0][None],
        summed[1][None],
        summed[2][None],
        summed[3][None],
        summed[4][None],
        summed[5][None],
        summed[6][None],
        summed[7][None],
    )


def place():
    pipe, seq, dp = (lax.axis_index("pipe"), lax.axis_index("seq"), lax.axis_index("dp"))
    core = lax.rem(dp, 2)
    pair = lax.div(dp, 2)
    return (pipe, seq, dp, core, pair)


def neighbours(pipe, seq, dp, core, pair):
    other_core = (pipe, seq, dp + 1 - 2 * core)
    other_pair = (pipe, seq, dp + 2 - 4 * pair)
    return (other_core, other_pair)


def greet(pipe, seq, dp, core, pair):
    barrier = pltpu.get_barrier_semaphore()
    other_core, other_pair = neighbours(pipe, seq, dp, core, pair)
    count = 0
    for step in range(LINE):
        for flip in range(2):
            if step == 0 and flip == 0:
                continue
            where = dp if flip == 0 else dp + 1 - 2 * core
            pl.semaphore_signal(
                barrier,
                inc=1,
                device_id=(pipe, lax.rem(seq + step, LINE), where),
                device_id_type=MESH,
            )
            count += 1
    pl.semaphore_signal(barrier, inc=1, device_id=other_pair, device_id_type=MESH)
    pl.semaphore_wait(barrier, count + 1)


def remote(source, target, send, recv, device):
    return pltpu.make_async_remote_copy(
        src_ref=source,
        dst_ref=target,
        send_sem=send,
        recv_sem=recv,
        device_id=device,
        device_id_type=MESH,
    )


def swap_rows(source, target, send, recv, local, where):
    pipe, seq, dp, core, pair = where
    half, rest = (lax.div(seq, 2), lax.rem(seq, 2))

    def each(action):
        for index in range(2):
            line = 2 * core + index
            here = jnp.logical_and(line == seq, half == core)
            copy = remote(
                source.at[index],
                target.at[rest],
                send.at[index],
                recv.at[rest],
                (pipe, line, dp - core + half),
            )
            arriving = remote(
                source.at[index],
                target.at[index],
                send.at[index],
                recv.at[index],
                (pipe, line, dp - core + half),
            )
            inside = pltpu.make_async_copy(source.at[index], target.at[rest], local)
            action(here, copy, arriving, inside)

    def start(here, copy, arriving, inside):
        pl.when(here)(inside.start)
        pl.when(jnp.logical_not(here))(copy.start)

    def finish(here, copy, arriving, inside):
        pl.when(here)(inside.wait)
        pl.when(jnp.logical_not(here))(copy.wait_send)
        pl.when(jnp.logical_not(here))(arriving.wait_recv)

    return (lambda: each(start), lambda: each(finish))


def gather_kernel(*refs):
    shards, refs = (refs[:6], refs[6:])
    piece, meta, rows = refs[:3]
    wholes, refs = (refs[3:9], refs[9:])
    piece_out, meta_out, rows_out = refs[:3]
    (
        own_sem,
        line_send,
        line_recv,
        pair_send,
        pair_recv,
        core_send,
        core_recv,
        piece_send,
        piece_recv,
        meta_send,
        meta_recv,
        rows_send,
        rows_recv,
    ) = refs[3:]
    where = place()
    pipe, seq, dp, core, pair = where
    other_core, other_pair = neighbours(*where)
    quarter = dp
    greet(*where)
    right, left = ((pipe, seq + 1, dp), (pipe, seq - 1, dp))

    def region(index, source, part):
        depth = shards[index].shape[0]
        share = depth // 4
        start = pl.multiple_of(source * depth + part * share, share)
        return wholes[index].at[pl.ds(start, share)]

    start_piece, finish_piece = swap_rows(
        piece, piece_out, piece_send, piece_recv, own_sem.at[7], where
    )
    start_meta, finish_meta = swap_rows(meta, meta_out, meta_send, meta_recv, own_sem.at[8], where)
    start_meta()
    start_piece()
    row_copies = []
    for step in range(1, LINE):
        target = (pipe, lax.rem(seq + step, LINE), dp)
        copy = remote(rows, rows_out.at[seq], rows_send.at[step - 1], rows_recv.at[seq], target)
        copy.start()
        row_copies.append(copy)
    own = [pltpu.make_async_copy(rows, rows_out.at[seq], own_sem.at[6])]
    for index in range(6):
        depth = shards[index].shape[0]
        own.append(
            pltpu.make_async_copy(
                shards[index],
                wholes[index].at[pl.ds(pl.multiple_of(seq * depth, depth), depth)],
                own_sem.at[index],
            )
        )

    for index in range(6):
        share = shards[index].shape[0] // 4
        mine = shards[index].at[pl.ds(pl.multiple_of(quarter * share, share), share)]

        @pl.when(seq < LINE - 1)
        def _():
            remote(
                mine,
                region(index, seq, quarter),
                line_send.at[0, seq, index],
                line_recv.at[seq, index],
                right,
            ).start()

        @pl.when(seq > 0)
        def _():
            remote(
                mine,
                region(index, seq, quarter),
                line_send.at[1, seq, index],
                line_recv.at[seq, index],
                left,
            ).start()

    for copy in own:
        copy.start()

    def over(kind, source, index, part, target):
        block = region(index, source, part)
        if kind == "pair":
            return remote(
                block, block, pair_send.at[source, index], pair_recv.at[source, index], target
            )
        lane = 0 if kind == "core" else 1
        return remote(
            block,
            block,
            core_send.at[lane, source, index],
            core_recv.at[lane, source, index],
            target,
        )

    def along(source, index, direction, target):
        block = region(index, source, quarter)
        return remote(
            block,
            block,
            line_send.at[direction, source, index],
            line_recv.at[source, index],
            target,
        )

    across = quarter + 2 - 4 * pair
    opposite = quarter + 1 - 2 * core
    opposite_across = across + 1 - 2 * core

    def arrive(step, index):
        for direction in range(2):
            source = seq - step if direction == 0 else seq + step
            present = source >= 0 if direction == 0 else source < LINE
            onward = seq < LINE - 1 if direction == 0 else seq > 0
            target = right if direction == 0 else left

            @pl.when(present)
            def _():
                along(source, index, direction, target).wait_recv()
                over("pair", source, index, quarter, other_pair).start()
                over("core", source, index, quarter, other_core).start()

            @pl.when(jnp.logical_and(present, onward))
            def _():
                along(source, index, direction, target).start()

    def forward(step, index):
        for direction in range(2):
            source = seq - step if direction == 0 else seq + step
            present = source >= 0 if direction == 0 else source < LINE

            @pl.when(present)
            def _():
                over("pair", source, index, across, other_pair).wait_recv()
                over("relay", source, index, across, other_core).start()

    events = [(step, index) for step in range(1, LINE) for index in range(6)]
    lag = 2
    for count in range(len(events) + lag):
        if count < len(events):
            arrive(*events[count])
        if count >= lag:
            forward(*events[count - lag])

    for index in range(6):

        @pl.when(seq < LINE - 1)
        def _():
            along(seq, index, 0, right).wait_send()

        @pl.when(seq > 0)
        def _():
            along(seq, index, 1, left).wait_send()

    for step, index in events:
        for direction in range(2):
            source = seq - step if direction == 0 else seq + step
            present = source >= 0 if direction == 0 else source < LINE
            onward = seq < LINE - 1 if direction == 0 else seq > 0
            target = right if direction == 0 else left

            @pl.when(present)
            def _():
                over("pair", source, index, quarter, other_pair).wait_send()
                over("core", source, index, quarter, other_core).wait_send()
                over("relay", source, index, across, other_core).wait_send()
                over("core", source, index, opposite, other_core).wait_recv()
                over("relay", source, index, opposite_across, other_core).wait_recv()

            @pl.when(jnp.logical_and(present, onward))
            def _():
                along(source, index, direction, target).wait_send()

    for copy in own:
        copy.wait()
    for step in range(1, LINE):
        source = lax.rem(seq + LINE - step, LINE)
        row_copies[step - 1].wait_send()
        remote(
            rows, rows_out.at[source], rows_send.at[step - 1], rows_recv.at[source], other_core
        ).wait_recv()
    finish_meta()
    finish_piece()


def gather_all(shards, piece, meta, rows):
    anywhere = pl.BlockSpec(memory_space=pl.ANY)
    dma = pltpu.SemaphoreType.DMA
    shapes = [
        jax.ShapeDtypeStruct((shard.shape[0] * LINE, shard.shape[1]), shard.dtype)
        for shard in shards
    ]
    shapes += [
        jax.ShapeDtypeStruct(piece.shape, piece.dtype),
        jax.ShapeDtypeStruct(meta.shape, meta.dtype),
        jax.ShapeDtypeStruct((LINE,) + rows.shape, rows.dtype),
    ]
    return pl.pallas_call(
        gather_kernel,
        out_shape=shapes,
        in_specs=[anywhere] * 9,
        out_specs=[anywhere] * 9,
        scratch_shapes=[
            dma((9,)),
            dma((2, LINE, 6)),
            dma((LINE, 6)),
            dma((LINE, 6)),
            dma((LINE, 6)),
            dma((2, LINE, 6)),
            dma((2, LINE, 6)),
            dma((2,)),
            dma((2,)),
            dma((2,)),
            dma((2,)),
            dma((LINE - 1,)),
            dma((LINE,)),
        ],
        compiler_params=pltpu.CompilerParams(collective_id=0, has_side_effects=True),
        name="gather_weights",
    )(*shards, piece, meta, rows)


def reduce_kernel(chunks, paired, *refs):
    grads, vector, first, second, cost = refs[:5]
    out, vector_out, first_out, second_out, cost_out = refs[5:10]
    (
        mine,
        from_core,
        from_pair,
        from_left,
        from_right,
        late_pair,
        vec_core,
        vec_pair,
        vec_line,
        load_sem,
        core_send,
        core_recv,
        pair_send,
        pair_recv,
        line_send,
        left_recv,
        right_recv,
        late_send,
        late_recv,
        share_send,
        share_recv,
        out_sem,
        first_send,
        first_recv,
        second_send,
        second_recv,
        local_sem,
        vec_send,
        vec_recv,
        cost_send,
        cost_recv,
    ) = refs[10:]
    where = place()
    pipe, seq, dp, core, pair = where
    other_core, other_pair = neighbours(*where)
    right, left = ((pipe, seq + 1, dp), (pipe, seq - 1, dp))
    units = LINE * chunks
    depth = mine.shape[2]
    greet(*where)

    def unit_of(number):
        order = lax.div(number, chunks)
        chunk = number - order * chunks
        half = lax.div(order, 2)
        target = jnp.where(lax.rem(order, 2) == 0, LINE - 1 - half, half)
        return (target, chunk)

    def window(chunk):
        return pl.ds(pl.multiple_of(chunk * depth, depth), depth)

    def load(number, side):
        target, chunk = unit_of(number)
        return pltpu.make_async_copy(
            grads.at[target, 2 * side + core, window(chunk)],
            mine.at[number, side],
            load_sem.at[number, side],
        )

    def to_core(number, side):
        target, chunk = unit_of(number)
        return remote(
            grads.at[target, 2 * side + 1 - core, window(chunk)],
            from_core.at[number, side],
            core_send.at[number, side],
            core_recv.at[number, side],
            other_core,
        )

    def issue(number, carry):
        for side in range(2):
            to_core(number, side).start()
            load(number, side).start()
        return carry

    lax.fori_loop(0, units, issue, 0)

    start_first, finish_first = swap_rows(
        first, first_out, first_send, first_recv, local_sem.at[0], where
    )
    start_second, finish_second = swap_rows(
        second, second_out, second_send, second_recv, local_sem.at[1], where
    )
    start_first()
    start_second()

    vec_first = remote(vector, vec_core, vec_send.at[0], vec_recv.at[0], other_core)
    vec_first.start()
    sender = core == lax.div(seq, 2)
    spot = lax.rem(seq, 2)
    cost_own = pltpu.make_async_copy(cost, cost_out.at[spot], local_sem.at[2])
    cost_copies = [
        remote(
            cost,
            cost_out.at[spot],
            cost_send.at[step - 1],
            cost_recv.at[spot],
            (pipe, lax.rem(seq + step, LINE), dp),
        )
        for step in range(1, LINE)
    ]

    @pl.when(sender)
    def _():
        cost_own.start()
        for copy in cost_copies:
            copy.start()

    def add(left_value, right_value):
        return (left_value.astype(jnp.float32) + right_value.astype(jnp.float32)).astype(
            jnp.bfloat16
        )

    def to_pair(number):
        return remote(
            mine.at[number, 1 - pair],
            from_pair.at[number],
            pair_send.at[number],
            pair_recv.at[number],
            other_pair,
        )

    def arrive(number, side):
        load(number, side).wait()
        to_core(number, side).wait_recv()
        mine[number, side] = add(mine[number, side], from_core[number, side])

    def line_copy(number, single, direction):
        target = right if direction == 0 else left
        landing = from_left if direction == 0 else from_right
        sems = left_recv if direction == 0 else right_recv
        if single:
            return remote(
                mine.at[number, pair],
                landing.at[number, 0],
                line_send.at[number],
                sems.at[number],
                target,
            )
        return remote(
            mine.at[number], landing.at[number], line_send.at[number], sems.at[number], target
        )

    def take(number, single, direction):
        landing = from_left if direction == 0 else from_right
        line_copy(number, single, direction).wait_recv()
        if single:
            mine[number, pair] = add(mine[number, pair], landing[number, 0])
        else:
            for side in range(2):
                mine[number, side] = add(mine[number, side], landing[number, side])

    def late_copy(number, chunk, single):
        if single:
            return remote(
                mine.at[number, pair],
                out.at[dp, window(chunk)],
                late_send.at[chunk],
                late_recv.at[chunk],
                other_pair,
            )
        return remote(
            mine.at[number],
            late_pair.at[chunk],
            late_send.at[chunk],
            late_recv.at[chunk],
            other_pair,
        )

    def share_copy(number, chunk, side, relay):
        spot_out = out.at[2 * side + core, window(chunk)]
        return remote(
            spot_out if relay else mine.at[number, side],
            spot_out,
            share_send.at[side, chunk],
            share_recv.at[side, chunk],
            other_core,
        )

    def out_copy(number, chunk, side):
        return pltpu.make_async_copy(
            mine.at[number, side], out.at[2 * side + core, window(chunk)], out_sem.at[side, chunk]
        )

    def at(number, condition, body):
        clipped = jnp.clip(number, 0, units - 1)
        target, chunk = unit_of(clipped)
        valid = jnp.logical_and(number >= 0, number < units)
        valid = jnp.logical_and(valid, condition(target))
        if paired > 0:

            @pl.when(jnp.logical_and(valid, chunk < paired))
            def _():
                body(clipped, chunk, True)

        if paired < chunks:

            @pl.when(jnp.logical_and(valid, chunk >= paired))
            def _():
                body(clipped, chunk, False)

    def first_stage(number, chunk, single):
        if single:
            for half in range(2):
                side = 1 - pair if half == 0 else pair
                arrive(number, side)
                if half == 0:
                    to_pair(number).start()
        else:
            for side in range(2):
                arrive(number, side)

    def second_stage(number, chunk, single):
        if single:
            to_pair(number).wait_recv()
            mine[number, pair] = add(mine[number, pair], from_pair[number])

    def hop(direction):
        def body(number, chunk, single):
            @pl.when(seq > 0 if direction == 0 else seq < LINE - 1)
            def _():
                take(number, single, direction)

            line_copy(number, single, direction).start()

        return body

    def last_stage(number, chunk, single):
        for direction in range(2):

            @pl.when(seq > 0 if direction == 0 else seq < LINE - 1)
            def _():
                take(number, single, direction)

        late_copy(number, chunk, single).start()
        if single:
            out_copy(number, chunk, pair).start()
            share_copy(number, chunk, pair, False).start()

    def share_stage(number, chunk, single):
        if single:
            remote(
                mine.at[number, pair],
                out.at[dp + 2 - 4 * pair, window(chunk)],
                late_send.at[chunk],
                late_recv.at[chunk],
                other_pair,
            ).wait_recv()
            share_copy(number, chunk, 1 - pair, True).start()
        else:
            late_copy(number, chunk, False).wait()
            for side in range(2):
                mine[number, side] = add(mine[number, side], late_pair[chunk, side])
                out_copy(number, chunk, side).start()
                share_copy(number, chunk, side, False).start()

    pair_lag = 2
    always = lambda target: target >= 0
    far = jnp.maximum(seq, LINE - 1 - seq)

    def step(number, carry):
        at(number, always, first_stage)
        at(number - pair_lag, always, second_stage)
        at(number - pair_lag - seq, lambda target: target > seq, hop(0))
        at(number - pair_lag - (LINE - 1 - seq), lambda target: target < seq, hop(1))
        at(number - pair_lag - far, lambda target: target == seq, last_stage)
        at(number - pair_lag - far - pair_lag, lambda target: target == seq, share_stage)
        return carry

    lax.fori_loop(0, units + 2 * pair_lag + LINE - 1, step, 0)

    vec_first.wait()
    vec_core[...] = vector[...] + vec_core[...]
    vec_second = remote(vec_core, vec_pair, vec_send.at[1], vec_recv.at[1], other_pair)
    vec_second.start()
    vec_second.wait()
    vec_pair[...] = vec_core[...] + vec_pair[...]
    for move in range(1, LINE):
        goal = lax.rem(seq + move, LINE)
        remote(
            vec_pair.at[goal],
            vec_line.at[seq],
            vec_send.at[1 + move],
            vec_recv.at[2 + seq],
            (pipe, goal, dp),
        ).start()
    vec_line[seq] = vec_pair[seq]
    for move in range(1, LINE):
        goal = lax.rem(seq + move, LINE)
        source = lax.rem(seq + LINE - move, LINE)
        remote(
            vec_pair.at[goal],
            vec_line.at[source],
            vec_send.at[1 + move],
            vec_recv.at[2 + source],
            (pipe, goal, dp),
        ).wait()
    total = vec_line[0]
    for source in range(1, LINE):
        total = total + vec_line[source]
    vector_out[...] = total

    def drain(number, carry):
        for side in range(2):
            to_core(number, side).wait_send()

        def sends(number, chunk, single):
            if single:
                to_pair(number).wait_send()

        at(number, always, sends)
        at(
            number,
            lambda target: target > seq,
            lambda number, chunk, single: line_copy(number, single, 0).wait_send(),
        )
        at(
            number,
            lambda target: target < seq,
            lambda number, chunk, single: line_copy(number, single, 1).wait_send(),
        )

        def shared(number, chunk, single):
            if single:
                late_copy(number, chunk, True).wait_send()
                out_copy(number, chunk, pair).wait()
                share_copy(number, chunk, pair, False).wait_send()
                share_copy(number, chunk, 1 - pair, True).wait_send()
            else:
                for side in range(2):
                    out_copy(number, chunk, side).wait()
                    share_copy(number, chunk, side, False).wait_send()
            for side in range(2):
                spot_out = out.at[2 * side + 1 - core, window(chunk)]
                remote(
                    spot_out,
                    spot_out,
                    share_send.at[side, chunk],
                    share_recv.at[side, chunk],
                    other_core,
                ).wait_recv()

        at(number, lambda target: target == seq, shared)
        return carry

    lax.fori_loop(0, units, drain, 0)

    @pl.when(sender)
    def _():
        cost_own.wait()
        for copy in cost_copies:
            copy.wait_send()

    for index in range(2):

        @pl.when(2 * core + index != seq)
        def _():
            remote(
                cost, cost_out.at[index], cost_send.at[0], cost_recv.at[index], other_core
            ).wait_recv()

    finish_first()
    finish_second()


def reduce_all(grads, vector, first, second, cost):
    anywhere = pl.BlockSpec(memory_space=pl.ANY)
    inside = pl.BlockSpec(memory_space=pltpu.VMEM)
    dma = pltpu.SemaphoreType.DMA
    chunks, paired = (6, 4)
    rows, columns = grads.shape[2:]
    depth = rows // chunks
    units = LINE * chunks
    block = (depth, columns)
    return pl.pallas_call(
        functools.partial(reduce_kernel, chunks, paired),
        out_shape=[
            jax.ShapeDtypeStruct(grads.shape[1:], grads.dtype),
            jax.ShapeDtypeStruct(vector.shape[1:], vector.dtype),
            jax.ShapeDtypeStruct(first.shape, first.dtype),
            jax.ShapeDtypeStruct(second.shape, second.dtype),
            jax.ShapeDtypeStruct((2,) + cost.shape, cost.dtype),
        ],
        in_specs=[anywhere, inside, anywhere, anywhere, anywhere],
        out_specs=[anywhere, inside, anywhere, anywhere, anywhere],
        scratch_shapes=[
            pltpu.VMEM((units, 2) + block, jnp.bfloat16),
            pltpu.VMEM((units, 2) + block, jnp.bfloat16),
            pltpu.VMEM((units,) + block, jnp.bfloat16),
            pltpu.VMEM((units, 2) + block, jnp.bfloat16),
            pltpu.VMEM((units, 2) + block, jnp.bfloat16),
            pltpu.VMEM((chunks, 2) + block, jnp.bfloat16),
            pltpu.VMEM(vector.shape, jnp.float32),
            pltpu.VMEM(vector.shape, jnp.float32),
            pltpu.VMEM(vector.shape, jnp.float32),
            dma((units, 2)),
            dma((units, 2)),
            dma((units, 2)),
            dma((units,)),
            dma((units,)),
            dma((units,)),
            dma((units,)),
            dma((units,)),
            dma((chunks,)),
            dma((chunks,)),
            dma((2, chunks)),
            dma((2, chunks)),
            dma((2, chunks)),
            dma((2,)),
            dma((2,)),
            dma((2,)),
            dma((2,)),
            dma((3,)),
            dma((2 + LINE,)),
            dma((2 + LINE,)),
            dma((LINE - 1,)),
            dma((2,)),
        ],
        compiler_params=pltpu.CompilerParams(
            collective_id=1, has_side_effects=True, vmem_limit_bytes=60 * 2**20
        ),
        name="reduce_grads",
    )(grads, vector, first, second, cost)


def core_swap(value):
    return lax.ppermute(value, "dp", [(0, 1), (1, 0), (2, 3), (3, 2)])


def chip_forward(source_rows, family_residues, projection_tables, head_count, core):
    (
        horizontal_coefficients,
        w_row_out,
        vertical_coefficients,
        w_col_out,
        w_up,
        w_down,
        gain_rows,
        bias_rows,
    ) = projection_tables
    row_count, columns, model_width = source_rows.shape
    total_rows = 2 * row_count
    start = source_rows.astype(jnp.float32)
    layernorm_first = normed(start, gain_rows[0], bias_rows[0]).astype(jnp.bfloat16)
    horizontal_mixer = product(layernorm_first, horizontal_coefficients).astype(jnp.bfloat16)
    queries, key_rows, content_lines = row_split(horizontal_mixer, model_width, head_count)
    logit_factor = 1.0 / (math.sqrt(model_width // head_count) * math.sqrt(total_rows))
    partial_value = logit_factor * jnp.einsum(
        "rihe,rjhe->hij", queries, key_rows, preferred_element_type=jnp.float32
    )
    partial_value = partial_value.astype(jnp.bfloat16)
    logits = partial_value.astype(jnp.float32) + core_swap(partial_value).astype(jnp.float32)
    softmax_share = jax.nn.softmax(logits, axis=-1)
    log_probs = jax.nn.log_softmax(logits, axis=-1)
    entropy = -jnp.sum(softmax_share * log_probs, axis=-1)
    valid_residues = (jnp.arange(columns, dtype=jnp.int32) < family_residues).astype(jnp.float32)
    disorder_cost = jnp.sum(entropy * valid_residues[None, :]) / float(head_count * columns)
    blended_lines = jnp.einsum(
        "vyp,opvl->oyvl",
        softmax_share.astype(jnp.bfloat16),
        content_lines,
        preferred_element_type=jnp.float32,
    )
    blended_lines = blended_lines.reshape(row_count, columns, model_width).astype(jnp.bfloat16)
    after_row = start + product(blended_lines, w_row_out)
    layernorm_second = normed(after_row, gain_rows[1], bias_rows[1]).astype(jnp.bfloat16)
    vertical_mixer = product(layernorm_second, vertical_coefficients).astype(jnp.bfloat16)
    kept = vertical_mixer[..., model_width:]
    given = core_swap(kept)
    everyone = jnp.concatenate(
        [jnp.where(core == 0, kept, given), jnp.where(core == 0, given, kept)], axis=0
    )
    mixed_values, log_total = column_forward(
        vertical_mixer[..., :model_width],
        everyone[..., :model_width],
        everyone[..., model_width:],
        head_count,
    )
    column_state = (everyone, log_total)
    after_col = after_row + product(mixed_values, w_col_out)
    normal_c = normed(after_col, gain_rows[2], bias_rows[2]).astype(jnp.bfloat16)
    upward = product(normal_c, w_up)
    hidden = gelu_exact(upward).astype(jnp.bfloat16)
    result = after_col + product(hidden, w_down)
    kept_state = (
        source_rows,
        layernorm_first,
        horizontal_mixer,
        logits,
        blended_lines,
        after_row,
        layernorm_second,
        vertical_mixer,
        column_state,
        mixed_values,
        after_col,
        normal_c,
        upward,
        hidden,
    )
    return (result.astype(jnp.bfloat16), disorder_cost, kept_state)


def chip_backward(kept_state, family_residues, grad_result, projection_tables, head_count, core):
    (
        horizontal_coefficients,
        w_row_out,
        vertical_coefficients,
        w_col_out,
        w_up,
        w_down,
        gain_rows,
        bias_rows,
    ) = projection_tables
    (
        source_rows,
        layernorm_first,
        horizontal_mixer,
        logits,
        blended_lines,
        after_row,
        layernorm_second,
        vertical_mixer,
        column_state,
        mixed_values,
        after_col,
        normal_c,
        upward,
        hidden,
    ) = kept_state
    row_count, columns, model_width = source_rows.shape
    total_rows = 2 * row_count
    grad_branch_ffn = grad_result.astype(jnp.bfloat16)
    grad_hidden = product_back(grad_branch_ffn, w_down)
    grad_upward = jax.vjp(gelu_exact, upward)[1](grad_hidden)[0].astype(jnp.bfloat16)
    grad_normal_c = product_back(grad_upward, w_up)
    from_norm, gain_last, bias_last = jax.vjp(normed, after_col, gain_rows[2], bias_rows[2])[1](
        grad_normal_c
    )
    grad_col = grad_result + from_norm
    grad_branch_col = grad_col.astype(jnp.bfloat16)
    grad_attended = product_back(grad_branch_col, w_col_out).astype(jnp.bfloat16)
    everyone, log_total = column_state
    grad_query_col, grad_key_col, grad_value_col = column_backward(
        vertical_mixer[..., :model_width],
        everyone[..., :model_width],
        everyone[..., model_width:],
        log_total,
        grad_attended,
        head_count,
    )
    grad_kv = jnp.concatenate([grad_key_col, grad_value_col], axis=-1).astype(jnp.bfloat16)
    kept = jnp.where(core == 0, grad_kv[:row_count], grad_kv[row_count:])
    given = core_swap(jnp.where(core == 0, grad_kv[row_count:], grad_kv[:row_count]))
    grad_kv_rows = kept.astype(jnp.float32) + given.astype(jnp.float32)
    grad_col_proj = jnp.concatenate([grad_query_col, grad_kv_rows], axis=-1).astype(jnp.bfloat16)
    grad_normal_b = product_back(grad_col_proj, vertical_coefficients)
    from_norm, gain_middle, bias_middle = jax.vjp(normed, after_row, gain_rows[1], bias_rows[1])[1](
        grad_normal_b
    )
    grad_row = grad_col + from_norm
    grad_branch_row = grad_row.astype(jnp.bfloat16)
    grad_mixed = split_heads(
        product_back(grad_branch_row, w_row_out).astype(jnp.bfloat16), head_count
    )
    queries, key_rows, content_lines = row_split(horizontal_mixer, model_width, head_count)
    softmax_share = jax.nn.softmax(logits, axis=-1)
    log_probs = jax.nn.log_softmax(logits, axis=-1)
    entropy = -jnp.sum(softmax_share * log_probs, axis=-1)
    partial_value = jnp.einsum(
        "rihe,rjhe->hij", grad_mixed, content_lines, preferred_element_type=jnp.float32
    ).astype(jnp.bfloat16)
    grad_probs = partial_value.astype(jnp.float32) + core_swap(partial_value).astype(jnp.float32)
    grad_values = jnp.einsum(
        "hij,rihe->rjhe",
        softmax_share.astype(jnp.bfloat16),
        grad_mixed,
        preferred_element_type=jnp.float32,
    )
    valid_residues = (jnp.arange(columns, dtype=jnp.int32) < family_residues).astype(jnp.float32)
    column_weight = float(total_rows * columns) * valid_residues / float(head_count * columns)
    grad_logits = softmax_share * (
        grad_probs - jnp.sum(softmax_share * grad_probs, axis=-1, keepdims=True)
    )
    grad_logits = grad_logits - column_weight[None, :, None] * softmax_share * (
        log_probs + entropy[..., None]
    )
    grad_logits = grad_logits.astype(jnp.bfloat16)
    logit_factor = 1.0 / (math.sqrt(model_width // head_count) * math.sqrt(total_rows))
    grad_queries = logit_factor * jnp.einsum(
        "vyp,opvl->oyvl", grad_logits, key_rows, preferred_element_type=jnp.float32
    )
    grad_keys = logit_factor * jnp.einsum(
        "hij,rihe->rjhe", grad_logits, queries, preferred_element_type=jnp.float32
    )
    grad_row_proj = jnp.concatenate(
        [
            grad_queries.reshape(row_count, columns, model_width),
            grad_keys.reshape(row_count, columns, model_width),
            grad_values.reshape(row_count, columns, model_width),
        ],
        axis=-1,
    ).astype(jnp.bfloat16)
    grad_normal_a = product_back(grad_row_proj, horizontal_coefficients)
    from_norm, gain_first, bias_first = jax.vjp(
        normed, source_rows.astype(jnp.float32), gain_rows[0], bias_rows[0]
    )[1](grad_normal_a)
    grad_source = (grad_row + from_norm).astype(jnp.bfloat16)
    operand_pairs = (
        (layernorm_first, grad_row_proj),
        (blended_lines, grad_branch_row),
        (layernorm_second, grad_col_proj),
        (mixed_values, grad_branch_col),
        (normal_c, grad_upward),
        (hidden, grad_branch_ffn),
    )
    norm_grads = (
        jnp.stack([gain_first, gain_middle, gain_last]),
        jnp.stack([bias_first, bias_middle, bias_last]),
    )
    return (grad_source, operand_pairs, norm_grads)


def packed(term, lanes):
    share = term.shape[0] // (LINE * 4)
    parts = term.reshape(LINE, 4, share, term.shape[1] // lanes, lanes)
    return parts.transpose(0, 1, 3, 2, 4).reshape(LINE, 4, -1, lanes)


def unpacked(block, rows, columns, lanes):
    parts = block.reshape(4, columns // lanes, rows // 4, lanes)
    return parts.transpose(0, 2, 1, 3).reshape(rows, columns).astype(jnp.float32)


def on_device_lined(
    embedded_families,
    order,
    token_quarter_factor,
    genuine_residue_tally,
    standardizer_scales,
    standardizer_offsets,
    row_qkv,
    row_out,
    col_qkv,
    col_out,
    ffn_up,
    ffn_down,
    upstream_sensitivity,
):
    head_count = HEAD_TALLY
    segment_place = lax.axis_index("pipe")
    core = lax.rem(lax.axis_index("dp"), 2)
    sequence = order[0]
    columns, model_width = embedded_families.shape[2:]
    piece = jnp.where(
        segment_place == 0, embedded_families[sequence, 0], upstream_sensitivity[:, 0]
    )
    factor = token_quarter_factor[sequence, 0].astype(jnp.float32) * 0.25
    count = genuine_residue_tally[sequence].astype(jnp.float32)
    meta = jnp.concatenate(
        [
            jnp.broadcast_to(factor[:, :, None], (2, columns, 128)),
            jnp.broadcast_to(count[:, None, None], (2, 8, 128)),
        ],
        axis=1,
    )
    share = standardizer_scales.shape[-1]
    rows = jnp.pad(
        jnp.concatenate([standardizer_scales[0], standardizer_offsets[0]], axis=0),
        ((0, 2), (0, 256 - share)),
    )
    shards = (row_qkv[0], row_out[0], col_qkv[0], col_out[0], ffn_up[0], ffn_down[0])
    *wholes, piece, meta, rows = gather_all(shards, piece, meta, rows)
    rows = rows[:, :6, :share].transpose(1, 0, 2).reshape(6, model_width)
    projection_tables = tuple(wholes) + (rows[:3], rows[3:])
    family_residues = meta[0, columns, 0].astype(jnp.int32)

    early = chip_forward(piece, family_residues, projection_tables, head_count, core)
    received = lax.ppermute(early[0], "pipe", [(0, 1)])
    later = chip_forward(received, family_residues, projection_tables, head_count, core)
    activation, cost, kept_state = choose(segment_place == 0, early, later)

    outgrad = piece.astype(jnp.float32) * meta[:, :columns, :1]
    ahead = chip_backward(kept_state, family_residues, outgrad, projection_tables, head_count, core)
    grad_received = lax.ppermute(ahead[0], "pipe", [(1, 0)]).astype(jnp.float32)
    behind = chip_backward(
        kept_state, family_residues, grad_received, projection_tables, head_count, core
    )
    grad_source, operand_pairs, norm_grads = choose(segment_place == 1, ahead, behind)
    totals = [weight_term(left, right).astype(jnp.bfloat16) for left, right in operand_pairs]
    grads = jnp.concatenate([packed(total, model_width) for total in totals], axis=2)
    vector = jnp.concatenate(norm_grads, axis=0).reshape(6, LINE, share).transpose(1, 0, 2)
    vector = jnp.pad(vector, ((0, 0), (0, 2), (0, 256 - share)))
    out, vector, activations, derivs, costs = reduce_all(
        grads, vector, activation, grad_source, jnp.full((8, 128), cost, jnp.float32)
    )
    results = []
    base = 0
    for shard in shards:
        depth, wide = shard.shape
        length = depth // 4 * (wide // model_width)
        results.append(
            unpacked(out[:, base : base + length], depth, wide, model_width)[None]
        )
        base += length
    return (
        activations[None, :, None],
        derivs[None, :, None],
        costs[:, 0, 0][None],
        *results,
        vector[None, :3, :share],
        vector[None, 3:6, :share],
    )


def solution(mesh):
    in_specs = (
        P("dp", "seq", None, None),
        P("dp", None),
        P("dp", "seq", None),
        P("dp"),
        P("pipe", None, "seq"),
        P("pipe", None, "seq"),
        P("pipe", "seq", None),
        P("pipe", "seq", None),
        P("pipe", "seq", None),
        P("pipe", "seq", None),
        P("pipe", "seq", None),
        P("pipe", "seq", None),
        P("dp", "seq", None, None),
    )
    out_specs = (
        P("pipe", "dp", "seq", None, None),
        P("pipe", "dp", "seq", None, None),
        P("pipe", "dp"),
        P("pipe", "seq", None),
        P("pipe", "seq", None),
        P("pipe", "seq", None),
        P("pipe", "seq", None),
        P("pipe", "seq", None),
        P("pipe", "seq", None),
        P("pipe", None, "seq"),
        P("pipe", None, "seq"),
    )
    lined = mesh.shape["seq"] == LINE and mesh.shape["dp"] == 4 and mesh.shape["pipe"] == 2
    return jax.shard_map(
        on_device_lined if lined else on_device, mesh=mesh, in_specs=in_specs, out_specs=out_specs, check_vma=False
    )
```

```python
import functools
import math

import jax
import jax.numpy as jnp
from jax import lax
from jax.experimental import pallas as pl
from jax.experimental.pallas import tpu as pltpu
from jax.sharding import PartitionSpec as P

HEAD_TALLY = 12
LINE = 4
MESH = pl.DeviceIdType.MESH


norm_epsilon = 1e-05


def shifted(value, axis, steps):
    count = lax.axis_size(axis)
    initial, last = (max(0, -steps), min(count, count - steps))
    return lax.ppermute(value, axis, [(source, source + steps) for source in range(initial, last)])


def normed(values, gain_row, bias_row):
    average = jnp.mean(values, axis=-1, keepdims=True)
    centered = values - average
    variance = jnp.mean(centered * centered, axis=-1, keepdims=True)
    return centered * lax.rsqrt(variance + norm_epsilon) * gain_row + bias_row


def gelu_exact(values):
    return jax.nn.gelu(values, approximate=False)


def product(left, weight):
    return lax.dot_general(
        left, weight, (((left.ndim - 1,), (0,)), ((), ())), preferred_element_type=jnp.float32
    )


def product_back(left, weight):
    return lax.dot_general(
        left, weight, (((left.ndim - 1,), (1,)), ((), ())), preferred_element_type=jnp.float32
    )


def weight_term(left, right):
    return lax.dot_general(
        left, right, (((0, 1), (0, 1)), ((), ())), preferred_element_type=jnp.float32
    )


def split_heads(values, head_count):
    return values.reshape(values.shape[:-1] + (head_count, values.shape[-1] // head_count))


def choose(flag, first_tree, second_tree):
    return jax.tree.map(lambda early, later: jnp.where(flag, early, later), first_tree, second_tree)


def column_scores(queries, key_rows, head_count):
    query_heads = split_heads(queries, head_count)
    raw = jnp.einsum(
        "rche,sche->chrs",
        query_heads,
        split_heads(key_rows, head_count),
        preferred_element_type=jnp.float32,
    )
    return raw / math.sqrt(query_heads.shape[-1])


def column_forward(queries, key_rows, content_lines, head_count):
    scores = column_scores(queries, key_rows, head_count)
    log_total = jax.nn.logsumexp(scores, axis=-1)
    vertical_factors = jnp.exp(scores - log_total[..., None]).astype(jnp.bfloat16)
    mixed_cols = jnp.einsum(
        "gmqi,igmu->qgmu",
        vertical_factors,
        split_heads(content_lines, head_count),
        preferred_element_type=jnp.float32,
    )
    return (mixed_cols.reshape(queries.shape).astype(jnp.bfloat16), log_total)


def column_backward(queries, key_rows, content_lines, log_total, grad_mixed, head_count):
    scores = column_scores(queries, key_rows, head_count)
    softmax_share = jnp.exp(scores - log_total[..., None])
    grad_heads = split_heads(grad_mixed, head_count)
    grad_probs = jnp.einsum(
        "rche,sche->chrs",
        grad_heads,
        split_heads(content_lines, head_count),
        preferred_element_type=jnp.float32,
    )
    grad_values = jnp.einsum(
        "chrs,rche->sche",
        softmax_share.astype(jnp.bfloat16),
        grad_heads,
        preferred_element_type=jnp.float32,
    )
    grad_scores = (
        softmax_share * (grad_probs - jnp.sum(softmax_share * grad_probs, axis=-1, keepdims=True))
    ).astype(jnp.bfloat16)
    root_size = math.sqrt(queries.shape[-1] // head_count)
    grad_queries = (
        jnp.einsum(
            "gmqi,igmu->qgmu",
            grad_scores,
            split_heads(key_rows, head_count),
            preferred_element_type=jnp.float32,
        )
        / root_size
    )
    grad_keys = (
        jnp.einsum(
            "chrs,rche->sche",
            grad_scores,
            split_heads(queries, head_count),
            preferred_element_type=jnp.float32,
        )
        / root_size
    )
    return (
        grad_queries.reshape(queries.shape),
        grad_keys.reshape(key_rows.shape),
        grad_values.reshape(content_lines.shape),
    )


def row_split(horizontal_mixer, model_width, head_count):
    queries = split_heads(horizontal_mixer[..., :model_width], head_count)
    key_rows = split_heads(horizontal_mixer[..., model_width : 2 * model_width], head_count)
    content_lines = split_heads(horizontal_mixer[..., 2 * model_width :], head_count)
    return (queries, key_rows, content_lines)


def layer_forward(source_rows, family_residues, projection_tables, head_count):
    (
        horizontal_coefficients,
        w_row_out,
        vertical_coefficients,
        w_col_out,
        w_up,
        w_down,
        gain_rows,
        bias_rows,
    ) = projection_tables
    row_count, columns, model_width = source_rows.shape
    total_rows = row_count * lax.axis_size("seq")
    start = source_rows.astype(jnp.float32)
    layernorm_first = normed(start, gain_rows[0], bias_rows[0]).astype(jnp.bfloat16)
    horizontal_mixer = product(layernorm_first, horizontal_coefficients).astype(jnp.bfloat16)
    queries, key_rows, content_lines = row_split(horizontal_mixer, model_width, head_count)
    logit_factor = 1.0 / (math.sqrt(model_width // head_count) * math.sqrt(total_rows))
    partial_value = logit_factor * jnp.einsum(
        "rihe,rjhe->hij", queries, key_rows, preferred_element_type=jnp.float32
    )
    logits = lax.psum(partial_value.astype(jnp.bfloat16), "seq").astype(jnp.float32)
    softmax_share = jax.nn.softmax(logits, axis=-1)
    log_probs = jax.nn.log_softmax(logits, axis=-1)
    entropy = -jnp.sum(softmax_share * log_probs, axis=-1)
    valid_residues = (jnp.arange(columns, dtype=jnp.int32) < family_residues).astype(jnp.float32)
    disorder_cost = jnp.sum(entropy * valid_residues[None, :]) / float(head_count * columns)
    blended_lines = jnp.einsum(
        "vyp,opvl->oyvl",
        softmax_share.astype(jnp.bfloat16),
        content_lines,
        preferred_element_type=jnp.float32,
    )
    blended_lines = blended_lines.reshape(row_count, columns, model_width).astype(jnp.bfloat16)
    after_row = start + product(blended_lines, w_row_out)
    layernorm_second = normed(after_row, gain_rows[1], bias_rows[1]).astype(jnp.bfloat16)
    vertical_mixer = product(layernorm_second, vertical_coefficients).astype(jnp.bfloat16)
    everyone = lax.all_gather(vertical_mixer[..., model_width:], "seq", axis=0, tiled=True)
    mixed_values, log_total = column_forward(
        vertical_mixer[..., :model_width],
        everyone[..., :model_width],
        everyone[..., model_width:],
        head_count,
    )
    column_state = (everyone, log_total)
    after_col = after_row + product(mixed_values, w_col_out)
    normal_c = normed(after_col, gain_rows[2], bias_rows[2]).astype(jnp.bfloat16)
    upward = product(normal_c, w_up)
    hidden = gelu_exact(upward).astype(jnp.bfloat16)
    result = after_col + product(hidden, w_down)
    kept_state = (
        source_rows,
        layernorm_first,
        horizontal_mixer,
        logits,
        blended_lines,
        after_row,
        layernorm_second,
        vertical_mixer,
        column_state,
        mixed_values,
        after_col,
        normal_c,
        upward,
        hidden,
    )
    return (result.astype(jnp.bfloat16), disorder_cost, kept_state)


def layer_backward(kept_state, family_residues, grad_result, projection_tables, head_count):
    (
        horizontal_coefficients,
        w_row_out,
        vertical_coefficients,
        w_col_out,
        w_up,
        w_down,
        gain_rows,
        bias_rows,
    ) = projection_tables
    (
        source_rows,
        layernorm_first,
        horizontal_mixer,
        logits,
        blended_lines,
        after_row,
        layernorm_second,
        vertical_mixer,
        column_state,
        mixed_values,
        after_col,
        normal_c,
        upward,
        hidden,
    ) = kept_state
    row_count, columns, model_width = source_rows.shape
    total_rows = row_count * lax.axis_size("seq")
    grad_branch_ffn = grad_result.astype(jnp.bfloat16)
    grad_hidden = product_back(grad_branch_ffn, w_down)
    grad_upward = jax.vjp(gelu_exact, upward)[1](grad_hidden)[0].astype(jnp.bfloat16)
    grad_normal_c = product_back(grad_upward, w_up)
    from_norm, gain_last, bias_last = jax.vjp(normed, after_col, gain_rows[2], bias_rows[2])[1](
        grad_normal_c
    )
    grad_col = grad_result + from_norm
    grad_branch_col = grad_col.astype(jnp.bfloat16)
    grad_attended = product_back(grad_branch_col, w_col_out).astype(jnp.bfloat16)
    everyone, log_total = column_state
    grad_query_col, grad_key_col, grad_value_col = column_backward(
        vertical_mixer[..., :model_width],
        everyone[..., :model_width],
        everyone[..., model_width:],
        log_total,
        grad_attended,
        head_count,
    )
    grad_kv_rows = lax.psum_scatter(
        jnp.concatenate([grad_key_col, grad_value_col], axis=-1).astype(jnp.bfloat16),
        "seq",
        scatter_dimension=0,
        tiled=True,
    ).astype(jnp.float32)
    grad_col_proj = jnp.concatenate([grad_query_col, grad_kv_rows], axis=-1).astype(jnp.bfloat16)
    grad_normal_b = product_back(grad_col_proj, vertical_coefficients)
    from_norm, gain_middle, bias_middle = jax.vjp(normed, after_row, gain_rows[1], bias_rows[1])[1](
        grad_normal_b
    )
    grad_row = grad_col + from_norm
    grad_branch_row = grad_row.astype(jnp.bfloat16)
    grad_mixed = split_heads(
        product_back(grad_branch_row, w_row_out).astype(jnp.bfloat16), head_count
    )
    queries, key_rows, content_lines = row_split(horizontal_mixer, model_width, head_count)
    softmax_share = jax.nn.softmax(logits, axis=-1)
    log_probs = jax.nn.log_softmax(logits, axis=-1)
    entropy = -jnp.sum(softmax_share * log_probs, axis=-1)
    partial_value = jnp.einsum(
        "rihe,rjhe->hij", grad_mixed, content_lines, preferred_element_type=jnp.float32
    )
    grad_probs = lax.psum(partial_value.astype(jnp.bfloat16), "seq").astype(jnp.float32)
    grad_values = jnp.einsum(
        "hij,rihe->rjhe",
        softmax_share.astype(jnp.bfloat16),
        grad_mixed,
        preferred_element_type=jnp.float32,
    )
    valid_residues = (jnp.arange(columns, dtype=jnp.int32) < family_residues).astype(jnp.float32)
    column_weight = float(total_rows * columns) * valid_residues / float(head_count * columns)
    grad_logits = softmax_share * (
        grad_probs - jnp.sum(softmax_share * grad_probs, axis=-1, keepdims=True)
    )
    grad_logits = grad_logits - column_weight[None, :, None] * softmax_share * (
        log_probs + entropy[..., None]
    )
    grad_logits = grad_logits.astype(jnp.bfloat16)
    logit_factor = 1.0 / (math.sqrt(model_width // head_count) * math.sqrt(total_rows))
    grad_queries = logit_factor * jnp.einsum(
        "vyp,opvl->oyvl", grad_logits, key_rows, preferred_element_type=jnp.float32
    )
    grad_keys = logit_factor * jnp.einsum(
        "hij,rihe->rjhe", grad_logits, queries, preferred_element_type=jnp.float32
    )
    grad_row_proj = jnp.concatenate(
        [
            grad_queries.reshape(row_count, columns, model_width),
            grad_keys.reshape(row_count, columns, model_width),
            grad_values.reshape(row_count, columns, model_width),
        ],
        axis=-1,
    ).astype(jnp.bfloat16)
    grad_normal_a = product_back(grad_row_proj, horizontal_coefficients)
    from_norm, gain_first, bias_first = jax.vjp(
        normed, source_rows.astype(jnp.float32), gain_rows[0], bias_rows[0]
    )[1](grad_normal_a)
    grad_source = (grad_row + from_norm).astype(jnp.bfloat16)
    operand_pairs = (
        (layernorm_first, grad_row_proj),
        (blended_lines, grad_branch_row),
        (layernorm_second, grad_col_proj),
        (mixed_values, grad_branch_col),
        (normal_c, grad_upward),
        (hidden, grad_branch_ffn),
    )
    norm_grads = (
        jnp.stack([gain_first, gain_middle, gain_last]),
        jnp.stack([bias_first, bias_middle, bias_last]),
    )
    return (grad_source, operand_pairs, norm_grads)


def on_device(
    embedded_families,
    order,
    token_quarter_factor,
    genuine_residue_tally,
    standardizer_scales,
    standardizer_offsets,
    row_qkv,
    row_out,
    col_qkv,
    col_out,
    ffn_up,
    ffn_down,
    upstream_sensitivity,
):
    head_count = HEAD_TALLY
    segment_place = lax.axis_index("pipe")
    gathered = (
        lax.all_gather(row_qkv, "seq", axis=1, tiled=True),
        lax.all_gather(row_out, "seq", axis=1, tiled=True),
        lax.all_gather(col_qkv, "seq", axis=1, tiled=True),
        lax.all_gather(col_out, "seq", axis=1, tiled=True),
        lax.all_gather(ffn_up, "seq", axis=1, tiled=True),
        lax.all_gather(ffn_down, "seq", axis=1, tiled=True),
        lax.all_gather(standardizer_scales.astype(jnp.bfloat16), "seq", axis=2, tiled=True).astype(
            standardizer_scales.dtype
        ),
        lax.all_gather(standardizer_offsets.astype(jnp.bfloat16), "seq", axis=2, tiled=True).astype(
            standardizer_offsets.dtype
        ),
    )
    projection_tables = tuple((gathered_piece[0] for gathered_piece in gathered))
    small_batch_number = embedded_families.shape[0]
    sequence = order[0]
    received = jnp.zeros(embedded_families.shape[1:], jnp.bfloat16)
    results = []
    focus_spread_levies = []
    kept_list = []
    for period in range(small_batch_number + 1):
        slot_here = jnp.clip(period - segment_place, 0, small_batch_number - 1)
        align_here = sequence[slot_here]
        source_rows = jnp.where(segment_place == 0, embedded_families[align_here], received)
        result, disorder_cost, kept_state = layer_forward(
            source_rows, genuine_residue_tally[align_here], projection_tables, head_count
        )
        results.append(result)
        focus_spread_levies.append(disorder_cost)
        kept_list.append(kept_state)
        if period < small_batch_number:
            received = shifted(result, "pipe", 1)
    activations = lax.dynamic_slice_in_dim(jnp.stack(results), segment_place, small_batch_number, 0)
    penalty_output = lax.dynamic_slice_in_dim(
        jnp.stack(focus_spread_levies), segment_place, small_batch_number, 0
    )
    grad_received = jnp.zeros(embedded_families.shape[1:], jnp.bfloat16)
    left_lists = [[] for index in range(6)]
    right_lists = [[] for index in range(6)]
    gain_total = None
    bias_total = None
    grad_sources = []
    for period in range(small_batch_number + 1):
        slot_raw = period - 1 + segment_place
        in_range = jnp.logical_and(slot_raw >= 0, slot_raw < small_batch_number)
        slot_here = jnp.clip(slot_raw, 0, small_batch_number - 1)
        align_here = sequence[slot_here]
        kept_state = choose(
            segment_place == 0,
            kept_list[max(period - 1, 0)],
            kept_list[min(period + 1, small_batch_number)],
        )
        outgrad = (
            upstream_sensitivity[slot_here].astype(jnp.float32)
            * token_quarter_factor[align_here].astype(jnp.float32)[..., None]
            * 0.25
        )
        incoming_grad = jnp.where(segment_place == 1, outgrad, grad_received.astype(jnp.float32))
        grad_source, operand_pairs, norm_grads = layer_backward(
            kept_state,
            genuine_residue_tally[align_here],
            incoming_grad,
            projection_tables,
            head_count,
        )
        for index in range(6):
            left_lists[index].append(operand_pairs[index][0])
            right_lists[index].append(
                jnp.where(
                    in_range, operand_pairs[index][1], jnp.zeros_like(operand_pairs[index][1])
                )
            )
        gain_term = jnp.where(in_range, norm_grads[0], jnp.zeros_like(norm_grads[0]))
        bias_term = jnp.where(in_range, norm_grads[1], jnp.zeros_like(norm_grads[1]))
        gain_total = gain_term if gain_total is None else gain_total + gain_term
        bias_total = bias_term if bias_total is None else bias_total + bias_term
        grad_sources.append(grad_source)
        if period < small_batch_number:
            grad_received = shifted(grad_source, "pipe", -1)
    block_entry_derivs = lax.dynamic_slice_in_dim(
        jnp.stack(grad_sources), 1 - segment_place, small_batch_number, 0
    )
    weight_totals = [
        weight_term(
            jnp.concatenate(left_lists[index], axis=0), jnp.concatenate(right_lists[index], axis=0)
        )
        for index in range(6)
    ]
    shared = (
        lax.psum_scatter(
            weight_totals[0].astype(jnp.bfloat16), "seq", scatter_dimension=0, tiled=True
        ).astype(jnp.float32),
        lax.psum_scatter(
            weight_totals[1].astype(jnp.bfloat16), "seq", scatter_dimension=0, tiled=True
        ).astype(jnp.float32),
        lax.psum_scatter(
            weight_totals[2].astype(jnp.bfloat16), "seq", scatter_dimension=0, tiled=True
        ).astype(jnp.float32),
        lax.psum_scatter(
            weight_totals[3].astype(jnp.bfloat16), "seq", scatter_dimension=0, tiled=True
        ).astype(jnp.float32),
        lax.psum_scatter(
            weight_totals[4].astype(jnp.bfloat16), "seq", scatter_dimension=0, tiled=True
        ).astype(jnp.float32),
        lax.psum_scatter(
            weight_totals[5].astype(jnp.bfloat16), "seq", scatter_dimension=0, tiled=True
        ).astype(jnp.float32),
        lax.psum_scatter(
            gain_total.astype(jnp.bfloat16), "seq", scatter_dimension=1, tiled=True
        ).astype(jnp.float32),
        lax.psum_scatter(
            bias_total.astype(jnp.bfloat16), "seq", scatter_dimension=1, tiled=True
        ).astype(jnp.float32),
    )
    (
        shared_row_qkv,
        shared_row_out,
        shared_col_qkv,
        shared_col_out,
        shared_up,
        shared_down,
        shared_gain,
        shared_bias,
    ) = shared
    summed = (
        lax.psum(shared_row_qkv.astype(jnp.bfloat16), "dp").astype(jnp.float32),
        lax.psum(shared_row_out.astype(jnp.bfloat16), "dp").astype(jnp.float32),
        lax.psum(shared_col_qkv.astype(jnp.bfloat16), "dp").astype(jnp.float32),
        lax.psum(shared_col_out.astype(jnp.bfloat16), "dp").astype(jnp.float32),
        lax.psum(shared_up.astype(jnp.bfloat16), "dp").astype(jnp.float32),
        lax.psum(shared_down.astype(jnp.bfloat16), "dp").astype(jnp.float32),
        lax.psum(shared_gain.astype(jnp.bfloat16), "dp").astype(jnp.float32),
        lax.psum(shared_bias.astype(jnp.bfloat16), "dp").astype(jnp.float32),
    )
    return (
        activations[None],
        block_entry_derivs[None],
        penalty_output[None],
        summed[0][None],
        summed[1][None],
        summed[2][None],
        summed[3][None],
        summed[4][None],
        summed[5][None],
        summed[6][None],
        summed[7][None],
    )


def place():
    pipe, seq, dp = (lax.axis_index("pipe"), lax.axis_index("seq"), lax.axis_index("dp"))
    core = lax.rem(dp, 2)
    pair = lax.div(dp, 2)
    return (pipe, seq, dp, core, pair)


def neighbours(pipe, seq, dp, core, pair):
    other_core = (pipe, seq, dp + 1 - 2 * core)
    other_pair = (pipe, seq, dp + 2 - 4 * pair)
    return (other_core, other_pair)


def greet(pipe, seq, dp, core, pair):
    barrier = pltpu.get_barrier_semaphore()
    other_core, other_pair = neighbours(pipe, seq, dp, core, pair)
    count = 0
    for step in range(LINE):
        for flip in range(2):
            if step == 0 and flip == 0:
                continue
            where = dp if flip == 0 else dp + 1 - 2 * core
            pl.semaphore_signal(
                barrier,
                inc=1,
                device_id=(pipe, lax.rem(seq + step, LINE), where),
                device_id_type=MESH,
            )
            count += 1
    pl.semaphore_signal(barrier, inc=1, device_id=other_pair, device_id_type=MESH)
    pl.semaphore_wait(barrier, count + 1)


def remote(source, target, send, recv, device):
    return pltpu.make_async_remote_copy(
        src_ref=source,
        dst_ref=target,
        send_sem=send,
        recv_sem=recv,
        device_id=device,
        device_id_type=MESH,
    )


def swap_rows(source, target, send, recv, local, where):
    pipe, seq, dp, core, pair = where
    half, rest = (lax.div(seq, 2), lax.rem(seq, 2))

    def each(action):
        for index in range(2):
            line = 2 * core + index
            here = jnp.logical_and(line == seq, half == core)
            copy = remote(
                source.at[index],
                target.at[rest],
                send.at[index],
                recv.at[rest],
                (pipe, line, dp - core + half),
            )
            arriving = remote(
                source.at[index],
                target.at[index],
                send.at[index],
                recv.at[index],
                (pipe, line, dp - core + half),
            )
            inside = pltpu.make_async_copy(source.at[index], target.at[rest], local)
            action(here, copy, arriving, inside)

    def start(here, copy, arriving, inside):
        pl.when(here)(inside.start)
        pl.when(jnp.logical_not(here))(copy.start)

    def finish(here, copy, arriving, inside):
        pl.when(here)(inside.wait)
        pl.when(jnp.logical_not(here))(copy.wait_send)
        pl.when(jnp.logical_not(here))(arriving.wait_recv)

    return (lambda: each(start), lambda: each(finish))


def gather_kernel(*refs):
    shards, refs = (refs[:6], refs[6:])
    piece, meta, rows = refs[:3]
    wholes, refs = (refs[3:9], refs[9:])
    piece_out, meta_out, rows_out = refs[:3]
    (
        own_sem,
        line_send,
        line_recv,
        pair_send,
        pair_recv,
        core_send,
        core_recv,
        piece_send,
        piece_recv,
        meta_send,
        meta_recv,
        rows_send,
        rows_recv,
    ) = refs[3:]
    where = place()
    pipe, seq, dp, core, pair = where
    other_core, other_pair = neighbours(*where)
    quarter = dp
    greet(*where)
    right, left = ((pipe, seq + 1, dp), (pipe, seq - 1, dp))

    def region(index, source, part):
        depth = shards[index].shape[0]
        share = depth // 4
        start = pl.multiple_of(source * depth + part * share, share)
        return wholes[index].at[pl.ds(start, share)]

    start_piece, finish_piece = swap_rows(
        piece, piece_out, piece_send, piece_recv, own_sem.at[7], where
    )
    start_meta, finish_meta = swap_rows(meta, meta_out, meta_send, meta_recv, own_sem.at[8], where)
    start_meta()
    start_piece()
    row_copies = []
    for step in range(1, LINE):
        target = (pipe, lax.rem(seq + step, LINE), dp)
        copy = remote(rows, rows_out.at[seq], rows_send.at[step - 1], rows_recv.at[seq], target)
        copy.start()
        row_copies.append(copy)
    own = [pltpu.make_async_copy(rows, rows_out.at[seq], own_sem.at[6])]
    for index in range(6):
        depth = shards[index].shape[0]
        own.append(
            pltpu.make_async_copy(
                shards[index],
                wholes[index].at[pl.ds(pl.multiple_of(seq * depth, depth), depth)],
                own_sem.at[index],
            )
        )

    for index in range(6):
        share = shards[index].shape[0] // 4
        mine = shards[index].at[pl.ds(pl.multiple_of(quarter * share, share), share)]

        @pl.when(seq < LINE - 1)
        def _():
            remote(
                mine,
                region(index, seq, quarter),
                line_send.at[0, seq, index],
                line_recv.at[seq, index],
                right,
            ).start()

        @pl.when(seq > 0)
        def _():
            remote(
                mine,
                region(index, seq, quarter),
                line_send.at[1, seq, index],
                line_recv.at[seq, index],
                left,
            ).start()

    for copy in own:
        copy.start()

    def over(kind, source, index, part, target):
        block = region(index, source, part)
        if kind == "pair":
            return remote(
                block, block, pair_send.at[source, index], pair_recv.at[source, index], target
            )
        lane = 0 if kind == "core" else 1
        return remote(
            block,
            block,
            core_send.at[lane, source, index],
            core_recv.at[lane, source, index],
            target,
        )

    def along(source, index, direction, target):
        block = region(index, source, quarter)
        return remote(
            block,
            block,
            line_send.at[direction, source, index],
            line_recv.at[source, index],
            target,
        )

    across = quarter + 2 - 4 * pair
    opposite = quarter + 1 - 2 * core
    opposite_across = across + 1 - 2 * core

    def arrive(step, index):
        for direction in range(2):
            source = seq - step if direction == 0 else seq + step
            present = source >= 0 if direction == 0 else source < LINE
            onward = seq < LINE - 1 if direction == 0 else seq > 0
            target = right if direction == 0 else left

            @pl.when(present)
            def _():
                along(source, index, direction, target).wait_recv()
                over("pair", source, index, quarter, other_pair).start()
                over("core", source, index, quarter, other_core).start()

            @pl.when(jnp.logical_and(present, onward))
            def _():
                along(source, index, direction, target).start()

    def forward(step, index):
        for direction in range(2):
            source = seq - step if direction == 0 else seq + step
            present = source >= 0 if direction == 0 else source < LINE

            @pl.when(present)
            def _():
                over("pair", source, index, across, other_pair).wait_recv()
                over("relay", source, index, across, other_core).start()

    events = [(step, index) for step in range(1, LINE) for index in range(6)]
    lag = 2
    for count in range(len(events) + lag):
        if count < len(events):
            arrive(*events[count])
        if count >= lag:
            forward(*events[count - lag])

    for index in range(6):

        @pl.when(seq < LINE - 1)
        def _():
            along(seq, index, 0, right).wait_send()

        @pl.when(seq > 0)
        def _():
            along(seq, index, 1, left).wait_send()

    for step, index in events:
        for direction in range(2):
            source = seq - step if direction == 0 else seq + step
            present = source >= 0 if direction == 0 else source < LINE
            onward = seq < LINE - 1 if direction == 0 else seq > 0
            target = right if direction == 0 else left

            @pl.when(present)
            def _():
                over("pair", source, index, quarter, other_pair).wait_send()
                over("core", source, index, quarter, other_core).wait_send()
                over("relay", source, index, across, other_core).wait_send()
                over("core", source, index, opposite, other_core).wait_recv()
                over("relay", source, index, opposite_across, other_core).wait_recv()

            @pl.when(jnp.logical_and(present, onward))
            def _():
                along(source, index, direction, target).wait_send()

    for copy in own:
        copy.wait()
    for step in range(1, LINE):
        source = lax.rem(seq + LINE - step, LINE)
        row_copies[step - 1].wait_send()
        remote(
            rows, rows_out.at[source], rows_send.at[step - 1], rows_recv.at[source], other_core
        ).wait_recv()
    finish_meta()
    finish_piece()


def gather_all(shards, piece, meta, rows):
    anywhere = pl.BlockSpec(memory_space=pl.ANY)
    dma = pltpu.SemaphoreType.DMA
    shapes = [
        jax.ShapeDtypeStruct((shard.shape[0] * LINE, shard.shape[1]), shard.dtype)
        for shard in shards
    ]
    shapes += [
        jax.ShapeDtypeStruct(piece.shape, piece.dtype),
        jax.ShapeDtypeStruct(meta.shape, meta.dtype),
        jax.ShapeDtypeStruct((LINE,) + rows.shape, rows.dtype),
    ]
    return pl.pallas_call(
        gather_kernel,
        out_shape=shapes,
        in_specs=[anywhere] * 9,
        out_specs=[anywhere] * 9,
        scratch_shapes=[
            dma((9,)),
            dma((2, LINE, 6)),
            dma((LINE, 6)),
            dma((LINE, 6)),
            dma((LINE, 6)),
            dma((2, LINE, 6)),
            dma((2, LINE, 6)),
            dma((2,)),
            dma((2,)),
            dma((2,)),
            dma((2,)),
            dma((LINE - 1,)),
            dma((LINE,)),
        ],
        compiler_params=pltpu.CompilerParams(collective_id=0, has_side_effects=True),
        name="gather_weights",
    )(*shards, piece, meta, rows)


def reduce_kernel(chunks, paired, *refs):
    grads, vector, first, second, cost = refs[:5]
    out, vector_out, first_out, second_out, cost_out = refs[5:10]
    (
        mine,
        from_core,
        from_pair,
        from_left,
        from_right,
        late_pair,
        vec_core,
        vec_pair,
        vec_line,
        load_sem,
        core_send,
        core_recv,
        pair_send,
        pair_recv,
        line_send,
        left_recv,
        right_recv,
        late_send,
        late_recv,
        share_send,
        share_recv,
        out_sem,
        first_send,
        first_recv,
        second_send,
        second_recv,
        local_sem,
        vec_send,
        vec_recv,
        cost_send,
        cost_recv,
    ) = refs[10:]
    where = place()
    pipe, seq, dp, core, pair = where
    other_core, other_pair = neighbours(*where)
    right, left = ((pipe, seq + 1, dp), (pipe, seq - 1, dp))
    units = LINE * chunks
    depth = mine.shape[2]
    greet(*where)

    def unit_of(number):
        order = lax.div(number, chunks)
        chunk = number - order * chunks
        half = lax.div(order, 2)
        target = jnp.where(lax.rem(order, 2) == 0, LINE - 1 - half, half)
        return (target, chunk)

    def window(chunk):
        return pl.ds(pl.multiple_of(chunk * depth, depth), depth)

    def load(number, side):
        target, chunk = unit_of(number)
        return pltpu.make_async_copy(
            grads.at[target, 2 * side + core, window(chunk)],
            mine.at[number, side],
            load_sem.at[number, side],
        )

    def to_core(number, side):
        target, chunk = unit_of(number)
        return remote(
            grads.at[target, 2 * side + 1 - core, window(chunk)],
            from_core.at[number, side],
            core_send.at[number, side],
            core_recv.at[number, side],
            other_core,
        )

    def issue(number, carry):
        for side in range(2):
            to_core(number, side).start()
            load(number, side).start()
        return carry

    lax.fori_loop(0, units, issue, 0)

    start_first, finish_first = swap_rows(
        first, first_out, first_send, first_recv, local_sem.at[0], where
    )
    start_second, finish_second = swap_rows(
        second, second_out, second_send, second_recv, local_sem.at[1], where
    )
    start_first()
    start_second()

    vec_first = remote(vector, vec_core, vec_send.at[0], vec_recv.at[0], other_core)
    vec_first.start()
    sender = core == lax.div(seq, 2)
    spot = lax.rem(seq, 2)
    cost_own = pltpu.make_async_copy(cost, cost_out.at[spot], local_sem.at[2])
    cost_copies = [
        remote(
            cost,
            cost_out.at[spot],
            cost_send.at[step - 1],
            cost_recv.at[spot],
            (pipe, lax.rem(seq + step, LINE), dp),
        )
        for step in range(1, LINE)
    ]

    @pl.when(sender)
    def _():
        cost_own.start()
        for copy in cost_copies:
            copy.start()

    def add(left_value, right_value):
        return (left_value.astype(jnp.float32) + right_value.astype(jnp.float32)).astype(
            jnp.bfloat16
        )

    def to_pair(number):
        return remote(
            mine.at[number, 1 - pair],
            from_pair.at[number],
            pair_send.at[number],
            pair_recv.at[number],
            other_pair,
        )

    def arrive(number, side):
        load(number, side).wait()
        to_core(number, side).wait_recv()
        mine[number, side] = add(mine[number, side], from_core[number, side])

    def line_copy(number, single, direction):
        target = right if direction == 0 else left
        landing = from_left if direction == 0 else from_right
        sems = left_recv if direction == 0 else right_recv
        if single:
            return remote(
                mine.at[number, pair],
                landing.at[number, 0],
                line_send.at[number],
                sems.at[number],
                target,
            )
        return remote(
            mine.at[number], landing.at[number], line_send.at[number], sems.at[number], target
        )

    def take(number, single, direction):
        landing = from_left if direction == 0 else from_right
        line_copy(number, single, direction).wait_recv()
        if single:
            mine[number, pair] = add(mine[number, pair], landing[number, 0])
        else:
            for side in range(2):
                mine[number, side] = add(mine[number, side], landing[number, side])

    def late_copy(number, chunk, single):
        if single:
            return remote(
                mine.at[number, pair],
                out.at[dp, window(chunk)],
                late_send.at[chunk],
                late_recv.at[chunk],
                other_pair,
            )
        return remote(
            mine.at[number],
            late_pair.at[chunk],
            late_send.at[chunk],
            late_recv.at[chunk],
            other_pair,
        )

    def share_copy(number, chunk, side, relay):
        spot_out = out.at[2 * side + core, window(chunk)]
        return remote(
            spot_out if relay else mine.at[number, side],
            spot_out,
            share_send.at[side, chunk],
            share_recv.at[side, chunk],
            other_core,
        )

    def out_copy(number, chunk, side):
        return pltpu.make_async_copy(
            mine.at[number, side], out.at[2 * side + core, window(chunk)], out_sem.at[side, chunk]
        )

    def at(number, condition, body):
        clipped = jnp.clip(number, 0, units - 1)
        target, chunk = unit_of(clipped)
        valid = jnp.logical_and(number >= 0, number < units)
        valid = jnp.logical_and(valid, condition(target))
        if paired > 0:

            @pl.when(jnp.logical_and(valid, chunk < paired))
            def _():
                body(clipped, chunk, True)

        if paired < chunks:

            @pl.when(jnp.logical_and(valid, chunk >= paired))
            def _():
                body(clipped, chunk, False)

    def first_stage(number, chunk, single):
        if single:
            for half in range(2):
                side = 1 - pair if half == 0 else pair
                arrive(number, side)
                if half == 0:
                    to_pair(number).start()
        else:
            for side in range(2):
                arrive(number, side)

    def second_stage(number, chunk, single):
        if single:
            to_pair(number).wait_recv()
            mine[number, pair] = add(mine[number, pair], from_pair[number])

    def hop(direction):
        def body(number, chunk, single):
            @pl.when(seq > 0 if direction == 0 else seq < LINE - 1)
            def _():
                take(number, single, direction)

            line_copy(number, single, direction).start()

        return body

    def last_stage(number, chunk, single):
        for direction in range(2):

            @pl.when(seq > 0 if direction == 0 else seq < LINE - 1)
            def _():
                take(number, single, direction)

        late_copy(number, chunk, single).start()
        if single:
            out_copy(number, chunk, pair).start()
            share_copy(number, chunk, pair, False).start()

    def share_stage(number, chunk, single):
        if single:
            remote(
                mine.at[number, pair],
                out.at[dp + 2 - 4 * pair, window(chunk)],
                late_send.at[chunk],
                late_recv.at[chunk],
                other_pair,
            ).wait_recv()
            share_copy(number, chunk, 1 - pair, True).start()
        else:
            late_copy(number, chunk, False).wait()
            for side in range(2):
                mine[number, side] = add(mine[number, side], late_pair[chunk, side])
                out_copy(number, chunk, side).start()
                share_copy(number, chunk, side, False).start()

    pair_lag = 2
    always = lambda target: target >= 0
    far = jnp.maximum(seq, LINE - 1 - seq)

    def step(number, carry):
        at(number, always, first_stage)
        at(number - pair_lag, always, second_stage)
        at(number - pair_lag - seq, lambda target: target > seq, hop(0))
        at(number - pair_lag - (LINE - 1 - seq), lambda target: target < seq, hop(1))
        at(number - pair_lag - far, lambda target: target == seq, last_stage)
        at(number - pair_lag - far - pair_lag, lambda target: target == seq, share_stage)
        return carry

    lax.fori_loop(0, units + 2 * pair_lag + LINE - 1, step, 0)

    vec_first.wait()
    vec_core[...] = vector[...] + vec_core[...]
    vec_second = remote(vec_core, vec_pair, vec_send.at[1], vec_recv.at[1], other_pair)
    vec_second.start()
    vec_second.wait()
    vec_pair[...] = vec_core[...] + vec_pair[...]
    for move in range(1, LINE):
        goal = lax.rem(seq + move, LINE)
        remote(
            vec_pair.at[goal],
            vec_line.at[seq],
            vec_send.at[1 + move],
            vec_recv.at[2 + seq],
            (pipe, goal, dp),
        ).start()
    vec_line[seq] = vec_pair[seq]
    for move in range(1, LINE):
        goal = lax.rem(seq + move, LINE)
        source = lax.rem(seq + LINE - move, LINE)
        remote(
            vec_pair.at[goal],
            vec_line.at[source],
            vec_send.at[1 + move],
            vec_recv.at[2 + source],
            (pipe, goal, dp),
        ).wait()
    total = vec_line[0]
    for source in range(1, LINE):
        total = total + vec_line[source]
    vector_out[...] = total

    def drain(number, carry):
        for side in range(2):
            to_core(number, side).wait_send()

        def sends(number, chunk, single):
            if single:
                to_pair(number).wait_send()

        at(number, always, sends)
        at(
            number,
            lambda target: target > seq,
            lambda number, chunk, single: line_copy(number, single, 0).wait_send(),
        )
        at(
            number,
            lambda target: target < seq,
            lambda number, chunk, single: line_copy(number, single, 1).wait_send(),
        )

        def shared(number, chunk, single):
            if single:
                late_copy(number, chunk, True).wait_send()
                out_copy(number, chunk, pair).wait()
                share_copy(number, chunk, pair, False).wait_send()
                share_copy(number, chunk, 1 - pair, True).wait_send()
            else:
                for side in range(2):
                    out_copy(number, chunk, side).wait()
                    share_copy(number, chunk, side, False).wait_send()
            for side in range(2):
                spot_out = out.at[2 * side + 1 - core, window(chunk)]
                remote(
                    spot_out,
                    spot_out,
                    share_send.at[side, chunk],
                    share_recv.at[side, chunk],
                    other_core,
                ).wait_recv()

        at(number, lambda target: target == seq, shared)
        return carry

    lax.fori_loop(0, units, drain, 0)

    @pl.when(sender)
    def _():
        cost_own.wait()
        for copy in cost_copies:
            copy.wait_send()

    for index in range(2):

        @pl.when(2 * core + index != seq)
        def _():
            remote(
                cost, cost_out.at[index], cost_send.at[0], cost_recv.at[index], other_core
            ).wait_recv()

    finish_first()
    finish_second()


def reduce_all(grads, vector, first, second, cost):
    anywhere = pl.BlockSpec(memory_space=pl.ANY)
    inside = pl.BlockSpec(memory_space=pltpu.VMEM)
    dma = pltpu.SemaphoreType.DMA
    chunks, paired = (6, 4)
    rows, columns = grads.shape[2:]
    depth = rows // chunks
    units = LINE * chunks
    block = (depth, columns)
    return pl.pallas_call(
        functools.partial(reduce_kernel, chunks, paired),
        out_shape=[
            jax.ShapeDtypeStruct(grads.shape[1:], grads.dtype),
            jax.ShapeDtypeStruct(vector.shape[1:], vector.dtype),
            jax.ShapeDtypeStruct(first.shape, first.dtype),
            jax.ShapeDtypeStruct(second.shape, second.dtype),
            jax.ShapeDtypeStruct((2,) + cost.shape, cost.dtype),
        ],
        in_specs=[anywhere, inside, anywhere, anywhere, anywhere],
        out_specs=[anywhere, inside, anywhere, anywhere, anywhere],
        scratch_shapes=[
            pltpu.VMEM((units, 2) + block, jnp.bfloat16),
            pltpu.VMEM((units, 2) + block, jnp.bfloat16),
            pltpu.VMEM((units,) + block, jnp.bfloat16),
            pltpu.VMEM((units, 2) + block, jnp.bfloat16),
            pltpu.VMEM((units, 2) + block, jnp.bfloat16),
            pltpu.VMEM((chunks, 2) + block, jnp.bfloat16),
            pltpu.VMEM(vector.shape, jnp.float32),
            pltpu.VMEM(vector.shape, jnp.float32),
            pltpu.VMEM(vector.shape, jnp.float32),
            dma((units, 2)),
            dma((units, 2)),
            dma((units, 2)),
            dma((units,)),
            dma((units,)),
            dma((units,)),
            dma((units,)),
            dma((units,)),
            dma((chunks,)),
            dma((chunks,)),
            dma((2, chunks)),
            dma((2, chunks)),
            dma((2, chunks)),
            dma((2,)),
            dma((2,)),
            dma((2,)),
            dma((2,)),
            dma((3,)),
            dma((2 + LINE,)),
            dma((2 + LINE,)),
            dma((LINE - 1,)),
            dma((2,)),
        ],
        compiler_params=pltpu.CompilerParams(
            collective_id=1, has_side_effects=True, vmem_limit_bytes=60 * 2**20
        ),
        name="reduce_grads",
    )(grads, vector, first, second, cost)


def dot(left, right, left_axis, right_axis):
    return lax.dot_general(
        left,
        right,
        (((left_axis,), (right_axis,)), ((), ())),
        preferred_element_type=jnp.float32,
    )


def unit_rows(values):
    average = jnp.mean(values, axis=-1, keepdims=True)
    centered = values - average
    variance = jnp.mean(centered * centered, axis=-1, keepdims=True)
    root = lax.rsqrt(variance + norm_epsilon)
    return (centered * root, root)


def unit_rows_back(grad, values, gain_row):
    unit, root = unit_rows(values)
    scaled = grad * gain_row
    inner = jnp.mean(scaled * unit, axis=-1, keepdims=True)
    term = root * (scaled - jnp.mean(scaled, axis=-1, keepdims=True) - unit * inner)
    gain = jnp.sum(grad * unit, axis=0, keepdims=True)
    bias = jnp.sum(grad, axis=0, keepdims=True)
    return (term, gain, bias)


def layers_kernel(
    entry,
    factor,
    count,
    rows,
    w_row_any,
    w_row_out_any,
    w_col_any,
    w_col_out_any,
    w_up_any,
    w_down_any,
    act,
    der,
    cost,
    vector,
    grads,
    w_row,
    w_row_out,
    w_col,
    w_col_out,
    w_up,
    w_down,
    source,
    normal_a,
    normal_b,
    normal_c,
    mixer,
    mixer_col,
    blended,
    mixed,
    after_row,
    after_col,
    log_share,
    col_share,
    hidden,
    slope,
    total_grad,
    grad_in,
    branch_ffn,
    branch_col,
    branch_row,
    grad_up,
    grad_mixer_col,
    grad_mixer,
    logit_send,
    logit_recv,
    keys_recv,
    keys_send,
    keys_back,
    probs_send,
    probs_recv,
    halves,
    segment,
    spread,
    stage,
    stage_down,
    weight_sem,
    logit_sems,
    keys_sems,
    back_sems,
    probs_sems,
    pipe_sems,
    stage_sems,
):
    pipe, seq, dp, core, pair = place()
    other_core = (pipe, seq, dp + 1 - 2 * core)
    other_pipe = (1 - pipe, seq, dp)
    tokens, width = entry.shape
    columns = tokens // 2
    heads = HEAD_TALLY
    size = width // heads
    twin = 2 * size
    couples = heads // 2
    total_rows = LINE
    bf16, f32 = (jnp.bfloat16, jnp.float32)

    weights = [
        pltpu.make_async_copy(far, near, weight_sem.at[index])
        for index, (far, near) in enumerate(
            (
                (w_row_any, w_row),
                (w_row_out_any, w_row_out),
                (w_col_any, w_col),
                (w_col_out_any, w_col_out),
                (w_up_any, w_up),
                (w_down_any, w_down),
            )
        )
    ]
    for copy in weights:
        copy.start()

    barrier = pltpu.get_barrier_semaphore()
    for device in (other_core, other_pipe):
        pl.semaphore_signal(barrier, inc=1, device_id=device, device_id_type=MESH)

    lane = lax.broadcasted_iota(jnp.int32, (columns, 2 * twin), 1)
    early = (lax.rem(lane, twin) < size).astype(f32)
    halves[0] = early.astype(bf16)
    halves[1] = (1.0 - early).astype(bf16)
    feature = lax.broadcasted_iota(jnp.int32, (width, 128), 0)
    head = lax.broadcasted_iota(jnp.int32, (width, 128), 1)
    belongs = jnp.logical_and(feature >= head * size, feature < head * size + size)
    segment[...] = belongs.astype(f32).astype(bf16)
    head = lax.broadcasted_iota(jnp.int32, (128, width), 0)
    feature = lax.broadcasted_iota(jnp.int32, (128, width), 1)
    belongs = jnp.logical_and(feature >= head * size, feature < head * size + size)
    spread[...] = belongs.astype(f32).astype(bf16)
    pl.semaphore_wait(barrier, 2)

    def gain_of(index):
        return rows[index : index + 1, :]

    def bias_of(index):
        return rows[3 + index : 4 + index, :]

    def both(ref, start):
        return jnp.concatenate(
            [ref[0:columns, start : start + twin], ref[columns:tokens, start : start + twin]],
            axis=1,
        )

    def stacked(ref, start):
        wide = both(ref, start)
        return jnp.concatenate([wide * halves[0], wide * halves[1]], axis=0)

    def unstack(wide):
        early_lane = lax.rem(lax.broadcasted_iota(jnp.int32, (columns, 2 * twin), 1), twin) < size
        return jnp.where(early_lane, wide[0:columns], wide[columns:])

    def put(ref, start, wide):
        ref[0:columns, start : start + twin] = wide[:, 0:twin].astype(bf16)
        ref[columns:tokens, start : start + twin] = wide[:, twin:].astype(bf16)

    def to_core(source_ref, target_ref, sems, index):
        return remote(
            source_ref, target_ref, sems.at[0, index], sems.at[1, index], other_core
        )

    send_on = remote(act, source, pipe_sems.at[0], pipe_sems.at[1], other_pipe)
    send_back = remote(der, grad_in, pipe_sems.at[2], pipe_sems.at[3], other_pipe)

    @pl.when(pipe == 0)
    def _():
        source[...] = entry[...]

    @pl.when(pipe == 1)
    def _():
        send_on.wait_recv()

    unit, _ = unit_rows(source[...].astype(f32))
    normal_a[...] = (unit * gain_of(0) + bias_of(0)).astype(bf16)
    weights[0].wait()
    for part in range(3):
        window = slice(part * width, (part + 1) * width)
        mixer[:, window] = dot(normal_a[...], w_row[:, window], 1, 0).astype(bf16)
    logit_factor = 1.0 / (math.sqrt(size) * math.sqrt(total_rows))
    logit_copies = []
    for couple in range(couples):
        partial_value = logit_factor * dot(
            both(mixer, couple * twin), stacked(mixer, width + couple * twin), 1, 1
        )
        logit_send[couple] = partial_value.astype(bf16)
        copy = to_core(logit_send.at[couple], logit_recv.at[couple], logit_sems, couple)
        copy.start()
        logit_copies.append(copy)
    valid = (
        lax.broadcasted_iota(jnp.int32, (columns, 1), 0).astype(f32) < count[0:1, 0:1]
    ).astype(f32)
    disorder = jnp.zeros((columns, 1), f32)
    for couple in range(couples):
        logit_copies[couple].wait_recv()
        wide = logit_send[couple].astype(f32) + logit_recv[couple].astype(f32)
        shares = []
        for half in range(2):
            logits = wide[:, half * columns : (half + 1) * columns]
            shifted_logits = logits - jnp.max(logits, axis=-1, keepdims=True)
            powers = jnp.exp(shifted_logits)
            total = jnp.sum(powers, axis=-1, keepdims=True)
            logs = shifted_logits - jnp.log(total)
            share = powers / total
            log_share[couple, :, half * columns : (half + 1) * columns] = logs
            disorder = disorder - jnp.sum(share * logs, axis=-1, keepdims=True) * valid
            shares.append(share.astype(bf16))
        put(
            blended,
            couple * twin,
            dot(
                jnp.concatenate(shares, axis=1), stacked(mixer, 2 * width + couple * twin), 1, 0
            ),
        )
    cost[...] = jnp.broadcast_to(
        jnp.sum(disorder, axis=0, keepdims=True) / float(heads * columns), cost.shape
    )
    weights[1].wait()
    after_row[...] = source[...].astype(f32) + dot(blended[...], w_row_out[...], 1, 0)
    unit, _ = unit_rows(after_row[...])
    normal_b[...] = (unit * gain_of(1) + bias_of(1)).astype(bf16)
    weights[2].wait()
    keys_copies = []
    for part in (1, 2, 0):
        window = slice(part * width, (part + 1) * width)
        mixer_col[:, window] = dot(normal_b[...], w_col[:, window], 1, 0).astype(bf16)
        if part > 0:
            copy = to_core(
                mixer_col.at[:, window], keys_recv.at[part - 1], keys_sems, part - 1
            )
            copy.start()
            keys_copies.append(copy)

    def line_of(part, place_of):
        if place_of < 2:
            rows_of = slice(place_of * columns, (place_of + 1) * columns)
            return mixer_col[rows_of, (1 + part) * width : (2 + part) * width]
        rows_of = slice((place_of - 2) * columns, (place_of - 1) * columns)
        return keys_recv[part, rows_of, :]

    def sums_by_head(wide_ref, start, line):
        products = [
            wide_ref[index * columns : (index + 1) * columns, start : start + width] * line
            for index in range(2)
        ]
        return dot(jnp.concatenate(products, axis=0), segment[...], 1, 0)

    def spread_heads(narrow):
        return dot(narrow, spread[...], 1, 0)

    scores = []
    for place_of in range(4):
        if place_of == 2:
            keys_copies[0].wait_recv()
        scores.append(sums_by_head(mixer_col, 0, line_of(0, place_of)) / math.sqrt(size))
    highest = functools.reduce(jnp.maximum, scores)
    powers = [jnp.exp(score - highest) for score in scores]
    total = functools.reduce(jnp.add, powers)
    keys_copies[1].wait_recv()
    gathered_mix = None
    for place_of in range(4):
        share = powers[place_of] / total
        col_share[place_of] = share
        wide = spread_heads(share.astype(bf16))
        line = line_of(1, place_of).astype(f32)
        term = jnp.concatenate([wide[0:columns] * line, wide[columns:] * line], axis=0)
        gathered_mix = term if gathered_mix is None else gathered_mix + term
    mixed[...] = gathered_mix.astype(bf16)
    weights[3].wait()
    after_col[...] = after_row[...] + dot(mixed[...], w_col_out[...], 1, 0)
    unit, _ = unit_rows(after_col[...])
    normal_c[...] = (unit * gain_of(2) + bias_of(2)).astype(bf16)
    weights[4].wait()
    weights[5].wait()
    parts = hidden.shape[1] // width
    result = after_col[...]
    for part in range(parts):
        window = slice(part * width, (part + 1) * width)
        upward = dot(normal_c[...], w_up[:, window], 1, 0)
        inner = 0.5 + 0.5 * lax.erf(upward * math.sqrt(0.5))
        density = jnp.exp(-0.5 * upward * upward) * (1.0 / math.sqrt(2.0 * math.pi))
        hidden[:, window] = (upward * inner).astype(bf16)
        slope[:, window] = (inner + upward * density).astype(bf16)
        result = result + dot(hidden[:, window], w_down[window, :], 1, 0)
    act[...] = result.astype(bf16)

    @pl.when(pipe == 0)
    def _():
        send_on.start()

    @pl.when(pipe == 1)
    def _():
        total_grad[...] = entry[...].astype(f32) * factor[:, 0:1]

    @pl.when(pipe == 0)
    def _():
        send_back.wait_recv()
        total_grad[...] = grad_in[...].astype(f32)

    branch_ffn[...] = total_grad[...].astype(bf16)
    grad_normal = None
    for part in range(parts):
        window = slice(part * width, (part + 1) * width)
        grad_hidden = dot(branch_ffn[...], w_down[window, :], 1, 1)
        grad_up[:, window] = (grad_hidden * slope[:, window].astype(f32)).astype(bf16)
        term = dot(grad_up[:, window], w_up[:, window], 1, 1)
        grad_normal = term if grad_normal is None else grad_normal + term
    term, gain, bias = unit_rows_back(grad_normal, after_col[...], gain_of(2))
    vector[2:3, :] = gain
    vector[5:6, :] = bias
    total_grad[...] = total_grad[...] + term
    branch_col[...] = total_grad[...].astype(bf16)
    grad_mixed = dot(branch_col[...], w_col_out[...], 1, 1).astype(bf16)
    grad_probs = []
    for place_of in range(4):
        line = line_of(1, place_of)
        products = [grad_mixed[0:columns] * line, grad_mixed[columns:] * line]
        grad_probs.append(dot(jnp.concatenate(products, axis=0), segment[...], 1, 0))
    inner = functools.reduce(
        jnp.add, [col_share[place_of] * grad_probs[place_of] for place_of in range(4)]
    )
    root_size = math.sqrt(size)
    grad_query = None
    local_terms = []
    back_copies = []
    grad_lines = grad_mixed.astype(f32)
    query_lines = mixer_col[:, 0:width].astype(f32)
    for place_of in (2, 3, 0, 1):
        share = col_share[place_of]
        narrow = (share * (grad_probs[place_of] - inner)).astype(bf16)
        wide = spread_heads(narrow)
        line = line_of(0, place_of).astype(f32)
        term = jnp.concatenate([wide[0:columns] * line, wide[columns:] * line], axis=0)
        grad_query = term if grad_query is None else grad_query + term
        key_term = wide[0:columns] * query_lines[0:columns] + wide[columns:] * query_lines[columns:]
        key_term = key_term / root_size
        wide = spread_heads(share.astype(bf16))
        value_term = wide[0:columns] * grad_lines[0:columns] + wide[columns:] * grad_lines[columns:]
        if place_of >= 2:
            index = place_of - 2
            rows_of = slice(index * columns, (index + 1) * columns)
            keys_send[rows_of, 0:width] = key_term.astype(bf16)
            keys_send[rows_of, width:] = value_term.astype(bf16)
            copy = to_core(keys_send.at[rows_of, :], keys_back.at[rows_of, :], back_sems, index)
            copy.start()
            back_copies.append(copy)
        else:
            local_terms.append((key_term, value_term))
    grad_mixer_col[:, 0:width] = (grad_query / root_size).astype(bf16)
    for place_of in range(2):
        back_copies[place_of].wait()
        rows_of = slice(place_of * columns, (place_of + 1) * columns)
        for part in range(2):
            window = slice(part * width, (part + 1) * width)
            grad_mixer_col[rows_of, (1 + part) * width : (2 + part) * width] = (
                local_terms[place_of][part] + keys_back[rows_of, window].astype(f32)
            ).astype(bf16)
    grad_normal = None
    for part in range(3):
        window = slice(part * width, (part + 1) * width)
        term = dot(grad_mixer_col[:, window], w_col[:, window], 1, 1)
        grad_normal = term if grad_normal is None else grad_normal + term
    term, gain, bias = unit_rows_back(grad_normal, after_row[...], gain_of(1))
    vector[1:2, :] = gain
    vector[4:5, :] = bias
    total_grad[...] = total_grad[...] + term
    branch_row[...] = total_grad[...].astype(bf16)
    keys_send[:, 0:width] = dot(branch_row[...], w_row_out[...], 1, 1).astype(bf16)
    probs_copies = []
    for couple in range(couples):
        partial_value = dot(
            both(keys_send, couple * twin), stacked(mixer, 2 * width + couple * twin), 1, 1
        )
        probs_send[couple] = partial_value.astype(bf16)
        copy = to_core(probs_send.at[couple], probs_recv.at[couple], probs_sems, couple)
        copy.start()
        probs_copies.append(copy)
    column_weight = (float(total_rows * columns) / float(heads * columns)) * valid
    for couple in range(couples):
        start = couple * twin
        logs = log_share[couple]
        share = jnp.exp(logs)
        grad_wide = both(keys_send, start)
        put(
            grad_mixer,
            2 * width + start,
            unstack(dot(share.astype(bf16), grad_wide, 0, 0)),
        )
        probs_copies[couple].wait_recv()
        wide = probs_send[couple].astype(f32) + probs_recv[couple].astype(f32)
        pieces = []
        for half in range(2):
            window = slice(half * columns, (half + 1) * columns)
            part_share, part_logs, part_grad = (share[:, window], logs[:, window], wide[:, window])
            entropy = -jnp.sum(part_share * part_logs, axis=-1, keepdims=True)
            inner = jnp.sum(part_share * part_grad, axis=-1, keepdims=True)
            piece = part_share * (part_grad - inner)
            piece = piece - column_weight * part_share * (part_logs + entropy)
            pieces.append(piece.astype(bf16))
        grad_logits = jnp.concatenate(pieces, axis=1)
        put(
            grad_mixer,
            start,
            logit_factor * dot(grad_logits, stacked(mixer, width + start), 1, 0),
        )
        put(
            grad_mixer,
            width + start,
            logit_factor * unstack(dot(grad_logits, both(mixer, start), 0, 0)),
        )
    grad_normal = None
    for part in range(3):
        window = slice(part * width, (part + 1) * width)
        term = dot(grad_mixer[:, window], w_row[:, window], 1, 1)
        grad_normal = term if grad_normal is None else grad_normal + term
    term, gain, bias = unit_rows_back(grad_normal, source[...].astype(f32), gain_of(0))
    vector[0:1, :] = gain
    vector[3:4, :] = bias
    vector[6:8, :] = jnp.zeros((2, width), f32)
    der[...] = (total_grad[...] + term).astype(bf16)

    @pl.when(pipe == 1)
    def _():
        send_back.start()

    pairs = (
        (normal_a, grad_mixer),
        (blended, branch_row),
        (normal_b, grad_mixer_col),
        (mixed, branch_col),
        (normal_c, grad_up),
    )
    share = width // (4 * LINE)
    base = 0
    waiting = {}
    number = 0
    for left, right in pairs:
        for part in range(right.shape[1] // width):
            slot = number % 2
            if slot in waiting:
                for copy in waiting.pop(slot):
                    copy.wait()
            window = slice(part * width, (part + 1) * width)
            term = dot(left[...], right[:, window], 0, 0).astype(bf16)
            stage[slot] = term.reshape(LINE, 4, share, width)
            copies = [
                pltpu.make_async_copy(
                    stage.at[slot, target],
                    grads.at[target, :, pl.ds(base, share)],
                    stage_sems.at[slot, target],
                )
                for target in range(LINE)
            ]
            for copy in copies:
                copy.start()
            waiting[slot] = copies
            base += share
            number += 1
    for part in range(parts):
        slot = 2 + part % 2
        if slot in waiting:
            for copy in waiting.pop(slot):
                copy.wait()
        window = slice(part * width, (part + 1) * width)
        term = dot(hidden[:, window], branch_ffn[...], 0, 0).astype(bf16)
        stage_down[slot - 2] = term.reshape(4, width // 4, width)
        copy = pltpu.make_async_copy(
            stage_down.at[slot - 2],
            grads.at[part, :, pl.ds(base, width // 4)],
            stage_sems.at[slot, 0],
        )
        copy.start()
        waiting[slot] = [copy]
    for copies in waiting.values():
        for copy in copies:
            copy.wait()
    for copy in logit_copies + keys_copies + probs_copies:
        copy.wait_send()

    @pl.when(pipe == 0)
    def _():
        send_on.wait_send()

    @pl.when(pipe == 1)
    def _():
        send_back.wait_send()


def run_layers(entry, factor, count, rows, wholes):
    tokens, width = entry.shape
    columns = tokens // 2
    couples = HEAD_TALLY // 2
    wide = wholes[4].shape[1]
    anywhere = pl.BlockSpec(memory_space=pl.ANY)
    inside = pl.BlockSpec(memory_space=pltpu.VMEM)
    dma = pltpu.SemaphoreType.DMA
    bf16, f32 = (jnp.bfloat16, jnp.float32)
    rows_of = lambda columns_of, kind=bf16: pltpu.VMEM((tokens, columns_of), kind)
    scores = pltpu.VMEM((couples, columns, 2 * columns), bf16)
    packed_rows = sum(whole.shape[0] * whole.shape[1] for whole in wholes) // (16 * width)
    return pl.pallas_call(
        layers_kernel,
        out_shape=[
            jax.ShapeDtypeStruct((tokens, width), bf16),
            jax.ShapeDtypeStruct((tokens, width), bf16),
            jax.ShapeDtypeStruct((8, 128), f32),
            jax.ShapeDtypeStruct((8, width), f32),
            jax.ShapeDtypeStruct((LINE, 4, packed_rows, width), bf16),
        ],
        in_specs=[inside] * 4 + [anywhere] * 6,
        out_specs=[inside] * 4 + [anywhere],
        scratch_shapes=[pltpu.VMEM(whole.shape, bf16) for whole in wholes]
        + [
            rows_of(width),
            rows_of(width),
            rows_of(width),
            rows_of(width),
            rows_of(3 * width),
            rows_of(3 * width),
            rows_of(width),
            rows_of(width),
            rows_of(width, f32),
            rows_of(width, f32),
            pltpu.VMEM((couples, columns, 2 * columns), f32),
            pltpu.VMEM((4, tokens, 128), f32),
            rows_of(wide),
            rows_of(wide),
            rows_of(width, f32),
            rows_of(width),
            rows_of(width),
            rows_of(width),
            rows_of(width),
            rows_of(wide),
            rows_of(3 * width),
            rows_of(3 * width),
            scores,
            scores,
            pltpu.VMEM((2, tokens, width), bf16),
            rows_of(2 * width),
            rows_of(2 * width),
            scores,
            scores,
            pltpu.VMEM((2, columns, 2 * columns), bf16),
            pltpu.VMEM((width, 128), bf16),
            pltpu.VMEM((128, width), bf16),
            pltpu.VMEM((2, LINE, 4, width // (4 * LINE), width), bf16),
            pltpu.VMEM((2, 4, width // 4, width), bf16),
            dma((6,)),
            dma((2, couples)),
            dma((2, 2)),
            dma((2, 2)),
            dma((2, couples)),
            dma((4,)),
            dma((4, LINE)),
        ],
        compiler_params=pltpu.CompilerParams(
            collective_id=2, has_side_effects=True, vmem_limit_bytes=60 * 2**20
        ),
        name="two_layers",
    )(entry, factor, count, rows, *wholes)


def unpacked(block, rows, columns, lanes):
    parts = block.reshape(4, columns // lanes, rows // 4, lanes)
    return parts.transpose(0, 2, 1, 3).reshape(rows, columns).astype(jnp.float32)


def on_device_lined(
    embedded_families,
    order,
    token_quarter_factor,
    genuine_residue_tally,
    standardizer_scales,
    standardizer_offsets,
    row_qkv,
    row_out,
    col_qkv,
    col_out,
    ffn_up,
    ffn_down,
    upstream_sensitivity,
):
    segment_place = lax.axis_index("pipe")
    sequence = order[0]
    columns, model_width = embedded_families.shape[2:]
    piece = jnp.where(
        segment_place == 0, embedded_families[sequence, 0], upstream_sensitivity[:, 0]
    )
    factor = token_quarter_factor[sequence, 0].astype(jnp.float32) * 0.25
    count = genuine_residue_tally[sequence].astype(jnp.float32)
    meta = jnp.concatenate(
        [
            jnp.broadcast_to(factor[:, :, None], (2, columns, 128)),
            jnp.broadcast_to(count[:, None, None], (2, 8, 128)),
        ],
        axis=1,
    )
    share = standardizer_scales.shape[-1]
    rows = jnp.pad(
        jnp.concatenate([standardizer_scales[0], standardizer_offsets[0]], axis=0),
        ((0, 2), (0, 256 - share)),
    )
    shards = (row_qkv[0], row_out[0], col_qkv[0], col_out[0], ffn_up[0], ffn_down[0])
    *wholes, piece, meta, rows = gather_all(shards, piece, meta, rows)
    rows = rows[:, :6, :share].transpose(1, 0, 2).reshape(6, model_width)
    tokens = 2 * columns
    activation, grad_source, cost, vector, grads = run_layers(
        piece.reshape(tokens, model_width),
        meta[:, :columns].reshape(tokens, 128),
        meta[0, columns:],
        jnp.pad(rows, ((0, 2), (0, 0))),
        wholes,
    )
    vector = jnp.pad(
        vector.reshape(8, LINE, share).transpose(1, 0, 2), ((0, 0), (0, 0), (0, 256 - share))
    )
    out, vector, activations, derivs, costs = reduce_all(
        grads,
        vector,
        activation.reshape(piece.shape),
        grad_source.reshape(piece.shape),
        cost,
    )
    results = []
    base = 0
    for shard in shards:
        depth, wide = shard.shape
        length = depth // 4 * (wide // model_width)
        results.append(
            unpacked(out[:, base : base + length], depth, wide, model_width)[None]
        )
        base += length
    return (
        activations[None, :, None],
        derivs[None, :, None],
        costs[:, 0, 0][None],
        *results,
        vector[None, :3, :share],
        vector[None, 3:6, :share],
    )


def solution(mesh):
    in_specs = (
        P("dp", "seq", None, None),
        P("dp", None),
        P("dp", "seq", None),
        P("dp"),
        P("pipe", None, "seq"),
        P("pipe", None, "seq"),
        P("pipe", "seq", None),
        P("pipe", "seq", None),
        P("pipe", "seq", None),
        P("pipe", "seq", None),
        P("pipe", "seq", None),
        P("pipe", "seq", None),
        P("dp", "seq", None, None),
    )
    out_specs = (
        P("pipe", "dp", "seq", None, None),
        P("pipe", "dp", "seq", None, None),
        P("pipe", "dp"),
        P("pipe", "seq", None),
        P("pipe", "seq", None),
        P("pipe", "seq", None),
        P("pipe", "seq", None),
        P("pipe", "seq", None),
        P("pipe", "seq", None),
        P("pipe", None, "seq"),
        P("pipe", None, "seq"),
    )
    lined = mesh.shape["seq"] == LINE and mesh.shape["dp"] == 4 and mesh.shape["pipe"] == 2
    return jax.shard_map(
        on_device_lined if lined else on_device, mesh=mesh, in_specs=in_specs, out_specs=out_specs, check_vma=False
    )
```

```python
import functools
import math

import jax
import jax.numpy as jnp
from jax import lax
from jax.experimental import pallas as pl
from jax.experimental.pallas import tpu as pltpu
from jax.sharding import PartitionSpec as P

HEAD_TALLY = 12
LINE = 4
MESH = pl.DeviceIdType.MESH


norm_epsilon = 1e-05


def shifted(value, axis, steps):
    count = lax.axis_size(axis)
    initial, last = (max(0, -steps), min(count, count - steps))
    return lax.ppermute(value, axis, [(source, source + steps) for source in range(initial, last)])


def normed(values, gain_row, bias_row):
    average = jnp.mean(values, axis=-1, keepdims=True)
    centered = values - average
    variance = jnp.mean(centered * centered, axis=-1, keepdims=True)
    return centered * lax.rsqrt(variance + norm_epsilon) * gain_row + bias_row


def gelu_exact(values):
    return jax.nn.gelu(values, approximate=False)


def product(left, weight):
    return lax.dot_general(
        left, weight, (((left.ndim - 1,), (0,)), ((), ())), preferred_element_type=jnp.float32
    )


def product_back(left, weight):
    return lax.dot_general(
        left, weight, (((left.ndim - 1,), (1,)), ((), ())), preferred_element_type=jnp.float32
    )


def weight_term(left, right):
    return lax.dot_general(
        left, right, (((0, 1), (0, 1)), ((), ())), preferred_element_type=jnp.float32
    )


def split_heads(values, head_count):
    return values.reshape(values.shape[:-1] + (head_count, values.shape[-1] // head_count))


def choose(flag, first_tree, second_tree):
    return jax.tree.map(lambda early, later: jnp.where(flag, early, later), first_tree, second_tree)


def column_scores(queries, key_rows, head_count):
    query_heads = split_heads(queries, head_count)
    raw = jnp.einsum(
        "rche,sche->chrs",
        query_heads,
        split_heads(key_rows, head_count),
        preferred_element_type=jnp.float32,
    )
    return raw / math.sqrt(query_heads.shape[-1])


def column_forward(queries, key_rows, content_lines, head_count):
    scores = column_scores(queries, key_rows, head_count)
    log_total = jax.nn.logsumexp(scores, axis=-1)
    vertical_factors = jnp.exp(scores - log_total[..., None]).astype(jnp.bfloat16)
    mixed_cols = jnp.einsum(
        "gmqi,igmu->qgmu",
        vertical_factors,
        split_heads(content_lines, head_count),
        preferred_element_type=jnp.float32,
    )
    return (mixed_cols.reshape(queries.shape).astype(jnp.bfloat16), log_total)


def column_backward(queries, key_rows, content_lines, log_total, grad_mixed, head_count):
    scores = column_scores(queries, key_rows, head_count)
    softmax_share = jnp.exp(scores - log_total[..., None])
    grad_heads = split_heads(grad_mixed, head_count)
    grad_probs = jnp.einsum(
        "rche,sche->chrs",
        grad_heads,
        split_heads(content_lines, head_count),
        preferred_element_type=jnp.float32,
    )
    grad_values = jnp.einsum(
        "chrs,rche->sche",
        softmax_share.astype(jnp.bfloat16),
        grad_heads,
        preferred_element_type=jnp.float32,
    )
    grad_scores = (
        softmax_share * (grad_probs - jnp.sum(softmax_share * grad_probs, axis=-1, keepdims=True))
    ).astype(jnp.bfloat16)
    root_size = math.sqrt(queries.shape[-1] // head_count)
    grad_queries = (
        jnp.einsum(
            "gmqi,igmu->qgmu",
            grad_scores,
            split_heads(key_rows, head_count),
            preferred_element_type=jnp.float32,
        )
        / root_size
    )
    grad_keys = (
        jnp.einsum(
            "chrs,rche->sche",
            grad_scores,
            split_heads(queries, head_count),
            preferred_element_type=jnp.float32,
        )
        / root_size
    )
    return (
        grad_queries.reshape(queries.shape),
        grad_keys.reshape(key_rows.shape),
        grad_values.reshape(content_lines.shape),
    )


def row_split(horizontal_mixer, model_width, head_count):
    queries = split_heads(horizontal_mixer[..., :model_width], head_count)
    key_rows = split_heads(horizontal_mixer[..., model_width : 2 * model_width], head_count)
    content_lines = split_heads(horizontal_mixer[..., 2 * model_width :], head_count)
    return (queries, key_rows, content_lines)


def layer_forward(source_rows, family_residues, projection_tables, head_count):
    (
        horizontal_coefficients,
        w_row_out,
        vertical_coefficients,
        w_col_out,
        w_up,
        w_down,
        gain_rows,
        bias_rows,
    ) = projection_tables
    row_count, columns, model_width = source_rows.shape
    total_rows = row_count * lax.axis_size("seq")
    start = source_rows.astype(jnp.float32)
    layernorm_first = normed(start, gain_rows[0], bias_rows[0]).astype(jnp.bfloat16)
    horizontal_mixer = product(layernorm_first, horizontal_coefficients).astype(jnp.bfloat16)
    queries, key_rows, content_lines = row_split(horizontal_mixer, model_width, head_count)
    logit_factor = 1.0 / (math.sqrt(model_width // head_count) * math.sqrt(total_rows))
    partial_value = logit_factor * jnp.einsum(
        "rihe,rjhe->hij", queries, key_rows, preferred_element_type=jnp.float32
    )
    logits = lax.psum(partial_value.astype(jnp.bfloat16), "seq").astype(jnp.float32)
    softmax_share = jax.nn.softmax(logits, axis=-1)
    log_probs = jax.nn.log_softmax(logits, axis=-1)
    entropy = -jnp.sum(softmax_share * log_probs, axis=-1)
    valid_residues = (jnp.arange(columns, dtype=jnp.int32) < family_residues).astype(jnp.float32)
    disorder_cost = jnp.sum(entropy * valid_residues[None, :]) / float(head_count * columns)
    blended_lines = jnp.einsum(
        "vyp,opvl->oyvl",
        softmax_share.astype(jnp.bfloat16),
        content_lines,
        preferred_element_type=jnp.float32,
    )
    blended_lines = blended_lines.reshape(row_count, columns, model_width).astype(jnp.bfloat16)
    after_row = start + product(blended_lines, w_row_out)
    layernorm_second = normed(after_row, gain_rows[1], bias_rows[1]).astype(jnp.bfloat16)
    vertical_mixer = product(layernorm_second, vertical_coefficients).astype(jnp.bfloat16)
    everyone = lax.all_gather(vertical_mixer[..., model_width:], "seq", axis=0, tiled=True)
    mixed_values, log_total = column_forward(
        vertical_mixer[..., :model_width],
        everyone[..., :model_width],
        everyone[..., model_width:],
        head_count,
    )
    column_state = (everyone, log_total)
    after_col = after_row + product(mixed_values, w_col_out)
    normal_c = normed(after_col, gain_rows[2], bias_rows[2]).astype(jnp.bfloat16)
    upward = product(normal_c, w_up)
    hidden = gelu_exact(upward).astype(jnp.bfloat16)
    result = after_col + product(hidden, w_down)
    kept_state = (
        source_rows,
        layernorm_first,
        horizontal_mixer,
        logits,
        blended_lines,
        after_row,
        layernorm_second,
        vertical_mixer,
        column_state,
        mixed_values,
        after_col,
        normal_c,
        upward,
        hidden,
    )
    return (result.astype(jnp.bfloat16), disorder_cost, kept_state)


def layer_backward(kept_state, family_residues, grad_result, projection_tables, head_count):
    (
        horizontal_coefficients,
        w_row_out,
        vertical_coefficients,
        w_col_out,
        w_up,
        w_down,
        gain_rows,
        bias_rows,
    ) = projection_tables
    (
        source_rows,
        layernorm_first,
        horizontal_mixer,
        logits,
        blended_lines,
        after_row,
        layernorm_second,
        vertical_mixer,
        column_state,
        mixed_values,
        after_col,
        normal_c,
        upward,
        hidden,
    ) = kept_state
    row_count, columns, model_width = source_rows.shape
    total_rows = row_count * lax.axis_size("seq")
    grad_branch_ffn = grad_result.astype(jnp.bfloat16)
    grad_hidden = product_back(grad_branch_ffn, w_down)
    grad_upward = jax.vjp(gelu_exact, upward)[1](grad_hidden)[0].astype(jnp.bfloat16)
    grad_normal_c = product_back(grad_upward, w_up)
    from_norm, gain_last, bias_last = jax.vjp(normed, after_col, gain_rows[2], bias_rows[2])[1](
        grad_normal_c
    )
    grad_col = grad_result + from_norm
    grad_branch_col = grad_col.astype(jnp.bfloat16)
    grad_attended = product_back(grad_branch_col, w_col_out).astype(jnp.bfloat16)
    everyone, log_total = column_state
    grad_query_col, grad_key_col, grad_value_col = column_backward(
        vertical_mixer[..., :model_width],
        everyone[..., :model_width],
        everyone[..., model_width:],
        log_total,
        grad_attended,
        head_count,
    )
    grad_kv_rows = lax.psum_scatter(
        jnp.concatenate([grad_key_col, grad_value_col], axis=-1).astype(jnp.bfloat16),
        "seq",
        scatter_dimension=0,
        tiled=True,
    ).astype(jnp.float32)
    grad_col_proj = jnp.concatenate([grad_query_col, grad_kv_rows], axis=-1).astype(jnp.bfloat16)
    grad_normal_b = product_back(grad_col_proj, vertical_coefficients)
    from_norm, gain_middle, bias_middle = jax.vjp(normed, after_row, gain_rows[1], bias_rows[1])[1](
        grad_normal_b
    )
    grad_row = grad_col + from_norm
    grad_branch_row = grad_row.astype(jnp.bfloat16)
    grad_mixed = split_heads(
        product_back(grad_branch_row, w_row_out).astype(jnp.bfloat16), head_count
    )
    queries, key_rows, content_lines = row_split(horizontal_mixer, model_width, head_count)
    softmax_share = jax.nn.softmax(logits, axis=-1)
    log_probs = jax.nn.log_softmax(logits, axis=-1)
    entropy = -jnp.sum(softmax_share * log_probs, axis=-1)
    partial_value = jnp.einsum(
        "rihe,rjhe->hij", grad_mixed, content_lines, preferred_element_type=jnp.float32
    )
    grad_probs = lax.psum(partial_value.astype(jnp.bfloat16), "seq").astype(jnp.float32)
    grad_values = jnp.einsum(
        "hij,rihe->rjhe",
        softmax_share.astype(jnp.bfloat16),
        grad_mixed,
        preferred_element_type=jnp.float32,
    )
    valid_residues = (jnp.arange(columns, dtype=jnp.int32) < family_residues).astype(jnp.float32)
    column_weight = float(total_rows * columns) * valid_residues / float(head_count * columns)
    grad_logits = softmax_share * (
        grad_probs - jnp.sum(softmax_share * grad_probs, axis=-1, keepdims=True)
    )
    grad_logits = grad_logits - column_weight[None, :, None] * softmax_share * (
        log_probs + entropy[..., None]
    )
    grad_logits = grad_logits.astype(jnp.bfloat16)
    logit_factor = 1.0 / (math.sqrt(model_width // head_count) * math.sqrt(total_rows))
    grad_queries = logit_factor * jnp.einsum(
        "vyp,opvl->oyvl", grad_logits, key_rows, preferred_element_type=jnp.float32
    )
    grad_keys = logit_factor * jnp.einsum(
        "hij,rihe->rjhe", grad_logits, queries, preferred_element_type=jnp.float32
    )
    grad_row_proj = jnp.concatenate(
        [
            grad_queries.reshape(row_count, columns, model_width),
            grad_keys.reshape(row_count, columns, model_width),
            grad_values.reshape(row_count, columns, model_width),
        ],
        axis=-1,
    ).astype(jnp.bfloat16)
    grad_normal_a = product_back(grad_row_proj, horizontal_coefficients)
    from_norm, gain_first, bias_first = jax.vjp(
        normed, source_rows.astype(jnp.float32), gain_rows[0], bias_rows[0]
    )[1](grad_normal_a)
    grad_source = (grad_row + from_norm).astype(jnp.bfloat16)
    operand_pairs = (
        (layernorm_first, grad_row_proj),
        (blended_lines, grad_branch_row),
        (layernorm_second, grad_col_proj),
        (mixed_values, grad_branch_col),
        (normal_c, grad_upward),
        (hidden, grad_branch_ffn),
    )
    norm_grads = (
        jnp.stack([gain_first, gain_middle, gain_last]),
        jnp.stack([bias_first, bias_middle, bias_last]),
    )
    return (grad_source, operand_pairs, norm_grads)


def on_device(
    embedded_families,
    order,
    token_quarter_factor,
    genuine_residue_tally,
    standardizer_scales,
    standardizer_offsets,
    row_qkv,
    row_out,
    col_qkv,
    col_out,
    ffn_up,
    ffn_down,
    upstream_sensitivity,
):
    head_count = HEAD_TALLY
    segment_place = lax.axis_index("pipe")
    gathered = (
        lax.all_gather(row_qkv, "seq", axis=1, tiled=True),
        lax.all_gather(row_out, "seq", axis=1, tiled=True),
        lax.all_gather(col_qkv, "seq", axis=1, tiled=True),
        lax.all_gather(col_out, "seq", axis=1, tiled=True),
        lax.all_gather(ffn_up, "seq", axis=1, tiled=True),
        lax.all_gather(ffn_down, "seq", axis=1, tiled=True),
        lax.all_gather(standardizer_scales.astype(jnp.bfloat16), "seq", axis=2, tiled=True).astype(
            standardizer_scales.dtype
        ),
        lax.all_gather(standardizer_offsets.astype(jnp.bfloat16), "seq", axis=2, tiled=True).astype(
            standardizer_offsets.dtype
        ),
    )
    projection_tables = tuple((gathered_piece[0] for gathered_piece in gathered))
    small_batch_number = embedded_families.shape[0]
    sequence = order[0]
    received = jnp.zeros(embedded_families.shape[1:], jnp.bfloat16)
    results = []
    focus_spread_levies = []
    kept_list = []
    for period in range(small_batch_number + 1):
        slot_here = jnp.clip(period - segment_place, 0, small_batch_number - 1)
        align_here = sequence[slot_here]
        source_rows = jnp.where(segment_place == 0, embedded_families[align_here], received)
        result, disorder_cost, kept_state = layer_forward(
            source_rows, genuine_residue_tally[align_here], projection_tables, head_count
        )
        results.append(result)
        focus_spread_levies.append(disorder_cost)
        kept_list.append(kept_state)
        if period < small_batch_number:
            received = shifted(result, "pipe", 1)
    activations = lax.dynamic_slice_in_dim(jnp.stack(results), segment_place, small_batch_number, 0)
    penalty_output = lax.dynamic_slice_in_dim(
        jnp.stack(focus_spread_levies), segment_place, small_batch_number, 0
    )
    grad_received = jnp.zeros(embedded_families.shape[1:], jnp.bfloat16)
    left_lists = [[] for index in range(6)]
    right_lists = [[] for index in range(6)]
    gain_total = None
    bias_total = None
    grad_sources = []
    for period in range(small_batch_number + 1):
        slot_raw = period - 1 + segment_place
        in_range = jnp.logical_and(slot_raw >= 0, slot_raw < small_batch_number)
        slot_here = jnp.clip(slot_raw, 0, small_batch_number - 1)
        align_here = sequence[slot_here]
        kept_state = choose(
            segment_place == 0,
            kept_list[max(period - 1, 0)],
            kept_list[min(period + 1, small_batch_number)],
        )
        outgrad = (
            upstream_sensitivity[slot_here].astype(jnp.float32)
            * token_quarter_factor[align_here].astype(jnp.float32)[..., None]
            * 0.25
        )
        incoming_grad = jnp.where(segment_place == 1, outgrad, grad_received.astype(jnp.float32))
        grad_source, operand_pairs, norm_grads = layer_backward(
            kept_state,
            genuine_residue_tally[align_here],
            incoming_grad,
            projection_tables,
            head_count,
        )
        for index in range(6):
            left_lists[index].append(operand_pairs[index][0])
            right_lists[index].append(
                jnp.where(
                    in_range, operand_pairs[index][1], jnp.zeros_like(operand_pairs[index][1])
                )
            )
        gain_term = jnp.where(in_range, norm_grads[0], jnp.zeros_like(norm_grads[0]))
        bias_term = jnp.where(in_range, norm_grads[1], jnp.zeros_like(norm_grads[1]))
        gain_total = gain_term if gain_total is None else gain_total + gain_term
        bias_total = bias_term if bias_total is None else bias_total + bias_term
        grad_sources.append(grad_source)
        if period < small_batch_number:
            grad_received = shifted(grad_source, "pipe", -1)
    block_entry_derivs = lax.dynamic_slice_in_dim(
        jnp.stack(grad_sources), 1 - segment_place, small_batch_number, 0
    )
    weight_totals = [
        weight_term(
            jnp.concatenate(left_lists[index], axis=0), jnp.concatenate(right_lists[index], axis=0)
        )
        for index in range(6)
    ]
    shared = (
        lax.psum_scatter(
            weight_totals[0].astype(jnp.bfloat16), "seq", scatter_dimension=0, tiled=True
        ).astype(jnp.float32),
        lax.psum_scatter(
            weight_totals[1].astype(jnp.bfloat16), "seq", scatter_dimension=0, tiled=True
        ).astype(jnp.float32),
        lax.psum_scatter(
            weight_totals[2].astype(jnp.bfloat16), "seq", scatter_dimension=0, tiled=True
        ).astype(jnp.float32),
        lax.psum_scatter(
            weight_totals[3].astype(jnp.bfloat16), "seq", scatter_dimension=0, tiled=True
        ).astype(jnp.float32),
        lax.psum_scatter(
            weight_totals[4].astype(jnp.bfloat16), "seq", scatter_dimension=0, tiled=True
        ).astype(jnp.float32),
        lax.psum_scatter(
            weight_totals[5].astype(jnp.bfloat16), "seq", scatter_dimension=0, tiled=True
        ).astype(jnp.float32),
        lax.psum_scatter(
            gain_total.astype(jnp.bfloat16), "seq", scatter_dimension=1, tiled=True
        ).astype(jnp.float32),
        lax.psum_scatter(
            bias_total.astype(jnp.bfloat16), "seq", scatter_dimension=1, tiled=True
        ).astype(jnp.float32),
    )
    (
        shared_row_qkv,
        shared_row_out,
        shared_col_qkv,
        shared_col_out,
        shared_up,
        shared_down,
        shared_gain,
        shared_bias,
    ) = shared
    summed = (
        lax.psum(shared_row_qkv.astype(jnp.bfloat16), "dp").astype(jnp.float32),
        lax.psum(shared_row_out.astype(jnp.bfloat16), "dp").astype(jnp.float32),
        lax.psum(shared_col_qkv.astype(jnp.bfloat16), "dp").astype(jnp.float32),
        lax.psum(shared_col_out.astype(jnp.bfloat16), "dp").astype(jnp.float32),
        lax.psum(shared_up.astype(jnp.bfloat16), "dp").astype(jnp.float32),
        lax.psum(shared_down.astype(jnp.bfloat16), "dp").astype(jnp.float32),
        lax.psum(shared_gain.astype(jnp.bfloat16), "dp").astype(jnp.float32),
        lax.psum(shared_bias.astype(jnp.bfloat16), "dp").astype(jnp.float32),
    )
    return (
        activations[None],
        block_entry_derivs[None],
        penalty_output[None],
        summed[0][None],
        summed[1][None],
        summed[2][None],
        summed[3][None],
        summed[4][None],
        summed[5][None],
        summed[6][None],
        summed[7][None],
    )


def place():
    pipe, seq, dp = (lax.axis_index("pipe"), lax.axis_index("seq"), lax.axis_index("dp"))
    core = lax.rem(dp, 2)
    pair = lax.div(dp, 2)
    return (pipe, seq, dp, core, pair)


def neighbours(pipe, seq, dp, core, pair):
    other_core = (pipe, seq, dp + 1 - 2 * core)
    other_pair = (pipe, seq, dp + 2 - 4 * pair)
    return (other_core, other_pair)


def greet(pipe, seq, dp, core, pair, across_pipe=False):
    barrier = pltpu.get_barrier_semaphore()
    other_core, other_pair = neighbours(pipe, seq, dp, core, pair)
    count = 0
    for step in range(LINE):
        for flip in range(2):
            if step == 0 and flip == 0:
                continue
            where = dp if flip == 0 else dp + 1 - 2 * core
            pl.semaphore_signal(
                barrier,
                inc=1,
                device_id=(pipe, lax.rem(seq + step, LINE), where),
                device_id_type=MESH,
            )
            count += 1
    last = (1 - pipe, seq, dp) if across_pipe else other_pair
    pl.semaphore_signal(barrier, inc=1, device_id=last, device_id_type=MESH)

    def hear():
        pl.semaphore_wait(barrier, count + 1)

    return hear


def remote(source, target, send, recv, device):
    return pltpu.make_async_remote_copy(
        src_ref=source,
        dst_ref=target,
        send_sem=send,
        recv_sem=recv,
        device_id=device,
        device_id_type=MESH,
    )


def swap_rows(source, target, send, recv, local, where):
    pipe, seq, dp, core, pair = where
    half, rest = (lax.div(seq, 2), lax.rem(seq, 2))

    def each(action):
        for index in range(2):
            line = 2 * core + index
            here = jnp.logical_and(line == seq, half == core)
            copy = remote(
                source.at[index],
                target.at[rest],
                send.at[index],
                recv.at[rest],
                (pipe, line, dp - core + half),
            )
            arriving = remote(
                source.at[index],
                target.at[index],
                send.at[index],
                recv.at[index],
                (pipe, line, dp - core + half),
            )
            inside = pltpu.make_async_copy(source.at[index], target.at[rest], local)
            action(here, copy, arriving, inside)

    def start(here, copy, arriving, inside):
        pl.when(here)(inside.start)
        pl.when(jnp.logical_not(here))(copy.start)

    def finish(here, copy, arriving, inside):
        pl.when(here)(inside.wait)
        pl.when(jnp.logical_not(here))(copy.wait_send)
        pl.when(jnp.logical_not(here))(arriving.wait_recv)

    return (lambda: each(start), lambda: each(finish))


def gather_kernel(*refs):
    shards, refs = ([ref.at[0] for ref in refs[:6]], refs[6:])
    families, upstream, order, quarters, tally, scales, offsets = refs[:7]
    wholes, refs = (refs[7:13], refs[13:])
    piece_out, meta_out, rows_out = refs[:3]
    (
        piece,
        meta,
        rows,
        own_sem,
        own_recv,
        line_send,
        line_recv,
        pair_send,
        pair_recv,
        core_send,
        core_recv,
        piece_send,
        piece_recv,
        meta_send,
        meta_recv,
        rows_send,
        rows_recv,
    ) = refs[3:]
    where = place()
    pipe, seq, dp, core, pair = where
    other_core, other_pair = neighbours(*where)
    quarter = dp
    hear = greet(*where)
    right, left = ((pipe, seq + 1, dp), (pipe, seq - 1, dp))
    straight = order[0, 0] == 0
    columns = families.shape[2]
    share_of_width = scales.shape[2]
    for index in range(2):
        chosen = jnp.where(straight, families[index, 0], families[1 - index, 0])
        piece[index] = jnp.where(pipe == 0, chosen, upstream[index, 0])
        chosen = jnp.where(straight, quarters[index], quarters[1 - index])
        factor = jnp.broadcast_to(chosen.astype(jnp.float32) * 0.25, (columns, columns))
        meta[index, 0:columns] = factor.T
        number = jnp.where(straight, tally[index], tally[1 - index])
        meta[index, columns:] = jnp.broadcast_to(number, (8, columns)).astype(jnp.float32)
    rows[...] = jnp.zeros(rows.shape, jnp.float32)
    rows[0:3, 0:share_of_width] = scales[0]
    rows[3:6, 0:share_of_width] = offsets[0]
    hear()

    def region(index, source, part):
        depth = shards[index].shape[0]
        share = depth // 4
        start = pl.multiple_of(source * depth + part * share, share)
        return wholes[index].at[pl.ds(start, share)]

    start_piece, finish_piece = swap_rows(
        piece, piece_out, piece_send, piece_recv, own_sem.at[7], where
    )
    start_meta, finish_meta = swap_rows(meta, meta_out, meta_send, meta_recv, own_sem.at[8], where)
    start_meta()
    start_piece()
    row_copies = []
    for step in range(1, LINE):
        target = (pipe, lax.rem(seq + step, LINE), dp)
        copy = remote(rows, rows_out.at[seq], rows_send.at[step - 1], rows_recv.at[seq], target)
        copy.start()
        row_copies.append(copy)
    own = [pltpu.make_async_copy(rows, rows_out.at[seq], own_sem.at[6])]
    for index in range(6):
        depth = shards[index].shape[0]
        own.append(
            remote(
                shards[index],
                wholes[index].at[pl.ds(pl.multiple_of(seq * depth, depth), depth)],
                own_sem.at[index],
                own_recv.at[index],
                other_core,
            )
        )

    for index in range(6):
        share = shards[index].shape[0] // 4
        mine = shards[index].at[pl.ds(pl.multiple_of(quarter * share, share), share)]

        @pl.when(seq < LINE - 1)
        def _():
            remote(
                mine,
                region(index, seq, quarter),
                line_send.at[0, seq, index],
                line_recv.at[seq, index],
                right,
            ).start()

        @pl.when(seq > 0)
        def _():
            remote(
                mine,
                region(index, seq, quarter),
                line_send.at[1, seq, index],
                line_recv.at[seq, index],
                left,
            ).start()

    for copy in own:
        copy.start()

    def over(kind, source, index, part, target):
        block = region(index, source, part)
        if kind == "pair":
            return remote(
                block, block, pair_send.at[source, index], pair_recv.at[source, index], target
            )
        lane = 0 if kind == "core" else 1
        return remote(
            block,
            block,
            core_send.at[lane, source, index],
            core_recv.at[lane, source, index],
            target,
        )

    def along(source, index, direction, target):
        block = region(index, source, quarter)
        return remote(
            block,
            block,
            line_send.at[direction, source, index],
            line_recv.at[source, index],
            target,
        )

    across = quarter + 2 - 4 * pair
    opposite = quarter + 1 - 2 * core
    opposite_across = across + 1 - 2 * core

    def arrive(step, index):
        for direction in range(2):
            source = seq - step if direction == 0 else seq + step
            present = source >= 0 if direction == 0 else source < LINE
            onward = seq < LINE - 1 if direction == 0 else seq > 0
            target = right if direction == 0 else left

            @pl.when(present)
            def _():
                along(source, index, direction, target).wait_recv()
                over("pair", source, index, quarter, other_pair).start()
                over("core", source, index, quarter, other_core).start()

            @pl.when(jnp.logical_and(present, onward))
            def _():
                along(source, index, direction, target).start()

    def forward(step, index):
        for direction in range(2):
            source = seq - step if direction == 0 else seq + step
            present = source >= 0 if direction == 0 else source < LINE

            @pl.when(present)
            def _():
                over("pair", source, index, across, other_pair).wait_recv()
                over("relay", source, index, across, other_core).start()

    events = [(step, index) for step in range(1, LINE) for index in range(6)]
    lag = 10
    for count in range(len(events) + lag):
        if count < len(events):
            arrive(*events[count])
        if count >= lag:
            forward(*events[count - lag])

    for index in range(6):

        @pl.when(seq < LINE - 1)
        def _():
            along(seq, index, 0, right).wait_send()

        @pl.when(seq > 0)
        def _():
            along(seq, index, 1, left).wait_send()

    for step, index in events:
        for direction in range(2):
            source = seq - step if direction == 0 else seq + step
            present = source >= 0 if direction == 0 else source < LINE
            onward = seq < LINE - 1 if direction == 0 else seq > 0
            target = right if direction == 0 else left

            @pl.when(present)
            def _():
                over("pair", source, index, quarter, other_pair).wait_send()
                over("core", source, index, quarter, other_core).wait_send()
                over("relay", source, index, across, other_core).wait_send()
                over("core", source, index, opposite, other_core).wait_recv()
                over("relay", source, index, opposite_across, other_core).wait_recv()

            @pl.when(jnp.logical_and(present, onward))
            def _():
                along(source, index, direction, target).wait_send()

    for copy in own:
        copy.wait()
    for step in range(1, LINE):
        source = lax.rem(seq + LINE - step, LINE)
        row_copies[step - 1].wait_send()
        remote(
            rows, rows_out.at[source], rows_send.at[step - 1], rows_recv.at[source], other_core
        ).wait_recv()
    finish_meta()
    finish_piece()


def gather_all(shards, families, upstream, order, quarters, tally, scales, offsets):
    anywhere = pl.BlockSpec(memory_space=pl.ANY)
    inside = pl.BlockSpec(memory_space=pltpu.VMEM)
    scalars = pl.BlockSpec(memory_space=pltpu.SMEM)
    columns, width = families.shape[2:]
    piece = jax.ShapeDtypeStruct((2, columns, width), families.dtype)
    meta = jax.ShapeDtypeStruct((2, columns + 8, columns), jnp.float32)
    rows = jax.ShapeDtypeStruct((8, 256), jnp.float32)
    dma = pltpu.SemaphoreType.DMA
    shapes = [
        jax.ShapeDtypeStruct((shard.shape[1] * LINE, shard.shape[2]), shard.dtype)
        for shard in shards
    ]
    shapes += [piece, meta, jax.ShapeDtypeStruct((LINE,) + rows.shape, rows.dtype)]
    return pl.pallas_call(
        gather_kernel,
        out_shape=shapes,
        in_specs=[anywhere] * 6 + [inside, inside, scalars, inside, scalars, inside, inside],
        out_specs=[anywhere] * 9,
        scratch_shapes=[
            pltpu.VMEM(piece.shape, piece.dtype),
            pltpu.VMEM(meta.shape, meta.dtype),
            pltpu.VMEM(rows.shape, rows.dtype),
            dma((9,)),
            dma((6,)),
            dma((2, LINE, 6)),
            dma((LINE, 6)),
            dma((LINE, 6)),
            dma((LINE, 6)),
            dma((2, LINE, 6)),
            dma((2, LINE, 6)),
            dma((2,)),
            dma((2,)),
            dma((2,)),
            dma((2,)),
            dma((LINE - 1,)),
            dma((LINE,)),
        ],
        compiler_params=pltpu.CompilerParams(
            collective_id=0, has_side_effects=True, vmem_limit_bytes=60 * 2**20
        ),
        name="gather_weights",
    )(*shards, families, upstream, order, quarters, tally, scales, offsets)


def reduce_kernel(chunks, paired, *refs):
    grads, vector, out, vector_out = refs[:4]
    (
        mine,
        from_core,
        from_pair,
        from_left,
        from_right,
        late_pair,
        vec_core,
        vec_pair,
        vec_line,
        load_sem,
        core_send,
        core_recv,
        pair_send,
        pair_recv,
        line_send,
        left_recv,
        right_recv,
        late_send,
        late_recv,
        share_send,
        share_recv,
        out_sem,
        vec_send,
        vec_recv,
    ) = refs[4:]
    where = place()
    pipe, seq, dp, core, pair = where
    other_core, other_pair = neighbours(*where)
    right, left = ((pipe, seq + 1, dp), (pipe, seq - 1, dp))
    units = LINE * chunks
    depth = mine.shape[2]
    greet(*where)()

    def unit_of(number):
        turn = lax.div(number, LINE)
        order = number - turn * LINE
        half = lax.div(order, 2)
        target = jnp.where(lax.rem(order, 2) == 0, LINE - 1 - half, half)
        return (target, chunks - 1 - turn)

    def window(chunk):
        return pl.ds(pl.multiple_of(chunk * depth, depth), depth)

    def load(number, side):
        target, chunk = unit_of(number)
        return pltpu.make_async_copy(
            grads.at[target, 2 * side + core, window(chunk)],
            mine.at[number, side],
            load_sem.at[number, side],
        )

    def to_core(number, side):
        target, chunk = unit_of(number)
        return remote(
            grads.at[target, 2 * side + 1 - core, window(chunk)],
            from_core.at[number, side],
            core_send.at[number, side],
            core_recv.at[number, side],
            other_core,
        )

    def issue(number, carry):
        for side in range(2):
            to_core(number, side).start()
            load(number, side).start()
        return carry

    lax.fori_loop(0, units, issue, 0)

    vec_first = remote(vector, vec_core, vec_send.at[0], vec_recv.at[0], other_core)
    vec_first.start()
    def add(left_value, right_value):
        return (left_value.astype(jnp.float32) + right_value.astype(jnp.float32)).astype(
            jnp.bfloat16
        )

    def to_pair(number):
        return remote(
            mine.at[number, 1 - pair],
            from_pair.at[number],
            pair_send.at[number],
            pair_recv.at[number],
            other_pair,
        )

    def arrive(number, side):
        load(number, side).wait()
        to_core(number, side).wait_recv()
        mine[number, side] = add(mine[number, side], from_core[number, side])

    def line_copy(number, single, direction):
        target = right if direction == 0 else left
        landing = from_left if direction == 0 else from_right
        sems = left_recv if direction == 0 else right_recv
        if single:
            return remote(
                mine.at[number, pair],
                landing.at[number, 0],
                line_send.at[number],
                sems.at[number],
                target,
            )
        return remote(
            mine.at[number], landing.at[number], line_send.at[number], sems.at[number], target
        )

    def take(number, single, direction):
        landing = from_left if direction == 0 else from_right
        line_copy(number, single, direction).wait_recv()
        if single:
            mine[number, pair] = add(mine[number, pair], landing[number, 0])
        else:
            for side in range(2):
                mine[number, side] = add(mine[number, side], landing[number, side])

    def late_copy(number, chunk, single):
        if single:
            return remote(
                mine.at[number, pair],
                out.at[dp, window(chunk)],
                late_send.at[chunk],
                late_recv.at[chunk],
                other_pair,
            )
        return remote(
            mine.at[number],
            late_pair.at[chunk],
            late_send.at[chunk],
            late_recv.at[chunk],
            other_pair,
        )

    def share_copy(number, chunk, side, relay):
        spot_out = out.at[2 * side + core, window(chunk)]
        return remote(
            spot_out if relay else mine.at[number, side],
            spot_out,
            share_send.at[side, chunk],
            share_recv.at[side, chunk],
            other_core,
        )

    def out_copy(number, chunk, side):
        return pltpu.make_async_copy(
            mine.at[number, side], out.at[2 * side + core, window(chunk)], out_sem.at[side, chunk]
        )

    def at(number, condition, body):
        clipped = jnp.clip(number, 0, units - 1)
        target, chunk = unit_of(clipped)
        valid = jnp.logical_and(number >= 0, number < units)
        valid = jnp.logical_and(valid, condition(target))
        if paired > 0:

            @pl.when(jnp.logical_and(valid, chunk < paired))
            def _():
                body(clipped, chunk, True)

        if paired < chunks:

            @pl.when(jnp.logical_and(valid, chunk >= paired))
            def _():
                body(clipped, chunk, False)

    def first_stage(number, chunk, single):
        if single:
            for half in range(2):
                side = 1 - pair if half == 0 else pair
                arrive(number, side)
                if half == 0:
                    to_pair(number).start()
        else:
            for side in range(2):
                arrive(number, side)

    def second_stage(number, chunk, single):
        if single:
            to_pair(number).wait_recv()
            mine[number, pair] = add(mine[number, pair], from_pair[number])

    def hop(direction):
        def body(number, chunk, single):
            @pl.when(seq > 0 if direction == 0 else seq < LINE - 1)
            def _():
                take(number, single, direction)

            line_copy(number, single, direction).start()

        return body

    def last_stage(number, chunk, single):
        for direction in range(2):

            @pl.when(seq > 0 if direction == 0 else seq < LINE - 1)
            def _():
                take(number, single, direction)

        late_copy(number, chunk, single).start()
        if single:
            out_copy(number, chunk, pair).start()
            share_copy(number, chunk, pair, False).start()

    def share_stage(number, chunk, single):
        if single:
            remote(
                mine.at[number, pair],
                out.at[dp + 2 - 4 * pair, window(chunk)],
                late_send.at[chunk],
                late_recv.at[chunk],
                other_pair,
            ).wait_recv()
            share_copy(number, chunk, 1 - pair, True).start()
        else:
            late_copy(number, chunk, False).wait()
            for side in range(2):
                mine[number, side] = add(mine[number, side], late_pair[chunk, side])
                out_copy(number, chunk, side).start()
                share_copy(number, chunk, side, False).start()

    always = lambda target: target >= 0
    far = jnp.maximum(seq, LINE - 1 - seq)
    ahead, pair_lag, hop_lag, share_lag = (2, 3, 4, 4)

    def step(number, carry):
        for index in range(ahead):
            at(ahead * number + index, always, first_stage)
        base = number - pair_lag
        at(base, always, second_stage)
        at(base - hop_lag * seq, lambda target: target > seq, hop(0))
        at(base - hop_lag * (LINE - 1 - seq), lambda target: target < seq, hop(1))
        at(base - hop_lag * far, lambda target: target == seq, last_stage)
        at(base - hop_lag * far - share_lag, lambda target: target == seq, share_stage)
        return carry

    lax.fori_loop(0, units + pair_lag + hop_lag * (LINE - 1) + share_lag, step, 0)

    vec_first.wait()
    vec_core[...] = vector[...] + vec_core[...]
    vec_second = remote(vec_core, vec_pair, vec_send.at[1], vec_recv.at[1], other_pair)
    vec_second.start()
    vec_second.wait()
    vec_pair[...] = vec_core[...] + vec_pair[...]
    for move in range(1, LINE):
        goal = lax.rem(seq + move, LINE)
        remote(
            vec_pair.at[goal],
            vec_line.at[seq],
            vec_send.at[1 + move],
            vec_recv.at[2 + seq],
            (pipe, goal, dp),
        ).start()
    vec_line[seq] = vec_pair[seq]
    for move in range(1, LINE):
        goal = lax.rem(seq + move, LINE)
        source = lax.rem(seq + LINE - move, LINE)
        remote(
            vec_pair.at[goal],
            vec_line.at[source],
            vec_send.at[1 + move],
            vec_recv.at[2 + source],
            (pipe, goal, dp),
        ).wait()
    total = vec_line[0]
    for source in range(1, LINE):
        total = total + vec_line[source]
    vector_out[...] = total

    def drain(number, carry):
        for side in range(2):
            to_core(number, side).wait_send()

        def sends(number, chunk, single):
            if single:
                to_pair(number).wait_send()

        at(number, always, sends)
        at(
            number,
            lambda target: target > seq,
            lambda number, chunk, single: line_copy(number, single, 0).wait_send(),
        )
        at(
            number,
            lambda target: target < seq,
            lambda number, chunk, single: line_copy(number, single, 1).wait_send(),
        )

        def shared(number, chunk, single):
            if single:
                late_copy(number, chunk, True).wait_send()
                out_copy(number, chunk, pair).wait()
                share_copy(number, chunk, pair, False).wait_send()
                share_copy(number, chunk, 1 - pair, True).wait_send()
            else:
                for side in range(2):
                    out_copy(number, chunk, side).wait()
                    share_copy(number, chunk, side, False).wait_send()
            for side in range(2):
                spot_out = out.at[2 * side + 1 - core, window(chunk)]
                remote(
                    spot_out,
                    spot_out,
                    share_send.at[side, chunk],
                    share_recv.at[side, chunk],
                    other_core,
                ).wait_recv()

        at(number, lambda target: target == seq, shared)
        return carry

    lax.fori_loop(0, units, drain, 0)


def reduce_all(grads, vector):
    anywhere = pl.BlockSpec(memory_space=pl.ANY)
    inside = pl.BlockSpec(memory_space=pltpu.VMEM)
    dma = pltpu.SemaphoreType.DMA
    chunks, paired = (6, 4)
    rows, columns = grads.shape[2:]
    depth = rows // chunks
    units = LINE * chunks
    block = (depth, columns)
    return pl.pallas_call(
        functools.partial(reduce_kernel, chunks, paired),
        out_shape=[
            jax.ShapeDtypeStruct(grads.shape[1:], grads.dtype),
            jax.ShapeDtypeStruct(vector.shape[1:], vector.dtype),
        ],
        in_specs=[anywhere, inside],
        out_specs=[anywhere, inside],
        scratch_shapes=[
            pltpu.VMEM((units, 2) + block, jnp.bfloat16),
            pltpu.VMEM((units, 2) + block, jnp.bfloat16),
            pltpu.VMEM((units,) + block, jnp.bfloat16),
            pltpu.VMEM((units, 2) + block, jnp.bfloat16),
            pltpu.VMEM((units, 2) + block, jnp.bfloat16),
            pltpu.VMEM((chunks, 2) + block, jnp.bfloat16),
            pltpu.VMEM(vector.shape, jnp.float32),
            pltpu.VMEM(vector.shape, jnp.float32),
            pltpu.VMEM(vector.shape, jnp.float32),
            dma((units, 2)),
            dma((units, 2)),
            dma((units, 2)),
            dma((units,)),
            dma((units,)),
            dma((units,)),
            dma((units,)),
            dma((units,)),
            dma((chunks,)),
            dma((chunks,)),
            dma((2, chunks)),
            dma((2, chunks)),
            dma((2, chunks)),
            dma((2 + LINE,)),
            dma((2 + LINE,)),
        ],
        compiler_params=pltpu.CompilerParams(
            collective_id=1, has_side_effects=True, vmem_limit_bytes=60 * 2**20
        ),
        name="reduce_grads",
    )(grads, vector)


def dot(left, right, left_axis, right_axis):
    return lax.dot_general(
        left,
        right,
        (((left_axis,), (right_axis,)), ((), ())),
        preferred_element_type=jnp.float32,
    )


def unit_rows(values):
    average = jnp.mean(values, axis=-1, keepdims=True)
    centered = values - average
    variance = jnp.mean(centered * centered, axis=-1, keepdims=True)
    root = lax.rsqrt(variance + norm_epsilon)
    return (centered * root, root)


def unit_rows_back(grad, values, gain_row):
    unit, root = unit_rows(values)
    scaled = grad * gain_row
    inner = jnp.mean(scaled * unit, axis=-1, keepdims=True)
    term = root * (scaled - jnp.mean(scaled, axis=-1, keepdims=True) - unit * inner)
    gain = jnp.sum(grad * unit, axis=0, keepdims=True)
    bias = jnp.sum(grad, axis=0, keepdims=True)
    return (term, gain, bias)


def layers_kernel(
    entry,
    meta,
    rows,
    w_row_any,
    w_row_out_any,
    w_col_any,
    w_col_out_any,
    w_up_any,
    w_down_any,
    act_out,
    der_out,
    cost_out,
    vector,
    grads,
    w_row,
    w_row_out,
    w_col,
    w_col_out,
    w_up,
    w_down,
    source,
    normal_a,
    normal_b,
    normal_c,
    mixer,
    mixer_col,
    blended,
    mixed,
    after_row,
    after_col,
    log_share,
    col_share,
    hidden,
    slope,
    total_grad,
    grad_in,
    branch_ffn,
    branch_col,
    branch_row,
    grad_up,
    grad_mixer_col,
    grad_mixer,
    logit_send,
    logit_recv,
    keys_recv,
    keys_send,
    keys_back,
    probs_send,
    probs_recv,
    halves,
    segment,
    spread,
    stage,
    stage_down,
    act,
    der,
    cost,
    weight_sem,
    logit_sems,
    keys_sems,
    back_sems,
    probs_sems,
    pipe_sems,
    stage_sems,
    home_sems,
    home_local,
    cost_send,
    cost_recv,
):
    where = place()
    pipe, seq, dp, core, pair = where
    other_core = (pipe, seq, dp + 1 - 2 * core)
    other_pipe = (1 - pipe, seq, dp)
    _, columns, width = entry.shape
    tokens = 2 * columns
    heads = HEAD_TALLY
    size = width // heads
    twin = 2 * size
    couples = heads // 2
    total_rows = LINE
    bf16, f32 = (jnp.bfloat16, jnp.float32)

    weights = [
        pltpu.make_async_copy(far, near, weight_sem.at[index])
        for index, (far, near) in enumerate(
            (
                (w_row_any, w_row),
                (w_row_out_any, w_row_out),
                (w_col_any, w_col),
                (w_col_out_any, w_col_out),
                (w_up_any, w_up),
                (w_down_any, w_down),
            )
        )
    ]
    for copy in weights:
        copy.start()

    hear = greet(*where, across_pipe=True)
    lane = lax.broadcasted_iota(jnp.int32, (columns, 2 * twin), 1)
    early = (lax.rem(lane, twin) < size).astype(f32)
    halves[0] = early.astype(bf16)
    halves[1] = (1.0 - early).astype(bf16)
    feature = lax.broadcasted_iota(jnp.int32, (width, 128), 0)
    head = lax.broadcasted_iota(jnp.int32, (width, 128), 1)
    belongs = jnp.logical_and(feature >= head * size, feature < head * size + size)
    segment[...] = belongs.astype(f32).astype(bf16)
    head = lax.broadcasted_iota(jnp.int32, (128, width), 0)
    feature = lax.broadcasted_iota(jnp.int32, (128, width), 1)
    belongs = jnp.logical_and(feature >= head * size, feature < head * size + size)
    spread[...] = belongs.astype(f32).astype(bf16)
    hear()

    def gain_of(index):
        return rows[index : index + 1, :]

    def bias_of(index):
        return rows[3 + index : 4 + index, :]

    def keep_vector(index, gain, bias):
        part = width // LINE
        for target in range(LINE):
            window = slice(target * part, (target + 1) * part)
            vector[target, index : index + 1, 0:part] = gain[:, window]
            vector[target, 3 + index : 4 + index, 0:part] = bias[:, window]

    vector[...] = jnp.zeros(vector.shape, f32)

    def both(ref, start):
        return jnp.concatenate(
            [ref[0:columns, start : start + twin], ref[columns:tokens, start : start + twin]],
            axis=1,
        )

    def stacked(ref, start):
        wide = both(ref, start)
        return jnp.concatenate([wide * halves[0], wide * halves[1]], axis=0)

    def unstack(wide):
        early_lane = lax.rem(lax.broadcasted_iota(jnp.int32, (columns, 2 * twin), 1), twin) < size
        return jnp.where(early_lane, wide[0:columns], wide[columns:])

    def put(ref, start, wide):
        ref[0:columns, start : start + twin] = wide[:, 0:twin].astype(bf16)
        ref[columns:tokens, start : start + twin] = wide[:, twin:].astype(bf16)

    def to_core(source_ref, target_ref, sems, index):
        return remote(
            source_ref, target_ref, sems.at[0, index], sems.at[1, index], other_core
        )

    start_act, finish_act = swap_rows(
        act, act_out, home_sems.at[0], home_sems.at[1], home_local.at[0], where
    )
    start_der, finish_der = swap_rows(
        der, der_out, home_sems.at[2], home_sems.at[3], home_local.at[1], where
    )
    sender = core == lax.div(seq, 2)
    spot = lax.rem(seq, 2)
    cost_own = pltpu.make_async_copy(cost, cost_out.at[spot], home_local.at[2])
    cost_copies = [
        remote(
            cost,
            cost_out.at[spot],
            cost_send.at[step - 1],
            cost_recv.at[spot],
            (pipe, lax.rem(seq + step, LINE), dp),
        )
        for step in range(1, LINE)
    ]

    send_on = remote(act, source, pipe_sems.at[0], pipe_sems.at[1], other_pipe)
    send_back = remote(der, grad_in, pipe_sems.at[2], pipe_sems.at[3], other_pipe)

    @pl.when(pipe == 0)
    def _():
        source[...] = entry[...]

    @pl.when(pipe == 1)
    def _():
        send_on.wait_recv()

    unit, _ = unit_rows(source[...].reshape(tokens, width).astype(f32))
    normal_a[...] = (unit * gain_of(0) + bias_of(0)).astype(bf16)
    weights[0].wait()
    for part in range(3):
        window = slice(part * width, (part + 1) * width)
        mixer[:, window] = dot(normal_a[...], w_row[:, window], 1, 0).astype(bf16)
    logit_factor = 1.0 / (math.sqrt(size) * math.sqrt(total_rows))
    logit_copies = []
    for couple in range(couples):
        partial_value = logit_factor * dot(
            both(mixer, couple * twin), stacked(mixer, width + couple * twin), 1, 1
        )
        logit_send[couple] = partial_value.astype(bf16)
        copy = to_core(logit_send.at[couple], logit_recv.at[couple], logit_sems, couple)
        copy.start()
        logit_copies.append(copy)
    valid = (
        lax.broadcasted_iota(jnp.int32, (columns, 1), 0).astype(f32) < meta[0, columns : columns + 1, 0:1]
    ).astype(f32)
    disorder = jnp.zeros((columns, 1), f32)
    for couple in range(couples):
        logit_copies[couple].wait_recv()
        wide = logit_send[couple].astype(f32) + logit_recv[couple].astype(f32)
        shares = []
        for half in range(2):
            logits = wide[:, half * columns : (half + 1) * columns]
            shifted_logits = logits - jnp.max(logits, axis=-1, keepdims=True)
            powers = jnp.exp(shifted_logits)
            total = jnp.sum(powers, axis=-1, keepdims=True)
            logs = shifted_logits - jnp.log(total)
            share = powers / total
            log_share[couple, :, half * columns : (half + 1) * columns] = logs
            disorder = disorder - jnp.sum(share * logs, axis=-1, keepdims=True) * valid
            shares.append(share.astype(bf16))
        put(
            blended,
            couple * twin,
            dot(
                jnp.concatenate(shares, axis=1), stacked(mixer, 2 * width + couple * twin), 1, 0
            ),
        )
    cost[...] = jnp.broadcast_to(
        jnp.sum(disorder, axis=0, keepdims=True) / float(heads * columns), cost.shape
    )
    weights[1].wait()
    after_row[...] = source[...].reshape(tokens, width).astype(f32) + dot(blended[...], w_row_out[...], 1, 0)
    unit, _ = unit_rows(after_row[...])
    normal_b[...] = (unit * gain_of(1) + bias_of(1)).astype(bf16)
    weights[2].wait()
    keys_copies = []
    for part in (1, 2, 0):
        window = slice(part * width, (part + 1) * width)
        mixer_col[:, window] = dot(normal_b[...], w_col[:, window], 1, 0).astype(bf16)
        if part > 0:
            copy = to_core(
                mixer_col.at[:, window], keys_recv.at[part - 1], keys_sems, part - 1
            )
            copy.start()
            keys_copies.append(copy)

    def line_of(part, place_of):
        if place_of < 2:
            rows_of = slice(place_of * columns, (place_of + 1) * columns)
            return mixer_col[rows_of, (1 + part) * width : (2 + part) * width]
        rows_of = slice((place_of - 2) * columns, (place_of - 1) * columns)
        return keys_recv[part, rows_of, :]

    def sums_by_head(wide_ref, start, line):
        products = [
            wide_ref[index * columns : (index + 1) * columns, start : start + width] * line
            for index in range(2)
        ]
        return dot(jnp.concatenate(products, axis=0), segment[...], 1, 0)

    def spread_heads(narrow):
        return dot(narrow, spread[...], 1, 0)

    scores = []
    for place_of in range(4):
        if place_of == 2:
            keys_copies[0].wait_recv()
        scores.append(sums_by_head(mixer_col, 0, line_of(0, place_of)) / math.sqrt(size))
    highest = functools.reduce(jnp.maximum, scores)
    powers = [jnp.exp(score - highest) for score in scores]
    total = functools.reduce(jnp.add, powers)
    keys_copies[1].wait_recv()
    gathered_mix = None
    for place_of in range(4):
        share = powers[place_of] / total
        col_share[place_of] = share
        wide = spread_heads(share.astype(bf16))
        line = line_of(1, place_of).astype(f32)
        term = jnp.concatenate([wide[0:columns] * line, wide[columns:] * line], axis=0)
        gathered_mix = term if gathered_mix is None else gathered_mix + term
    mixed[...] = gathered_mix.astype(bf16)
    weights[3].wait()
    after_col[...] = after_row[...] + dot(mixed[...], w_col_out[...], 1, 0)
    unit, _ = unit_rows(after_col[...])
    normal_c[...] = (unit * gain_of(2) + bias_of(2)).astype(bf16)
    weights[4].wait()
    weights[5].wait()
    parts = hidden.shape[1] // width
    result = after_col[...]
    for part in range(parts):
        window = slice(part * width, (part + 1) * width)
        upward = dot(normal_c[...], w_up[:, window], 1, 0)
        inner = 0.5 + 0.5 * lax.erf(upward * math.sqrt(0.5))
        density = jnp.exp(-0.5 * upward * upward) * (1.0 / math.sqrt(2.0 * math.pi))
        hidden[:, window] = (upward * inner).astype(bf16)
        slope[:, window] = (inner + upward * density).astype(bf16)
        result = result + dot(hidden[:, window], w_down[window, :], 1, 0)
    act[...] = result.astype(bf16).reshape(2, columns, width)

    @pl.when(pipe == 0)
    def _():
        send_on.start()

    start_act()

    @pl.when(sender)
    def _():
        cost_own.start()
        for copy in cost_copies:
            copy.start()

    @pl.when(pipe == 1)
    def _():
        for index in range(2):
            total_grad[index * columns : (index + 1) * columns, :] = (
                entry[index].astype(f32) * meta[index, 0:columns, 0:1]
            )

    @pl.when(pipe == 0)
    def _():
        send_back.wait_recv()
        total_grad[...] = grad_in[...].reshape(tokens, width).astype(f32)

    branch_ffn[...] = total_grad[...].astype(bf16)
    grad_normal = None
    for part in range(parts):
        window = slice(part * width, (part + 1) * width)
        grad_hidden = dot(branch_ffn[...], w_down[window, :], 1, 1)
        grad_up[:, window] = (grad_hidden * slope[:, window].astype(f32)).astype(bf16)
        term = dot(grad_up[:, window], w_up[:, window], 1, 1)
        grad_normal = term if grad_normal is None else grad_normal + term
    term, gain, bias = unit_rows_back(grad_normal, after_col[...], gain_of(2))
    keep_vector(2, gain, bias)
    total_grad[...] = total_grad[...] + term
    branch_col[...] = total_grad[...].astype(bf16)
    grad_mixed = dot(branch_col[...], w_col_out[...], 1, 1).astype(bf16)
    grad_probs = []
    for place_of in range(4):
        line = line_of(1, place_of)
        products = [grad_mixed[0:columns] * line, grad_mixed[columns:] * line]
        grad_probs.append(dot(jnp.concatenate(products, axis=0), segment[...], 1, 0))
    inner = functools.reduce(
        jnp.add, [col_share[place_of] * grad_probs[place_of] for place_of in range(4)]
    )
    root_size = math.sqrt(size)
    grad_query = None
    local_terms = []
    back_copies = []
    grad_lines = grad_mixed.astype(f32)
    query_lines = mixer_col[:, 0:width].astype(f32)
    for place_of in (2, 3, 0, 1):
        share = col_share[place_of]
        narrow = (share * (grad_probs[place_of] - inner)).astype(bf16)
        wide = spread_heads(narrow)
        line = line_of(0, place_of).astype(f32)
        term = jnp.concatenate([wide[0:columns] * line, wide[columns:] * line], axis=0)
        grad_query = term if grad_query is None else grad_query + term
        key_term = wide[0:columns] * query_lines[0:columns] + wide[columns:] * query_lines[columns:]
        key_term = key_term / root_size
        wide = spread_heads(share.astype(bf16))
        value_term = wide[0:columns] * grad_lines[0:columns] + wide[columns:] * grad_lines[columns:]
        if place_of >= 2:
            index = place_of - 2
            rows_of = slice(index * columns, (index + 1) * columns)
            keys_send[rows_of, 0:width] = key_term.astype(bf16)
            keys_send[rows_of, width:] = value_term.astype(bf16)
            copy = to_core(keys_send.at[rows_of, :], keys_back.at[rows_of, :], back_sems, index)
            copy.start()
            back_copies.append(copy)
        else:
            local_terms.append((key_term, value_term))
    grad_mixer_col[:, 0:width] = (grad_query / root_size).astype(bf16)
    for place_of in range(2):
        back_copies[place_of].wait()
        rows_of = slice(place_of * columns, (place_of + 1) * columns)
        for part in range(2):
            window = slice(part * width, (part + 1) * width)
            grad_mixer_col[rows_of, (1 + part) * width : (2 + part) * width] = (
                local_terms[place_of][part] + keys_back[rows_of, window].astype(f32)
            ).astype(bf16)
    grad_normal = None
    for part in range(3):
        window = slice(part * width, (part + 1) * width)
        term = dot(grad_mixer_col[:, window], w_col[:, window], 1, 1)
        grad_normal = term if grad_normal is None else grad_normal + term
    term, gain, bias = unit_rows_back(grad_normal, after_row[...], gain_of(1))
    keep_vector(1, gain, bias)
    total_grad[...] = total_grad[...] + term
    branch_row[...] = total_grad[...].astype(bf16)
    keys_send[:, 0:width] = dot(branch_row[...], w_row_out[...], 1, 1).astype(bf16)
    probs_copies = []
    for couple in range(couples):
        partial_value = dot(
            both(keys_send, couple * twin), stacked(mixer, 2 * width + couple * twin), 1, 1
        )
        probs_send[couple] = partial_value.astype(bf16)
        copy = to_core(probs_send.at[couple], probs_recv.at[couple], probs_sems, couple)
        copy.start()
        probs_copies.append(copy)
    column_weight = (float(total_rows * columns) / float(heads * columns)) * valid
    for couple in range(couples):
        start = couple * twin
        logs = log_share[couple]
        share = jnp.exp(logs)
        grad_wide = both(keys_send, start)
        put(
            grad_mixer,
            2 * width + start,
            unstack(dot(share.astype(bf16), grad_wide, 0, 0)),
        )
        probs_copies[couple].wait_recv()
        wide = probs_send[couple].astype(f32) + probs_recv[couple].astype(f32)
        pieces = []
        for half in range(2):
            window = slice(half * columns, (half + 1) * columns)
            part_share, part_logs, part_grad = (share[:, window], logs[:, window], wide[:, window])
            entropy = -jnp.sum(part_share * part_logs, axis=-1, keepdims=True)
            inner = jnp.sum(part_share * part_grad, axis=-1, keepdims=True)
            piece = part_share * (part_grad - inner)
            piece = piece - column_weight * part_share * (part_logs + entropy)
            pieces.append(piece.astype(bf16))
        grad_logits = jnp.concatenate(pieces, axis=1)
        put(
            grad_mixer,
            start,
            logit_factor * dot(grad_logits, stacked(mixer, width + start), 1, 0),
        )
        put(
            grad_mixer,
            width + start,
            logit_factor * unstack(dot(grad_logits, both(mixer, start), 0, 0)),
        )
    grad_normal = None
    for part in range(3):
        window = slice(part * width, (part + 1) * width)
        term = dot(grad_mixer[:, window], w_row[:, window], 1, 1)
        grad_normal = term if grad_normal is None else grad_normal + term
    term, gain, bias = unit_rows_back(grad_normal, source[...].reshape(tokens, width).astype(f32), gain_of(0))
    keep_vector(0, gain, bias)
    der[...] = (total_grad[...] + term).astype(bf16).reshape(2, columns, width)

    @pl.when(pipe == 1)
    def _():
        send_back.start()

    start_der()

    pairs = (
        (normal_a, grad_mixer),
        (blended, branch_row),
        (normal_b, grad_mixer_col),
        (mixed, branch_col),
        (normal_c, grad_up),
    )
    share = width // (4 * LINE)
    base = 0
    waiting = {}
    number = 0
    for left, right in pairs:
        for part in range(right.shape[1] // width):
            slot = number % 2
            if slot in waiting:
                for copy in waiting.pop(slot):
                    copy.wait()
            window = slice(part * width, (part + 1) * width)
            term = dot(left[...], right[:, window], 0, 0).astype(bf16)
            stage[slot] = term.reshape(LINE, 4, share, width)
            copies = [
                pltpu.make_async_copy(
                    stage.at[slot, target],
                    grads.at[target, :, pl.ds(base, share)],
                    stage_sems.at[slot, target],
                )
                for target in range(LINE)
            ]
            for copy in copies:
                copy.start()
            waiting[slot] = copies
            base += share
            number += 1
    for part in range(parts):
        slot = 2 + part % 2
        if slot in waiting:
            for copy in waiting.pop(slot):
                copy.wait()
        window = slice(part * width, (part + 1) * width)
        term = dot(hidden[:, window], branch_ffn[...], 0, 0).astype(bf16)
        stage_down[slot - 2] = term.reshape(4, width // 4, width)
        copy = pltpu.make_async_copy(
            stage_down.at[slot - 2],
            grads.at[part, :, pl.ds(base, width // 4)],
            stage_sems.at[slot, 0],
        )
        copy.start()
        waiting[slot] = [copy]
    for copies in waiting.values():
        for copy in copies:
            copy.wait()
    for copy in logit_copies + keys_copies + probs_copies:
        copy.wait_send()

    @pl.when(pipe == 0)
    def _():
        send_on.wait_send()

    @pl.when(pipe == 1)
    def _():
        send_back.wait_send()

    finish_act()
    finish_der()

    @pl.when(sender)
    def _():
        cost_own.wait()
        for copy in cost_copies:
            copy.wait_send()

    for index in range(2):

        @pl.when(2 * core + index != seq)
        def _():
            remote(
                cost, cost_out.at[index], cost_send.at[0], cost_recv.at[index], other_core
            ).wait_recv()


def run_layers(entry, meta, rows, wholes):
    _, columns, width = entry.shape
    tokens = 2 * columns
    couples = HEAD_TALLY // 2
    wide = wholes[4].shape[1]
    anywhere = pl.BlockSpec(memory_space=pl.ANY)
    inside = pl.BlockSpec(memory_space=pltpu.VMEM)
    dma = pltpu.SemaphoreType.DMA
    bf16, f32 = (jnp.bfloat16, jnp.float32)
    rows_of = lambda columns_of, kind=bf16: pltpu.VMEM((tokens, columns_of), kind)
    scores = pltpu.VMEM((couples, columns, 2 * columns), bf16)
    packed_rows = sum(whole.shape[0] * whole.shape[1] for whole in wholes) // (16 * width)
    return pl.pallas_call(
        layers_kernel,
        out_shape=[
            jax.ShapeDtypeStruct(entry.shape, bf16),
            jax.ShapeDtypeStruct(entry.shape, bf16),
            jax.ShapeDtypeStruct((2, 8, 128), f32),
            jax.ShapeDtypeStruct((LINE, 8, 256), f32),
            jax.ShapeDtypeStruct((LINE, 4, packed_rows, width), bf16),
        ],
        in_specs=[inside] * 3 + [anywhere] * 6,
        out_specs=[anywhere, anywhere, inside, inside, anywhere],
        scratch_shapes=[pltpu.VMEM(whole.shape, bf16) for whole in wholes]
        + [
            pltpu.VMEM(entry.shape, bf16),
            rows_of(width),
            rows_of(width),
            rows_of(width),
            rows_of(3 * width),
            rows_of(3 * width),
            rows_of(width),
            rows_of(width),
            rows_of(width, f32),
            rows_of(width, f32),
            pltpu.VMEM((couples, columns, 2 * columns), f32),
            pltpu.VMEM((4, tokens, 128), f32),
            rows_of(wide),
            rows_of(wide),
            rows_of(width, f32),
            pltpu.VMEM(entry.shape, bf16),
            rows_of(width),
            rows_of(width),
            rows_of(width),
            rows_of(wide),
            rows_of(3 * width),
            rows_of(3 * width),
            scores,
            scores,
            pltpu.VMEM((2, tokens, width), bf16),
            rows_of(2 * width),
            rows_of(2 * width),
            scores,
            scores,
            pltpu.VMEM((2, columns, 2 * columns), bf16),
            pltpu.VMEM((width, 128), bf16),
            pltpu.VMEM((128, width), bf16),
            pltpu.VMEM((2, LINE, 4, width // (4 * LINE), width), bf16),
            pltpu.VMEM((2, 4, width // 4, width), bf16),
            pltpu.VMEM(entry.shape, bf16),
            pltpu.VMEM(entry.shape, bf16),
            pltpu.VMEM((8, 128), f32),
            dma((6,)),
            dma((2, couples)),
            dma((2, 2)),
            dma((2, 2)),
            dma((2, couples)),
            dma((4,)),
            dma((4, LINE)),
            dma((4, 2)),
            dma((3,)),
            dma((LINE - 1,)),
            dma((2,)),
        ],
        compiler_params=pltpu.CompilerParams(
            collective_id=2, has_side_effects=True, vmem_limit_bytes=60 * 2**20
        ),
        name="two_layers",
    )(entry, meta, rows, *wholes)


def unpack_kernel(blocks, vector, *refs):
    results, gain, bias = (refs[:6], refs[6], refs[7])
    width = blocks.shape[2]
    base = 0
    for result in results:
        depth, wide = result.shape[1:]
        for part in range(wide // width):
            result[0, :, part * width : (part + 1) * width] = blocks[
                0, base : base + depth, :
            ].astype(jnp.float32)
            base += depth
    share = gain.shape[2]
    gain[0] = vector[0:3, 0:share]
    bias[0] = vector[3:6, 0:share]


def unpack_all(blocks, vector, shapes, share):
    width = blocks.shape[2]
    small = jax.ShapeDtypeStruct((1, 3, share), jnp.float32)
    return pl.pallas_call(
        unpack_kernel,
        grid=(4,),
        out_shape=[jax.ShapeDtypeStruct((1,) + shape, jnp.float32) for shape in shapes]
        + [small, small],
        in_specs=[
            pl.BlockSpec((1,) + blocks.shape[1:], lambda step: (step, 0, 0)),
            pl.BlockSpec(vector.shape, lambda step: (0, 0)),
        ],
        out_specs=[
            pl.BlockSpec((1, shape[0] // 4, shape[1]), lambda step: (0, step, 0))
            for shape in shapes
        ]
        + [pl.BlockSpec(small.shape, lambda step: (0, 0, 0))] * 2,
        compiler_params=pltpu.CompilerParams(vmem_limit_bytes=60 * 2**20),
        cost_estimate=pl.CostEstimate(
            flops=blocks.size, bytes_accessed=6 * blocks.size, transcendentals=0
        ),
        name="unpack_grads",
    )(blocks, vector)


def on_device_lined(
    embedded_families,
    order,
    token_quarter_factor,
    genuine_residue_tally,
    standardizer_scales,
    standardizer_offsets,
    row_qkv,
    row_out,
    col_qkv,
    col_out,
    ffn_up,
    ffn_down,
    upstream_sensitivity,
):
    model_width = embedded_families.shape[-1]
    share = standardizer_scales.shape[-1]
    shards = (row_qkv, row_out, col_qkv, col_out, ffn_up, ffn_down)
    *wholes, piece, meta, rows = gather_all(
        shards,
        embedded_families,
        upstream_sensitivity,
        order,
        token_quarter_factor,
        genuine_residue_tally,
        standardizer_scales,
        standardizer_offsets,
    )
    rows = rows[:, :, :share].transpose(1, 0, 2).reshape(8, model_width)
    activations, derivs, costs, vector, grads = run_layers(piece, meta, rows, wholes)
    out, vector = reduce_all(grads, vector)
    results = unpack_all(out, vector, [shard.shape[1:] for shard in shards], share)
    return (
        activations[None, :, None],
        derivs[None, :, None],
        costs[:, 0, 0][None],
        *results,
    )


def solution(mesh):
    in_specs = (
        P("dp", "seq", None, None),
        P("dp", None),
        P("dp", "seq", None),
        P("dp"),
        P("pipe", None, "seq"),
        P("pipe", None, "seq"),
        P("pipe", "seq", None),
        P("pipe", "seq", None),
        P("pipe", "seq", None),
        P("pipe", "seq", None),
        P("pipe", "seq", None),
        P("pipe", "seq", None),
        P("dp", "seq", None, None),
    )
    out_specs = (
        P("pipe", "dp", "seq", None, None),
        P("pipe", "dp", "seq", None, None),
        P("pipe", "dp"),
        P("pipe", "seq", None),
        P("pipe", "seq", None),
        P("pipe", "seq", None),
        P("pipe", "seq", None),
        P("pipe", "seq", None),
        P("pipe", "seq", None),
        P("pipe", None, "seq"),
        P("pipe", None, "seq"),
    )
    lined = mesh.shape["seq"] == LINE and mesh.shape["dp"] == 4 and mesh.shape["pipe"] == 2
    return jax.shard_map(
        on_device_lined if lined else on_device, mesh=mesh, in_specs=in_specs, out_specs=out_specs, check_vma=False
    )
```

```python
import functools
import math

import jax
import jax.numpy as jnp
from jax import lax
from jax.experimental import pallas as pl
from jax.experimental.pallas import tpu as pltpu
from jax.sharding import PartitionSpec as P

HEAD_TALLY = 12
LINE = 4
MESH = pl.DeviceIdType.MESH


norm_epsilon = 1e-05


def shifted(value, axis, steps):
    count = lax.axis_size(axis)
    initial, last = (max(0, -steps), min(count, count - steps))
    return lax.ppermute(value, axis, [(source, source + steps) for source in range(initial, last)])


def normed(values, gain_row, bias_row):
    average = jnp.mean(values, axis=-1, keepdims=True)
    centered = values - average
    variance = jnp.mean(centered * centered, axis=-1, keepdims=True)
    return centered * lax.rsqrt(variance + norm_epsilon) * gain_row + bias_row


def gelu_exact(values):
    return jax.nn.gelu(values, approximate=False)


def product(left, weight):
    return lax.dot_general(
        left, weight, (((left.ndim - 1,), (0,)), ((), ())), preferred_element_type=jnp.float32
    )


def product_back(left, weight):
    return lax.dot_general(
        left, weight, (((left.ndim - 1,), (1,)), ((), ())), preferred_element_type=jnp.float32
    )


def weight_term(left, right):
    return lax.dot_general(
        left, right, (((0, 1), (0, 1)), ((), ())), preferred_element_type=jnp.float32
    )


def split_heads(values, head_count):
    return values.reshape(values.shape[:-1] + (head_count, values.shape[-1] // head_count))


def choose(flag, first_tree, second_tree):
    return jax.tree.map(lambda early, later: jnp.where(flag, early, later), first_tree, second_tree)


def column_scores(queries, key_rows, head_count):
    query_heads = split_heads(queries, head_count)
    raw = jnp.einsum(
        "rche,sche->chrs",
        query_heads,
        split_heads(key_rows, head_count),
        preferred_element_type=jnp.float32,
    )
    return raw / math.sqrt(query_heads.shape[-1])


def column_forward(queries, key_rows, content_lines, head_count):
    scores = column_scores(queries, key_rows, head_count)
    log_total = jax.nn.logsumexp(scores, axis=-1)
    vertical_factors = jnp.exp(scores - log_total[..., None]).astype(jnp.bfloat16)
    mixed_cols = jnp.einsum(
        "gmqi,igmu->qgmu",
        vertical_factors,
        split_heads(content_lines, head_count),
        preferred_element_type=jnp.float32,
    )
    return (mixed_cols.reshape(queries.shape).astype(jnp.bfloat16), log_total)


def column_backward(queries, key_rows, content_lines, log_total, grad_mixed, head_count):
    scores = column_scores(queries, key_rows, head_count)
    softmax_share = jnp.exp(scores - log_total[..., None])
    grad_heads = split_heads(grad_mixed, head_count)
    grad_probs = jnp.einsum(
        "rche,sche->chrs",
        grad_heads,
        split_heads(content_lines, head_count),
        preferred_element_type=jnp.float32,
    )
    grad_values = jnp.einsum(
        "chrs,rche->sche",
        softmax_share.astype(jnp.bfloat16),
        grad_heads,
        preferred_element_type=jnp.float32,
    )
    grad_scores = (
        softmax_share * (grad_probs - jnp.sum(softmax_share * grad_probs, axis=-1, keepdims=True))
    ).astype(jnp.bfloat16)
    root_size = math.sqrt(queries.shape[-1] // head_count)
    grad_queries = (
        jnp.einsum(
            "gmqi,igmu->qgmu",
            grad_scores,
            split_heads(key_rows, head_count),
            preferred_element_type=jnp.float32,
        )
        / root_size
    )
    grad_keys = (
        jnp.einsum(
            "chrs,rche->sche",
            grad_scores,
            split_heads(queries, head_count),
            preferred_element_type=jnp.float32,
        )
        / root_size
    )
    return (
        grad_queries.reshape(queries.shape),
        grad_keys.reshape(key_rows.shape),
        grad_values.reshape(content_lines.shape),
    )


def row_split(horizontal_mixer, model_width, head_count):
    queries = split_heads(horizontal_mixer[..., :model_width], head_count)
    key_rows = split_heads(horizontal_mixer[..., model_width : 2 * model_width], head_count)
    content_lines = split_heads(horizontal_mixer[..., 2 * model_width :], head_count)
    return (queries, key_rows, content_lines)


def layer_forward(source_rows, family_residues, projection_tables, head_count):
    (
        horizontal_coefficients,
        w_row_out,
        vertical_coefficients,
        w_col_out,
        w_up,
        w_down,
        gain_rows,
        bias_rows,
    ) = projection_tables
    row_count, columns, model_width = source_rows.shape
    total_rows = row_count * lax.axis_size("seq")
    start = source_rows.astype(jnp.float32)
    layernorm_first = normed(start, gain_rows[0], bias_rows[0]).astype(jnp.bfloat16)
    horizontal_mixer = product(layernorm_first, horizontal_coefficients).astype(jnp.bfloat16)
    queries, key_rows, content_lines = row_split(horizontal_mixer, model_width, head_count)
    logit_factor = 1.0 / (math.sqrt(model_width // head_count) * math.sqrt(total_rows))
    partial_value = logit_factor * jnp.einsum(
        "rihe,rjhe->hij", queries, key_rows, preferred_element_type=jnp.float32
    )
    logits = lax.psum(partial_value.astype(jnp.bfloat16), "seq").astype(jnp.float32)
    softmax_share = jax.nn.softmax(logits, axis=-1)
    log_probs = jax.nn.log_softmax(logits, axis=-1)
    entropy = -jnp.sum(softmax_share * log_probs, axis=-1)
    valid_residues = (jnp.arange(columns, dtype=jnp.int32) < family_residues).astype(jnp.float32)
    disorder_cost = jnp.sum(entropy * valid_residues[None, :]) / float(head_count * columns)
    blended_lines = jnp.einsum(
        "vyp,opvl->oyvl",
        softmax_share.astype(jnp.bfloat16),
        content_lines,
        preferred_element_type=jnp.float32,
    )
    blended_lines = blended_lines.reshape(row_count, columns, model_width).astype(jnp.bfloat16)
    after_row = start + product(blended_lines, w_row_out)
    layernorm_second = normed(after_row, gain_rows[1], bias_rows[1]).astype(jnp.bfloat16)
    vertical_mixer = product(layernorm_second, vertical_coefficients).astype(jnp.bfloat16)
    everyone = lax.all_gather(vertical_mixer[..., model_width:], "seq", axis=0, tiled=True)
    mixed_values, log_total = column_forward(
        vertical_mixer[..., :model_width],
        everyone[..., :model_width],
        everyone[..., model_width:],
        head_count,
    )
    column_state = (everyone, log_total)
    after_col = after_row + product(mixed_values, w_col_out)
    normal_c = normed(after_col, gain_rows[2], bias_rows[2]).astype(jnp.bfloat16)
    upward = product(normal_c, w_up)
    hidden = gelu_exact(upward).astype(jnp.bfloat16)
    result = after_col + product(hidden, w_down)
    kept_state = (
        source_rows,
        layernorm_first,
        horizontal_mixer,
        logits,
        blended_lines,
        after_row,
        layernorm_second,
        vertical_mixer,
        column_state,
        mixed_values,
        after_col,
        normal_c,
        upward,
        hidden,
    )
    return (result.astype(jnp.bfloat16), disorder_cost, kept_state)


def layer_backward(kept_state, family_residues, grad_result, projection_tables, head_count):
    (
        horizontal_coefficients,
        w_row_out,
        vertical_coefficients,
        w_col_out,
        w_up,
        w_down,
        gain_rows,
        bias_rows,
    ) = projection_tables
    (
        source_rows,
        layernorm_first,
        horizontal_mixer,
        logits,
        blended_lines,
        after_row,
        layernorm_second,
        vertical_mixer,
        column_state,
        mixed_values,
        after_col,
        normal_c,
        upward,
        hidden,
    ) = kept_state
    row_count, columns, model_width = source_rows.shape
    total_rows = row_count * lax.axis_size("seq")
    grad_branch_ffn = grad_result.astype(jnp.bfloat16)
    grad_hidden = product_back(grad_branch_ffn, w_down)
    grad_upward = jax.vjp(gelu_exact, upward)[1](grad_hidden)[0].astype(jnp.bfloat16)
    grad_normal_c = product_back(grad_upward, w_up)
    from_norm, gain_last, bias_last = jax.vjp(normed, after_col, gain_rows[2], bias_rows[2])[1](
        grad_normal_c
    )
    grad_col = grad_result + from_norm
    grad_branch_col = grad_col.astype(jnp.bfloat16)
    grad_attended = product_back(grad_branch_col, w_col_out).astype(jnp.bfloat16)
    everyone, log_total = column_state
    grad_query_col, grad_key_col, grad_value_col = column_backward(
        vertical_mixer[..., :model_width],
        everyone[..., :model_width],
        everyone[..., model_width:],
        log_total,
        grad_attended,
        head_count,
    )
    grad_kv_rows = lax.psum_scatter(
        jnp.concatenate([grad_key_col, grad_value_col], axis=-1).astype(jnp.bfloat16),
        "seq",
        scatter_dimension=0,
        tiled=True,
    ).astype(jnp.float32)
    grad_col_proj = jnp.concatenate([grad_query_col, grad_kv_rows], axis=-1).astype(jnp.bfloat16)
    grad_normal_b = product_back(grad_col_proj, vertical_coefficients)
    from_norm, gain_middle, bias_middle = jax.vjp(normed, after_row, gain_rows[1], bias_rows[1])[1](
        grad_normal_b
    )
    grad_row = grad_col + from_norm
    grad_branch_row = grad_row.astype(jnp.bfloat16)
    grad_mixed = split_heads(
        product_back(grad_branch_row, w_row_out).astype(jnp.bfloat16), head_count
    )
    queries, key_rows, content_lines = row_split(horizontal_mixer, model_width, head_count)
    softmax_share = jax.nn.softmax(logits, axis=-1)
    log_probs = jax.nn.log_softmax(logits, axis=-1)
    entropy = -jnp.sum(softmax_share * log_probs, axis=-1)
    partial_value = jnp.einsum(
        "rihe,rjhe->hij", grad_mixed, content_lines, preferred_element_type=jnp.float32
    )
    grad_probs = lax.psum(partial_value.astype(jnp.bfloat16), "seq").astype(jnp.float32)
    grad_values = jnp.einsum(
        "hij,rihe->rjhe",
        softmax_share.astype(jnp.bfloat16),
        grad_mixed,
        preferred_element_type=jnp.float32,
    )
    valid_residues = (jnp.arange(columns, dtype=jnp.int32) < family_residues).astype(jnp.float32)
    column_weight = float(total_rows * columns) * valid_residues / float(head_count * columns)
    grad_logits = softmax_share * (
        grad_probs - jnp.sum(softmax_share * grad_probs, axis=-1, keepdims=True)
    )
    grad_logits = grad_logits - column_weight[None, :, None] * softmax_share * (
        log_probs + entropy[..., None]
    )
    grad_logits = grad_logits.astype(jnp.bfloat16)
    logit_factor = 1.0 / (math.sqrt(model_width // head_count) * math.sqrt(total_rows))
    grad_queries = logit_factor * jnp.einsum(
        "vyp,opvl->oyvl", grad_logits, key_rows, preferred_element_type=jnp.float32
    )
    grad_keys = logit_factor * jnp.einsum(
        "hij,rihe->rjhe", grad_logits, queries, preferred_element_type=jnp.float32
    )
    grad_row_proj = jnp.concatenate(
        [
            grad_queries.reshape(row_count, columns, model_width),
            grad_keys.reshape(row_count, columns, model_width),
            grad_values.reshape(row_count, columns, model_width),
        ],
        axis=-1,
    ).astype(jnp.bfloat16)
    grad_normal_a = product_back(grad_row_proj, horizontal_coefficients)
    from_norm, gain_first, bias_first = jax.vjp(
        normed, source_rows.astype(jnp.float32), gain_rows[0], bias_rows[0]
    )[1](grad_normal_a)
    grad_source = (grad_row + from_norm).astype(jnp.bfloat16)
    operand_pairs = (
        (layernorm_first, grad_row_proj),
        (blended_lines, grad_branch_row),
        (layernorm_second, grad_col_proj),
        (mixed_values, grad_branch_col),
        (normal_c, grad_upward),
        (hidden, grad_branch_ffn),
    )
    norm_grads = (
        jnp.stack([gain_first, gain_middle, gain_last]),
        jnp.stack([bias_first, bias_middle, bias_last]),
    )
    return (grad_source, operand_pairs, norm_grads)


def on_device(
    embedded_families,
    order,
    token_quarter_factor,
    genuine_residue_tally,
    standardizer_scales,
    standardizer_offsets,
    row_qkv,
    row_out,
    col_qkv,
    col_out,
    ffn_up,
    ffn_down,
    upstream_sensitivity,
):
    head_count = HEAD_TALLY
    segment_place = lax.axis_index("pipe")
    gathered = (
        lax.all_gather(row_qkv, "seq", axis=1, tiled=True),
        lax.all_gather(row_out, "seq", axis=1, tiled=True),
        lax.all_gather(col_qkv, "seq", axis=1, tiled=True),
        lax.all_gather(col_out, "seq", axis=1, tiled=True),
        lax.all_gather(ffn_up, "seq", axis=1, tiled=True),
        lax.all_gather(ffn_down, "seq", axis=1, tiled=True),
        lax.all_gather(standardizer_scales.astype(jnp.bfloat16), "seq", axis=2, tiled=True).astype(
            standardizer_scales.dtype
        ),
        lax.all_gather(standardizer_offsets.astype(jnp.bfloat16), "seq", axis=2, tiled=True).astype(
            standardizer_offsets.dtype
        ),
    )
    projection_tables = tuple((gathered_piece[0] for gathered_piece in gathered))
    small_batch_number = embedded_families.shape[0]
    sequence = order[0]
    received = jnp.zeros(embedded_families.shape[1:], jnp.bfloat16)
    results = []
    focus_spread_levies = []
    kept_list = []
    for period in range(small_batch_number + 1):
        slot_here = jnp.clip(period - segment_place, 0, small_batch_number - 1)
        align_here = sequence[slot_here]
        source_rows = jnp.where(segment_place == 0, embedded_families[align_here], received)
        result, disorder_cost, kept_state = layer_forward(
            source_rows, genuine_residue_tally[align_here], projection_tables, head_count
        )
        results.append(result)
        focus_spread_levies.append(disorder_cost)
        kept_list.append(kept_state)
        if period < small_batch_number:
            received = shifted(result, "pipe", 1)
    activations = lax.dynamic_slice_in_dim(jnp.stack(results), segment_place, small_batch_number, 0)
    penalty_output = lax.dynamic_slice_in_dim(
        jnp.stack(focus_spread_levies), segment_place, small_batch_number, 0
    )
    grad_received = jnp.zeros(embedded_families.shape[1:], jnp.bfloat16)
    left_lists = [[] for index in range(6)]
    right_lists = [[] for index in range(6)]
    gain_total = None
    bias_total = None
    grad_sources = []
    for period in range(small_batch_number + 1):
        slot_raw = period - 1 + segment_place
        in_range = jnp.logical_and(slot_raw >= 0, slot_raw < small_batch_number)
        slot_here = jnp.clip(slot_raw, 0, small_batch_number - 1)
        align_here = sequence[slot_here]
        kept_state = choose(
            segment_place == 0,
            kept_list[max(period - 1, 0)],
            kept_list[min(period + 1, small_batch_number)],
        )
        outgrad = (
            upstream_sensitivity[slot_here].astype(jnp.float32)
            * token_quarter_factor[align_here].astype(jnp.float32)[..., None]
            * 0.25
        )
        incoming_grad = jnp.where(segment_place == 1, outgrad, grad_received.astype(jnp.float32))
        grad_source, operand_pairs, norm_grads = layer_backward(
            kept_state,
            genuine_residue_tally[align_here],
            incoming_grad,
            projection_tables,
            head_count,
        )
        for index in range(6):
            left_lists[index].append(operand_pairs[index][0])
            right_lists[index].append(
                jnp.where(
                    in_range, operand_pairs[index][1], jnp.zeros_like(operand_pairs[index][1])
                )
            )
        gain_term = jnp.where(in_range, norm_grads[0], jnp.zeros_like(norm_grads[0]))
        bias_term = jnp.where(in_range, norm_grads[1], jnp.zeros_like(norm_grads[1]))
        gain_total = gain_term if gain_total is None else gain_total + gain_term
        bias_total = bias_term if bias_total is None else bias_total + bias_term
        grad_sources.append(grad_source)
        if period < small_batch_number:
            grad_received = shifted(grad_source, "pipe", -1)
    block_entry_derivs = lax.dynamic_slice_in_dim(
        jnp.stack(grad_sources), 1 - segment_place, small_batch_number, 0
    )
    weight_totals = [
        weight_term(
            jnp.concatenate(left_lists[index], axis=0), jnp.concatenate(right_lists[index], axis=0)
        )
        for index in range(6)
    ]
    shared = (
        lax.psum_scatter(
            weight_totals[0].astype(jnp.bfloat16), "seq", scatter_dimension=0, tiled=True
        ).astype(jnp.float32),
        lax.psum_scatter(
            weight_totals[1].astype(jnp.bfloat16), "seq", scatter_dimension=0, tiled=True
        ).astype(jnp.float32),
        lax.psum_scatter(
            weight_totals[2].astype(jnp.bfloat16), "seq", scatter_dimension=0, tiled=True
        ).astype(jnp.float32),
        lax.psum_scatter(
            weight_totals[3].astype(jnp.bfloat16), "seq", scatter_dimension=0, tiled=True
        ).astype(jnp.float32),
        lax.psum_scatter(
            weight_totals[4].astype(jnp.bfloat16), "seq", scatter_dimension=0, tiled=True
        ).astype(jnp.float32),
        lax.psum_scatter(
            weight_totals[5].astype(jnp.bfloat16), "seq", scatter_dimension=0, tiled=True
        ).astype(jnp.float32),
        lax.psum_scatter(
            gain_total.astype(jnp.bfloat16), "seq", scatter_dimension=1, tiled=True
        ).astype(jnp.float32),
        lax.psum_scatter(
            bias_total.astype(jnp.bfloat16), "seq", scatter_dimension=1, tiled=True
        ).astype(jnp.float32),
    )
    (
        shared_row_qkv,
        shared_row_out,
        shared_col_qkv,
        shared_col_out,
        shared_up,
        shared_down,
        shared_gain,
        shared_bias,
    ) = shared
    summed = (
        lax.psum(shared_row_qkv.astype(jnp.bfloat16), "dp").astype(jnp.float32),
        lax.psum(shared_row_out.astype(jnp.bfloat16), "dp").astype(jnp.float32),
        lax.psum(shared_col_qkv.astype(jnp.bfloat16), "dp").astype(jnp.float32),
        lax.psum(shared_col_out.astype(jnp.bfloat16), "dp").astype(jnp.float32),
        lax.psum(shared_up.astype(jnp.bfloat16), "dp").astype(jnp.float32),
        lax.psum(shared_down.astype(jnp.bfloat16), "dp").astype(jnp.float32),
        lax.psum(shared_gain.astype(jnp.bfloat16), "dp").astype(jnp.float32),
        lax.psum(shared_bias.astype(jnp.bfloat16), "dp").astype(jnp.float32),
    )
    return (
        activations[None],
        block_entry_derivs[None],
        penalty_output[None],
        summed[0][None],
        summed[1][None],
        summed[2][None],
        summed[3][None],
        summed[4][None],
        summed[5][None],
        summed[6][None],
        summed[7][None],
    )


def place():
    pipe, seq, dp = (lax.axis_index("pipe"), lax.axis_index("seq"), lax.axis_index("dp"))
    core = lax.rem(dp, 2)
    pair = lax.div(dp, 2)
    return (pipe, seq, dp, core, pair)


def neighbours(pipe, seq, dp, core, pair):
    other_core = (pipe, seq, dp + 1 - 2 * core)
    other_pair = (pipe, seq, dp + 2 - 4 * pair)
    return (other_core, other_pair)


def greet(pipe, seq, dp, core, pair, across_pipe=False):
    barrier = pltpu.get_barrier_semaphore()
    other_core, other_pair = neighbours(pipe, seq, dp, core, pair)
    count = 0
    for step in range(LINE):
        for flip in range(2):
            if step == 0 and flip == 0:
                continue
            where = dp if flip == 0 else dp + 1 - 2 * core
            pl.semaphore_signal(
                barrier,
                inc=1,
                device_id=(pipe, lax.rem(seq + step, LINE), where),
                device_id_type=MESH,
            )
            count += 1
    more = [other_pair] + ([(1 - pipe, seq, dp)] if across_pipe else [])
    for device in more:
        pl.semaphore_signal(barrier, inc=1, device_id=device, device_id_type=MESH)

    def hear():
        pl.semaphore_wait(barrier, count + len(more))

    return hear


def remote(source, target, send, recv, device):
    return pltpu.make_async_remote_copy(
        src_ref=source,
        dst_ref=target,
        send_sem=send,
        recv_sem=recv,
        device_id=device,
        device_id_type=MESH,
    )


def swap_rows(source, target, send, recv, local, where):
    pipe, seq, dp, core, pair = where
    half, rest = (lax.div(seq, 2), lax.rem(seq, 2))

    def each(action):
        for index in range(2):
            line = 2 * core + index
            here = jnp.logical_and(line == seq, half == core)
            copy = remote(
                source.at[index],
                target.at[rest],
                send.at[index],
                recv.at[rest],
                (pipe, line, dp - core + half),
            )
            arriving = remote(
                source.at[index],
                target.at[index],
                send.at[index],
                recv.at[index],
                (pipe, line, dp - core + half),
            )
            inside = pltpu.make_async_copy(source.at[index], target.at[rest], local)
            action(here, copy, arriving, inside)

    def start(here, copy, arriving, inside):
        pl.when(here)(inside.start)
        pl.when(jnp.logical_not(here))(copy.start)

    def finish(here, copy, arriving, inside):
        pl.when(here)(inside.wait)
        pl.when(jnp.logical_not(here))(copy.wait_send)
        pl.when(jnp.logical_not(here))(arriving.wait_recv)

    return (lambda: each(start), lambda: each(finish))


def reduce_kernel(chunks, paired, *refs):
    grads, vector, out, vector_out = refs[:4]
    (
        mine,
        from_core,
        from_pair,
        from_left,
        from_right,
        late_pair,
        vec_core,
        vec_pair,
        vec_line,
        load_sem,
        core_send,
        core_recv,
        pair_send,
        pair_recv,
        line_send,
        left_recv,
        right_recv,
        late_send,
        late_recv,
        share_send,
        share_recv,
        out_sem,
        vec_send,
        vec_recv,
    ) = refs[4:]
    where = place()
    pipe, seq, dp, core, pair = where
    other_core, other_pair = neighbours(*where)
    right, left = ((pipe, seq + 1, dp), (pipe, seq - 1, dp))
    units = LINE * chunks
    depth = mine.shape[2]
    greet(*where)()

    def unit_of(number):
        turn = lax.div(number, LINE)
        order = number - turn * LINE
        half = lax.div(order, 2)
        target = jnp.where(lax.rem(order, 2) == 0, LINE - 1 - half, half)
        return (target, chunks - 1 - turn)

    def window(chunk):
        return pl.ds(pl.multiple_of(chunk * depth, depth), depth)

    def load(number, side):
        target, chunk = unit_of(number)
        return pltpu.make_async_copy(
            grads.at[target, 2 * side + core, window(chunk)],
            mine.at[number, side],
            load_sem.at[number, side],
        )

    def to_core(number, side):
        target, chunk = unit_of(number)
        return remote(
            grads.at[target, 2 * side + 1 - core, window(chunk)],
            from_core.at[number, side],
            core_send.at[number, side],
            core_recv.at[number, side],
            other_core,
        )

    def issue(number, carry):
        for side in range(2):
            to_core(number, side).start()
            load(number, side).start()
        return carry

    lax.fori_loop(0, units, issue, 0)

    vec_first = remote(vector, vec_core, vec_send.at[0], vec_recv.at[0], other_core)
    vec_first.start()
    def add(left_value, right_value):
        return (left_value.astype(jnp.float32) + right_value.astype(jnp.float32)).astype(
            jnp.bfloat16
        )

    def to_pair(number):
        return remote(
            mine.at[number, 1 - pair],
            from_pair.at[number],
            pair_send.at[number],
            pair_recv.at[number],
            other_pair,
        )

    def arrive(number, side):
        load(number, side).wait()
        to_core(number, side).wait_recv()
        mine[number, side] = add(mine[number, side], from_core[number, side])

    def line_copy(number, single, direction):
        target = right if direction == 0 else left
        landing = from_left if direction == 0 else from_right
        sems = left_recv if direction == 0 else right_recv
        if single:
            return remote(
                mine.at[number, pair],
                landing.at[number, 0],
                line_send.at[number],
                sems.at[number],
                target,
            )
        return remote(
            mine.at[number], landing.at[number], line_send.at[number], sems.at[number], target
        )

    def take(number, single, direction):
        landing = from_left if direction == 0 else from_right
        line_copy(number, single, direction).wait_recv()
        if single:
            mine[number, pair] = add(mine[number, pair], landing[number, 0])
        else:
            for side in range(2):
                mine[number, side] = add(mine[number, side], landing[number, side])

    def late_copy(number, chunk, single):
        if single:
            return remote(
                mine.at[number, pair],
                out.at[dp, window(chunk)],
                late_send.at[chunk],
                late_recv.at[chunk],
                other_pair,
            )
        return remote(
            mine.at[number],
            late_pair.at[chunk],
            late_send.at[chunk],
            late_recv.at[chunk],
            other_pair,
        )

    def share_copy(number, chunk, side, relay):
        spot_out = out.at[2 * side + core, window(chunk)]
        return remote(
            spot_out if relay else mine.at[number, side],
            spot_out,
            share_send.at[side, chunk],
            share_recv.at[side, chunk],
            other_core,
        )

    def out_copy(number, chunk, side):
        return pltpu.make_async_copy(
            mine.at[number, side], out.at[2 * side + core, window(chunk)], out_sem.at[side, chunk]
        )

    def at(number, condition, body):
        clipped = jnp.clip(number, 0, units - 1)
        target, chunk = unit_of(clipped)
        valid = jnp.logical_and(number >= 0, number < units)
        valid = jnp.logical_and(valid, condition(target))
        if paired > 0:

            @pl.when(jnp.logical_and(valid, chunk < paired))
            def _():
                body(clipped, chunk, True)

        if paired < chunks:

            @pl.when(jnp.logical_and(valid, chunk >= paired))
            def _():
                body(clipped, chunk, False)

    def first_stage(number, chunk, single):
        if single:
            for half in range(2):
                side = 1 - pair if half == 0 else pair
                arrive(number, side)
                if half == 0:
                    to_pair(number).start()
        else:
            for side in range(2):
                arrive(number, side)

    def second_stage(number, chunk, single):
        if single:
            to_pair(number).wait_recv()
            mine[number, pair] = add(mine[number, pair], from_pair[number])

    def hop(direction):
        def body(number, chunk, single):
            @pl.when(seq > 0 if direction == 0 else seq < LINE - 1)
            def _():
                take(number, single, direction)

            line_copy(number, single, direction).start()

        return body

    def last_stage(number, chunk, single):
        for direction in range(2):

            @pl.when(seq > 0 if direction == 0 else seq < LINE - 1)
            def _():
                take(number, single, direction)

        late_copy(number, chunk, single).start()
        if single:
            out_copy(number, chunk, pair).start()
            share_copy(number, chunk, pair, False).start()

    def share_stage(number, chunk, single):
        if single:
            remote(
                mine.at[number, pair],
                out.at[dp + 2 - 4 * pair, window(chunk)],
                late_send.at[chunk],
                late_recv.at[chunk],
                other_pair,
            ).wait_recv()
            share_copy(number, chunk, 1 - pair, True).start()
        else:
            late_copy(number, chunk, False).wait()
            for side in range(2):
                mine[number, side] = add(mine[number, side], late_pair[chunk, side])
                out_copy(number, chunk, side).start()
                share_copy(number, chunk, side, False).start()

    always = lambda target: target >= 0
    far = jnp.maximum(seq, LINE - 1 - seq)
    ahead, pair_lag, hop_lag, share_lag = (2, 3, 4, 4)

    def step(number, carry):
        for index in range(ahead):
            at(ahead * number + index, always, first_stage)
        base = number - pair_lag
        at(base, always, second_stage)
        at(base - hop_lag * seq, lambda target: target > seq, hop(0))
        at(base - hop_lag * (LINE - 1 - seq), lambda target: target < seq, hop(1))
        at(base - hop_lag * far, lambda target: target == seq, last_stage)
        at(base - hop_lag * far - share_lag, lambda target: target == seq, share_stage)
        return carry

    lax.fori_loop(0, units + pair_lag + hop_lag * (LINE - 1) + share_lag, step, 0)

    vec_first.wait()
    vec_core[...] = vector[...] + vec_core[...]
    vec_second = remote(vec_core, vec_pair, vec_send.at[1], vec_recv.at[1], other_pair)
    vec_second.start()
    vec_second.wait()
    vec_pair[...] = vec_core[...] + vec_pair[...]
    for move in range(1, LINE):
        goal = lax.rem(seq + move, LINE)
        remote(
            vec_pair.at[goal],
            vec_line.at[seq],
            vec_send.at[1 + move],
            vec_recv.at[2 + seq],
            (pipe, goal, dp),
        ).start()
    vec_line[seq] = vec_pair[seq]
    for move in range(1, LINE):
        goal = lax.rem(seq + move, LINE)
        source = lax.rem(seq + LINE - move, LINE)
        remote(
            vec_pair.at[goal],
            vec_line.at[source],
            vec_send.at[1 + move],
            vec_recv.at[2 + source],
            (pipe, goal, dp),
        ).wait()
    total = vec_line[0]
    for source in range(1, LINE):
        total = total + vec_line[source]
    vector_out[...] = total

    def drain(number, carry):
        for side in range(2):
            to_core(number, side).wait_send()

        def sends(number, chunk, single):
            if single:
                to_pair(number).wait_send()

        at(number, always, sends)
        at(
            number,
            lambda target: target > seq,
            lambda number, chunk, single: line_copy(number, single, 0).wait_send(),
        )
        at(
            number,
            lambda target: target < seq,
            lambda number, chunk, single: line_copy(number, single, 1).wait_send(),
        )

        def shared(number, chunk, single):
            if single:
                late_copy(number, chunk, True).wait_send()
                out_copy(number, chunk, pair).wait()
                share_copy(number, chunk, pair, False).wait_send()
                share_copy(number, chunk, 1 - pair, True).wait_send()
            else:
                for side in range(2):
                    out_copy(number, chunk, side).wait()
                    share_copy(number, chunk, side, False).wait_send()
            for side in range(2):
                spot_out = out.at[2 * side + 1 - core, window(chunk)]
                remote(
                    spot_out,
                    spot_out,
                    share_send.at[side, chunk],
                    share_recv.at[side, chunk],
                    other_core,
                ).wait_recv()

        at(number, lambda target: target == seq, shared)
        return carry

    lax.fori_loop(0, units, drain, 0)


def reduce_all(grads, vector):
    anywhere = pl.BlockSpec(memory_space=pl.ANY)
    inside = pl.BlockSpec(memory_space=pltpu.VMEM)
    dma = pltpu.SemaphoreType.DMA
    chunks, paired = (6, 4)
    rows, columns = grads.shape[2:]
    depth = rows // chunks
    units = LINE * chunks
    block = (depth, columns)
    return pl.pallas_call(
        functools.partial(reduce_kernel, chunks, paired),
        out_shape=[
            jax.ShapeDtypeStruct(grads.shape[1:], grads.dtype),
            jax.ShapeDtypeStruct(vector.shape[1:], vector.dtype),
        ],
        in_specs=[anywhere, inside],
        out_specs=[anywhere, inside],
        scratch_shapes=[
            pltpu.VMEM((units, 2) + block, jnp.bfloat16),
            pltpu.VMEM((units, 2) + block, jnp.bfloat16),
            pltpu.VMEM((units,) + block, jnp.bfloat16),
            pltpu.VMEM((units, 2) + block, jnp.bfloat16),
            pltpu.VMEM((units, 2) + block, jnp.bfloat16),
            pltpu.VMEM((chunks, 2) + block, jnp.bfloat16),
            pltpu.VMEM(vector.shape, jnp.float32),
            pltpu.VMEM(vector.shape, jnp.float32),
            pltpu.VMEM(vector.shape, jnp.float32),
            dma((units, 2)),
            dma((units, 2)),
            dma((units, 2)),
            dma((units,)),
            dma((units,)),
            dma((units,)),
            dma((units,)),
            dma((units,)),
            dma((chunks,)),
            dma((chunks,)),
            dma((2, chunks)),
            dma((2, chunks)),
            dma((2, chunks)),
            dma((2 + LINE,)),
            dma((2 + LINE,)),
        ],
        compiler_params=pltpu.CompilerParams(
            collective_id=1, has_side_effects=True, vmem_limit_bytes=60 * 2**20
        ),
        name="reduce_grads",
    )(grads, vector)


def dot(left, right, left_axis, right_axis):
    return lax.dot_general(
        left,
        right,
        (((left_axis,), (right_axis,)), ((), ())),
        preferred_element_type=jnp.float32,
    )


def unit_rows(values):
    average = jnp.mean(values, axis=-1, keepdims=True)
    centered = values - average
    variance = jnp.mean(centered * centered, axis=-1, keepdims=True)
    root = lax.rsqrt(variance + norm_epsilon)
    return (centered * root, root)


def unit_rows_back(grad, values, gain_row):
    unit, root = unit_rows(values)
    scaled = grad * gain_row
    inner = jnp.mean(scaled * unit, axis=-1, keepdims=True)
    term = root * (scaled - jnp.mean(scaled, axis=-1, keepdims=True) - unit * inner)
    gain = jnp.sum(grad * unit, axis=0, keepdims=True)
    bias = jnp.sum(grad, axis=0, keepdims=True)
    return (term, gain, bias)


def layers_kernel(
    shard_row,
    shard_row_out,
    shard_col,
    shard_col_out,
    shard_up,
    shard_down,
    families,
    upstream,
    order,
    quarters,
    tally,
    norms,
    act_out,
    der_out,
    cost_out,
    vector,
    grads,
    w_row,
    w_row_out,
    w_col,
    w_col_out,
    w_up,
    w_down,
    source,
    normal_a,
    normal_b,
    normal_c,
    mixer,
    mixer_col,
    blended,
    mixed,
    after_row,
    after_col,
    log_share,
    col_share,
    hidden,
    slope,
    total_grad,
    grad_in,
    branch_ffn,
    branch_col,
    branch_row,
    grad_up,
    grad_mixer_col,
    grad_mixer,
    logit_send,
    logit_recv,
    keys_recv,
    keys_send,
    keys_back,
    probs_send,
    probs_recv,
    halves,
    segment,
    spread,
    stage,
    stage_down,
    act,
    der,
    cost,
    piece,
    piece_in,
    sensitivity,
    factor,
    factor_in,
    counts,
    counts_in,
    norms_in,
    rows,
    own_sem,
    line_send,
    line_recv,
    pair_send,
    pair_recv,
    core_send,
    core_recv,
    entry_sems,
    entry_local,
    norm_send,
    norm_recv,
    logit_sems,
    keys_sems,
    back_sems,
    probs_sems,
    pipe_sems,
    stage_sems,
    home_sems,
    home_local,
    cost_send,
    cost_recv,
):
    where = place()
    pipe, seq, dp, core, pair = where
    other_core = (pipe, seq, dp + 1 - 2 * core)
    other_pipe = (1 - pipe, seq, dp)
    columns, width = families.shape[2:]
    tokens = 2 * columns
    heads = HEAD_TALLY
    size = width // heads
    twin = 2 * size
    couples = heads // 2
    total_rows = LINE
    bf16, f32 = (jnp.bfloat16, jnp.float32)
    part_width = width // LINE
    shards = [
        ref.at[0]
        for ref in (shard_row, shard_row_out, shard_col, shard_col_out, shard_up, shard_down)
    ]
    wholes = (w_row, w_row_out, w_col, w_col_out, w_up, w_down)
    other_pair = (pipe, seq, dp + 2 - 4 * pair)
    right, left = ((pipe, seq + 1, dp), (pipe, seq - 1, dp))
    later = pipe == 1

    hear = greet(*where, across_pipe=True)
    straight = order[0, 0] == 0
    for index in range(2):
        piece[index] = jnp.where(straight, families[index, 0], families[1 - index, 0])
        chosen = jnp.where(straight, quarters[index], quarters[1 - index])
        factor[index] = jnp.broadcast_to(chosen.astype(f32) * 0.25, (columns, columns)).T
        number = jnp.where(straight, tally[index], tally[1 - index])
        counts[index] = jnp.broadcast_to(number, (8, 128)).astype(f32)
    hear()

    def entering(number, source_ref, target_ref):
        return swap_rows(
            source_ref,
            target_ref,
            entry_sems.at[2 * number],
            entry_sems.at[2 * number + 1],
            entry_local.at[number],
            where,
        )

    start_counts, finish_counts = entering(0, counts, counts_in)
    start_piece, finish_piece = entering(1, piece, piece_in)
    start_sensitivity, finish_sensitivity = entering(2, upstream.at[:, 0], sensitivity)
    start_factor, finish_factor = entering(3, factor, factor_in)
    start_counts()
    pl.when(later)(start_piece)

    def norm_copy(step, source):
        return remote(
            norms,
            norms_in.at[source],
            norm_send.at[step - 1],
            norm_recv.at[source],
            (pipe, lax.rem(seq + step, LINE), dp),
        )

    for step in range(1, LINE):
        norm_copy(step, seq).start()
    norms_in[seq] = norms[...]

    def region(index, source, part):
        depth = shards[index].shape[0]
        share = depth // 4
        start = pl.multiple_of(source * depth + part * share, share)
        return wholes[index].at[pl.ds(start, share)]

    def mine_of(index):
        share = shards[index].shape[0] // 4
        return shards[index].at[pl.ds(pl.multiple_of(dp * share, share), share)]

    def own_copy(index):
        depth = shards[index].shape[0]
        return pltpu.make_async_copy(
            shards[index],
            wholes[index].at[pl.ds(pl.multiple_of(seq * depth, depth), depth)],
            own_sem.at[index],
        )

    def own_line(index, direction):
        return remote(
            mine_of(index),
            region(index, seq, dp),
            line_send.at[direction, seq, index],
            line_recv.at[seq, index],
            right if direction == 0 else left,
        )

    def along(source, index, direction):
        block = region(index, source, dp)
        return remote(
            block,
            block,
            line_send.at[direction, source, index],
            line_recv.at[source, index],
            right if direction == 0 else left,
        )

    across = dp + 2 - 4 * pair
    opposite = dp + 1 - 2 * core
    opposite_across = across + 1 - 2 * core

    def over_pair(source, index, part):
        block = region(index, source, part)
        return remote(
            block, block, pair_send.at[source, index], pair_recv.at[source, index], other_pair
        )

    def over_core(lane_of, source, index, part):
        block = region(index, source, part)
        return remote(
            block,
            block,
            core_send.at[lane_of, source, index],
            core_recv.at[lane_of, source, index],
            other_core,
        )

    has = (seq < LINE - 1, seq > 0)

    def sources(step):
        for direction in range(2):
            source = seq - step if direction == 0 else seq + step
            yield (direction, source, source >= 0 if direction == 0 else source < LINE)

    def begin(index):
        for direction in range(2):
            pl.when(has[direction])(own_line(index, direction).start)
        own_copy(index).start()

    def arrive(index, step):
        for direction, source, present in sources(step):

            @pl.when(present)
            def _():
                along(source, index, direction).wait_recv()

                @pl.when(has[direction])
                def _():
                    along(source, index, direction).start()

                over_pair(source, index, dp).start()
                over_core(0, source, index, dp).start()

    def relay(index, step):
        for direction, source, present in sources(step):

            @pl.when(present)
            def _():
                over_pair(source, index, across).wait_recv()
                over_core(1, source, index, across).start()

    def settle(index):
        own_copy(index).wait()
        for step in range(1, LINE):
            for direction, source, present in sources(step):

                @pl.when(present)
                def _():
                    over_core(0, source, index, opposite).wait_recv()
                    over_core(1, source, index, opposite_across).wait_recv()

    def drain(index):
        for direction in range(2):
            pl.when(has[direction])(own_line(index, direction).wait_send)
        for step in range(1, LINE):
            for direction, source, present in sources(step):

                @pl.when(present)
                def _():
                    pl.when(has[direction])(along(source, index, direction).wait_send)
                    over_pair(source, index, dp).wait_send()
                    over_core(0, source, index, dp).wait_send()
                    over_core(1, source, index, across).wait_send()

    def wave(number):
        if number + 1 < 6:
            begin(number + 1)
        for step in range(1, LINE):
            if 0 <= number + 1 - step < 6:
                arrive(number + 1 - step, step)
        for step in range(1, LINE):
            if 0 <= number - step < 6:
                relay(number - step, step)

    def gather(*waves):
        @pl.when(jnp.logical_not(later))
        def _():
            for number in waves:
                wave(number)

    def ready(index):
        pl.when(jnp.logical_not(later))(lambda: settle(index))

    begin(0)
    hop = remote(piece_in, source, pipe_sems.at[4], pipe_sems.at[5], other_pipe)

    @pl.when(later)
    def _():
        finish_piece()
        hop.start()
        for number in range(9):
            wave(number)
        start_sensitivity()
        start_factor()
        for index in range(6):
            settle(index)
            drain(index)
        hop.wait_send()

    lane = lax.broadcasted_iota(jnp.int32, (columns, 2 * twin), 1)
    early = (lax.rem(lane, twin) < size).astype(f32)
    halves[0] = early.astype(bf16)
    halves[1] = (1.0 - early).astype(bf16)
    feature = lax.broadcasted_iota(jnp.int32, (width, 128), 0)
    head = lax.broadcasted_iota(jnp.int32, (width, 128), 1)
    belongs = jnp.logical_and(feature >= head * size, feature < head * size + size)
    segment[...] = belongs.astype(f32).astype(bf16)
    head = lax.broadcasted_iota(jnp.int32, (128, width), 0)
    feature = lax.broadcasted_iota(jnp.int32, (128, width), 1)
    belongs = jnp.logical_and(feature >= head * size, feature < head * size + size)
    spread[...] = belongs.astype(f32).astype(bf16)
    for step in range(1, LINE):
        norm_copy(step, lax.rem(seq + LINE - step, LINE)).wait()
    for part in range(LINE):
        rows[:, part * part_width : (part + 1) * part_width] = norms_in[part, :, 0:part_width]
    finish_counts()

    def gain_of(index):
        return rows[index : index + 1, :]

    def bias_of(index):
        return rows[3 + index : 4 + index, :]

    def keep_vector(index, gain, bias):
        part = width // LINE
        for target in range(LINE):
            window = slice(target * part, (target + 1) * part)
            vector[target, index : index + 1, 0:part] = gain[:, window]
            vector[target, 3 + index : 4 + index, 0:part] = bias[:, window]

    vector[...] = jnp.zeros(vector.shape, f32)

    def both(ref, start):
        return jnp.concatenate(
            [ref[0:columns, start : start + twin], ref[columns:tokens, start : start + twin]],
            axis=1,
        )

    def stacked(ref, start):
        wide = both(ref, start)
        return jnp.concatenate([wide * halves[0], wide * halves[1]], axis=0)

    def unstack(wide):
        early_lane = lax.rem(lax.broadcasted_iota(jnp.int32, (columns, 2 * twin), 1), twin) < size
        return jnp.where(early_lane, wide[0:columns], wide[columns:])

    def put(ref, start, wide):
        ref[0:columns, start : start + twin] = wide[:, 0:twin].astype(bf16)
        ref[columns:tokens, start : start + twin] = wide[:, twin:].astype(bf16)

    def to_core(source_ref, target_ref, sems, index):
        return remote(
            source_ref, target_ref, sems.at[0, index], sems.at[1, index], other_core
        )

    start_act, finish_act = swap_rows(
        act, act_out, home_sems.at[0], home_sems.at[1], home_local.at[0], where
    )
    start_der, finish_der = swap_rows(
        der, der_out, home_sems.at[2], home_sems.at[3], home_local.at[1], where
    )
    sender = core == lax.div(seq, 2)
    spot = lax.rem(seq, 2)
    cost_own = pltpu.make_async_copy(cost, cost_out.at[spot], home_local.at[2])
    cost_copies = [
        remote(
            cost,
            cost_out.at[spot],
            cost_send.at[step - 1],
            cost_recv.at[spot],
            (pipe, lax.rem(seq + step, LINE), dp),
        )
        for step in range(1, LINE)
    ]

    send_on = remote(act, source, pipe_sems.at[0], pipe_sems.at[1], other_pipe)
    send_back = remote(der, grad_in, pipe_sems.at[2], pipe_sems.at[3], other_pipe)

    @pl.when(later)
    def _():
        send_on.wait_recv()

    gather(0, 1)

    @pl.when(jnp.logical_not(later))
    def _():
        hop.wait_recv()

    unit, _ = unit_rows(source[...].reshape(tokens, width).astype(f32))
    normal_a[...] = (unit * gain_of(0) + bias_of(0)).astype(bf16)
    gather(2, 3)
    ready(0)
    for part in range(3):
        window = slice(part * width, (part + 1) * width)
        mixer[:, window] = dot(normal_a[...], w_row[:, window], 1, 0).astype(bf16)
    logit_factor = 1.0 / (math.sqrt(size) * math.sqrt(total_rows))
    logit_copies = []
    for couple in range(couples):
        partial_value = logit_factor * dot(
            both(mixer, couple * twin), stacked(mixer, width + couple * twin), 1, 1
        )
        logit_send[couple] = partial_value.astype(bf16)
        copy = to_core(logit_send.at[couple], logit_recv.at[couple], logit_sems, couple)
        copy.start()
        logit_copies.append(copy)
    gather(4)
    valid = (
        lax.broadcasted_iota(jnp.int32, (columns, 1), 0).astype(f32) < counts_in[0, 0:1, 0:1]
    ).astype(f32)
    disorder = jnp.zeros((columns, 1), f32)
    for couple in range(couples):
        logit_copies[couple].wait_recv()
        wide = logit_send[couple].astype(f32) + logit_recv[couple].astype(f32)
        shares = []
        for half in range(2):
            logits = wide[:, half * columns : (half + 1) * columns]
            shifted_logits = logits - jnp.max(logits, axis=-1, keepdims=True)
            powers = jnp.exp(shifted_logits)
            total = jnp.sum(powers, axis=-1, keepdims=True)
            logs = shifted_logits - jnp.log(total)
            share = powers / total
            log_share[couple, :, half * columns : (half + 1) * columns] = logs
            disorder = disorder - jnp.sum(share * logs, axis=-1, keepdims=True) * valid
            shares.append(share.astype(bf16))
        put(
            blended,
            couple * twin,
            dot(
                jnp.concatenate(shares, axis=1), stacked(mixer, 2 * width + couple * twin), 1, 0
            ),
        )
    cost[...] = jnp.broadcast_to(
        jnp.sum(disorder, axis=0, keepdims=True) / float(heads * columns), cost.shape
    )
    ready(1)
    after_row[...] = source[...].reshape(tokens, width).astype(f32) + dot(blended[...], w_row_out[...], 1, 0)
    unit, _ = unit_rows(after_row[...])
    normal_b[...] = (unit * gain_of(1) + bias_of(1)).astype(bf16)
    gather(5)
    ready(2)
    keys_copies = []
    for part in (1, 2, 0):
        window = slice(part * width, (part + 1) * width)
        mixer_col[:, window] = dot(normal_b[...], w_col[:, window], 1, 0).astype(bf16)
        if part > 0:
            copy = to_core(
                mixer_col.at[:, window], keys_recv.at[part - 1], keys_sems, part - 1
            )
            copy.start()
            keys_copies.append(copy)

    def line_of(part, place_of):
        if place_of < 2:
            rows_of = slice(place_of * columns, (place_of + 1) * columns)
            return mixer_col[rows_of, (1 + part) * width : (2 + part) * width]
        rows_of = slice((place_of - 2) * columns, (place_of - 1) * columns)
        return keys_recv[part, rows_of, :]

    def sums_by_head(wide_ref, start, line):
        products = [
            wide_ref[index * columns : (index + 1) * columns, start : start + width] * line
            for index in range(2)
        ]
        return dot(jnp.concatenate(products, axis=0), segment[...], 1, 0)

    def spread_heads(narrow):
        return dot(narrow, spread[...], 1, 0)

    gather(6)
    scores = []
    for place_of in range(4):
        if place_of == 2:
            keys_copies[0].wait_recv()
        scores.append(sums_by_head(mixer_col, 0, line_of(0, place_of)) / math.sqrt(size))
    highest = functools.reduce(jnp.maximum, scores)
    powers = [jnp.exp(score - highest) for score in scores]
    total = functools.reduce(jnp.add, powers)
    keys_copies[1].wait_recv()
    gathered_mix = None
    for place_of in range(4):
        share = powers[place_of] / total
        col_share[place_of] = share
        wide = spread_heads(share.astype(bf16))
        line = line_of(1, place_of).astype(f32)
        term = jnp.concatenate([wide[0:columns] * line, wide[columns:] * line], axis=0)
        gathered_mix = term if gathered_mix is None else gathered_mix + term
    mixed[...] = gathered_mix.astype(bf16)
    ready(3)
    after_col[...] = after_row[...] + dot(mixed[...], w_col_out[...], 1, 0)
    unit, _ = unit_rows(after_col[...])
    normal_c[...] = (unit * gain_of(2) + bias_of(2)).astype(bf16)
    gather(7)
    ready(4)
    parts = hidden.shape[1] // width
    result = after_col[...]
    for part in range(parts):
        window = slice(part * width, (part + 1) * width)
        upward = dot(normal_c[...], w_up[:, window], 1, 0)
        inner = 0.5 + 0.5 * lax.erf(upward * math.sqrt(0.5))
        density = jnp.exp(-0.5 * upward * upward) * (1.0 / math.sqrt(2.0 * math.pi))
        hidden[:, window] = (upward * inner).astype(bf16)
        slope[:, window] = (inner + upward * density).astype(bf16)
    gather(8)
    ready(5)
    for part in range(parts):
        window = slice(part * width, (part + 1) * width)
        result = result + dot(hidden[:, window], w_down[window, :], 1, 0)
    act[...] = result.astype(bf16).reshape(2, columns, width)

    @pl.when(pipe == 0)
    def _():
        send_on.start()

    start_act()

    @pl.when(sender)
    def _():
        cost_own.start()
        for copy in cost_copies:
            copy.start()

    @pl.when(pipe == 1)
    def _():
        finish_sensitivity()
        finish_factor()
        for index in range(2):
            total_grad[index * columns : (index + 1) * columns, :] = (
                sensitivity[index].astype(f32) * factor_in[index, :, 0:1]
            )

    @pl.when(pipe == 0)
    def _():
        for index in range(6):
            drain(index)
        send_back.wait_recv()
        total_grad[...] = grad_in[...].reshape(tokens, width).astype(f32)

    branch_ffn[...] = total_grad[...].astype(bf16)
    grad_normal = None
    for part in range(parts):
        window = slice(part * width, (part + 1) * width)
        grad_hidden = dot(branch_ffn[...], w_down[window, :], 1, 1)
        grad_up[:, window] = (grad_hidden * slope[:, window].astype(f32)).astype(bf16)
        term = dot(grad_up[:, window], w_up[:, window], 1, 1)
        grad_normal = term if grad_normal is None else grad_normal + term
    term, gain, bias = unit_rows_back(grad_normal, after_col[...], gain_of(2))
    keep_vector(2, gain, bias)
    total_grad[...] = total_grad[...] + term
    branch_col[...] = total_grad[...].astype(bf16)
    grad_mixed = dot(branch_col[...], w_col_out[...], 1, 1).astype(bf16)
    grad_probs = []
    for place_of in range(4):
        line = line_of(1, place_of)
        products = [grad_mixed[0:columns] * line, grad_mixed[columns:] * line]
        grad_probs.append(dot(jnp.concatenate(products, axis=0), segment[...], 1, 0))
    inner = functools.reduce(
        jnp.add, [col_share[place_of] * grad_probs[place_of] for place_of in range(4)]
    )
    root_size = math.sqrt(size)
    grad_query = None
    local_terms = []
    back_copies = []
    grad_lines = grad_mixed.astype(f32)
    query_lines = mixer_col[:, 0:width].astype(f32)
    for place_of in (2, 3, 0, 1):
        share = col_share[place_of]
        narrow = (share * (grad_probs[place_of] - inner)).astype(bf16)
        wide = spread_heads(narrow)
        line = line_of(0, place_of).astype(f32)
        term = jnp.concatenate([wide[0:columns] * line, wide[columns:] * line], axis=0)
        grad_query = term if grad_query is None else grad_query + term
        key_term = wide[0:columns] * query_lines[0:columns] + wide[columns:] * query_lines[columns:]
        key_term = key_term / root_size
        wide = spread_heads(share.astype(bf16))
        value_term = wide[0:columns] * grad_lines[0:columns] + wide[columns:] * grad_lines[columns:]
        if place_of >= 2:
            index = place_of - 2
            rows_of = slice(index * columns, (index + 1) * columns)
            keys_send[rows_of, 0:width] = key_term.astype(bf16)
            keys_send[rows_of, width:] = value_term.astype(bf16)
            copy = to_core(keys_send.at[rows_of, :], keys_back.at[rows_of, :], back_sems, index)
            copy.start()
            back_copies.append(copy)
        else:
            local_terms.append((key_term, value_term))
    grad_mixer_col[:, 0:width] = (grad_query / root_size).astype(bf16)
    for place_of in range(2):
        back_copies[place_of].wait()
        rows_of = slice(place_of * columns, (place_of + 1) * columns)
        for part in range(2):
            window = slice(part * width, (part + 1) * width)
            grad_mixer_col[rows_of, (1 + part) * width : (2 + part) * width] = (
                local_terms[place_of][part] + keys_back[rows_of, window].astype(f32)
            ).astype(bf16)
    grad_normal = None
    for part in range(3):
        window = slice(part * width, (part + 1) * width)
        term = dot(grad_mixer_col[:, window], w_col[:, window], 1, 1)
        grad_normal = term if grad_normal is None else grad_normal + term
    term, gain, bias = unit_rows_back(grad_normal, after_row[...], gain_of(1))
    keep_vector(1, gain, bias)
    total_grad[...] = total_grad[...] + term
    branch_row[...] = total_grad[...].astype(bf16)
    keys_send[:, 0:width] = dot(branch_row[...], w_row_out[...], 1, 1).astype(bf16)
    probs_copies = []
    for couple in range(couples):
        partial_value = dot(
            both(keys_send, couple * twin), stacked(mixer, 2 * width + couple * twin), 1, 1
        )
        probs_send[couple] = partial_value.astype(bf16)
        copy = to_core(probs_send.at[couple], probs_recv.at[couple], probs_sems, couple)
        copy.start()
        probs_copies.append(copy)
    column_weight = (float(total_rows * columns) / float(heads * columns)) * valid
    for couple in range(couples):
        start = couple * twin
        logs = log_share[couple]
        share = jnp.exp(logs)
        grad_wide = both(keys_send, start)
        put(
            grad_mixer,
            2 * width + start,
            unstack(dot(share.astype(bf16), grad_wide, 0, 0)),
        )
        probs_copies[couple].wait_recv()
        wide = probs_send[couple].astype(f32) + probs_recv[couple].astype(f32)
        pieces = []
        for half in range(2):
            window = slice(half * columns, (half + 1) * columns)
            part_share, part_logs, part_grad = (share[:, window], logs[:, window], wide[:, window])
            entropy = -jnp.sum(part_share * part_logs, axis=-1, keepdims=True)
            inner = jnp.sum(part_share * part_grad, axis=-1, keepdims=True)
            piece = part_share * (part_grad - inner)
            piece = piece - column_weight * part_share * (part_logs + entropy)
            pieces.append(piece.astype(bf16))
        grad_logits = jnp.concatenate(pieces, axis=1)
        put(
            grad_mixer,
            start,
            logit_factor * dot(grad_logits, stacked(mixer, width + start), 1, 0),
        )
        put(
            grad_mixer,
            width + start,
            logit_factor * unstack(dot(grad_logits, both(mixer, start), 0, 0)),
        )
    grad_normal = None
    for part in range(3):
        window = slice(part * width, (part + 1) * width)
        term = dot(grad_mixer[:, window], w_row[:, window], 1, 1)
        grad_normal = term if grad_normal is None else grad_normal + term
    term, gain, bias = unit_rows_back(grad_normal, source[...].reshape(tokens, width).astype(f32), gain_of(0))
    keep_vector(0, gain, bias)
    der[...] = (total_grad[...] + term).astype(bf16).reshape(2, columns, width)

    @pl.when(pipe == 1)
    def _():
        send_back.start()

    start_der()

    pairs = (
        (normal_a, grad_mixer),
        (blended, branch_row),
        (normal_b, grad_mixer_col),
        (mixed, branch_col),
        (normal_c, grad_up),
    )
    share = width // (4 * LINE)
    base = 0
    waiting = {}
    number = 0
    for left, right in pairs:
        for part in range(right.shape[1] // width):
            slot = number % 2
            if slot in waiting:
                for copy in waiting.pop(slot):
                    copy.wait()
            window = slice(part * width, (part + 1) * width)
            term = dot(left[...], right[:, window], 0, 0).astype(bf16)
            stage[slot] = term.reshape(LINE, 4, share, width)
            copies = [
                pltpu.make_async_copy(
                    stage.at[slot, target],
                    grads.at[target, :, pl.ds(base, share)],
                    stage_sems.at[slot, target],
                )
                for target in range(LINE)
            ]
            for copy in copies:
                copy.start()
            waiting[slot] = copies
            base += share
            number += 1
    for part in range(parts):
        slot = 2 + part % 2
        if slot in waiting:
            for copy in waiting.pop(slot):
                copy.wait()
        window = slice(part * width, (part + 1) * width)
        term = dot(hidden[:, window], branch_ffn[...], 0, 0).astype(bf16)
        stage_down[slot - 2] = term.reshape(4, width // 4, width)
        copy = pltpu.make_async_copy(
            stage_down.at[slot - 2],
            grads.at[part, :, pl.ds(base, width // 4)],
            stage_sems.at[slot, 0],
        )
        copy.start()
        waiting[slot] = [copy]
    for copies in waiting.values():
        for copy in copies:
            copy.wait()
    for copy in logit_copies + keys_copies + probs_copies:
        copy.wait_send()

    @pl.when(pipe == 0)
    def _():
        send_on.wait_send()

    @pl.when(pipe == 1)
    def _():
        send_back.wait_send()

    finish_act()
    finish_der()

    @pl.when(sender)
    def _():
        cost_own.wait()
        for copy in cost_copies:
            copy.wait_send()

    for index in range(2):

        @pl.when(2 * core + index != seq)
        def _():
            remote(
                cost, cost_out.at[index], cost_send.at[0], cost_recv.at[index], other_core
            ).wait_recv()


def run_layers(shards, families, upstream, order, quarters, tally, norms):
    columns, width = families.shape[2:]
    tokens = 2 * columns
    couples = HEAD_TALLY // 2
    wide = shards[4].shape[2]
    entry = jax.ShapeDtypeStruct((2, columns, width), families.dtype)
    wholes = [
        jax.ShapeDtypeStruct((shard.shape[1] * LINE, shard.shape[2]), shard.dtype)
        for shard in shards
    ]
    anywhere = pl.BlockSpec(memory_space=pl.ANY)
    inside = pl.BlockSpec(memory_space=pltpu.VMEM)
    scalars = pl.BlockSpec(memory_space=pltpu.SMEM)
    dma = pltpu.SemaphoreType.DMA
    bf16, f32 = (jnp.bfloat16, jnp.float32)
    rows_of = lambda columns_of, kind=bf16: pltpu.VMEM((tokens, columns_of), kind)
    scores = pltpu.VMEM((couples, columns, 2 * columns), bf16)
    packed_rows = sum(whole.shape[0] * whole.shape[1] for whole in wholes) // (16 * width)
    return pl.pallas_call(
        layers_kernel,
        out_shape=[
            jax.ShapeDtypeStruct(entry.shape, bf16),
            jax.ShapeDtypeStruct(entry.shape, bf16),
            jax.ShapeDtypeStruct((2, 8, 128), f32),
            jax.ShapeDtypeStruct((LINE, 8, 256), f32),
            jax.ShapeDtypeStruct((LINE, 4, packed_rows, width), bf16),
        ],
        in_specs=[anywhere] * 6 + [inside, inside, scalars, inside, scalars, inside],
        out_specs=[anywhere, anywhere, inside, inside, anywhere],
        scratch_shapes=[pltpu.VMEM(whole.shape, bf16) for whole in wholes]
        + [
            pltpu.VMEM(entry.shape, bf16),
            rows_of(width),
            rows_of(width),
            rows_of(width),
            rows_of(3 * width),
            rows_of(3 * width),
            rows_of(width),
            rows_of(width),
            rows_of(width, f32),
            rows_of(width, f32),
            pltpu.VMEM((couples, columns, 2 * columns), f32),
            pltpu.VMEM((4, tokens, 128), f32),
            rows_of(wide),
            rows_of(wide),
            rows_of(width, f32),
            pltpu.VMEM(entry.shape, bf16),
            rows_of(width),
            rows_of(width),
            rows_of(width),
            rows_of(wide),
            rows_of(3 * width),
            rows_of(3 * width),
            scores,
            scores,
            pltpu.VMEM((2, tokens, width), bf16),
            rows_of(2 * width),
            rows_of(2 * width),
            scores,
            scores,
            pltpu.VMEM((2, columns, 2 * columns), bf16),
            pltpu.VMEM((width, 128), bf16),
            pltpu.VMEM((128, width), bf16),
            pltpu.VMEM((2, LINE, 4, width // (4 * LINE), width), bf16),
            pltpu.VMEM((2, 4, width // 4, width), bf16),
            pltpu.VMEM(entry.shape, bf16),
            pltpu.VMEM(entry.shape, bf16),
            pltpu.VMEM((8, 128), f32),
            pltpu.VMEM(entry.shape, bf16),
            pltpu.VMEM(entry.shape, bf16),
            pltpu.VMEM(entry.shape, bf16),
            pltpu.VMEM((2, columns, columns), f32),
            pltpu.VMEM((2, columns, columns), f32),
            pltpu.VMEM((2, 8, 128), f32),
            pltpu.VMEM((2, 8, 128), f32),
            pltpu.VMEM((LINE, 8, 256), f32),
            pltpu.VMEM((8, width), f32),
            dma((6,)),
            dma((2, LINE, 6)),
            dma((LINE, 6)),
            dma((LINE, 6)),
            dma((LINE, 6)),
            dma((2, LINE, 6)),
            dma((2, LINE, 6)),
            dma((8, 2)),
            dma((4,)),
            dma((LINE - 1,)),
            dma((LINE,)),
            dma((2, couples)),
            dma((2, 2)),
            dma((2, 2)),
            dma((2, couples)),
            dma((6,)),
            dma((4, LINE)),
            dma((4, 2)),
            dma((3,)),
            dma((LINE - 1,)),
            dma((2,)),
        ],
        compiler_params=pltpu.CompilerParams(
            collective_id=2, has_side_effects=True, vmem_limit_bytes=60 * 2**20
        ),
        name="two_layers",
    )(*shards, families, upstream, order, quarters, tally, norms)


def unpack_kernel(blocks, vector, act, der, costs, *refs):
    results, gain, bias, act_out, der_out, cost_out = (refs[:6], *refs[6:])
    width = blocks.shape[2]
    base = 0
    for result in results:
        depth, wide = result.shape[1:]
        for part in range(wide // width):
            result[0, :, part * width : (part + 1) * width] = blocks[
                0, base : base + depth, :
            ].astype(jnp.float32)
            base += depth
    share = gain.shape[2]
    gain[0] = vector[0:3, 0:share]
    bias[0] = vector[3:6, 0:share]
    act_out[0, :, 0] = act[...]
    der_out[0, :, 0] = der[...]
    cost_out[...] = jnp.concatenate([costs[0, 0:1, 0:1], costs[1, 0:1, 0:1]], axis=1)


def unpack_all(blocks, vector, act, der, costs, shapes, share):
    columns, width = act.shape[1:]
    small = jax.ShapeDtypeStruct((1, 3, share), jnp.float32)
    large = jax.ShapeDtypeStruct((1, 2, 1, columns, width), act.dtype)
    part = pl.BlockSpec((2, columns // 4, width), lambda step: (0, step, 0))
    wide = pl.BlockSpec((1, 2, 1, columns // 4, width), lambda step: (0, 0, 0, step, 0))
    return pl.pallas_call(
        unpack_kernel,
        grid=(4,),
        out_shape=[jax.ShapeDtypeStruct((1,) + shape, jnp.float32) for shape in shapes]
        + [small, small, large, large, jax.ShapeDtypeStruct((1, 2), jnp.float32)],
        in_specs=[
            pl.BlockSpec((1,) + blocks.shape[1:], lambda step: (step, 0, 0)),
            pl.BlockSpec(vector.shape, lambda step: (0, 0)),
            part,
            part,
            pl.BlockSpec(costs.shape, lambda step: (0, 0, 0)),
        ],
        out_specs=[
            pl.BlockSpec((1, shape[0] // 4, shape[1]), lambda step: (0, step, 0))
            for shape in shapes
        ]
        + [pl.BlockSpec(small.shape, lambda step: (0, 0, 0))] * 2
        + [wide, wide, pl.BlockSpec((1, 2), lambda step: (0, 0))],
        compiler_params=pltpu.CompilerParams(vmem_limit_bytes=60 * 2**20),
        cost_estimate=pl.CostEstimate(
            flops=blocks.size, bytes_accessed=6 * blocks.size, transcendentals=0
        ),
        name="unpack_grads",
    )(blocks, vector, act, der, costs)


def on_device_lined(
    embedded_families,
    order,
    token_quarter_factor,
    genuine_residue_tally,
    standardizer_scales,
    standardizer_offsets,
    row_qkv,
    row_out,
    col_qkv,
    col_out,
    ffn_up,
    ffn_down,
    upstream_sensitivity,
):
    model_width = embedded_families.shape[-1]
    share = standardizer_scales.shape[-1]
    shards = (row_qkv, row_out, col_qkv, col_out, ffn_up, ffn_down)
    norms = jnp.pad(
        jnp.concatenate([standardizer_scales[0], standardizer_offsets[0]], axis=0),
        ((0, 2), (0, 256 - share)),
    )
    activations, derivs, costs, vector, grads = run_layers(
        shards,
        embedded_families,
        upstream_sensitivity,
        order,
        token_quarter_factor,
        genuine_residue_tally,
        norms,
    )
    out, vector = reduce_all(grads, vector)
    *results, activations, derivs, costs = unpack_all(
        out,
        vector,
        activations,
        derivs,
        costs,
        [shard.shape[1:] for shard in shards],
        share,
    )
    return (activations, derivs, costs, *results)


def solution(mesh):
    in_specs = (
        P("dp", "seq", None, None),
        P("dp", None),
        P("dp", "seq", None),
        P("dp"),
        P("pipe", None, "seq"),
        P("pipe", None, "seq"),
        P("pipe", "seq", None),
        P("pipe", "seq", None),
        P("pipe", "seq", None),
        P("pipe", "seq", None),
        P("pipe", "seq", None),
        P("pipe", "seq", None),
        P("dp", "seq", None, None),
    )
    out_specs = (
        P("pipe", "dp", "seq", None, None),
        P("pipe", "dp", "seq", None, None),
        P("pipe", "dp"),
        P("pipe", "seq", None),
        P("pipe", "seq", None),
        P("pipe", "seq", None),
        P("pipe", "seq", None),
        P("pipe", "seq", None),
        P("pipe", "seq", None),
        P("pipe", None, "seq"),
        P("pipe", None, "seq"),
    )
    lined = mesh.shape["seq"] == LINE and mesh.shape["dp"] == 4 and mesh.shape["pipe"] == 2
    return jax.shard_map(
        on_device_lined if lined else on_device, mesh=mesh, in_specs=in_specs, out_specs=out_specs, check_vma=False
    )
```

```python
import functools
import math

import jax
import jax.numpy as jnp
from jax import lax
from jax.experimental import pallas as pl
from jax.experimental.pallas import tpu as pltpu
from jax.sharding import PartitionSpec as P

HEAD_TALLY = 12
LINE = 4
MESH = pl.DeviceIdType.MESH
EARLY = 4
AT_ONCE = 2
MORE = 2


norm_epsilon = 1e-05


def shifted(value, axis, steps):
    count = lax.axis_size(axis)
    initial, last = (max(0, -steps), min(count, count - steps))
    return lax.ppermute(value, axis, [(source, source + steps) for source in range(initial, last)])


def normed(values, gain_row, bias_row):
    average = jnp.mean(values, axis=-1, keepdims=True)
    centered = values - average
    variance = jnp.mean(centered * centered, axis=-1, keepdims=True)
    return centered * lax.rsqrt(variance + norm_epsilon) * gain_row + bias_row


def gelu_exact(values):
    return jax.nn.gelu(values, approximate=False)


def product(left, weight):
    return lax.dot_general(
        left, weight, (((left.ndim - 1,), (0,)), ((), ())), preferred_element_type=jnp.float32
    )


def product_back(left, weight):
    return lax.dot_general(
        left, weight, (((left.ndim - 1,), (1,)), ((), ())), preferred_element_type=jnp.float32
    )


def weight_term(left, right):
    return lax.dot_general(
        left, right, (((0, 1), (0, 1)), ((), ())), preferred_element_type=jnp.float32
    )


def split_heads(values, head_count):
    return values.reshape(values.shape[:-1] + (head_count, values.shape[-1] // head_count))


def choose(flag, first_tree, second_tree):
    return jax.tree.map(lambda early, later: jnp.where(flag, early, later), first_tree, second_tree)


def column_scores(queries, key_rows, head_count):
    query_heads = split_heads(queries, head_count)
    raw = jnp.einsum(
        "rche,sche->chrs",
        query_heads,
        split_heads(key_rows, head_count),
        preferred_element_type=jnp.float32,
    )
    return raw / math.sqrt(query_heads.shape[-1])


def column_forward(queries, key_rows, content_lines, head_count):
    scores = column_scores(queries, key_rows, head_count)
    log_total = jax.nn.logsumexp(scores, axis=-1)
    vertical_factors = jnp.exp(scores - log_total[..., None]).astype(jnp.bfloat16)
    mixed_cols = jnp.einsum(
        "gmqi,igmu->qgmu",
        vertical_factors,
        split_heads(content_lines, head_count),
        preferred_element_type=jnp.float32,
    )
    return (mixed_cols.reshape(queries.shape).astype(jnp.bfloat16), log_total)


def column_backward(queries, key_rows, content_lines, log_total, grad_mixed, head_count):
    scores = column_scores(queries, key_rows, head_count)
    softmax_share = jnp.exp(scores - log_total[..., None])
    grad_heads = split_heads(grad_mixed, head_count)
    grad_probs = jnp.einsum(
        "rche,sche->chrs",
        grad_heads,
        split_heads(content_lines, head_count),
        preferred_element_type=jnp.float32,
    )
    grad_values = jnp.einsum(
        "chrs,rche->sche",
        softmax_share.astype(jnp.bfloat16),
        grad_heads,
        preferred_element_type=jnp.float32,
    )
    grad_scores = (
        softmax_share * (grad_probs - jnp.sum(softmax_share * grad_probs, axis=-1, keepdims=True))
    ).astype(jnp.bfloat16)
    root_size = math.sqrt(queries.shape[-1] // head_count)
    grad_queries = (
        jnp.einsum(
            "gmqi,igmu->qgmu",
            grad_scores,
            split_heads(key_rows, head_count),
            preferred_element_type=jnp.float32,
        )
        / root_size
    )
    grad_keys = (
        jnp.einsum(
            "chrs,rche->sche",
            grad_scores,
            split_heads(queries, head_count),
            preferred_element_type=jnp.float32,
        )
        / root_size
    )
    return (
        grad_queries.reshape(queries.shape),
        grad_keys.reshape(key_rows.shape),
        grad_values.reshape(content_lines.shape),
    )


def row_split(horizontal_mixer, model_width, head_count):
    queries = split_heads(horizontal_mixer[..., :model_width], head_count)
    key_rows = split_heads(horizontal_mixer[..., model_width : 2 * model_width], head_count)
    content_lines = split_heads(horizontal_mixer[..., 2 * model_width :], head_count)
    return (queries, key_rows, content_lines)


def layer_forward(source_rows, family_residues, projection_tables, head_count):
    (
        horizontal_coefficients,
        w_row_out,
        vertical_coefficients,
        w_col_out,
        w_up,
        w_down,
        gain_rows,
        bias_rows,
    ) = projection_tables
    row_count, columns, model_width = source_rows.shape
    total_rows = row_count * lax.axis_size("seq")
    start = source_rows.astype(jnp.float32)
    layernorm_first = normed(start, gain_rows[0], bias_rows[0]).astype(jnp.bfloat16)
    horizontal_mixer = product(layernorm_first, horizontal_coefficients).astype(jnp.bfloat16)
    queries, key_rows, content_lines = row_split(horizontal_mixer, model_width, head_count)
    logit_factor = 1.0 / (math.sqrt(model_width // head_count) * math.sqrt(total_rows))
    partial_value = logit_factor * jnp.einsum(
        "rihe,rjhe->hij", queries, key_rows, preferred_element_type=jnp.float32
    )
    logits = lax.psum(partial_value.astype(jnp.bfloat16), "seq").astype(jnp.float32)
    softmax_share = jax.nn.softmax(logits, axis=-1)
    log_probs = jax.nn.log_softmax(logits, axis=-1)
    entropy = -jnp.sum(softmax_share * log_probs, axis=-1)
    valid_residues = (jnp.arange(columns, dtype=jnp.int32) < family_residues).astype(jnp.float32)
    disorder_cost = jnp.sum(entropy * valid_residues[None, :]) / float(head_count * columns)
    blended_lines = jnp.einsum(
        "vyp,opvl->oyvl",
        softmax_share.astype(jnp.bfloat16),
        content_lines,
        preferred_element_type=jnp.float32,
    )
    blended_lines = blended_lines.reshape(row_count, columns, model_width).astype(jnp.bfloat16)
    after_row = start + product(blended_lines, w_row_out)
    layernorm_second = normed(after_row, gain_rows[1], bias_rows[1]).astype(jnp.bfloat16)
    vertical_mixer = product(layernorm_second, vertical_coefficients).astype(jnp.bfloat16)
    everyone = lax.all_gather(vertical_mixer[..., model_width:], "seq", axis=0, tiled=True)
    mixed_values, log_total = column_forward(
        vertical_mixer[..., :model_width],
        everyone[..., :model_width],
        everyone[..., model_width:],
        head_count,
    )
    column_state = (everyone, log_total)
    after_col = after_row + product(mixed_values, w_col_out)
    normal_c = normed(after_col, gain_rows[2], bias_rows[2]).astype(jnp.bfloat16)
    upward = product(normal_c, w_up)
    hidden = gelu_exact(upward).astype(jnp.bfloat16)
    result = after_col + product(hidden, w_down)
    kept_state = (
        source_rows,
        layernorm_first,
        horizontal_mixer,
        logits,
        blended_lines,
        after_row,
        layernorm_second,
        vertical_mixer,
        column_state,
        mixed_values,
        after_col,
        normal_c,
        upward,
        hidden,
    )
    return (result.astype(jnp.bfloat16), disorder_cost, kept_state)


def layer_backward(kept_state, family_residues, grad_result, projection_tables, head_count):
    (
        horizontal_coefficients,
        w_row_out,
        vertical_coefficients,
        w_col_out,
        w_up,
        w_down,
        gain_rows,
        bias_rows,
    ) = projection_tables
    (
        source_rows,
        layernorm_first,
        horizontal_mixer,
        logits,
        blended_lines,
        after_row,
        layernorm_second,
        vertical_mixer,
        column_state,
        mixed_values,
        after_col,
        normal_c,
        upward,
        hidden,
    ) = kept_state
    row_count, columns, model_width = source_rows.shape
    total_rows = row_count * lax.axis_size("seq")
    grad_branch_ffn = grad_result.astype(jnp.bfloat16)
    grad_hidden = product_back(grad_branch_ffn, w_down)
    grad_upward = jax.vjp(gelu_exact, upward)[1](grad_hidden)[0].astype(jnp.bfloat16)
    grad_normal_c = product_back(grad_upward, w_up)
    from_norm, gain_last, bias_last = jax.vjp(normed, after_col, gain_rows[2], bias_rows[2])[1](
        grad_normal_c
    )
    grad_col = grad_result + from_norm
    grad_branch_col = grad_col.astype(jnp.bfloat16)
    grad_attended = product_back(grad_branch_col, w_col_out).astype(jnp.bfloat16)
    everyone, log_total = column_state
    grad_query_col, grad_key_col, grad_value_col = column_backward(
        vertical_mixer[..., :model_width],
        everyone[..., :model_width],
        everyone[..., model_width:],
        log_total,
        grad_attended,
        head_count,
    )
    grad_kv_rows = lax.psum_scatter(
        jnp.concatenate([grad_key_col, grad_value_col], axis=-1).astype(jnp.bfloat16),
        "seq",
        scatter_dimension=0,
        tiled=True,
    ).astype(jnp.float32)
    grad_col_proj = jnp.concatenate([grad_query_col, grad_kv_rows], axis=-1).astype(jnp.bfloat16)
    grad_normal_b = product_back(grad_col_proj, vertical_coefficients)
    from_norm, gain_middle, bias_middle = jax.vjp(normed, after_row, gain_rows[1], bias_rows[1])[1](
        grad_normal_b
    )
    grad_row = grad_col + from_norm
    grad_branch_row = grad_row.astype(jnp.bfloat16)
    grad_mixed = split_heads(
        product_back(grad_branch_row, w_row_out).astype(jnp.bfloat16), head_count
    )
    queries, key_rows, content_lines = row_split(horizontal_mixer, model_width, head_count)
    softmax_share = jax.nn.softmax(logits, axis=-1)
    log_probs = jax.nn.log_softmax(logits, axis=-1)
    entropy = -jnp.sum(softmax_share * log_probs, axis=-1)
    partial_value = jnp.einsum(
        "rihe,rjhe->hij", grad_mixed, content_lines, preferred_element_type=jnp.float32
    )
    grad_probs = lax.psum(partial_value.astype(jnp.bfloat16), "seq").astype(jnp.float32)
    grad_values = jnp.einsum(
        "hij,rihe->rjhe",
        softmax_share.astype(jnp.bfloat16),
        grad_mixed,
        preferred_element_type=jnp.float32,
    )
    valid_residues = (jnp.arange(columns, dtype=jnp.int32) < family_residues).astype(jnp.float32)
    column_weight = float(total_rows * columns) * valid_residues / float(head_count * columns)
    grad_logits = softmax_share * (
        grad_probs - jnp.sum(softmax_share * grad_probs, axis=-1, keepdims=True)
    )
    grad_logits = grad_logits - column_weight[None, :, None] * softmax_share * (
        log_probs + entropy[..., None]
    )
    grad_logits = grad_logits.astype(jnp.bfloat16)
    logit_factor = 1.0 / (math.sqrt(model_width // head_count) * math.sqrt(total_rows))
    grad_queries = logit_factor * jnp.einsum(
        "vyp,opvl->oyvl", grad_logits, key_rows, preferred_element_type=jnp.float32
    )
    grad_keys = logit_factor * jnp.einsum(
        "hij,rihe->rjhe", grad_logits, queries, preferred_element_type=jnp.float32
    )
    grad_row_proj = jnp.concatenate(
        [
            grad_queries.reshape(row_count, columns, model_width),
            grad_keys.reshape(row_count, columns, model_width),
            grad_values.reshape(row_count, columns, model_width),
        ],
        axis=-1,
    ).astype(jnp.bfloat16)
    grad_normal_a = product_back(grad_row_proj, horizontal_coefficients)
    from_norm, gain_first, bias_first = jax.vjp(
        normed, source_rows.astype(jnp.float32), gain_rows[0], bias_rows[0]
    )[1](grad_normal_a)
    grad_source = (grad_row + from_norm).astype(jnp.bfloat16)
    operand_pairs = (
        (layernorm_first, grad_row_proj),
        (blended_lines, grad_branch_row),
        (layernorm_second, grad_col_proj),
        (mixed_values, grad_branch_col),
        (normal_c, grad_upward),
        (hidden, grad_branch_ffn),
    )
    norm_grads = (
        jnp.stack([gain_first, gain_middle, gain_last]),
        jnp.stack([bias_first, bias_middle, bias_last]),
    )
    return (grad_source, operand_pairs, norm_grads)


def on_device(
    embedded_families,
    order,
    token_quarter_factor,
    genuine_residue_tally,
    standardizer_scales,
    standardizer_offsets,
    row_qkv,
    row_out,
    col_qkv,
    col_out,
    ffn_up,
    ffn_down,
    upstream_sensitivity,
):
    head_count = HEAD_TALLY
    segment_place = lax.axis_index("pipe")
    gathered = (
        lax.all_gather(row_qkv, "seq", axis=1, tiled=True),
        lax.all_gather(row_out, "seq", axis=1, tiled=True),
        lax.all_gather(col_qkv, "seq", axis=1, tiled=True),
        lax.all_gather(col_out, "seq", axis=1, tiled=True),
        lax.all_gather(ffn_up, "seq", axis=1, tiled=True),
        lax.all_gather(ffn_down, "seq", axis=1, tiled=True),
        lax.all_gather(standardizer_scales.astype(jnp.bfloat16), "seq", axis=2, tiled=True).astype(
            standardizer_scales.dtype
        ),
        lax.all_gather(standardizer_offsets.astype(jnp.bfloat16), "seq", axis=2, tiled=True).astype(
            standardizer_offsets.dtype
        ),
    )
    projection_tables = tuple((gathered_piece[0] for gathered_piece in gathered))
    small_batch_number = embedded_families.shape[0]
    sequence = order[0]
    received = jnp.zeros(embedded_families.shape[1:], jnp.bfloat16)
    results = []
    focus_spread_levies = []
    kept_list = []
    for period in range(small_batch_number + 1):
        slot_here = jnp.clip(period - segment_place, 0, small_batch_number - 1)
        align_here = sequence[slot_here]
        source_rows = jnp.where(segment_place == 0, embedded_families[align_here], received)
        result, disorder_cost, kept_state = layer_forward(
            source_rows, genuine_residue_tally[align_here], projection_tables, head_count
        )
        results.append(result)
        focus_spread_levies.append(disorder_cost)
        kept_list.append(kept_state)
        if period < small_batch_number:
            received = shifted(result, "pipe", 1)
    activations = lax.dynamic_slice_in_dim(jnp.stack(results), segment_place, small_batch_number, 0)
    penalty_output = lax.dynamic_slice_in_dim(
        jnp.stack(focus_spread_levies), segment_place, small_batch_number, 0
    )
    grad_received = jnp.zeros(embedded_families.shape[1:], jnp.bfloat16)
    left_lists = [[] for index in range(6)]
    right_lists = [[] for index in range(6)]
    gain_total = None
    bias_total = None
    grad_sources = []
    for period in range(small_batch_number + 1):
        slot_raw = period - 1 + segment_place
        in_range = jnp.logical_and(slot_raw >= 0, slot_raw < small_batch_number)
        slot_here = jnp.clip(slot_raw, 0, small_batch_number - 1)
        align_here = sequence[slot_here]
        kept_state = choose(
            segment_place == 0,
            kept_list[max(period - 1, 0)],
            kept_list[min(period + 1, small_batch_number)],
        )
        outgrad = (
            upstream_sensitivity[slot_here].astype(jnp.float32)
            * token_quarter_factor[align_here].astype(jnp.float32)[..., None]
            * 0.25
        )
        incoming_grad = jnp.where(segment_place == 1, outgrad, grad_received.astype(jnp.float32))
        grad_source, operand_pairs, norm_grads = layer_backward(
            kept_state,
            genuine_residue_tally[align_here],
            incoming_grad,
            projection_tables,
            head_count,
        )
        for index in range(6):
            left_lists[index].append(operand_pairs[index][0])
            right_lists[index].append(
                jnp.where(
                    in_range, operand_pairs[index][1], jnp.zeros_like(operand_pairs[index][1])
                )
            )
        gain_term = jnp.where(in_range, norm_grads[0], jnp.zeros_like(norm_grads[0]))
        bias_term = jnp.where(in_range, norm_grads[1], jnp.zeros_like(norm_grads[1]))
        gain_total = gain_term if gain_total is None else gain_total + gain_term
        bias_total = bias_term if bias_total is None else bias_total + bias_term
        grad_sources.append(grad_source)
        if period < small_batch_number:
            grad_received = shifted(grad_source, "pipe", -1)
    block_entry_derivs = lax.dynamic_slice_in_dim(
        jnp.stack(grad_sources), 1 - segment_place, small_batch_number, 0
    )
    weight_totals = [
        weight_term(
            jnp.concatenate(left_lists[index], axis=0), jnp.concatenate(right_lists[index], axis=0)
        )
        for index in range(6)
    ]
    shared = (
        lax.psum_scatter(
            weight_totals[0].astype(jnp.bfloat16), "seq", scatter_dimension=0, tiled=True
        ).astype(jnp.float32),
        lax.psum_scatter(
            weight_totals[1].astype(jnp.bfloat16), "seq", scatter_dimension=0, tiled=True
        ).astype(jnp.float32),
        lax.psum_scatter(
            weight_totals[2].astype(jnp.bfloat16), "seq", scatter_dimension=0, tiled=True
        ).astype(jnp.float32),
        lax.psum_scatter(
            weight_totals[3].astype(jnp.bfloat16), "seq", scatter_dimension=0, tiled=True
        ).astype(jnp.float32),
        lax.psum_scatter(
            weight_totals[4].astype(jnp.bfloat16), "seq", scatter_dimension=0, tiled=True
        ).astype(jnp.float32),
        lax.psum_scatter(
            weight_totals[5].astype(jnp.bfloat16), "seq", scatter_dimension=0, tiled=True
        ).astype(jnp.float32),
        lax.psum_scatter(
            gain_total.astype(jnp.bfloat16), "seq", scatter_dimension=1, tiled=True
        ).astype(jnp.float32),
        lax.psum_scatter(
            bias_total.astype(jnp.bfloat16), "seq", scatter_dimension=1, tiled=True
        ).astype(jnp.float32),
    )
    (
        shared_row_qkv,
        shared_row_out,
        shared_col_qkv,
        shared_col_out,
        shared_up,
        shared_down,
        shared_gain,
        shared_bias,
    ) = shared
    summed = (
        lax.psum(shared_row_qkv.astype(jnp.bfloat16), "dp").astype(jnp.float32),
        lax.psum(shared_row_out.astype(jnp.bfloat16), "dp").astype(jnp.float32),
        lax.psum(shared_col_qkv.astype(jnp.bfloat16), "dp").astype(jnp.float32),
        lax.psum(shared_col_out.astype(jnp.bfloat16), "dp").astype(jnp.float32),
        lax.psum(shared_up.astype(jnp.bfloat16), "dp").astype(jnp.float32),
        lax.psum(shared_down.astype(jnp.bfloat16), "dp").astype(jnp.float32),
        lax.psum(shared_gain.astype(jnp.bfloat16), "dp").astype(jnp.float32),
        lax.psum(shared_bias.astype(jnp.bfloat16), "dp").astype(jnp.float32),
    )
    return (
        activations[None],
        block_entry_derivs[None],
        penalty_output[None],
        summed[0][None],
        summed[1][None],
        summed[2][None],
        summed[3][None],
        summed[4][None],
        summed[5][None],
        summed[6][None],
        summed[7][None],
    )


def place():
    pipe, seq, dp = (lax.axis_index("pipe"), lax.axis_index("seq"), lax.axis_index("dp"))
    core = lax.rem(dp, 2)
    pair = lax.div(dp, 2)
    return (pipe, seq, dp, core, pair)


def neighbours(pipe, seq, dp, core, pair):
    other_core = (pipe, seq, dp + 1 - 2 * core)
    other_pair = (pipe, seq, dp + 2 - 4 * pair)
    return (other_core, other_pair)


def greet(pipe, seq, dp, core, pair, across_pipe=False):
    barrier = pltpu.get_barrier_semaphore()
    other_core, other_pair = neighbours(pipe, seq, dp, core, pair)
    count = 0
    for step in range(LINE):
        for flip in range(2):
            if step == 0 and flip == 0:
                continue
            where = dp if flip == 0 else dp + 1 - 2 * core
            pl.semaphore_signal(
                barrier,
                inc=1,
                device_id=(pipe, lax.rem(seq + step, LINE), where),
                device_id_type=MESH,
            )
            count += 1
    more = [other_pair] + ([(1 - pipe, seq, dp)] if across_pipe else [])
    for device in more:
        pl.semaphore_signal(barrier, inc=1, device_id=device, device_id_type=MESH)

    def hear():
        pl.semaphore_wait(barrier, count + len(more))

    return hear


def remote(source, target, send, recv, device):
    return pltpu.make_async_remote_copy(
        src_ref=source,
        dst_ref=target,
        send_sem=send,
        recv_sem=recv,
        device_id=device,
        device_id_type=MESH,
    )


def swap_rows(source, target, send, recv, local, where):
    pipe, seq, dp, core, pair = where
    half, rest = (lax.div(seq, 2), lax.rem(seq, 2))

    def each(action):
        for index in range(2):
            line = 2 * core + index
            here = jnp.logical_and(line == seq, half == core)
            copy = remote(
                source.at[index],
                target.at[rest],
                send.at[index],
                recv.at[rest],
                (pipe, line, dp - core + half),
            )
            arriving = remote(
                source.at[index],
                target.at[index],
                send.at[index],
                recv.at[index],
                (pipe, line, dp - core + half),
            )
            inside = pltpu.make_async_copy(source.at[index], target.at[rest], local)
            action(here, copy, arriving, inside)

    def start(here, copy, arriving, inside):
        pl.when(here)(inside.start)
        pl.when(jnp.logical_not(here))(copy.start)

    def finish(here, copy, arriving, inside):
        pl.when(here)(inside.wait)
        pl.when(jnp.logical_not(here))(copy.wait_send)
        pl.when(jnp.logical_not(here))(arriving.wait_recv)

    return (lambda: each(start), lambda: each(finish))


def dot(left, right, left_axis, right_axis):
    return lax.dot_general(
        left,
        right,
        (((left_axis,), (right_axis,)), ((), ())),
        preferred_element_type=jnp.float32,
    )


def unit_rows(values):
    average = jnp.mean(values, axis=-1, keepdims=True)
    centered = values - average
    variance = jnp.mean(centered * centered, axis=-1, keepdims=True)
    root = lax.rsqrt(variance + norm_epsilon)
    return (centered * root, root)


def unit_rows_back(grad, values, gain_row):
    unit, root = unit_rows(values)
    scaled = grad * gain_row
    inner = jnp.mean(scaled * unit, axis=-1, keepdims=True)
    term = root * (scaled - jnp.mean(scaled, axis=-1, keepdims=True) - unit * inner)
    gain = jnp.sum(grad * unit, axis=0, keepdims=True)
    bias = jnp.sum(grad, axis=0, keepdims=True)
    return (term, gain, bias)


def layers_kernel(
    shard_row,
    shard_row_out,
    shard_col,
    shard_col_out,
    shard_up,
    shard_down,
    families,
    upstream,
    order,
    quarters,
    tally,
    norms,
    act_out,
    der_out,
    cost_out,
    vector_out,
    grads,
    out,
    tiles,
    source,
    normal_a,
    normal_b,
    normal_c,
    mixer,
    mixer_col,
    blended,
    mixed,
    after_row,
    after_col,
    log_share,
    col_share,
    hidden,
    slope,
    total_grad,
    grad_in,
    branch_ffn,
    branch_col,
    branch_row,
    grad_up,
    grad_mixer_col,
    grad_mixer,
    logit_send,
    logit_recv,
    keys_recv,
    keys_send,
    keys_back,
    probs_send,
    probs_recv,
    halves,
    segment,
    spread,
    stage,
    stage_down,
    act,
    der,
    cost,
    piece,
    piece_in,
    sensitivity,
    factor,
    factor_in,
    counts,
    counts_in,
    norms_in,
    rows,
    own_sem,
    line_send,
    line_recv,
    pair_send,
    pair_recv,
    core_send,
    core_recv,
    entry_sems,
    entry_local,
    norm_send,
    norm_recv,
    landing,
    from_pair,
    late_pair,
    vector,
    vec_core,
    vec_pair,
    vec_line,
    load_sem,
    near_send,
    near_recv,
    far_send,
    far_recv,
    hop_send,
    left_recv,
    right_recv,
    late_send,
    late_recv,
    share_send,
    share_recv,
    out_sem,
    vec_send,
    vec_recv,
    logit_sems,
    keys_sems,
    back_sems,
    probs_sems,
    pipe_sems,
    stage_sems,
    home_sems,
    home_local,
    cost_send,
    cost_recv,
):
    where = place()
    pipe, seq, dp, core, pair = where
    other_core = (pipe, seq, dp + 1 - 2 * core)
    other_pipe = (1 - pipe, seq, dp)
    columns, width = families.shape[2:]
    tokens = 2 * columns
    heads = HEAD_TALLY
    size = width // heads
    twin = 2 * size
    couples = heads // 2
    total_rows = LINE
    bf16, f32 = (jnp.bfloat16, jnp.float32)
    part_width = width // LINE
    shards = [
        ref.at[0]
        for ref in (shard_row, shard_row_out, shard_col, shard_col_out, shard_up, shard_down)
    ]
    first_tile = (0, 3, 4, 7, 8, 12)
    other_pair = (pipe, seq, dp + 2 - 4 * pair)
    right, left = ((pipe, seq + 1, dp), (pipe, seq - 1, dp))
    later = pipe == 1

    hear = greet(*where, across_pipe=True)
    straight = order[0, 0] == 0
    for index in range(2):
        piece[index] = jnp.where(straight, families[index, 0], families[1 - index, 0])
        chosen = jnp.where(straight, quarters[index], quarters[1 - index])
        factor[index] = jnp.broadcast_to(chosen.astype(f32) * 0.25, (columns, columns)).T
        number = jnp.where(straight, tally[index], tally[1 - index])
        counts[index] = jnp.broadcast_to(number, (8, 128)).astype(f32)
    hear()

    def entering(number, source_ref, target_ref):
        return swap_rows(
            source_ref,
            target_ref,
            entry_sems.at[2 * number],
            entry_sems.at[2 * number + 1],
            entry_local.at[number],
            where,
        )

    start_counts, finish_counts = entering(0, counts, counts_in)
    start_piece, finish_piece = entering(1, piece, piece_in)
    start_sensitivity, finish_sensitivity = entering(2, upstream.at[:, 0], sensitivity)
    start_factor, finish_factor = entering(3, factor, factor_in)
    start_counts()
    pl.when(later)(start_piece)

    def norm_copy(step, source):
        return remote(
            norms,
            norms_in.at[source],
            norm_send.at[step - 1],
            norm_recv.at[source],
            (pipe, lax.rem(seq + step, LINE), dp),
        )

    for step in range(1, LINE):
        norm_copy(step, seq).start()
    norms_in[seq] = norms[...]

    def block_of(index, source, start, length):
        depth, wide = shards[index].shape
        if wide == width and depth == width:
            return tiles.at[first_tile[index] + source, pl.ds(start, length)]
        start = pl.multiple_of(source * depth + start, 16)
        return tiles.at[pl.ds(first_tile[index], wide // width), pl.ds(start, length)]

    def region(index, source, part):
        share = shards[index].shape[0] // 4
        return block_of(index, source, pl.multiple_of(part * share, share), share)

    def cut(index, start, length):
        depth, wide = shards[index].shape
        if wide == width and depth == width:
            yield (
                shards[index].at[pl.ds(start, length)],
                tiles.at[first_tile[index] + seq, pl.ds(start, length)],
            )
            return
        target = pl.multiple_of(seq * depth + start, 16)
        for part in range(wide // width):
            yield (
                shards[index].at[pl.ds(start, length), pl.ds(part * width, width)],
                tiles.at[first_tile[index] + part, pl.ds(target, length)],
            )

    def start_own(index):
        for near, far in cut(index, 0, shards[index].shape[0]):
            pltpu.make_async_copy(near, far, own_sem.at[index]).start()

    def wait_own(index):
        block = block_of(index, seq, 0, shards[index].shape[0])
        pltpu.make_async_copy(block, block, own_sem.at[index]).wait()

    def start_line(index, direction):
        share = shards[index].shape[0] // 4
        for near, far in cut(index, pl.multiple_of(dp * share, share), share):
            remote(
                near,
                far,
                line_send.at[direction, seq, index],
                line_recv.at[seq, index],
                right if direction == 0 else left,
            ).start()

    def along(source, index, direction):
        block = region(index, source, dp)
        return remote(
            block,
            block,
            line_send.at[direction, source, index],
            line_recv.at[source, index],
            right if direction == 0 else left,
        )

    across = dp + 2 - 4 * pair
    opposite = dp + 1 - 2 * core
    opposite_across = across + 1 - 2 * core

    def over_pair(source, index, part):
        block = region(index, source, part)
        return remote(
            block, block, pair_send.at[source, index], pair_recv.at[source, index], other_pair
        )

    def over_core(lane_of, source, index, part):
        block = region(index, source, part)
        return remote(
            block,
            block,
            core_send.at[lane_of, source, index],
            core_recv.at[lane_of, source, index],
            other_core,
        )

    has = (seq < LINE - 1, seq > 0)

    def sources(step):
        for direction in range(2):
            source = seq - step if direction == 0 else seq + step
            yield (direction, source, source >= 0 if direction == 0 else source < LINE)

    def begin(index):
        for direction in range(2):
            pl.when(has[direction])(functools.partial(start_line, index, direction))
        start_own(index)

    def arrive(index, step):
        for direction, source, present in sources(step):

            @pl.when(present)
            def _():
                along(source, index, direction).wait_recv()

                @pl.when(has[direction])
                def _():
                    along(source, index, direction).start()

                over_pair(source, index, dp).start()
                over_core(0, source, index, dp).start()

    def relay(index, step):
        for direction, source, present in sources(step):

            @pl.when(present)
            def _():
                over_pair(source, index, across).wait_recv()
                over_core(1, source, index, across).start()

    def settle(index):
        wait_own(index)
        for step in range(1, LINE):
            for direction, source, present in sources(step):

                @pl.when(present)
                def _():
                    over_core(0, source, index, opposite).wait_recv()
                    over_core(1, source, index, opposite_across).wait_recv()

    def drain(index):
        for direction in range(2):
            pl.when(has[direction])(along(seq, index, direction).wait_send)
        for step in range(1, LINE):
            for direction, source, present in sources(step):

                @pl.when(present)
                def _():
                    pl.when(has[direction])(along(source, index, direction).wait_send)
                    over_pair(source, index, dp).wait_send()
                    over_core(0, source, index, dp).wait_send()
                    over_core(1, source, index, across).wait_send()

    def wave(number):
        if number + 1 < 6:
            begin(number + 1)
        for step in range(1, LINE):
            if 0 <= number + 1 - step < 6:
                arrive(number + 1 - step, step)
        for step in range(1, LINE):
            if 0 <= number - step < 6:
                relay(number - step, step)

    def gather(*waves):
        @pl.when(jnp.logical_not(later))
        def _():
            for number in waves:
                wave(number)

    def ready(index):
        pl.when(jnp.logical_not(later))(lambda: settle(index))

    begin(0)
    hop = remote(piece_in, source, pipe_sems.at[4], pipe_sems.at[5], other_pipe)

    @pl.when(later)
    def _():
        finish_piece()
        hop.start()
        for number in range(9):
            wave(number)
        start_sensitivity()
        start_factor()
        for index in range(6):
            settle(index)
            drain(index)
        hop.wait_send()

    lane = lax.broadcasted_iota(jnp.int32, (columns, 2 * twin), 1)
    early = (lax.rem(lane, twin) < size).astype(f32)
    halves[0] = early.astype(bf16)
    halves[1] = (1.0 - early).astype(bf16)
    feature = lax.broadcasted_iota(jnp.int32, (width, 128), 0)
    head = lax.broadcasted_iota(jnp.int32, (width, 128), 1)
    belongs = jnp.logical_and(feature >= head * size, feature < head * size + size)
    segment[...] = belongs.astype(f32).astype(bf16)
    head = lax.broadcasted_iota(jnp.int32, (128, width), 0)
    feature = lax.broadcasted_iota(jnp.int32, (128, width), 1)
    belongs = jnp.logical_and(feature >= head * size, feature < head * size + size)
    spread[...] = belongs.astype(f32).astype(bf16)
    for step in range(1, LINE):
        norm_copy(step, lax.rem(seq + LINE - step, LINE)).wait()
    for part in range(LINE):
        rows[:, part * part_width : (part + 1) * part_width] = norms_in[part, :, 0:part_width]
    finish_counts()

    def gain_of(index):
        return rows[index : index + 1, :]

    def bias_of(index):
        return rows[3 + index : 4 + index, :]

    def keep_vector(index, gain, bias):
        part = width // LINE
        for target in range(LINE):
            window = slice(target * part, (target + 1) * part)
            vector[target, index : index + 1, 0:part] = gain[:, window]
            vector[target, 3 + index : 4 + index, 0:part] = bias[:, window]

    vector[...] = jnp.zeros(vector.shape, f32)

    def both(ref, start):
        return jnp.concatenate(
            [ref[0:columns, start : start + twin], ref[columns:tokens, start : start + twin]],
            axis=1,
        )

    def stacked(ref, start):
        wide = both(ref, start)
        return jnp.concatenate([wide * halves[0], wide * halves[1]], axis=0)

    def unstack(wide):
        early_lane = lax.rem(lax.broadcasted_iota(jnp.int32, (columns, 2 * twin), 1), twin) < size
        return jnp.where(early_lane, wide[0:columns], wide[columns:])

    def put(ref, start, wide):
        ref[0:columns, start : start + twin] = wide[:, 0:twin].astype(bf16)
        ref[columns:tokens, start : start + twin] = wide[:, twin:].astype(bf16)

    def to_core(source_ref, target_ref, sems, index):
        return remote(
            source_ref, target_ref, sems.at[0, index], sems.at[1, index], other_core
        )

    start_act, finish_act = swap_rows(
        act, act_out, home_sems.at[0], home_sems.at[1], home_local.at[0], where
    )
    start_der, finish_der = swap_rows(
        der, der_out, home_sems.at[2], home_sems.at[3], home_local.at[1], where
    )
    sender = core == lax.div(seq, 2)
    spot = lax.rem(seq, 2)
    cost_own = pltpu.make_async_copy(cost, cost_out.at[spot], home_local.at[2])
    cost_copies = [
        remote(
            cost,
            cost_out.at[spot],
            cost_send.at[step - 1],
            cost_recv.at[spot],
            (pipe, lax.rem(seq + step, LINE), dp),
        )
        for step in range(1, LINE)
    ]

    send_on = remote(act, source, pipe_sems.at[0], pipe_sems.at[1], other_pipe)
    send_back = remote(der, grad_in, pipe_sems.at[2], pipe_sems.at[3], other_pipe)

    @pl.when(later)
    def _():
        send_on.wait_recv()

    gather(0, 1)

    @pl.when(jnp.logical_not(later))
    def _():
        hop.wait_recv()

    chunks, cycle = (6, 3)
    whole_turns = chunks // cycle
    paired = chunks - whole_turns
    depth = width // chunks
    units = LINE * chunks
    mid = units // 2
    always = lambda target: target >= 0
    far = jnp.maximum(seq, LINE - 1 - seq)
    pair_lag, hop_lag, share_lag = (3, 4, 4)

    def unit_of(number):
        turn = lax.div(number, LINE)
        rank = number - turn * LINE
        halfway = lax.div(rank, 2)
        target = jnp.where(lax.rem(rank, 2) == 0, LINE - 1 - halfway, halfway)
        return (target, chunks - 1 - turn)

    def rank_of(chunk):
        turn = chunks - 1 - chunk
        early_turns = lax.div(turn, cycle)
        return (early_turns, turn - early_turns - 1)

    def is_single(chunk):
        turn = chunks - 1 - chunk
        return lax.rem(turn, cycle) != 0

    def window_of(chunk):
        return pl.ds(pl.multiple_of(chunk * depth, depth), depth)

    def spot_of(number, side, shift, count=1):
        block = jnp.where(
            number < mid, 2 * units + 2 * number + side, 2 * (number - mid) + side
        )
        block = block + shift
        tile = lax.div(block, chunks)
        row = pl.multiple_of((block - tile * chunks) * depth, depth)
        return (tile, pl.ds(row, count * depth))

    def mine_at(number, side, count=1):
        return tiles.at[spot_of(number, side, 0, count)]

    def near_at(number, side):
        return tiles.at[spot_of(number, side, units)]

    def add_into(number, side, ref, start=None):
        spot = spot_of(number, side, 0)
        value = ref[...] if start is None else ref[pl.ds(start, depth), :]
        tiles[spot] = (tiles[spot].astype(f32) + value.astype(f32)).astype(bf16)

    def load(number, side):
        target, chunk = unit_of(number)
        return pltpu.make_async_copy(
            grads.at[target, 2 * side + core, window_of(chunk)],
            mine_at(number, side),
            load_sem.at[number, side],
        )

    def to_near(number, side):
        target, chunk = unit_of(number)
        return remote(
            grads.at[target, 2 * side + 1 - core, window_of(chunk)],
            near_at(number, side),
            near_send.at[number, side],
            near_recv.at[number, side],
            other_core,
        )

    def issue(number, carry):
        for side in range(2):
            to_near(number, side).start()
            load(number, side).start()
        return carry

    def issue_all(start, stop):
        lax.fori_loop(start, stop, issue, 0)

    def pair_start(number):
        turn = lax.div(number, LINE)
        _, rank = rank_of(chunks - 1 - turn)
        return pl.multiple_of((LINE * rank + number - LINE * turn) * depth, depth)

    def to_pair(number):
        return remote(
            mine_at(number, 1 - pair),
            from_pair.at[pl.ds(pair_start(number), depth)],
            far_send.at[number],
            far_recv.at[number],
            other_pair,
        )

    def arrive_near(number, side):
        load(number, side).wait()
        to_near(number, side).wait_recv()
        add_into(number, side, near_at(number, side))

    def land_slot(number, chunk, single, second):
        whole_rank, single_rank = rank_of(chunk)
        turn = chunks - 1 - chunk
        rank = number - LINE * turn
        base = 2 * LINE * whole_turns
        extra = base + LINE * paired
        if single:
            slot = base + LINE * single_rank + rank
            slot = jnp.where(second, extra + 2 * whole_turns + single_rank, slot)
        else:
            slot = 2 * (LINE * whole_rank + rank)
            slot = jnp.where(second, extra + 2 * whole_rank, slot)
        return pl.multiple_of(slot * depth, depth)

    def hop_copy(number, chunk, single, direction):
        target, _ = unit_of(number)
        second = jnp.logical_and(direction == 1, target == seq - 1)
        count = 1 if single else 2
        sems = left_recv if direction == 0 else right_recv
        return remote(
            mine_at(number, pair if single else 0, count),
            landing.at[pl.ds(land_slot(number, chunk, single, second), count * depth)],
            hop_send.at[number],
            sems.at[number],
            right if direction == 0 else left,
        )

    def take(number, chunk, single, direction):
        target, _ = unit_of(number)
        second = jnp.logical_and(direction == 1, target == seq)
        count = 1 if single else 2
        start = land_slot(number, chunk, single, second)
        sems = left_recv if direction == 0 else right_recv
        remote(
            mine_at(number, pair if single else 0, count),
            landing.at[pl.ds(start, count * depth)],
            hop_send.at[number],
            sems.at[number],
            right if direction == 0 else left,
        ).wait_recv()
        if single:
            add_into(number, pair, landing, start)
        else:
            for side in range(2):
                add_into(number, side, landing, start + side * depth)

    def late_start(chunk):
        return pl.multiple_of(2 * rank_of(chunk)[0] * depth, depth)

    def late_copy(number, chunk, single):
        if single:
            return remote(
                mine_at(number, pair),
                out.at[dp, window_of(chunk)],
                late_send.at[chunk],
                late_recv.at[chunk],
                other_pair,
            )
        return remote(
            mine_at(number, 0, 2),
            late_pair.at[pl.ds(late_start(chunk), 2 * depth)],
            late_send.at[chunk],
            late_recv.at[chunk],
            other_pair,
        )

    def share_copy(number, chunk, side, relayed):
        spot_out = out.at[2 * side + core, window_of(chunk)]
        return remote(
            spot_out if relayed else mine_at(number, side),
            spot_out,
            share_send.at[side, chunk],
            share_recv.at[side, chunk],
            other_core,
        )

    def out_copy(number, chunk, side):
        return pltpu.make_async_copy(
            mine_at(number, side), out.at[2 * side + core, window_of(chunk)], out_sem.at[side, chunk]
        )

    def at(number, condition, body):
        clipped = jnp.clip(number, 0, units - 1)
        target, chunk = unit_of(clipped)
        valid = jnp.logical_and(number >= 0, number < units)
        valid = jnp.logical_and(valid, condition(target))

        @pl.when(jnp.logical_and(valid, is_single(chunk)))
        def _():
            body(clipped, chunk, True)

        @pl.when(jnp.logical_and(valid, jnp.logical_not(is_single(chunk))))
        def _():
            body(clipped, chunk, False)

    def first_stage(number, chunk, single):
        if single:
            arrive_near(number, 1 - pair)
            to_pair(number).start()
            arrive_near(number, pair)
        else:
            for side in range(2):
                arrive_near(number, side)

    def first_body(number, carry):
        at(number, always, first_stage)
        return carry

    def second_stage(number, chunk, single):
        if single:
            to_pair(number).wait_recv()
            add_into(number, pair, from_pair, pair_start(number))

    def hop_stage(direction):
        def body(number, chunk, single):
            @pl.when(has[1 - direction])
            def _():
                take(number, chunk, single, direction)

            hop_copy(number, chunk, single, direction).start()

        return body

    def last_stage(number, chunk, single):
        for direction in range(2):

            @pl.when(has[1 - direction])
            def _():
                take(number, chunk, single, direction)

        late_copy(number, chunk, single).start()
        if single:
            out_copy(number, chunk, pair).start()
            share_copy(number, chunk, pair, False).start()

    def share_stage(number, chunk, single):
        if single:
            remote(
                mine_at(number, pair),
                out.at[dp + 2 - 4 * pair, window_of(chunk)],
                late_send.at[chunk],
                late_recv.at[chunk],
                other_pair,
            ).wait_recv()
            share_copy(number, chunk, 1 - pair, True).start()
        else:
            late_copy(number, chunk, False).wait()
            for side in range(2):
                add_into(number, side, late_pair, late_start(chunk) + side * depth)
                out_copy(number, chunk, side).start()
                share_copy(number, chunk, side, False).start()

    def hop_stages(base):
        at(base, always, second_stage)
        at(base - hop_lag * seq, lambda target: target > seq, hop_stage(0))
        at(base - hop_lag * (LINE - 1 - seq), lambda target: target < seq, hop_stage(1))
        at(base - hop_lag * far, lambda target: target == seq, last_stage)
        at(base - hop_lag * far - share_lag, lambda target: target == seq, share_stage)

    def hops(start, stop):
        def body(number, carry):
            hop_stages(number)
            return carry

        lax.fori_loop(start, stop, body, 0)

    def finish_unit(number, carry):
        for side in range(2):
            to_near(number, side).wait_send()

        def sends(number, chunk, single):
            if single:
                to_pair(number).wait_send()

        at(number, always, sends)
        at(
            number,
            lambda target: target > seq,
            lambda number, chunk, single: hop_copy(number, chunk, single, 0).wait_send(),
        )
        at(
            number,
            lambda target: target < seq,
            lambda number, chunk, single: hop_copy(number, chunk, single, 1).wait_send(),
        )

        def shared(number, chunk, single):
            if single:
                late_copy(number, chunk, True).wait_send()
                out_copy(number, chunk, pair).wait()
                share_copy(number, chunk, pair, False).wait_send()
                share_copy(number, chunk, 1 - pair, True).wait_send()
            else:
                for side in range(2):
                    out_copy(number, chunk, side).wait()
                    share_copy(number, chunk, side, False).wait_send()
            for side in range(2):
                spot_out = out.at[2 * side + 1 - core, window_of(chunk)]
                remote(
                    spot_out,
                    spot_out,
                    share_send.at[side, chunk],
                    share_recv.at[side, chunk],
                    other_core,
                ).wait_recv()

        at(number, lambda target: target == seq, shared)
        return carry

    vec_first = remote(vector, vec_core, vec_send.at[0], vec_recv.at[0], other_core)
    vec_second = remote(vec_core, vec_pair, vec_send.at[1], vec_recv.at[1], other_pair)

    def move_copy(step, source):
        goal = lax.rem(seq + step, LINE)
        return remote(
            vec_pair.at[goal],
            vec_line.at[source],
            vec_send.at[1 + step],
            vec_recv.at[2 + source],
            (pipe, goal, dp),
        )

    def vector_to_pair():
        vec_first.wait()
        vec_core[...] = vector[...] + vec_core[...]
        vec_second.start()

    def vector_to_line():
        vec_second.wait()
        vec_pair[...] = vec_core[...] + vec_pair[...]
        for step in range(1, LINE):
            move_copy(step, seq).start()
        vec_line[seq] = vec_pair[seq]

    def vector_end():
        for step in range(1, LINE):
            move_copy(step, lax.rem(seq + LINE - step, LINE)).wait()
        total_vector = vec_line[0]
        for source_of in range(1, LINE):
            total_vector = total_vector + vec_line[source_of]
        vector_out[...] = total_vector

    packed_share = width // (4 * LINE)

    def outer_terms():
        for part in range(4):
            slot = part % 2
            window = slice(part * width, (part + 1) * width)
            if part >= 2:
                down_copy(part - 2).wait()
            term = dot(hidden[:, window], branch_ffn[...], 0, 0).astype(bf16)
            stage_down[slot] = term.reshape(4, width // 4, width)
            down_copy(part).start()
        packed_terms(((normal_c, grad_up, 8 * packed_share),))
        for part in range(2, 4):
            down_copy(part).wait()

    def down_copy(part):
        return pltpu.make_async_copy(
            stage_down.at[part % 2],
            grads.at[part, :, pl.ds(12 * packed_share, width // 4)],
            stage_sems.at[2 + part % 2, 0],
        )

    def inner_terms():
        packed_terms(
            (
                (normal_b, grad_mixer_col, 4 * packed_share),
                (mixed, branch_col, 7 * packed_share),
                (normal_a, grad_mixer, 0),
                (blended, branch_row, 3 * packed_share),
            )
        )

    def packed_terms(pairs):
        waiting = [None, None]
        number = 0
        for first, second, base in pairs:
            for part in range(second.shape[1] // width):
                slot = number % 2
                if waiting[slot] is not None:
                    for copy in waiting[slot]:
                        copy.wait()
                window = slice(part * width, (part + 1) * width)
                term = dot(first[...], second[:, window], 0, 0).astype(bf16)
                stage[slot] = term.reshape(LINE, 4, packed_share, width)
                waiting[slot] = [
                    pltpu.make_async_copy(
                        stage.at[slot, target],
                        grads.at[target, :, pl.ds(base + part * packed_share, packed_share)],
                        stage_sems.at[slot, target],
                    )
                    for target in range(LINE)
                ]
                for copy in waiting[slot]:
                    copy.start()
                number += 1
        for copies in waiting:
            for copy in copies or ():
                copy.wait()

    unit, _ = unit_rows(source[...].reshape(tokens, width).astype(f32))
    normal_a[...] = (unit * gain_of(0) + bias_of(0)).astype(bf16)
    gather(2, 3)
    ready(0)
    for part in range(3):
        window = slice(part * width, (part + 1) * width)
        mixer[:, window] = dot(normal_a[...], tiles[part], 1, 0).astype(bf16)
    logit_factor = 1.0 / (math.sqrt(size) * math.sqrt(total_rows))
    logit_copies = []
    for couple in range(couples):
        partial_value = logit_factor * dot(
            both(mixer, couple * twin), stacked(mixer, width + couple * twin), 1, 1
        )
        logit_send[couple] = partial_value.astype(bf16)
        copy = to_core(logit_send.at[couple], logit_recv.at[couple], logit_sems, couple)
        copy.start()
        logit_copies.append(copy)
    gather(4)
    valid = (
        lax.broadcasted_iota(jnp.int32, (columns, 1), 0).astype(f32) < counts_in[0, 0:1, 0:1]
    ).astype(f32)
    disorder = jnp.zeros((columns, 1), f32)
    for couple in range(couples):
        logit_copies[couple].wait_recv()
        wide = logit_send[couple].astype(f32) + logit_recv[couple].astype(f32)
        shares = []
        for half in range(2):
            logits = wide[:, half * columns : (half + 1) * columns]
            shifted_logits = logits - jnp.max(logits, axis=-1, keepdims=True)
            powers = jnp.exp(shifted_logits)
            total = jnp.sum(powers, axis=-1, keepdims=True)
            logs = shifted_logits - jnp.log(total)
            share = powers / total
            log_share[couple, :, half * columns : (half + 1) * columns] = logs
            disorder = disorder - jnp.sum(share * logs, axis=-1, keepdims=True) * valid
            shares.append(share.astype(bf16))
        put(
            blended,
            couple * twin,
            dot(
                jnp.concatenate(shares, axis=1), stacked(mixer, 2 * width + couple * twin), 1, 0
            ),
        )
    cost[...] = jnp.broadcast_to(
        jnp.sum(disorder, axis=0, keepdims=True) / float(heads * columns), cost.shape
    )
    ready(1)
    after_row[...] = source[...].reshape(tokens, width).astype(f32) + dot(blended[...], tiles[3], 1, 0)
    unit, _ = unit_rows(after_row[...])
    normal_b[...] = (unit * gain_of(1) + bias_of(1)).astype(bf16)
    gather(5)
    ready(2)
    keys_copies = []
    for part in (1, 2, 0):
        window = slice(part * width, (part + 1) * width)
        mixer_col[:, window] = dot(normal_b[...], tiles[4 + part], 1, 0).astype(bf16)
        if part > 0:
            copy = to_core(
                mixer_col.at[:, window], keys_recv.at[part - 1], keys_sems, part - 1
            )
            copy.start()
            keys_copies.append(copy)

    def line_of(part, place_of):
        if place_of < 2:
            rows_of = slice(place_of * columns, (place_of + 1) * columns)
            return mixer_col[rows_of, (1 + part) * width : (2 + part) * width]
        rows_of = slice((place_of - 2) * columns, (place_of - 1) * columns)
        return keys_recv[part, rows_of, :]

    def sums_by_head(wide_ref, start, line):
        products = [
            wide_ref[index * columns : (index + 1) * columns, start : start + width] * line
            for index in range(2)
        ]
        return dot(jnp.concatenate(products, axis=0), segment[...], 1, 0)

    def spread_heads(narrow):
        return dot(narrow, spread[...], 1, 0)

    gather(6)
    scores = []
    for place_of in range(4):
        if place_of == 2:
            keys_copies[0].wait_recv()
        scores.append(sums_by_head(mixer_col, 0, line_of(0, place_of)) / math.sqrt(size))
    highest = functools.reduce(jnp.maximum, scores)
    powers = [jnp.exp(score - highest) for score in scores]
    total = functools.reduce(jnp.add, powers)
    keys_copies[1].wait_recv()
    gathered_mix = None
    for place_of in range(4):
        share = powers[place_of] / total
        col_share[place_of] = share
        wide = spread_heads(share.astype(bf16))
        line = line_of(1, place_of).astype(f32)
        term = jnp.concatenate([wide[0:columns] * line, wide[columns:] * line], axis=0)
        gathered_mix = term if gathered_mix is None else gathered_mix + term
    mixed[...] = gathered_mix.astype(bf16)
    ready(3)
    after_col[...] = after_row[...] + dot(mixed[...], tiles[7], 1, 0)
    unit, _ = unit_rows(after_col[...])
    normal_c[...] = (unit * gain_of(2) + bias_of(2)).astype(bf16)
    gather(7)
    ready(4)
    parts = hidden.shape[1] // width
    result = after_col[...]
    for part in range(parts):
        window = slice(part * width, (part + 1) * width)
        upward = dot(normal_c[...], tiles[8 + part], 1, 0)
        inner = 0.5 + 0.5 * lax.erf(upward * math.sqrt(0.5))
        density = jnp.exp(-0.5 * upward * upward) * (1.0 / math.sqrt(2.0 * math.pi))
        hidden[:, window] = (upward * inner).astype(bf16)
        slope[:, window] = (inner + upward * density).astype(bf16)
    gather(8)
    ready(5)
    for part in range(parts):
        window = slice(part * width, (part + 1) * width)
        result = result + dot(hidden[:, window], tiles[12 + part], 1, 0)
    act[...] = result.astype(bf16).reshape(2, columns, width)

    @pl.when(pipe == 0)
    def _():
        send_on.start()

    start_act()

    @pl.when(sender)
    def _():
        cost_own.start()
        for copy in cost_copies:
            copy.start()

    @pl.when(pipe == 1)
    def _():
        finish_sensitivity()
        finish_factor()
        for index in range(2):
            total_grad[index * columns : (index + 1) * columns, :] = (
                sensitivity[index].astype(f32) * factor_in[index, :, 0:1]
            )

    @pl.when(pipe == 0)
    def _():
        for index in range(6):
            drain(index)
        send_back.wait_recv()
        total_grad[...] = grad_in[...].reshape(tokens, width).astype(f32)

    branch_ffn[...] = total_grad[...].astype(bf16)
    grad_normal = None
    for part in range(parts):
        window = slice(part * width, (part + 1) * width)
        grad_hidden = dot(branch_ffn[...], tiles[12 + part], 1, 1)
        grad_up[:, window] = (grad_hidden * slope[:, window].astype(f32)).astype(bf16)
        term = dot(grad_up[:, window], tiles[8 + part], 1, 1)
        grad_normal = term if grad_normal is None else grad_normal + term
    pl.when(jnp.logical_not(later))(outer_terms)
    term, gain, bias = unit_rows_back(grad_normal, after_col[...], gain_of(2))
    keep_vector(2, gain, bias)
    total_grad[...] = total_grad[...] + term
    branch_col[...] = total_grad[...].astype(bf16)
    grad_mixed = dot(branch_col[...], tiles[7], 1, 1).astype(bf16)
    grad_probs = []
    for place_of in range(4):
        line = line_of(1, place_of)
        products = [grad_mixed[0:columns] * line, grad_mixed[columns:] * line]
        grad_probs.append(dot(jnp.concatenate(products, axis=0), segment[...], 1, 0))
    inner = functools.reduce(
        jnp.add, [col_share[place_of] * grad_probs[place_of] for place_of in range(4)]
    )
    root_size = math.sqrt(size)
    grad_query = None
    local_terms = []
    back_copies = []
    grad_lines = grad_mixed.astype(f32)
    query_lines = mixer_col[:, 0:width].astype(f32)
    for place_of in (2, 3, 0, 1):
        share = col_share[place_of]
        narrow = (share * (grad_probs[place_of] - inner)).astype(bf16)
        wide = spread_heads(narrow)
        line = line_of(0, place_of).astype(f32)
        term = jnp.concatenate([wide[0:columns] * line, wide[columns:] * line], axis=0)
        grad_query = term if grad_query is None else grad_query + term
        key_term = wide[0:columns] * query_lines[0:columns] + wide[columns:] * query_lines[columns:]
        key_term = key_term / root_size
        wide = spread_heads(share.astype(bf16))
        value_term = wide[0:columns] * grad_lines[0:columns] + wide[columns:] * grad_lines[columns:]
        if place_of >= 2:
            index = place_of - 2
            rows_of = slice(index * columns, (index + 1) * columns)
            keys_send[rows_of, 0:width] = key_term.astype(bf16)
            keys_send[rows_of, width:] = value_term.astype(bf16)
            copy = to_core(keys_send.at[rows_of, :], keys_back.at[rows_of, :], back_sems, index)
            copy.start()
            back_copies.append(copy)
        else:
            local_terms.append((key_term, value_term))
    grad_mixer_col[:, 0:width] = (grad_query / root_size).astype(bf16)
    for place_of in range(2):
        back_copies[place_of].wait()
        rows_of = slice(place_of * columns, (place_of + 1) * columns)
        for part in range(2):
            window = slice(part * width, (part + 1) * width)
            grad_mixer_col[rows_of, (1 + part) * width : (2 + part) * width] = (
                local_terms[place_of][part] + keys_back[rows_of, window].astype(f32)
            ).astype(bf16)
    pl.when(jnp.logical_not(later))(lambda: issue_all(0, mid))
    grad_normal = None
    for part in range(3):
        window = slice(part * width, (part + 1) * width)
        term = dot(grad_mixer_col[:, window], tiles[4 + part], 1, 1)
        grad_normal = term if grad_normal is None else grad_normal + term
    term, gain, bias = unit_rows_back(grad_normal, after_row[...], gain_of(1))
    keep_vector(1, gain, bias)
    total_grad[...] = total_grad[...] + term
    branch_row[...] = total_grad[...].astype(bf16)
    keys_send[:, 0:width] = dot(branch_row[...], tiles[3], 1, 1).astype(bf16)
    probs_copies = []
    for couple in range(couples):
        partial_value = dot(
            both(keys_send, couple * twin), stacked(mixer, 2 * width + couple * twin), 1, 1
        )
        probs_send[couple] = partial_value.astype(bf16)
        copy = to_core(probs_send.at[couple], probs_recv.at[couple], probs_sems, couple)
        copy.start()
        probs_copies.append(copy)

    @pl.when(jnp.logical_not(later))
    def _():
        lax.fori_loop(0, mid, first_body, 0)
        hops(0, EARLY)

    column_weight = (float(total_rows * columns) / float(heads * columns)) * valid
    for couple in range(couples):
        start = couple * twin
        logs = log_share[couple]
        share = jnp.exp(logs)
        grad_wide = both(keys_send, start)
        put(
            grad_mixer,
            2 * width + start,
            unstack(dot(share.astype(bf16), grad_wide, 0, 0)),
        )
        probs_copies[couple].wait_recv()
        wide = probs_send[couple].astype(f32) + probs_recv[couple].astype(f32)
        pieces = []
        for half in range(2):
            window = slice(half * columns, (half + 1) * columns)
            part_share, part_logs, part_grad = (share[:, window], logs[:, window], wide[:, window])
            entropy = -jnp.sum(part_share * part_logs, axis=-1, keepdims=True)
            inner = jnp.sum(part_share * part_grad, axis=-1, keepdims=True)
            piece = part_share * (part_grad - inner)
            piece = piece - column_weight * part_share * (part_logs + entropy)
            pieces.append(piece.astype(bf16))
        grad_logits = jnp.concatenate(pieces, axis=1)
        put(
            grad_mixer,
            start,
            logit_factor * dot(grad_logits, stacked(mixer, width + start), 1, 0),
        )
        put(
            grad_mixer,
            width + start,
            logit_factor * unstack(dot(grad_logits, both(mixer, start), 0, 0)),
        )
    grad_normal = None
    for part in range(3):
        window = slice(part * width, (part + 1) * width)
        term = dot(grad_mixer[:, window], tiles[part], 1, 1)
        grad_normal = term if grad_normal is None else grad_normal + term
    term, gain, bias = unit_rows_back(grad_normal, source[...].reshape(tokens, width).astype(f32), gain_of(0))
    keep_vector(0, gain, bias)
    der[...] = (total_grad[...] + term).astype(bf16).reshape(2, columns, width)

    @pl.when(pipe == 1)
    def _():
        send_back.start()

    start_der()
    vec_first.start()

    @pl.when(later)
    def _():
        outer_terms()
        issue_all(0, mid)
        lax.fori_loop(0, mid, first_body, 0)
        hops(0, EARLY)

    hops(EARLY, EARLY + MORE)
    inner_terms()
    issue_all(mid, units)
    vector_to_pair()

    def mix(number, carry):
        for index in range(AT_ONCE):
            at(mid + AT_ONCE * number + index, always, first_stage)
        hop_stages(EARLY + MORE + number)
        return carry

    lax.fori_loop(0, mid // AT_ONCE, mix, 0)
    hops(EARLY + MORE + mid // AT_ONCE, units)
    vector_to_line()
    hops(units, units + hop_lag * (LINE - 1) + share_lag)
    vector_end()
    lax.fori_loop(0, units, finish_unit, 0)
    for copy in logit_copies + keys_copies + probs_copies:
        copy.wait_send()

    @pl.when(pipe == 0)
    def _():
        send_on.wait_send()

    @pl.when(pipe == 1)
    def _():
        send_back.wait_send()

    finish_act()
    finish_der()

    @pl.when(sender)
    def _():
        cost_own.wait()
        for copy in cost_copies:
            copy.wait_send()

    for index in range(2):

        @pl.when(2 * core + index != seq)
        def _():
            remote(
                cost, cost_out.at[index], cost_send.at[0], cost_recv.at[index], other_core
            ).wait_recv()


def run_layers(shards, families, upstream, order, quarters, tally, norms):
    columns, width = families.shape[2:]
    tokens = 2 * columns
    couples = HEAD_TALLY // 2
    wide = shards[4].shape[2]
    entry = jax.ShapeDtypeStruct((2, columns, width), families.dtype)
    sizes = sum(shard.size for shard in shards) * LINE // (width * width)
    depth = width // 6
    block = lambda count: pltpu.VMEM((count * depth, width), bf16)
    anywhere = pl.BlockSpec(memory_space=pl.ANY)
    inside = pl.BlockSpec(memory_space=pltpu.VMEM)
    scalars = pl.BlockSpec(memory_space=pltpu.SMEM)
    dma = pltpu.SemaphoreType.DMA
    bf16, f32 = (jnp.bfloat16, jnp.float32)
    rows_of = lambda columns_of, kind=bf16: pltpu.VMEM((tokens, columns_of), kind)
    scores = pltpu.VMEM((couples, columns, 2 * columns), bf16)
    return pl.pallas_call(
        layers_kernel,
        out_shape=[
            jax.ShapeDtypeStruct(entry.shape, bf16),
            jax.ShapeDtypeStruct(entry.shape, bf16),
            jax.ShapeDtypeStruct((2, 8, 128), f32),
            jax.ShapeDtypeStruct((8, 256), f32),
            jax.ShapeDtypeStruct((LINE, 4, width, width), bf16),
            jax.ShapeDtypeStruct((4, width, width), bf16),
        ],
        in_specs=[anywhere] * 6 + [inside, inside, scalars, inside, scalars, inside],
        out_specs=[anywhere, anywhere, inside, inside, anywhere, anywhere],
        scratch_shapes=[
            pltpu.VMEM((sizes, width, width), bf16),
            pltpu.VMEM(entry.shape, bf16),
            rows_of(width),
            rows_of(width),
            rows_of(width),
            rows_of(3 * width),
            rows_of(3 * width),
            rows_of(width),
            rows_of(width),
            rows_of(width, f32),
            rows_of(width, f32),
            pltpu.VMEM((couples, columns, 2 * columns), f32),
            pltpu.VMEM((4, tokens, 128), f32),
            rows_of(wide),
            rows_of(wide),
            rows_of(width, f32),
            pltpu.VMEM(entry.shape, bf16),
            rows_of(width),
            rows_of(width),
            rows_of(width),
            rows_of(wide),
            rows_of(3 * width),
            rows_of(3 * width),
            scores,
            scores,
            pltpu.VMEM((2, tokens, width), bf16),
            rows_of(2 * width),
            rows_of(2 * width),
            scores,
            scores,
            pltpu.VMEM((2, columns, 2 * columns), bf16),
            pltpu.VMEM((width, 128), bf16),
            pltpu.VMEM((128, width), bf16),
            pltpu.VMEM((2, LINE, 4, width // (4 * LINE), width), bf16),
            pltpu.VMEM((2, 4, width // 4, width), bf16),
            pltpu.VMEM(entry.shape, bf16),
            pltpu.VMEM(entry.shape, bf16),
            pltpu.VMEM((8, 128), f32),
            pltpu.VMEM(entry.shape, bf16),
            pltpu.VMEM(entry.shape, bf16),
            pltpu.VMEM(entry.shape, bf16),
            pltpu.VMEM((2, columns, columns), f32),
            pltpu.VMEM((2, columns, columns), f32),
            pltpu.VMEM((2, 8, 128), f32),
            pltpu.VMEM((2, 8, 128), f32),
            pltpu.VMEM((LINE, 8, 256), f32),
            pltpu.VMEM((8, width), f32),
            dma((6,)),
            dma((2, LINE, 6)),
            dma((LINE, 6)),
            dma((LINE, 6)),
            dma((LINE, 6)),
            dma((2, LINE, 6)),
            dma((2, LINE, 6)),
            dma((8, 2)),
            dma((4,)),
            dma((LINE - 1,)),
            dma((LINE,)),
            block(40),
            block(16),
            block(4),
            pltpu.VMEM((LINE, 8, 256), f32),
            pltpu.VMEM((LINE, 8, 256), f32),
            pltpu.VMEM((LINE, 8, 256), f32),
            pltpu.VMEM((LINE, 8, 256), f32),
            dma((24, 2)),
            dma((24, 2)),
            dma((24, 2)),
            dma((24,)),
            dma((24,)),
            dma((24,)),
            dma((24,)),
            dma((24,)),
            dma((6,)),
            dma((6,)),
            dma((2, 6)),
            dma((2, 6)),
            dma((2, 6)),
            dma((2 + LINE,)),
            dma((2 + LINE,)),
            dma((2, couples)),
            dma((2, 2)),
            dma((2, 2)),
            dma((2, couples)),
            dma((6,)),
            dma((4, LINE)),
            dma((4, 2)),
            dma((3,)),
            dma((LINE - 1,)),
            dma((2,)),
        ],
        compiler_params=pltpu.CompilerParams(
            collective_id=2, has_side_effects=True, vmem_limit_bytes=63 * 2**20
        ),
        name="two_layers",
    )(*shards, families, upstream, order, quarters, tally, norms)


def unpack_kernel(blocks, vector, act, der, costs, *refs):
    results, gain, bias, act_out, der_out, cost_out = (refs[:6], *refs[6:])
    width = blocks.shape[2]
    base = 0
    for result in results:
        depth, wide = result.shape[1:]
        for part in range(wide // width):
            result[0, :, part * width : (part + 1) * width] = blocks[
                0, base : base + depth, :
            ].astype(jnp.float32)
            base += depth
    share = gain.shape[2]
    gain[0] = vector[0:3, 0:share]
    bias[0] = vector[3:6, 0:share]
    act_out[0, :, 0] = act[...]
    der_out[0, :, 0] = der[...]
    cost_out[...] = jnp.concatenate([costs[0, 0:1, 0:1], costs[1, 0:1, 0:1]], axis=1)


def unpack_all(blocks, vector, act, der, costs, shapes, share):
    columns, width = act.shape[1:]
    small = jax.ShapeDtypeStruct((1, 3, share), jnp.float32)
    large = jax.ShapeDtypeStruct((1, 2, 1, columns, width), act.dtype)
    part = pl.BlockSpec((2, columns // 4, width), lambda step: (0, step, 0))
    wide = pl.BlockSpec((1, 2, 1, columns // 4, width), lambda step: (0, 0, 0, step, 0))
    return pl.pallas_call(
        unpack_kernel,
        grid=(4,),
        out_shape=[jax.ShapeDtypeStruct((1,) + shape, jnp.float32) for shape in shapes]
        + [small, small, large, large, jax.ShapeDtypeStruct((1, 2), jnp.float32)],
        in_specs=[
            pl.BlockSpec((1,) + blocks.shape[1:], lambda step: (step, 0, 0)),
            pl.BlockSpec(vector.shape, lambda step: (0, 0)),
            part,
            part,
            pl.BlockSpec(costs.shape, lambda step: (0, 0, 0)),
        ],
        out_specs=[
            pl.BlockSpec((1, shape[0] // 4, shape[1]), lambda step: (0, step, 0))
            for shape in shapes
        ]
        + [pl.BlockSpec(small.shape, lambda step: (0, 0, 0))] * 2
        + [wide, wide, pl.BlockSpec((1, 2), lambda step: (0, 0))],
        compiler_params=pltpu.CompilerParams(vmem_limit_bytes=60 * 2**20),
        cost_estimate=pl.CostEstimate(
            flops=blocks.size, bytes_accessed=6 * blocks.size, transcendentals=0
        ),
        name="unpack_grads",
    )(blocks, vector, act, der, costs)


def on_device_lined(
    embedded_families,
    order,
    token_quarter_factor,
    genuine_residue_tally,
    standardizer_scales,
    standardizer_offsets,
    row_qkv,
    row_out,
    col_qkv,
    col_out,
    ffn_up,
    ffn_down,
    upstream_sensitivity,
):
    model_width = embedded_families.shape[-1]
    share = standardizer_scales.shape[-1]
    shards = (row_qkv, row_out, col_qkv, col_out, ffn_up, ffn_down)
    norms = jnp.pad(
        jnp.concatenate([standardizer_scales[0], standardizer_offsets[0]], axis=0),
        ((0, 2), (0, 256 - share)),
    )
    activations, derivs, costs, vector, _, out = run_layers(
        shards,
        embedded_families,
        upstream_sensitivity,
        order,
        token_quarter_factor,
        genuine_residue_tally,
        norms,
    )
    *results, activations, derivs, costs = unpack_all(
        out,
        vector,
        activations,
        derivs,
        costs,
        [shard.shape[1:] for shard in shards],
        share,
    )
    return (activations, derivs, costs, *results)


def solution(mesh):
    in_specs = (
        P("dp", "seq", None, None),
        P("dp", None),
        P("dp", "seq", None),
        P("dp"),
        P("pipe", None, "seq"),
        P("pipe", None, "seq"),
        P("pipe", "seq", None),
        P("pipe", "seq", None),
        P("pipe", "seq", None),
        P("pipe", "seq", None),
        P("pipe", "seq", None),
        P("pipe", "seq", None),
        P("dp", "seq", None, None),
    )
    out_specs = (
        P("pipe", "dp", "seq", None, None),
        P("pipe", "dp", "seq", None, None),
        P("pipe", "dp"),
        P("pipe", "seq", None),
        P("pipe", "seq", None),
        P("pipe", "seq", None),
        P("pipe", "seq", None),
        P("pipe", "seq", None),
        P("pipe", "seq", None),
        P("pipe", None, "seq"),
        P("pipe", None, "seq"),
    )
    lined = mesh.shape["seq"] == LINE and mesh.shape["dp"] == 4 and mesh.shape["pipe"] == 2
    return jax.shard_map(
        on_device_lined if lined else on_device, mesh=mesh, in_specs=in_specs, out_specs=out_specs, check_vma=False
    )
```

```python
import functools
import math

import jax
import jax.numpy as jnp
from jax import lax
from jax.experimental import pallas as pl
from jax.experimental.pallas import tpu as pltpu
from jax.sharding import PartitionSpec as P

HEAD_TALLY = 12
LINE = 4
MESH = pl.DeviceIdType.MESH
EARLY = 4
AT_ONCE = 2
MORE = 2
PIECES = 7


norm_epsilon = 1e-05


def shifted(value, axis, steps):
    count = lax.axis_size(axis)
    initial, last = (max(0, -steps), min(count, count - steps))
    return lax.ppermute(value, axis, [(source, source + steps) for source in range(initial, last)])


def normed(values, gain_row, bias_row):
    average = jnp.mean(values, axis=-1, keepdims=True)
    centered = values - average
    variance = jnp.mean(centered * centered, axis=-1, keepdims=True)
    return centered * lax.rsqrt(variance + norm_epsilon) * gain_row + bias_row


def gelu_exact(values):
    return jax.nn.gelu(values, approximate=False)


def product(left, weight):
    return lax.dot_general(
        left, weight, (((left.ndim - 1,), (0,)), ((), ())), preferred_element_type=jnp.float32
    )


def product_back(left, weight):
    return lax.dot_general(
        left, weight, (((left.ndim - 1,), (1,)), ((), ())), preferred_element_type=jnp.float32
    )


def weight_term(left, right):
    return lax.dot_general(
        left, right, (((0, 1), (0, 1)), ((), ())), preferred_element_type=jnp.float32
    )


def split_heads(values, head_count):
    return values.reshape(values.shape[:-1] + (head_count, values.shape[-1] // head_count))


def choose(flag, first_tree, second_tree):
    return jax.tree.map(lambda early, later: jnp.where(flag, early, later), first_tree, second_tree)


def column_scores(queries, key_rows, head_count):
    query_heads = split_heads(queries, head_count)
    raw = jnp.einsum(
        "rche,sche->chrs",
        query_heads,
        split_heads(key_rows, head_count),
        preferred_element_type=jnp.float32,
    )
    return raw / math.sqrt(query_heads.shape[-1])


def column_forward(queries, key_rows, content_lines, head_count):
    scores = column_scores(queries, key_rows, head_count)
    log_total = jax.nn.logsumexp(scores, axis=-1)
    vertical_factors = jnp.exp(scores - log_total[..., None]).astype(jnp.bfloat16)
    mixed_cols = jnp.einsum(
        "gmqi,igmu->qgmu",
        vertical_factors,
        split_heads(content_lines, head_count),
        preferred_element_type=jnp.float32,
    )
    return (mixed_cols.reshape(queries.shape).astype(jnp.bfloat16), log_total)


def column_backward(queries, key_rows, content_lines, log_total, grad_mixed, head_count):
    scores = column_scores(queries, key_rows, head_count)
    softmax_share = jnp.exp(scores - log_total[..., None])
    grad_heads = split_heads(grad_mixed, head_count)
    grad_probs = jnp.einsum(
        "rche,sche->chrs",
        grad_heads,
        split_heads(content_lines, head_count),
        preferred_element_type=jnp.float32,
    )
    grad_values = jnp.einsum(
        "chrs,rche->sche",
        softmax_share.astype(jnp.bfloat16),
        grad_heads,
        preferred_element_type=jnp.float32,
    )
    grad_scores = (
        softmax_share * (grad_probs - jnp.sum(softmax_share * grad_probs, axis=-1, keepdims=True))
    ).astype(jnp.bfloat16)
    root_size = math.sqrt(queries.shape[-1] // head_count)
    grad_queries = (
        jnp.einsum(
            "gmqi,igmu->qgmu",
            grad_scores,
            split_heads(key_rows, head_count),
            preferred_element_type=jnp.float32,
        )
        / root_size
    )
    grad_keys = (
        jnp.einsum(
            "chrs,rche->sche",
            grad_scores,
            split_heads(queries, head_count),
            preferred_element_type=jnp.float32,
        )
        / root_size
    )
    return (
        grad_queries.reshape(queries.shape),
        grad_keys.reshape(key_rows.shape),
        grad_values.reshape(content_lines.shape),
    )


def row_split(horizontal_mixer, model_width, head_count):
    queries = split_heads(horizontal_mixer[..., :model_width], head_count)
    key_rows = split_heads(horizontal_mixer[..., model_width : 2 * model_width], head_count)
    content_lines = split_heads(horizontal_mixer[..., 2 * model_width :], head_count)
    return (queries, key_rows, content_lines)


def layer_forward(source_rows, family_residues, projection_tables, head_count):
    (
        horizontal_coefficients,
        w_row_out,
        vertical_coefficients,
        w_col_out,
        w_up,
        w_down,
        gain_rows,
        bias_rows,
    ) = projection_tables
    row_count, columns, model_width = source_rows.shape
    total_rows = row_count * lax.axis_size("seq")
    start = source_rows.astype(jnp.float32)
    layernorm_first = normed(start, gain_rows[0], bias_rows[0]).astype(jnp.bfloat16)
    horizontal_mixer = product(layernorm_first, horizontal_coefficients).astype(jnp.bfloat16)
    queries, key_rows, content_lines = row_split(horizontal_mixer, model_width, head_count)
    logit_factor = 1.0 / (math.sqrt(model_width // head_count) * math.sqrt(total_rows))
    partial_value = logit_factor * jnp.einsum(
        "rihe,rjhe->hij", queries, key_rows, preferred_element_type=jnp.float32
    )
    logits = lax.psum(partial_value.astype(jnp.bfloat16), "seq").astype(jnp.float32)
    softmax_share = jax.nn.softmax(logits, axis=-1)
    log_probs = jax.nn.log_softmax(logits, axis=-1)
    entropy = -jnp.sum(softmax_share * log_probs, axis=-1)
    valid_residues = (jnp.arange(columns, dtype=jnp.int32) < family_residues).astype(jnp.float32)
    disorder_cost = jnp.sum(entropy * valid_residues[None, :]) / float(head_count * columns)
    blended_lines = jnp.einsum(
        "vyp,opvl->oyvl",
        softmax_share.astype(jnp.bfloat16),
        content_lines,
        preferred_element_type=jnp.float32,
    )
    blended_lines = blended_lines.reshape(row_count, columns, model_width).astype(jnp.bfloat16)
    after_row = start + product(blended_lines, w_row_out)
    layernorm_second = normed(after_row, gain_rows[1], bias_rows[1]).astype(jnp.bfloat16)
    vertical_mixer = product(layernorm_second, vertical_coefficients).astype(jnp.bfloat16)
    everyone = lax.all_gather(vertical_mixer[..., model_width:], "seq", axis=0, tiled=True)
    mixed_values, log_total = column_forward(
        vertical_mixer[..., :model_width],
        everyone[..., :model_width],
        everyone[..., model_width:],
        head_count,
    )
    column_state = (everyone, log_total)
    after_col = after_row + product(mixed_values, w_col_out)
    normal_c = normed(after_col, gain_rows[2], bias_rows[2]).astype(jnp.bfloat16)
    upward = product(normal_c, w_up)
    hidden = gelu_exact(upward).astype(jnp.bfloat16)
    result = after_col + product(hidden, w_down)
    kept_state = (
        source_rows,
        layernorm_first,
        horizontal_mixer,
        logits,
        blended_lines,
        after_row,
        layernorm_second,
        vertical_mixer,
        column_state,
        mixed_values,
        after_col,
        normal_c,
        upward,
        hidden,
    )
    return (result.astype(jnp.bfloat16), disorder_cost, kept_state)


def layer_backward(kept_state, family_residues, grad_result, projection_tables, head_count):
    (
        horizontal_coefficients,
        w_row_out,
        vertical_coefficients,
        w_col_out,
        w_up,
        w_down,
        gain_rows,
        bias_rows,
    ) = projection_tables
    (
        source_rows,
        layernorm_first,
        horizontal_mixer,
        logits,
        blended_lines,
        after_row,
        layernorm_second,
        vertical_mixer,
        column_state,
        mixed_values,
        after_col,
        normal_c,
        upward,
        hidden,
    ) = kept_state
    row_count, columns, model_width = source_rows.shape
    total_rows = row_count * lax.axis_size("seq")
    grad_branch_ffn = grad_result.astype(jnp.bfloat16)
    grad_hidden = product_back(grad_branch_ffn, w_down)
    grad_upward = jax.vjp(gelu_exact, upward)[1](grad_hidden)[0].astype(jnp.bfloat16)
    grad_normal_c = product_back(grad_upward, w_up)
    from_norm, gain_last, bias_last = jax.vjp(normed, after_col, gain_rows[2], bias_rows[2])[1](
        grad_normal_c
    )
    grad_col = grad_result + from_norm
    grad_branch_col = grad_col.astype(jnp.bfloat16)
    grad_attended = product_back(grad_branch_col, w_col_out).astype(jnp.bfloat16)
    everyone, log_total = column_state
    grad_query_col, grad_key_col, grad_value_col = column_backward(
        vertical_mixer[..., :model_width],
        everyone[..., :model_width],
        everyone[..., model_width:],
        log_total,
        grad_attended,
        head_count,
    )
    grad_kv_rows = lax.psum_scatter(
        jnp.concatenate([grad_key_col, grad_value_col], axis=-1).astype(jnp.bfloat16),
        "seq",
        scatter_dimension=0,
        tiled=True,
    ).astype(jnp.float32)
    grad_col_proj = jnp.concatenate([grad_query_col, grad_kv_rows], axis=-1).astype(jnp.bfloat16)
    grad_normal_b = product_back(grad_col_proj, vertical_coefficients)
    from_norm, gain_middle, bias_middle = jax.vjp(normed, after_row, gain_rows[1], bias_rows[1])[1](
        grad_normal_b
    )
    grad_row = grad_col + from_norm
    grad_branch_row = grad_row.astype(jnp.bfloat16)
    grad_mixed = split_heads(
        product_back(grad_branch_row, w_row_out).astype(jnp.bfloat16), head_count
    )
    queries, key_rows, content_lines = row_split(horizontal_mixer, model_width, head_count)
    softmax_share = jax.nn.softmax(logits, axis=-1)
    log_probs = jax.nn.log_softmax(logits, axis=-1)
    entropy = -jnp.sum(softmax_share * log_probs, axis=-1)
    partial_value = jnp.einsum(
        "rihe,rjhe->hij", grad_mixed, content_lines, preferred_element_type=jnp.float32
    )
    grad_probs = lax.psum(partial_value.astype(jnp.bfloat16), "seq").astype(jnp.float32)
    grad_values = jnp.einsum(
        "hij,rihe->rjhe",
        softmax_share.astype(jnp.bfloat16),
        grad_mixed,
        preferred_element_type=jnp.float32,
    )
    valid_residues = (jnp.arange(columns, dtype=jnp.int32) < family_residues).astype(jnp.float32)
    column_weight = float(total_rows * columns) * valid_residues / float(head_count * columns)
    grad_logits = softmax_share * (
        grad_probs - jnp.sum(softmax_share * grad_probs, axis=-1, keepdims=True)
    )
    grad_logits = grad_logits - column_weight[None, :, None] * softmax_share * (
        log_probs + entropy[..., None]
    )
    grad_logits = grad_logits.astype(jnp.bfloat16)
    logit_factor = 1.0 / (math.sqrt(model_width // head_count) * math.sqrt(total_rows))
    grad_queries = logit_factor * jnp.einsum(
        "vyp,opvl->oyvl", grad_logits, key_rows, preferred_element_type=jnp.float32
    )
    grad_keys = logit_factor * jnp.einsum(
        "hij,rihe->rjhe", grad_logits, queries, preferred_element_type=jnp.float32
    )
    grad_row_proj = jnp.concatenate(
        [
            grad_queries.reshape(row_count, columns, model_width),
            grad_keys.reshape(row_count, columns, model_width),
            grad_values.reshape(row_count, columns, model_width),
        ],
        axis=-1,
    ).astype(jnp.bfloat16)
    grad_normal_a = product_back(grad_row_proj, horizontal_coefficients)
    from_norm, gain_first, bias_first = jax.vjp(
        normed, source_rows.astype(jnp.float32), gain_rows[0], bias_rows[0]
    )[1](grad_normal_a)
    grad_source = (grad_row + from_norm).astype(jnp.bfloat16)
    operand_pairs = (
        (layernorm_first, grad_row_proj),
        (blended_lines, grad_branch_row),
        (layernorm_second, grad_col_proj),
        (mixed_values, grad_branch_col),
        (normal_c, grad_upward),
        (hidden, grad_branch_ffn),
    )
    norm_grads = (
        jnp.stack([gain_first, gain_middle, gain_last]),
        jnp.stack([bias_first, bias_middle, bias_last]),
    )
    return (grad_source, operand_pairs, norm_grads)


def on_device(
    embedded_families,
    order,
    token_quarter_factor,
    genuine_residue_tally,
    standardizer_scales,
    standardizer_offsets,
    row_qkv,
    row_out,
    col_qkv,
    col_out,
    ffn_up,
    ffn_down,
    upstream_sensitivity,
):
    head_count = HEAD_TALLY
    segment_place = lax.axis_index("pipe")
    gathered = (
        lax.all_gather(row_qkv, "seq", axis=1, tiled=True),
        lax.all_gather(row_out, "seq", axis=1, tiled=True),
        lax.all_gather(col_qkv, "seq", axis=1, tiled=True),
        lax.all_gather(col_out, "seq", axis=1, tiled=True),
        lax.all_gather(ffn_up, "seq", axis=1, tiled=True),
        lax.all_gather(ffn_down, "seq", axis=1, tiled=True),
        lax.all_gather(standardizer_scales.astype(jnp.bfloat16), "seq", axis=2, tiled=True).astype(
            standardizer_scales.dtype
        ),
        lax.all_gather(standardizer_offsets.astype(jnp.bfloat16), "seq", axis=2, tiled=True).astype(
            standardizer_offsets.dtype
        ),
    )
    projection_tables = tuple((gathered_piece[0] for gathered_piece in gathered))
    small_batch_number = embedded_families.shape[0]
    sequence = order[0]
    received = jnp.zeros(embedded_families.shape[1:], jnp.bfloat16)
    results = []
    focus_spread_levies = []
    kept_list = []
    for period in range(small_batch_number + 1):
        slot_here = jnp.clip(period - segment_place, 0, small_batch_number - 1)
        align_here = sequence[slot_here]
        source_rows = jnp.where(segment_place == 0, embedded_families[align_here], received)
        result, disorder_cost, kept_state = layer_forward(
            source_rows, genuine_residue_tally[align_here], projection_tables, head_count
        )
        results.append(result)
        focus_spread_levies.append(disorder_cost)
        kept_list.append(kept_state)
        if period < small_batch_number:
            received = shifted(result, "pipe", 1)
    activations = lax.dynamic_slice_in_dim(jnp.stack(results), segment_place, small_batch_number, 0)
    penalty_output = lax.dynamic_slice_in_dim(
        jnp.stack(focus_spread_levies), segment_place, small_batch_number, 0
    )
    grad_received = jnp.zeros(embedded_families.shape[1:], jnp.bfloat16)
    left_lists = [[] for index in range(6)]
    right_lists = [[] for index in range(6)]
    gain_total = None
    bias_total = None
    grad_sources = []
    for period in range(small_batch_number + 1):
        slot_raw = period - 1 + segment_place
        in_range = jnp.logical_and(slot_raw >= 0, slot_raw < small_batch_number)
        slot_here = jnp.clip(slot_raw, 0, small_batch_number - 1)
        align_here = sequence[slot_here]
        kept_state = choose(
            segment_place == 0,
            kept_list[max(period - 1, 0)],
            kept_list[min(period + 1, small_batch_number)],
        )
        outgrad = (
            upstream_sensitivity[slot_here].astype(jnp.float32)
            * token_quarter_factor[align_here].astype(jnp.float32)[..., None]
            * 0.25
        )
        incoming_grad = jnp.where(segment_place == 1, outgrad, grad_received.astype(jnp.float32))
        grad_source, operand_pairs, norm_grads = layer_backward(
            kept_state,
            genuine_residue_tally[align_here],
            incoming_grad,
            projection_tables,
            head_count,
        )
        for index in range(6):
            left_lists[index].append(operand_pairs[index][0])
            right_lists[index].append(
                jnp.where(
                    in_range, operand_pairs[index][1], jnp.zeros_like(operand_pairs[index][1])
                )
            )
        gain_term = jnp.where(in_range, norm_grads[0], jnp.zeros_like(norm_grads[0]))
        bias_term = jnp.where(in_range, norm_grads[1], jnp.zeros_like(norm_grads[1]))
        gain_total = gain_term if gain_total is None else gain_total + gain_term
        bias_total = bias_term if bias_total is None else bias_total + bias_term
        grad_sources.append(grad_source)
        if period < small_batch_number:
            grad_received = shifted(grad_source, "pipe", -1)
    block_entry_derivs = lax.dynamic_slice_in_dim(
        jnp.stack(grad_sources), 1 - segment_place, small_batch_number, 0
    )
    weight_totals = [
        weight_term(
            jnp.concatenate(left_lists[index], axis=0), jnp.concatenate(right_lists[index], axis=0)
        )
        for index in range(6)
    ]
    shared = (
        lax.psum_scatter(
            weight_totals[0].astype(jnp.bfloat16), "seq", scatter_dimension=0, tiled=True
        ).astype(jnp.float32),
        lax.psum_scatter(
            weight_totals[1].astype(jnp.bfloat16), "seq", scatter_dimension=0, tiled=True
        ).astype(jnp.float32),
        lax.psum_scatter(
            weight_totals[2].astype(jnp.bfloat16), "seq", scatter_dimension=0, tiled=True
        ).astype(jnp.float32),
        lax.psum_scatter(
            weight_totals[3].astype(jnp.bfloat16), "seq", scatter_dimension=0, tiled=True
        ).astype(jnp.float32),
        lax.psum_scatter(
            weight_totals[4].astype(jnp.bfloat16), "seq", scatter_dimension=0, tiled=True
        ).astype(jnp.float32),
        lax.psum_scatter(
            weight_totals[5].astype(jnp.bfloat16), "seq", scatter_dimension=0, tiled=True
        ).astype(jnp.float32),
        lax.psum_scatter(
            gain_total.astype(jnp.bfloat16), "seq", scatter_dimension=1, tiled=True
        ).astype(jnp.float32),
        lax.psum_scatter(
            bias_total.astype(jnp.bfloat16), "seq", scatter_dimension=1, tiled=True
        ).astype(jnp.float32),
    )
    (
        shared_row_qkv,
        shared_row_out,
        shared_col_qkv,
        shared_col_out,
        shared_up,
        shared_down,
        shared_gain,
        shared_bias,
    ) = shared
    summed = (
        lax.psum(shared_row_qkv.astype(jnp.bfloat16), "dp").astype(jnp.float32),
        lax.psum(shared_row_out.astype(jnp.bfloat16), "dp").astype(jnp.float32),
        lax.psum(shared_col_qkv.astype(jnp.bfloat16), "dp").astype(jnp.float32),
        lax.psum(shared_col_out.astype(jnp.bfloat16), "dp").astype(jnp.float32),
        lax.psum(shared_up.astype(jnp.bfloat16), "dp").astype(jnp.float32),
        lax.psum(shared_down.astype(jnp.bfloat16), "dp").astype(jnp.float32),
        lax.psum(shared_gain.astype(jnp.bfloat16), "dp").astype(jnp.float32),
        lax.psum(shared_bias.astype(jnp.bfloat16), "dp").astype(jnp.float32),
    )
    return (
        activations[None],
        block_entry_derivs[None],
        penalty_output[None],
        summed[0][None],
        summed[1][None],
        summed[2][None],
        summed[3][None],
        summed[4][None],
        summed[5][None],
        summed[6][None],
        summed[7][None],
    )


def place():
    pipe, seq, dp = (lax.axis_index("pipe"), lax.axis_index("seq"), lax.axis_index("dp"))
    core = lax.rem(dp, 2)
    pair = lax.div(dp, 2)
    return (pipe, seq, dp, core, pair)


def neighbours(pipe, seq, dp, core, pair):
    other_core = (pipe, seq, dp + 1 - 2 * core)
    other_pair = (pipe, seq, dp + 2 - 4 * pair)
    return (other_core, other_pair)


def greet(pipe, seq, dp, core, pair, across_pipe=False):
    barrier = pltpu.get_barrier_semaphore()
    other_core, other_pair = neighbours(pipe, seq, dp, core, pair)
    count = 0
    for step in range(LINE):
        for flip in range(2):
            if step == 0 and flip == 0:
                continue
            where = dp if flip == 0 else dp + 1 - 2 * core
            pl.semaphore_signal(
                barrier,
                inc=1,
                device_id=(pipe, lax.rem(seq + step, LINE), where),
                device_id_type=MESH,
            )
            count += 1
    more = [other_pair] + ([(1 - pipe, seq, dp)] if across_pipe else [])
    for device in more:
        pl.semaphore_signal(barrier, inc=1, device_id=device, device_id_type=MESH)

    def hear():
        pl.semaphore_wait(barrier, count + len(more))

    return hear


def remote(source, target, send, recv, device):
    return pltpu.make_async_remote_copy(
        src_ref=source,
        dst_ref=target,
        send_sem=send,
        recv_sem=recv,
        device_id=device,
        device_id_type=MESH,
    )


def swap_rows(source, target, send, recv, local, where):
    pipe, seq, dp, core, pair = where
    half, rest = (lax.div(seq, 2), lax.rem(seq, 2))

    def each(action):
        for index in range(2):
            line = 2 * core + index
            here = jnp.logical_and(line == seq, half == core)
            copy = remote(
                source.at[index],
                target.at[rest],
                send.at[index],
                recv.at[rest],
                (pipe, line, dp - core + half),
            )
            arriving = remote(
                source.at[index],
                target.at[index],
                send.at[index],
                recv.at[index],
                (pipe, line, dp - core + half),
            )
            inside = pltpu.make_async_copy(source.at[index], target.at[rest], local)
            action(here, copy, arriving, inside)

    def start(here, copy, arriving, inside):
        pl.when(here)(inside.start)
        pl.when(jnp.logical_not(here))(copy.start)

    def finish(here, copy, arriving, inside):
        pl.when(here)(inside.wait)
        pl.when(jnp.logical_not(here))(copy.wait_send)
        pl.when(jnp.logical_not(here))(arriving.wait_recv)

    return (lambda: each(start), lambda: each(finish))


def dot(left, right, left_axis, right_axis):
    return lax.dot_general(
        left,
        right,
        (((left_axis,), (right_axis,)), ((), ())),
        preferred_element_type=jnp.float32,
    )


def unit_rows(values):
    average = jnp.mean(values, axis=-1, keepdims=True)
    centered = values - average
    variance = jnp.mean(centered * centered, axis=-1, keepdims=True)
    root = lax.rsqrt(variance + norm_epsilon)
    return (centered * root, root)


def unit_rows_back(grad, values, gain_row):
    unit, root = unit_rows(values)
    scaled = grad * gain_row
    inner = jnp.mean(scaled * unit, axis=-1, keepdims=True)
    term = root * (scaled - jnp.mean(scaled, axis=-1, keepdims=True) - unit * inner)
    gain = jnp.sum(grad * unit, axis=0, keepdims=True)
    bias = jnp.sum(grad, axis=0, keepdims=True)
    return (term, gain, bias)


def layers_kernel(
    shard_row,
    shard_row_out,
    shard_col,
    shard_col_out,
    shard_up,
    shard_down,
    families,
    upstream,
    order,
    quarters,
    tally,
    norms,
    act_out,
    der_out,
    cost_out,
    vector_out,
    grads,
    out,
    tiles,
    source,
    normal_a,
    normal_b,
    normal_c,
    mixer,
    mixer_col,
    blended,
    mixed,
    after_row,
    after_col,
    log_share,
    col_share,
    hidden,
    slope,
    total_grad,
    grad_in,
    branch_ffn,
    branch_col,
    branch_row,
    grad_up,
    grad_mixer_col,
    grad_mixer,
    logit_send,
    logit_recv,
    keys_recv,
    keys_send,
    keys_back,
    probs_send,
    probs_recv,
    halves,
    segment,
    spread,
    stage,
    stage_down,
    act,
    der,
    cost,
    piece,
    piece_in,
    sensitivity,
    factor,
    factor_in,
    counts,
    counts_in,
    norms_in,
    rows,
    own_sem,
    line_send,
    line_recv,
    pair_send,
    pair_recv,
    core_send,
    core_recv,
    entry_sems,
    entry_local,
    norm_send,
    norm_recv,
    landing,
    from_pair,
    late_pair,
    der_back,
    vector,
    vec_core,
    vec_pair,
    vec_line,
    load_sem,
    near_send,
    near_recv,
    far_send,
    far_recv,
    hop_send,
    left_recv,
    right_recv,
    late_send,
    late_recv,
    share_send,
    share_recv,
    out_sem,
    vec_send,
    vec_recv,
    logit_sems,
    keys_sems,
    back_sems,
    probs_sems,
    pipe_sems,
    stage_sems,
    home_sems,
    home_local,
    cost_send,
    cost_recv,
):
    where = place()
    pipe, seq, dp, core, pair = where
    other_core = (pipe, seq, dp + 1 - 2 * core)
    other_pipe = (1 - pipe, seq, dp)
    columns, width = families.shape[2:]
    tokens = 2 * columns
    heads = HEAD_TALLY
    size = width // heads
    twin = 2 * size
    couples = heads // 2
    total_rows = LINE
    bf16, f32 = (jnp.bfloat16, jnp.float32)
    part_width = width // LINE
    shards = [
        ref.at[0]
        for ref in (shard_row, shard_row_out, shard_col, shard_col_out, shard_up, shard_down)
    ]
    first_tile = (0, 3, 4, 7, 8, 12)
    last_matrix = 5
    pieces = PIECES
    other_pair = (pipe, seq, dp + 2 - 4 * pair)
    right, left = ((pipe, seq + 1, dp), (pipe, seq - 1, dp))
    later = pipe == 1

    hear = greet(*where, across_pipe=True)
    straight = order[0, 0] == 0
    for index in range(2):
        piece[index] = jnp.where(straight, families[index, 0], families[1 - index, 0])
        chosen = jnp.where(straight, quarters[index], quarters[1 - index])
        factor[index] = jnp.broadcast_to(chosen.astype(f32) * 0.25, (columns, columns)).T
        number = jnp.where(straight, tally[index], tally[1 - index])
        counts[index] = jnp.broadcast_to(number, (8, 128)).astype(f32)
    hear()

    def entering(number, source_ref, target_ref):
        return swap_rows(
            source_ref,
            target_ref,
            entry_sems.at[2 * number],
            entry_sems.at[2 * number + 1],
            entry_local.at[number],
            where,
        )

    start_counts, finish_counts = entering(0, counts, counts_in)
    start_piece, finish_piece = entering(1, piece, piece_in)
    start_sensitivity, finish_sensitivity = entering(2, upstream.at[:, 0], sensitivity)
    start_factor, finish_factor = entering(3, factor, factor_in)
    pl.when(later)(start_piece)

    def norm_copy(step, source):
        return remote(
            norms,
            norms_in.at[source],
            norm_send.at[step - 1],
            norm_recv.at[source],
            (pipe, lax.rem(seq + step, LINE), dp),
        )


    def block_of(index, source, start, length):
        depth, wide = shards[index].shape
        if wide == width and depth == width:
            return tiles.at[first_tile[index] + source, pl.ds(start, length)]
        start = pl.multiple_of(source * depth + start, 16)
        return tiles.at[pl.ds(first_tile[index], wide // width), pl.ds(start, length)]

    def piece_of(index):
        matrix = min(index, last_matrix)
        share = shards[matrix].shape[0] // 4
        length = share // 2 if matrix == last_matrix else share
        return (matrix, share, (index - matrix) * length, length)

    def region(index, source, part):
        matrix, share, skip, length = piece_of(index)
        start = pl.multiple_of(part * share + skip, 16)
        return block_of(matrix, source, start, length)

    def cut(index, start, length):
        depth, wide = shards[index].shape
        if wide == width and depth == width:
            yield (
                shards[index].at[pl.ds(start, length)],
                tiles.at[first_tile[index] + seq, pl.ds(start, length)],
            )
            return
        target = pl.multiple_of(seq * depth + start, 16)
        for part in range(wide // width):
            yield (
                shards[index].at[pl.ds(start, length), pl.ds(part * width, width)],
                tiles.at[first_tile[index] + part, pl.ds(target, length)],
            )

    def start_own(index):
        for near, far in cut(index, 0, shards[index].shape[0]):
            pltpu.make_async_copy(near, far, own_sem.at[index]).start()

    def wait_own(index):
        block = block_of(index, seq, 0, shards[index].shape[0])
        pltpu.make_async_copy(block, block, own_sem.at[index]).wait()

    def start_line(index, direction):
        matrix, share, skip, length = piece_of(index)
        for near, far in cut(matrix, pl.multiple_of(dp * share + skip, 16), length):
            remote(
                near,
                far,
                line_send.at[direction, seq, index],
                line_recv.at[seq, index],
                right if direction == 0 else left,
            ).start()

    def along(source, index, direction):
        block = region(index, source, dp)
        return remote(
            block,
            block,
            line_send.at[direction, source, index],
            line_recv.at[source, index],
            right if direction == 0 else left,
        )

    across = dp + 2 - 4 * pair
    opposite = dp + 1 - 2 * core
    opposite_across = across + 1 - 2 * core

    def over_pair(source, index, part):
        block = region(index, source, part)
        return remote(
            block, block, pair_send.at[source, index], pair_recv.at[source, index], other_pair
        )

    def over_core(lane_of, source, index, part):
        block = region(index, source, part)
        return remote(
            block,
            block,
            core_send.at[lane_of, source, index],
            core_recv.at[lane_of, source, index],
            other_core,
        )

    has = (seq < LINE - 1, seq > 0)

    def sources(step):
        for direction in range(2):
            source = seq - step if direction == 0 else seq + step
            yield (direction, source, source >= 0 if direction == 0 else source < LINE)

    def begin(index):
        for direction in range(2):
            pl.when(has[direction])(functools.partial(start_line, index, direction))
        if index <= last_matrix:
            start_own(index)

    def arrive(index, step):
        for direction, source, present in sources(step):

            @pl.when(present)
            def _():
                along(source, index, direction).wait_recv()

                @pl.when(has[direction])
                def _():
                    along(source, index, direction).start()

                over_pair(source, index, dp).start()
                over_core(0, source, index, dp).start()

    def relay(index, step):
        for direction, source, present in sources(step):

            @pl.when(present)
            def _():
                over_pair(source, index, across).wait_recv()
                over_core(1, source, index, across).start()

    def settle(index):
        if index <= last_matrix:
            wait_own(index)
        for step in range(1, LINE):
            for direction, source, present in sources(step):

                @pl.when(present)
                def _():
                    over_core(0, source, index, opposite).wait_recv()
                    over_core(1, source, index, opposite_across).wait_recv()

    def drain(index):
        for direction in range(2):
            pl.when(has[direction])(along(seq, index, direction).wait_send)
        for step in range(1, LINE):
            for direction, source, present in sources(step):

                @pl.when(present)
                def _():
                    pl.when(has[direction])(along(source, index, direction).wait_send)
                    over_pair(source, index, dp).wait_send()
                    over_core(0, source, index, dp).wait_send()
                    over_core(1, source, index, across).wait_send()

    def wave(number):
        if number + 1 < pieces:
            begin(number + 1)
        for step in range(1, LINE):
            if 0 <= number + 1 - step < pieces:
                arrive(number + 1 - step, step)
        for step in range(1, LINE):
            if 0 <= number - step < pieces:
                relay(number - step, step)

    def gather(*waves):
        @pl.when(jnp.logical_not(later))
        def _():
            for number in waves:
                wave(number)

    def ready(index):
        pl.when(jnp.logical_not(later))(lambda: settle(index))

    begin(0)
    start_counts()
    for step in range(1, LINE):
        norm_copy(step, seq).start()
    norms_in[seq] = norms[...]
    hop = remote(piece_in, source, pipe_sems.at[4], pipe_sems.at[5], other_pipe)

    @pl.when(later)
    def _():
        finish_piece()
        hop.start()
        for number in range(pieces + LINE - 1):
            wave(number)
        start_sensitivity()
        start_factor()
        for index in range(pieces):
            settle(index)
            drain(index)
        hop.wait_send()

    lane = lax.broadcasted_iota(jnp.int32, (columns, 2 * twin), 1)
    early = (lax.rem(lane, twin) < size).astype(f32)
    halves[0] = early.astype(bf16)
    halves[1] = (1.0 - early).astype(bf16)
    feature = lax.broadcasted_iota(jnp.int32, (width, 128), 0)
    head = lax.broadcasted_iota(jnp.int32, (width, 128), 1)
    belongs = jnp.logical_and(feature >= head * size, feature < head * size + size)
    segment[...] = belongs.astype(f32).astype(bf16)
    head = lax.broadcasted_iota(jnp.int32, (128, width), 0)
    feature = lax.broadcasted_iota(jnp.int32, (128, width), 1)
    belongs = jnp.logical_and(feature >= head * size, feature < head * size + size)
    spread[...] = belongs.astype(f32).astype(bf16)
    for step in range(1, LINE):
        norm_copy(step, lax.rem(seq + LINE - step, LINE)).wait()
    for part in range(LINE):
        rows[:, part * part_width : (part + 1) * part_width] = norms_in[part, :, 0:part_width]
    finish_counts()

    def gain_of(index):
        return rows[index : index + 1, :]

    def bias_of(index):
        return rows[3 + index : 4 + index, :]

    def keep_vector(index, gain, bias):
        part = width // LINE
        for target in range(LINE):
            window = slice(target * part, (target + 1) * part)
            vector[target, index : index + 1, 0:part] = gain[:, window]
            vector[target, 3 + index : 4 + index, 0:part] = bias[:, window]

    vector[...] = jnp.zeros(vector.shape, f32)

    def both(ref, start):
        return jnp.concatenate(
            [ref[0:columns, start : start + twin], ref[columns:tokens, start : start + twin]],
            axis=1,
        )

    def stacked(ref, start):
        wide = both(ref, start)
        return jnp.concatenate([wide * halves[0], wide * halves[1]], axis=0)

    def unstack(wide):
        early_lane = lax.rem(lax.broadcasted_iota(jnp.int32, (columns, 2 * twin), 1), twin) < size
        return jnp.where(early_lane, wide[0:columns], wide[columns:])

    def put(ref, start, wide):
        ref[0:columns, start : start + twin] = wide[:, 0:twin].astype(bf16)
        ref[columns:tokens, start : start + twin] = wide[:, twin:].astype(bf16)

    def to_core(source_ref, target_ref, sems, index):
        return remote(
            source_ref, target_ref, sems.at[0, index], sems.at[1, index], other_core
        )

    start_act, finish_act = swap_rows(
        act, act_out, home_sems.at[0], home_sems.at[1], home_local.at[0], where
    )
    start_der, finish_der = swap_rows(
        der, der_out, home_sems.at[2], home_sems.at[3], home_local.at[1], where
    )
    sender = core == lax.div(seq, 2)
    spot = lax.rem(seq, 2)
    cost_own = pltpu.make_async_copy(cost, cost_out.at[spot], home_local.at[2])
    cost_copies = [
        remote(
            cost,
            cost_out.at[spot],
            cost_send.at[step - 1],
            cost_recv.at[spot],
            (pipe, lax.rem(seq + step, LINE), dp),
        )
        for step in range(1, LINE)
    ]

    der_over = remote(der, piece, pipe_sems.at[6], pipe_sems.at[7], other_pipe)
    der_home = remote(der_back, der_out, pipe_sems.at[8], pipe_sems.at[9], other_pipe)
    start_back, finish_back = swap_rows(
        piece, der_back, home_sems.at[4], home_sems.at[5], home_local.at[3], where
    )
    send_on = remote(act, source, pipe_sems.at[0], pipe_sems.at[1], other_pipe)
    send_back = remote(der, grad_in, pipe_sems.at[2], pipe_sems.at[3], other_pipe)

    @pl.when(later)
    def _():
        send_on.wait_recv()

    gather(0, 1)

    @pl.when(jnp.logical_not(later))
    def _():
        hop.wait_recv()

    chunks, cycle = (6, 3)
    whole_turns = chunks // cycle
    paired = chunks - whole_turns
    depth = width // chunks
    units = LINE * chunks
    mid = units // 2
    always = lambda target: target >= 0
    far = jnp.maximum(seq, LINE - 1 - seq)
    pair_lag, hop_lag, share_lag = (3, 4, 4)

    def unit_of(number):
        turn = lax.div(number, LINE)
        rank = number - turn * LINE
        halfway = lax.div(rank, 2)
        target = jnp.where(lax.rem(rank, 2) == 0, LINE - 1 - halfway, halfway)
        return (target, chunks - 1 - turn)

    def rank_of(chunk):
        turn = chunks - 1 - chunk
        early_turns = lax.div(turn, cycle)
        return (early_turns, turn - early_turns - 1)

    def is_single(chunk):
        turn = chunks - 1 - chunk
        return lax.rem(turn, cycle) != 0

    def window_of(chunk):
        return pl.ds(pl.multiple_of(chunk * depth, depth), depth)

    def spot_of(number, side, shift, count=1):
        block = jnp.where(
            number < mid, 2 * units + 2 * number + side, 2 * (number - mid) + side
        )
        block = block + shift
        tile = lax.div(block, chunks)
        row = pl.multiple_of((block - tile * chunks) * depth, depth)
        return (tile, pl.ds(row, count * depth))

    def mine_at(number, side, count=1):
        return tiles.at[spot_of(number, side, 0, count)]

    def near_at(number, side):
        return tiles.at[spot_of(number, side, units)]

    def add_into(number, side, ref, start=None):
        spot = spot_of(number, side, 0)
        value = ref[...] if start is None else ref[pl.ds(start, depth), :]
        tiles[spot] = (tiles[spot].astype(f32) + value.astype(f32)).astype(bf16)

    def load(number, side):
        target, chunk = unit_of(number)
        return pltpu.make_async_copy(
            grads.at[target, 2 * side + core, window_of(chunk)],
            mine_at(number, side),
            load_sem.at[number, side],
        )

    def to_near(number, side):
        target, chunk = unit_of(number)
        return remote(
            grads.at[target, 2 * side + 1 - core, window_of(chunk)],
            near_at(number, side),
            near_send.at[number, side],
            near_recv.at[number, side],
            other_core,
        )

    def issue(number, carry):
        for side in range(2):
            to_near(number, side).start()
            load(number, side).start()
        return carry

    def issue_all(start, stop):
        lax.fori_loop(start, stop, issue, 0)

    def pair_start(number):
        turn = lax.div(number, LINE)
        _, rank = rank_of(chunks - 1 - turn)
        return pl.multiple_of((LINE * rank + number - LINE * turn) * depth, depth)

    def to_pair(number):
        return remote(
            mine_at(number, 1 - pair),
            from_pair.at[pl.ds(pair_start(number), depth)],
            far_send.at[number],
            far_recv.at[number],
            other_pair,
        )

    def arrive_near(number, side):
        load(number, side).wait()
        to_near(number, side).wait_recv()
        add_into(number, side, near_at(number, side))

    def land_slot(number, chunk, single, second):
        whole_rank, single_rank = rank_of(chunk)
        turn = chunks - 1 - chunk
        rank = number - LINE * turn
        base = 2 * LINE * whole_turns
        extra = base + LINE * paired
        if single:
            slot = base + LINE * single_rank + rank
            slot = jnp.where(second, extra + 2 * whole_turns + single_rank, slot)
        else:
            slot = 2 * (LINE * whole_rank + rank)
            slot = jnp.where(second, extra + 2 * whole_rank, slot)
        return pl.multiple_of(slot * depth, depth)

    def hop_copy(number, chunk, single, direction):
        target, _ = unit_of(number)
        second = jnp.logical_and(direction == 1, target == seq - 1)
        count = 1 if single else 2
        sems = left_recv if direction == 0 else right_recv
        return remote(
            mine_at(number, pair if single else 0, count),
            landing.at[pl.ds(land_slot(number, chunk, single, second), count * depth)],
            hop_send.at[number],
            sems.at[number],
            right if direction == 0 else left,
        )

    def take(number, chunk, single, direction):
        target, _ = unit_of(number)
        second = jnp.logical_and(direction == 1, target == seq)
        count = 1 if single else 2
        start = land_slot(number, chunk, single, second)
        sems = left_recv if direction == 0 else right_recv
        remote(
            mine_at(number, pair if single else 0, count),
            landing.at[pl.ds(start, count * depth)],
            hop_send.at[number],
            sems.at[number],
            right if direction == 0 else left,
        ).wait_recv()
        if single:
            add_into(number, pair, landing, start)
        else:
            for side in range(2):
                add_into(number, side, landing, start + side * depth)

    def late_start(chunk):
        return pl.multiple_of(2 * rank_of(chunk)[0] * depth, depth)

    def late_copy(number, chunk, single):
        if single:
            return remote(
                mine_at(number, pair),
                out.at[dp, window_of(chunk)],
                late_send.at[chunk],
                late_recv.at[chunk],
                other_pair,
            )
        return remote(
            mine_at(number, 0, 2),
            late_pair.at[pl.ds(late_start(chunk), 2 * depth)],
            late_send.at[chunk],
            late_recv.at[chunk],
            other_pair,
        )

    def share_copy(number, chunk, side, relayed):
        spot_out = out.at[2 * side + core, window_of(chunk)]
        return remote(
            spot_out if relayed else mine_at(number, side),
            spot_out,
            share_send.at[side, chunk],
            share_recv.at[side, chunk],
            other_core,
        )

    def out_copy(number, chunk, side):
        return pltpu.make_async_copy(
            mine_at(number, side), out.at[2 * side + core, window_of(chunk)], out_sem.at[side, chunk]
        )

    def at(number, condition, body):
        clipped = jnp.clip(number, 0, units - 1)
        target, chunk = unit_of(clipped)
        valid = jnp.logical_and(number >= 0, number < units)
        valid = jnp.logical_and(valid, condition(target))

        @pl.when(jnp.logical_and(valid, is_single(chunk)))
        def _():
            body(clipped, chunk, True)

        @pl.when(jnp.logical_and(valid, jnp.logical_not(is_single(chunk))))
        def _():
            body(clipped, chunk, False)

    def first_stage(number, chunk, single):
        if single:
            arrive_near(number, 1 - pair)
            to_pair(number).start()
            arrive_near(number, pair)
        else:
            for side in range(2):
                arrive_near(number, side)

    def first_body(number, carry):
        at(number, always, first_stage)
        return carry

    def second_stage(number, chunk, single):
        if single:
            to_pair(number).wait_recv()
            add_into(number, pair, from_pair, pair_start(number))

    def hop_stage(direction):
        def body(number, chunk, single):
            @pl.when(has[1 - direction])
            def _():
                take(number, chunk, single, direction)

            hop_copy(number, chunk, single, direction).start()

        return body

    def last_stage(number, chunk, single):
        for direction in range(2):

            @pl.when(has[1 - direction])
            def _():
                take(number, chunk, single, direction)

        late_copy(number, chunk, single).start()
        if single:
            out_copy(number, chunk, pair).start()
            share_copy(number, chunk, pair, False).start()

    def share_stage(number, chunk, single):
        if single:
            remote(
                mine_at(number, pair),
                out.at[dp + 2 - 4 * pair, window_of(chunk)],
                late_send.at[chunk],
                late_recv.at[chunk],
                other_pair,
            ).wait_recv()
            share_copy(number, chunk, 1 - pair, True).start()
        else:
            late_copy(number, chunk, False).wait()
            for side in range(2):
                add_into(number, side, late_pair, late_start(chunk) + side * depth)
                out_copy(number, chunk, side).start()
                share_copy(number, chunk, side, False).start()

    def hop_stages(base):
        at(base, always, second_stage)
        at(base - hop_lag * seq, lambda target: target > seq, hop_stage(0))
        at(base - hop_lag * (LINE - 1 - seq), lambda target: target < seq, hop_stage(1))
        at(base - hop_lag * far, lambda target: target == seq, last_stage)
        at(base - hop_lag * far - share_lag, lambda target: target == seq, share_stage)

    def hops(start, stop):
        def body(number, carry):
            hop_stages(number)
            return carry

        lax.fori_loop(start, stop, body, 0)

    def finish_unit(number, carry):
        for side in range(2):
            to_near(number, side).wait_send()

        def sends(number, chunk, single):
            if single:
                to_pair(number).wait_send()

        at(number, always, sends)
        at(
            number,
            lambda target: target > seq,
            lambda number, chunk, single: hop_copy(number, chunk, single, 0).wait_send(),
        )
        at(
            number,
            lambda target: target < seq,
            lambda number, chunk, single: hop_copy(number, chunk, single, 1).wait_send(),
        )

        def shared(number, chunk, single):
            if single:
                late_copy(number, chunk, True).wait_send()
                out_copy(number, chunk, pair).wait()
                share_copy(number, chunk, pair, False).wait_send()
                share_copy(number, chunk, 1 - pair, True).wait_send()
            else:
                for side in range(2):
                    out_copy(number, chunk, side).wait()
                    share_copy(number, chunk, side, False).wait_send()
            for side in range(2):
                spot_out = out.at[2 * side + 1 - core, window_of(chunk)]
                remote(
                    spot_out,
                    spot_out,
                    share_send.at[side, chunk],
                    share_recv.at[side, chunk],
                    other_core,
                ).wait_recv()

        at(number, lambda target: target == seq, shared)
        return carry

    vec_first = remote(vector, vec_core, vec_send.at[0], vec_recv.at[0], other_core)
    vec_second = remote(vec_core, vec_pair, vec_send.at[1], vec_recv.at[1], other_pair)

    def move_copy(step, source):
        goal = lax.rem(seq + step, LINE)
        return remote(
            vec_pair.at[goal],
            vec_line.at[source],
            vec_send.at[1 + step],
            vec_recv.at[2 + source],
            (pipe, goal, dp),
        )

    def vector_to_pair():
        vec_first.wait()
        vec_core[...] = vector[...] + vec_core[...]
        vec_second.start()

    def vector_to_line():
        vec_second.wait()
        vec_pair[...] = vec_core[...] + vec_pair[...]
        for step in range(1, LINE):
            move_copy(step, seq).start()
        vec_line[seq] = vec_pair[seq]

    def vector_end():
        for step in range(1, LINE):
            move_copy(step, lax.rem(seq + LINE - step, LINE)).wait()
        total_vector = vec_line[0]
        for source_of in range(1, LINE):
            total_vector = total_vector + vec_line[source_of]
        vector_out[...] = total_vector

    packed_share = width // (4 * LINE)

    def outer_terms():
        for part in range(4):
            slot = part % 2
            window = slice(part * width, (part + 1) * width)
            if part >= 2:
                down_copy(part - 2).wait()
            term = dot(hidden[:, window], branch_ffn[...], 0, 0).astype(bf16)
            stage_down[slot] = term.reshape(4, width // 4, width)
            down_copy(part).start()
        packed_terms(((normal_c, grad_up, 8 * packed_share),))
        for part in range(2, 4):
            down_copy(part).wait()

    def down_copy(part):
        return pltpu.make_async_copy(
            stage_down.at[part % 2],
            grads.at[part, :, pl.ds(12 * packed_share, width // 4)],
            stage_sems.at[2 + part % 2, 0],
        )

    def inner_terms():
        packed_terms(
            (
                (normal_b, grad_mixer_col, 4 * packed_share),
                (mixed, branch_col, 7 * packed_share),
                (normal_a, grad_mixer, 0),
                (blended, branch_row, 3 * packed_share),
            )
        )

    def packed_terms(pairs):
        waiting = [None, None]
        number = 0
        for first, second, base in pairs:
            for part in range(second.shape[1] // width):
                slot = number % 2
                if waiting[slot] is not None:
                    for copy in waiting[slot]:
                        copy.wait()
                window = slice(part * width, (part + 1) * width)
                term = dot(first[...], second[:, window], 0, 0).astype(bf16)
                stage[slot] = term.reshape(LINE, 4, packed_share, width)
                waiting[slot] = [
                    pltpu.make_async_copy(
                        stage.at[slot, target],
                        grads.at[target, :, pl.ds(base + part * packed_share, packed_share)],
                        stage_sems.at[slot, target],
                    )
                    for target in range(LINE)
                ]
                for copy in waiting[slot]:
                    copy.start()
                number += 1
        for copies in waiting:
            for copy in copies or ():
                copy.wait()

    unit, _ = unit_rows(source[...].reshape(tokens, width).astype(f32))
    normal_a[...] = (unit * gain_of(0) + bias_of(0)).astype(bf16)
    gather(2, 3)
    ready(0)
    for part in range(3):
        window = slice(part * width, (part + 1) * width)
        mixer[:, window] = dot(normal_a[...], tiles[part], 1, 0).astype(bf16)
    logit_factor = 1.0 / (math.sqrt(size) * math.sqrt(total_rows))
    logit_copies = []
    for couple in range(couples):
        partial_value = logit_factor * dot(
            both(mixer, couple * twin), stacked(mixer, width + couple * twin), 1, 1
        )
        logit_send[couple] = partial_value.astype(bf16)
        copy = to_core(logit_send.at[couple], logit_recv.at[couple], logit_sems, couple)
        copy.start()
        logit_copies.append(copy)
    gather(4)
    valid = (
        lax.broadcasted_iota(jnp.int32, (columns, 1), 0).astype(f32) < counts_in[0, 0:1, 0:1]
    ).astype(f32)
    disorder = jnp.zeros((columns, 1), f32)
    for couple in range(couples):
        logit_copies[couple].wait_recv()
        wide = logit_send[couple].astype(f32) + logit_recv[couple].astype(f32)
        shares = []
        for half in range(2):
            logits = wide[:, half * columns : (half + 1) * columns]
            shifted_logits = logits - jnp.max(logits, axis=-1, keepdims=True)
            powers = jnp.exp(shifted_logits)
            total = jnp.sum(powers, axis=-1, keepdims=True)
            logs = shifted_logits - jnp.log(total)
            share = powers / total
            log_share[couple, :, half * columns : (half + 1) * columns] = logs
            disorder = disorder - jnp.sum(share * logs, axis=-1, keepdims=True) * valid
            shares.append(share.astype(bf16))
        put(
            blended,
            couple * twin,
            dot(
                jnp.concatenate(shares, axis=1), stacked(mixer, 2 * width + couple * twin), 1, 0
            ),
        )
    cost[...] = jnp.broadcast_to(
        jnp.sum(disorder, axis=0, keepdims=True) / float(heads * columns), cost.shape
    )
    ready(1)
    after_row[...] = source[...].reshape(tokens, width).astype(f32) + dot(blended[...], tiles[3], 1, 0)
    unit, _ = unit_rows(after_row[...])
    normal_b[...] = (unit * gain_of(1) + bias_of(1)).astype(bf16)
    gather(5)
    ready(2)
    keys_copies = []
    for part in (1, 2, 0):
        window = slice(part * width, (part + 1) * width)
        mixer_col[:, window] = dot(normal_b[...], tiles[4 + part], 1, 0).astype(bf16)
        if part > 0:
            copy = to_core(
                mixer_col.at[:, window], keys_recv.at[part - 1], keys_sems, part - 1
            )
            copy.start()
            keys_copies.append(copy)

    def line_of(part, place_of):
        if place_of < 2:
            rows_of = slice(place_of * columns, (place_of + 1) * columns)
            return mixer_col[rows_of, (1 + part) * width : (2 + part) * width]
        rows_of = slice((place_of - 2) * columns, (place_of - 1) * columns)
        return keys_recv[part, rows_of, :]

    def sums_by_head(wide_ref, start, line):
        products = [
            wide_ref[index * columns : (index + 1) * columns, start : start + width] * line
            for index in range(2)
        ]
        return dot(jnp.concatenate(products, axis=0), segment[...], 1, 0)

    def spread_heads(narrow):
        return dot(narrow, spread[...], 1, 0)

    gather(6)
    scores = []
    for place_of in range(4):
        if place_of == 2:
            keys_copies[0].wait_recv()
        scores.append(sums_by_head(mixer_col, 0, line_of(0, place_of)) / math.sqrt(size))
    highest = functools.reduce(jnp.maximum, scores)
    powers = [jnp.exp(score - highest) for score in scores]
    total = functools.reduce(jnp.add, powers)
    keys_copies[1].wait_recv()
    gathered_mix = None
    for place_of in range(4):
        share = powers[place_of] / total
        col_share[place_of] = share
        wide = spread_heads(share.astype(bf16))
        line = line_of(1, place_of).astype(f32)
        term = jnp.concatenate([wide[0:columns] * line, wide[columns:] * line], axis=0)
        gathered_mix = term if gathered_mix is None else gathered_mix + term
    mixed[...] = gathered_mix.astype(bf16)
    ready(3)
    after_col[...] = after_row[...] + dot(mixed[...], tiles[7], 1, 0)
    unit, _ = unit_rows(after_col[...])
    normal_c[...] = (unit * gain_of(2) + bias_of(2)).astype(bf16)
    gather(7)
    ready(4)
    parts = hidden.shape[1] // width
    result = after_col[...]
    for part in range(parts):
        if part == 2:
            gather(8)
        window = slice(part * width, (part + 1) * width)
        upward = dot(normal_c[...], tiles[8 + part], 1, 0)
        inner = 0.5 + 0.5 * lax.erf(upward * math.sqrt(0.5))
        density = jnp.exp(-0.5 * upward * upward) * (1.0 / math.sqrt(2.0 * math.pi))
        hidden[:, window] = (upward * inner).astype(bf16)
        slope[:, window] = (inner + upward * density).astype(bf16)
    gather(9)
    ready(5)
    ready(6)
    for part in range(parts):
        window = slice(part * width, (part + 1) * width)
        result = result + dot(hidden[:, window], tiles[12 + part], 1, 0)
    act[...] = result.astype(bf16).reshape(2, columns, width)

    @pl.when(pipe == 0)
    def _():
        send_on.start()

    start_act()

    @pl.when(sender)
    def _():
        cost_own.start()
        for copy in cost_copies:
            copy.start()

    @pl.when(pipe == 1)
    def _():
        finish_sensitivity()
        finish_factor()
        for index in range(2):
            total_grad[index * columns : (index + 1) * columns, :] = (
                sensitivity[index].astype(f32) * factor_in[index, :, 0:1]
            )

    @pl.when(pipe == 0)
    def _():
        for index in range(pieces):
            drain(index)
        send_back.wait_recv()
        total_grad[...] = grad_in[...].reshape(tokens, width).astype(f32)

    branch_ffn[...] = total_grad[...].astype(bf16)
    grad_normal = None
    for part in range(parts):
        window = slice(part * width, (part + 1) * width)
        grad_hidden = dot(branch_ffn[...], tiles[12 + part], 1, 1)
        grad_up[:, window] = (grad_hidden * slope[:, window].astype(f32)).astype(bf16)
        term = dot(grad_up[:, window], tiles[8 + part], 1, 1)
        grad_normal = term if grad_normal is None else grad_normal + term
    pl.when(jnp.logical_not(later))(outer_terms)
    term, gain, bias = unit_rows_back(grad_normal, after_col[...], gain_of(2))
    keep_vector(2, gain, bias)
    total_grad[...] = total_grad[...] + term
    branch_col[...] = total_grad[...].astype(bf16)
    grad_mixed = dot(branch_col[...], tiles[7], 1, 1).astype(bf16)
    grad_probs = []
    for place_of in range(4):
        line = line_of(1, place_of)
        products = [grad_mixed[0:columns] * line, grad_mixed[columns:] * line]
        grad_probs.append(dot(jnp.concatenate(products, axis=0), segment[...], 1, 0))
    inner = functools.reduce(
        jnp.add, [col_share[place_of] * grad_probs[place_of] for place_of in range(4)]
    )
    root_size = math.sqrt(size)
    grad_query = None
    local_terms = []
    back_copies = []
    grad_lines = grad_mixed.astype(f32)
    query_lines = mixer_col[:, 0:width].astype(f32)
    for place_of in (2, 3, 0, 1):
        share = col_share[place_of]
        narrow = (share * (grad_probs[place_of] - inner)).astype(bf16)
        wide = spread_heads(narrow)
        line = line_of(0, place_of).astype(f32)
        term = jnp.concatenate([wide[0:columns] * line, wide[columns:] * line], axis=0)
        grad_query = term if grad_query is None else grad_query + term
        key_term = wide[0:columns] * query_lines[0:columns] + wide[columns:] * query_lines[columns:]
        key_term = key_term / root_size
        wide = spread_heads(share.astype(bf16))
        value_term = wide[0:columns] * grad_lines[0:columns] + wide[columns:] * grad_lines[columns:]
        if place_of >= 2:
            index = place_of - 2
            rows_of = slice(index * columns, (index + 1) * columns)
            keys_send[rows_of, 0:width] = key_term.astype(bf16)
            keys_send[rows_of, width:] = value_term.astype(bf16)
            copy = to_core(keys_send.at[rows_of, :], keys_back.at[rows_of, :], back_sems, index)
            copy.start()
            back_copies.append(copy)
        else:
            local_terms.append((key_term, value_term))
    grad_mixer_col[:, 0:width] = (grad_query / root_size).astype(bf16)
    for place_of in range(2):
        back_copies[place_of].wait()
        rows_of = slice(place_of * columns, (place_of + 1) * columns)
        for part in range(2):
            window = slice(part * width, (part + 1) * width)
            grad_mixer_col[rows_of, (1 + part) * width : (2 + part) * width] = (
                local_terms[place_of][part] + keys_back[rows_of, window].astype(f32)
            ).astype(bf16)
    pl.when(jnp.logical_not(later))(lambda: issue_all(0, mid))
    grad_normal = None
    for part in range(3):
        window = slice(part * width, (part + 1) * width)
        term = dot(grad_mixer_col[:, window], tiles[4 + part], 1, 1)
        grad_normal = term if grad_normal is None else grad_normal + term
    term, gain, bias = unit_rows_back(grad_normal, after_row[...], gain_of(1))
    keep_vector(1, gain, bias)
    total_grad[...] = total_grad[...] + term
    branch_row[...] = total_grad[...].astype(bf16)
    keys_send[:, 0:width] = dot(branch_row[...], tiles[3], 1, 1).astype(bf16)
    probs_copies = []
    for couple in range(couples):
        partial_value = dot(
            both(keys_send, couple * twin), stacked(mixer, 2 * width + couple * twin), 1, 1
        )
        probs_send[couple] = partial_value.astype(bf16)
        copy = to_core(probs_send.at[couple], probs_recv.at[couple], probs_sems, couple)
        copy.start()
        probs_copies.append(copy)

    @pl.when(jnp.logical_not(later))
    def _():
        lax.fori_loop(0, mid, first_body, 0)
        hops(0, EARLY)

    column_weight = (float(total_rows * columns) / float(heads * columns)) * valid
    for couple in range(couples):
        start = couple * twin
        logs = log_share[couple]
        share = jnp.exp(logs)
        grad_wide = both(keys_send, start)
        put(
            grad_mixer,
            2 * width + start,
            unstack(dot(share.astype(bf16), grad_wide, 0, 0)),
        )
        probs_copies[couple].wait_recv()
        wide = probs_send[couple].astype(f32) + probs_recv[couple].astype(f32)
        pieces = []
        for half in range(2):
            window = slice(half * columns, (half + 1) * columns)
            part_share, part_logs, part_grad = (share[:, window], logs[:, window], wide[:, window])
            entropy = -jnp.sum(part_share * part_logs, axis=-1, keepdims=True)
            inner = jnp.sum(part_share * part_grad, axis=-1, keepdims=True)
            piece = part_share * (part_grad - inner)
            piece = piece - column_weight * part_share * (part_logs + entropy)
            pieces.append(piece.astype(bf16))
        grad_logits = jnp.concatenate(pieces, axis=1)
        put(
            grad_mixer,
            start,
            logit_factor * dot(grad_logits, stacked(mixer, width + start), 1, 0),
        )
        put(
            grad_mixer,
            width + start,
            logit_factor * unstack(dot(grad_logits, both(mixer, start), 0, 0)),
        )
    grad_normal = None
    for part in range(3):
        window = slice(part * width, (part + 1) * width)
        term = dot(grad_mixer[:, window], tiles[part], 1, 1)
        grad_normal = term if grad_normal is None else grad_normal + term
    term, gain, bias = unit_rows_back(grad_normal, source[...].reshape(tokens, width).astype(f32), gain_of(0))
    keep_vector(0, gain, bias)
    der[...] = (total_grad[...] + term).astype(bf16).reshape(2, columns, width)

    @pl.when(pipe == 1)
    def _():
        send_back.start()

    vec_first.start()

    @pl.when(later)
    def _():
        start_der()

    @pl.when(jnp.logical_not(later))
    def _():
        der_over.start()

    @pl.when(later)
    def _():
        outer_terms()
        issue_all(0, mid)
        lax.fori_loop(0, mid, first_body, 0)
        hops(0, EARLY)

    hops(EARLY, EARLY + MORE)
    inner_terms()
    issue_all(mid, units)
    vector_to_pair()

    def mix(number, carry):
        for index in range(AT_ONCE):
            at(mid + AT_ONCE * number + index, always, first_stage)
        hop_stages(EARLY + MORE + number)
        return carry

    lax.fori_loop(0, mid // AT_ONCE, mix, 0)

    @pl.when(later)
    def _():
        der_over.wait_recv()
        start_back()

    hops(EARLY + MORE + mid // AT_ONCE, units)
    vector_to_line()
    hops(units, units + hop_lag * (LINE - 1) + share_lag)
    vector_end()
    lax.fori_loop(0, units, finish_unit, 0)
    for copy in logit_copies + keys_copies + probs_copies:
        copy.wait_send()

    @pl.when(pipe == 0)
    def _():
        send_on.wait_send()

    @pl.when(pipe == 1)
    def _():
        send_back.wait_send()

    finish_act()

    @pl.when(later)
    def _():
        finish_back()
        der_home.start()
        finish_der()
        der_home.wait_send()

    @pl.when(jnp.logical_not(later))
    def _():
        der_over.wait_send()
        der_home.wait_recv()

    @pl.when(sender)
    def _():
        cost_own.wait()
        for copy in cost_copies:
            copy.wait_send()

    for index in range(2):

        @pl.when(2 * core + index != seq)
        def _():
            remote(
                cost, cost_out.at[index], cost_send.at[0], cost_recv.at[index], other_core
            ).wait_recv()


def run_layers(shards, families, upstream, order, quarters, tally, norms):
    columns, width = families.shape[2:]
    tokens = 2 * columns
    couples = HEAD_TALLY // 2
    wide = shards[4].shape[2]
    entry = jax.ShapeDtypeStruct((2, columns, width), families.dtype)
    sizes = sum(shard.size for shard in shards) * LINE // (width * width)
    depth = width // 6
    block = lambda count: pltpu.VMEM((count * depth, width), bf16)
    anywhere = pl.BlockSpec(memory_space=pl.ANY)
    inside = pl.BlockSpec(memory_space=pltpu.VMEM)
    scalars = pl.BlockSpec(memory_space=pltpu.SMEM)
    dma = pltpu.SemaphoreType.DMA
    bf16, f32 = (jnp.bfloat16, jnp.float32)
    rows_of = lambda columns_of, kind=bf16: pltpu.VMEM((tokens, columns_of), kind)
    scores = pltpu.VMEM((couples, columns, 2 * columns), bf16)
    return pl.pallas_call(
        layers_kernel,
        out_shape=[
            jax.ShapeDtypeStruct(entry.shape, bf16),
            jax.ShapeDtypeStruct(entry.shape, bf16),
            jax.ShapeDtypeStruct((2, 8, 128), f32),
            jax.ShapeDtypeStruct((8, 256), f32),
            jax.ShapeDtypeStruct((LINE, 4, width, width), bf16),
            jax.ShapeDtypeStruct((4, width, width), bf16),
        ],
        in_specs=[anywhere] * 6 + [inside, inside, scalars, inside, scalars, inside],
        out_specs=[anywhere, anywhere, inside, inside, anywhere, anywhere],
        scratch_shapes=[
            pltpu.VMEM((sizes, width, width), bf16),
            pltpu.VMEM(entry.shape, bf16),
            rows_of(width),
            rows_of(width),
            rows_of(width),
            rows_of(3 * width),
            rows_of(3 * width),
            rows_of(width),
            rows_of(width),
            rows_of(width, f32),
            rows_of(width, f32),
            pltpu.VMEM((couples, columns, 2 * columns), f32),
            pltpu.VMEM((4, tokens, 128), f32),
            rows_of(wide),
            rows_of(wide),
            rows_of(width, f32),
            pltpu.VMEM(entry.shape, bf16),
            rows_of(width),
            rows_of(width),
            rows_of(width),
            rows_of(wide),
            rows_of(3 * width),
            rows_of(3 * width),
            scores,
            scores,
            pltpu.VMEM((2, tokens, width), bf16),
            rows_of(2 * width),
            rows_of(2 * width),
            scores,
            scores,
            pltpu.VMEM((2, columns, 2 * columns), bf16),
            pltpu.VMEM((width, 128), bf16),
            pltpu.VMEM((128, width), bf16),
            pltpu.VMEM((2, LINE, 4, width // (4 * LINE), width), bf16),
            pltpu.VMEM((2, 4, width // 4, width), bf16),
            pltpu.VMEM(entry.shape, bf16),
            pltpu.VMEM(entry.shape, bf16),
            pltpu.VMEM((8, 128), f32),
            pltpu.VMEM(entry.shape, bf16),
            pltpu.VMEM(entry.shape, bf16),
            pltpu.VMEM(entry.shape, bf16),
            pltpu.VMEM((2, columns, columns), f32),
            pltpu.VMEM((2, columns, columns), f32),
            pltpu.VMEM((2, 8, 128), f32),
            pltpu.VMEM((2, 8, 128), f32),
            pltpu.VMEM((LINE, 8, 256), f32),
            pltpu.VMEM((8, width), f32),
            dma((6,)),
            dma((2, LINE, PIECES)),
            dma((LINE, PIECES)),
            dma((LINE, PIECES)),
            dma((LINE, PIECES)),
            dma((2, LINE, PIECES)),
            dma((2, LINE, PIECES)),
            dma((8, 2)),
            dma((4,)),
            dma((LINE - 1,)),
            dma((LINE,)),
            block(40),
            block(16),
            block(4),
            pltpu.VMEM(entry.shape, bf16),
            pltpu.VMEM((LINE, 8, 256), f32),
            pltpu.VMEM((LINE, 8, 256), f32),
            pltpu.VMEM((LINE, 8, 256), f32),
            pltpu.VMEM((LINE, 8, 256), f32),
            dma((24, 2)),
            dma((24, 2)),
            dma((24, 2)),
            dma((24,)),
            dma((24,)),
            dma((24,)),
            dma((24,)),
            dma((24,)),
            dma((6,)),
            dma((6,)),
            dma((2, 6)),
            dma((2, 6)),
            dma((2, 6)),
            dma((2 + LINE,)),
            dma((2 + LINE,)),
            dma((2, couples)),
            dma((2, 2)),
            dma((2, 2)),
            dma((2, couples)),
            dma((10,)),
            dma((4, LINE)),
            dma((6, 2)),
            dma((4,)),
            dma((LINE - 1,)),
            dma((2,)),
        ],
        compiler_params=pltpu.CompilerParams(
            collective_id=2, has_side_effects=True, vmem_limit_bytes=63 * 2**20
        ),
        name="two_layers",
    )(*shards, families, upstream, order, quarters, tally, norms)


def unpack_kernel(blocks, act, der, costs, *refs):
    results, act_out, der_out, cost_out = (refs[:6], *refs[6:])
    width = blocks.shape[2]
    base = 0
    for result in results:
        depth, wide = result.shape[1:]
        for part in range(wide // width):
            result[0, :, part * width : (part + 1) * width] = blocks[
                0, base : base + depth, :
            ].astype(jnp.float32)
            base += depth
    act_out[0, :, 0] = act[...]
    der_out[0, :, 0] = der[...]
    cost_out[...] = jnp.concatenate([costs[0, 0:1, 0:1], costs[1, 0:1, 0:1]], axis=1)


def unpack_all(blocks, act, der, costs, shapes):
    columns, width = act.shape[1:]
    large = jax.ShapeDtypeStruct((1, 2, 1, columns, width), act.dtype)
    part = pl.BlockSpec((2, columns // 4, width), lambda step: (0, step, 0))
    wide = pl.BlockSpec((1, 2, 1, columns // 4, width), lambda step: (0, 0, 0, step, 0))
    return pl.pallas_call(
        unpack_kernel,
        grid=(4,),
        out_shape=[jax.ShapeDtypeStruct((1,) + shape, jnp.float32) for shape in shapes]
        + [large, large, jax.ShapeDtypeStruct((1, 2), jnp.float32)],
        in_specs=[
            pl.BlockSpec((1,) + blocks.shape[1:], lambda step: (step, 0, 0)),
            part,
            part,
            pl.BlockSpec(costs.shape, lambda step: (0, 0, 0)),
        ],
        out_specs=[
            pl.BlockSpec((1, shape[0] // 4, shape[1]), lambda step: (0, step, 0))
            for shape in shapes
        ]
        + [wide, wide, pl.BlockSpec((1, 2), lambda step: (0, 0))],
        compiler_params=pltpu.CompilerParams(vmem_limit_bytes=60 * 2**20),
        cost_estimate=pl.CostEstimate(
            flops=blocks.size, bytes_accessed=6 * blocks.size, transcendentals=0
        ),
        name="unpack_grads",
    )(blocks, act, der, costs)


def on_device_lined(
    embedded_families,
    order,
    token_quarter_factor,
    genuine_residue_tally,
    standardizer_scales,
    standardizer_offsets,
    row_qkv,
    row_out,
    col_qkv,
    col_out,
    ffn_up,
    ffn_down,
    upstream_sensitivity,
):
    model_width = embedded_families.shape[-1]
    share = standardizer_scales.shape[-1]
    shards = (row_qkv, row_out, col_qkv, col_out, ffn_up, ffn_down)
    norms = jnp.pad(
        jnp.concatenate([standardizer_scales[0], standardizer_offsets[0]], axis=0),
        ((0, 2), (0, 256 - share)),
    )
    activations, derivs, costs, vector, _, out = run_layers(
        shards,
        embedded_families,
        upstream_sensitivity,
        order,
        token_quarter_factor,
        genuine_residue_tally,
        norms,
    )
    *results, activations, derivs, costs = unpack_all(
        out, activations, derivs, costs, [shard.shape[1:] for shard in shards]
    )
    return (
        activations,
        derivs,
        costs,
        *results,
        vector[None, 0:3, :share],
        vector[None, 3:6, :share],
    )


def solution(mesh):
    in_specs = (
        P("dp", "seq", None, None),
        P("dp", None),
        P("dp", "seq", None),
        P("dp"),
        P("pipe", None, "seq"),
        P("pipe", None, "seq"),
        P("pipe", "seq", None),
        P("pipe", "seq", None),
        P("pipe", "seq", None),
        P("pipe", "seq", None),
        P("pipe", "seq", None),
        P("pipe", "seq", None),
        P("dp", "seq", None, None),
    )
    out_specs = (
        P("pipe", "dp", "seq", None, None),
        P("pipe", "dp", "seq", None, None),
        P("pipe", "dp"),
        P("pipe", "seq", None),
        P("pipe", "seq", None),
        P("pipe", "seq", None),
        P("pipe", "seq", None),
        P("pipe", "seq", None),
        P("pipe", "seq", None),
        P("pipe", None, "seq"),
        P("pipe", None, "seq"),
    )
    lined = mesh.shape["seq"] == LINE and mesh.shape["dp"] == 4 and mesh.shape["pipe"] == 2
    return jax.shard_map(
        on_device_lined if lined else on_device, mesh=mesh, in_specs=in_specs, out_specs=out_specs, check_vma=False
    )
```

```python
import functools
import math

import jax
import jax.numpy as jnp
from jax import lax
from jax.experimental import pallas as pl
from jax.experimental.pallas import tpu as pltpu
from jax.sharding import PartitionSpec as P

HEAD_TALLY = 12
LINE = 4
MESH = pl.DeviceIdType.MESH
EARLY = 4
AT_ONCE = 2
MIDDLE = 0
MORE = 2
PIECES = 7


norm_epsilon = 1e-05


def shifted(value, axis, steps):
    count = lax.axis_size(axis)
    initial, last = (max(0, -steps), min(count, count - steps))
    return lax.ppermute(value, axis, [(source, source + steps) for source in range(initial, last)])


def normed(values, gain_row, bias_row):
    average = jnp.mean(values, axis=-1, keepdims=True)
    centered = values - average
    variance = jnp.mean(centered * centered, axis=-1, keepdims=True)
    return centered * lax.rsqrt(variance + norm_epsilon) * gain_row + bias_row


def gelu_exact(values):
    return jax.nn.gelu(values, approximate=False)


def product(left, weight):
    return lax.dot_general(
        left, weight, (((left.ndim - 1,), (0,)), ((), ())), preferred_element_type=jnp.float32
    )


def product_back(left, weight):
    return lax.dot_general(
        left, weight, (((left.ndim - 1,), (1,)), ((), ())), preferred_element_type=jnp.float32
    )


def weight_term(left, right):
    return lax.dot_general(
        left, right, (((0, 1), (0, 1)), ((), ())), preferred_element_type=jnp.float32
    )


def split_heads(values, head_count):
    return values.reshape(values.shape[:-1] + (head_count, values.shape[-1] // head_count))


def choose(flag, first_tree, second_tree):
    return jax.tree.map(lambda early, later: jnp.where(flag, early, later), first_tree, second_tree)


def column_scores(queries, key_rows, head_count):
    query_heads = split_heads(queries, head_count)
    raw = jnp.einsum(
        "rche,sche->chrs",
        query_heads,
        split_heads(key_rows, head_count),
        preferred_element_type=jnp.float32,
    )
    return raw / math.sqrt(query_heads.shape[-1])


def column_forward(queries, key_rows, content_lines, head_count):
    scores = column_scores(queries, key_rows, head_count)
    log_total = jax.nn.logsumexp(scores, axis=-1)
    vertical_factors = jnp.exp(scores - log_total[..., None]).astype(jnp.bfloat16)
    mixed_cols = jnp.einsum(
        "gmqi,igmu->qgmu",
        vertical_factors,
        split_heads(content_lines, head_count),
        preferred_element_type=jnp.float32,
    )
    return (mixed_cols.reshape(queries.shape).astype(jnp.bfloat16), log_total)


def column_backward(queries, key_rows, content_lines, log_total, grad_mixed, head_count):
    scores = column_scores(queries, key_rows, head_count)
    softmax_share = jnp.exp(scores - log_total[..., None])
    grad_heads = split_heads(grad_mixed, head_count)
    grad_probs = jnp.einsum(
        "rche,sche->chrs",
        grad_heads,
        split_heads(content_lines, head_count),
        preferred_element_type=jnp.float32,
    )
    grad_values = jnp.einsum(
        "chrs,rche->sche",
        softmax_share.astype(jnp.bfloat16),
        grad_heads,
        preferred_element_type=jnp.float32,
    )
    grad_scores = (
        softmax_share * (grad_probs - jnp.sum(softmax_share * grad_probs, axis=-1, keepdims=True))
    ).astype(jnp.bfloat16)
    root_size = math.sqrt(queries.shape[-1] // head_count)
    grad_queries = (
        jnp.einsum(
            "gmqi,igmu->qgmu",
            grad_scores,
            split_heads(key_rows, head_count),
            preferred_element_type=jnp.float32,
        )
        / root_size
    )
    grad_keys = (
        jnp.einsum(
            "chrs,rche->sche",
            grad_scores,
            split_heads(queries, head_count),
            preferred_element_type=jnp.float32,
        )
        / root_size
    )
    return (
        grad_queries.reshape(queries.shape),
        grad_keys.reshape(key_rows.shape),
        grad_values.reshape(content_lines.shape),
    )


def row_split(horizontal_mixer, model_width, head_count):
    queries = split_heads(horizontal_mixer[..., :model_width], head_count)
    key_rows = split_heads(horizontal_mixer[..., model_width : 2 * model_width], head_count)
    content_lines = split_heads(horizontal_mixer[..., 2 * model_width :], head_count)
    return (queries, key_rows, content_lines)


def layer_forward(source_rows, family_residues, projection_tables, head_count):
    (
        horizontal_coefficients,
        w_row_out,
        vertical_coefficients,
        w_col_out,
        w_up,
        w_down,
        gain_rows,
        bias_rows,
    ) = projection_tables
    row_count, columns, model_width = source_rows.shape
    total_rows = row_count * lax.axis_size("seq")
    start = source_rows.astype(jnp.float32)
    layernorm_first = normed(start, gain_rows[0], bias_rows[0]).astype(jnp.bfloat16)
    horizontal_mixer = product(layernorm_first, horizontal_coefficients).astype(jnp.bfloat16)
    queries, key_rows, content_lines = row_split(horizontal_mixer, model_width, head_count)
    logit_factor = 1.0 / (math.sqrt(model_width // head_count) * math.sqrt(total_rows))
    partial_value = logit_factor * jnp.einsum(
        "rihe,rjhe->hij", queries, key_rows, preferred_element_type=jnp.float32
    )
    logits = lax.psum(partial_value.astype(jnp.bfloat16), "seq").astype(jnp.float32)
    softmax_share = jax.nn.softmax(logits, axis=-1)
    log_probs = jax.nn.log_softmax(logits, axis=-1)
    entropy = -jnp.sum(softmax_share * log_probs, axis=-1)
    valid_residues = (jnp.arange(columns, dtype=jnp.int32) < family_residues).astype(jnp.float32)
    disorder_cost = jnp.sum(entropy * valid_residues[None, :]) / float(head_count * columns)
    blended_lines = jnp.einsum(
        "vyp,opvl->oyvl",
        softmax_share.astype(jnp.bfloat16),
        content_lines,
        preferred_element_type=jnp.float32,
    )
    blended_lines = blended_lines.reshape(row_count, columns, model_width).astype(jnp.bfloat16)
    after_row = start + product(blended_lines, w_row_out)
    layernorm_second = normed(after_row, gain_rows[1], bias_rows[1]).astype(jnp.bfloat16)
    vertical_mixer = product(layernorm_second, vertical_coefficients).astype(jnp.bfloat16)
    everyone = lax.all_gather(vertical_mixer[..., model_width:], "seq", axis=0, tiled=True)
    mixed_values, log_total = column_forward(
        vertical_mixer[..., :model_width],
        everyone[..., :model_width],
        everyone[..., model_width:],
        head_count,
    )
    column_state = (everyone, log_total)
    after_col = after_row + product(mixed_values, w_col_out)
    normal_c = normed(after_col, gain_rows[2], bias_rows[2]).astype(jnp.bfloat16)
    upward = product(normal_c, w_up)
    hidden = gelu_exact(upward).astype(jnp.bfloat16)
    result = after_col + product(hidden, w_down)
    kept_state = (
        source_rows,
        layernorm_first,
        horizontal_mixer,
        logits,
        blended_lines,
        after_row,
        layernorm_second,
        vertical_mixer,
        column_state,
        mixed_values,
        after_col,
        normal_c,
        upward,
        hidden,
    )
    return (result.astype(jnp.bfloat16), disorder_cost, kept_state)


def layer_backward(kept_state, family_residues, grad_result, projection_tables, head_count):
    (
        horizontal_coefficients,
        w_row_out,
        vertical_coefficients,
        w_col_out,
        w_up,
        w_down,
        gain_rows,
        bias_rows,
    ) = projection_tables
    (
        source_rows,
        layernorm_first,
        horizontal_mixer,
        logits,
        blended_lines,
        after_row,
        layernorm_second,
        vertical_mixer,
        column_state,
        mixed_values,
        after_col,
        normal_c,
        upward,
        hidden,
    ) = kept_state
    row_count, columns, model_width = source_rows.shape
    total_rows = row_count * lax.axis_size("seq")
    grad_branch_ffn = grad_result.astype(jnp.bfloat16)
    grad_hidden = product_back(grad_branch_ffn, w_down)
    grad_upward = jax.vjp(gelu_exact, upward)[1](grad_hidden)[0].astype(jnp.bfloat16)
    grad_normal_c = product_back(grad_upward, w_up)
    from_norm, gain_last, bias_last = jax.vjp(normed, after_col, gain_rows[2], bias_rows[2])[1](
        grad_normal_c
    )
    grad_col = grad_result + from_norm
    grad_branch_col = grad_col.astype(jnp.bfloat16)
    grad_attended = product_back(grad_branch_col, w_col_out).astype(jnp.bfloat16)
    everyone, log_total = column_state
    grad_query_col, grad_key_col, grad_value_col = column_backward(
        vertical_mixer[..., :model_width],
        everyone[..., :model_width],
        everyone[..., model_width:],
        log_total,
        grad_attended,
        head_count,
    )
    grad_kv_rows = lax.psum_scatter(
        jnp.concatenate([grad_key_col, grad_value_col], axis=-1).astype(jnp.bfloat16),
        "seq",
        scatter_dimension=0,
        tiled=True,
    ).astype(jnp.float32)
    grad_col_proj = jnp.concatenate([grad_query_col, grad_kv_rows], axis=-1).astype(jnp.bfloat16)
    grad_normal_b = product_back(grad_col_proj, vertical_coefficients)
    from_norm, gain_middle, bias_middle = jax.vjp(normed, after_row, gain_rows[1], bias_rows[1])[1](
        grad_normal_b
    )
    grad_row = grad_col + from_norm
    grad_branch_row = grad_row.astype(jnp.bfloat16)
    grad_mixed = split_heads(
        product_back(grad_branch_row, w_row_out).astype(jnp.bfloat16), head_count
    )
    queries, key_rows, content_lines = row_split(horizontal_mixer, model_width, head_count)
    softmax_share = jax.nn.softmax(logits, axis=-1)
    log_probs = jax.nn.log_softmax(logits, axis=-1)
    entropy = -jnp.sum(softmax_share * log_probs, axis=-1)
    partial_value = jnp.einsum(
        "rihe,rjhe->hij", grad_mixed, content_lines, preferred_element_type=jnp.float32
    )
    grad_probs = lax.psum(partial_value.astype(jnp.bfloat16), "seq").astype(jnp.float32)
    grad_values = jnp.einsum(
        "hij,rihe->rjhe",
        softmax_share.astype(jnp.bfloat16),
        grad_mixed,
        preferred_element_type=jnp.float32,
    )
    valid_residues = (jnp.arange(columns, dtype=jnp.int32) < family_residues).astype(jnp.float32)
    column_weight = float(total_rows * columns) * valid_residues / float(head_count * columns)
    grad_logits = softmax_share * (
        grad_probs - jnp.sum(softmax_share * grad_probs, axis=-1, keepdims=True)
    )
    grad_logits = grad_logits - column_weight[None, :, None] * softmax_share * (
        log_probs + entropy[..., None]
    )
    grad_logits = grad_logits.astype(jnp.bfloat16)
    logit_factor = 1.0 / (math.sqrt(model_width // head_count) * math.sqrt(total_rows))
    grad_queries = logit_factor * jnp.einsum(
        "vyp,opvl->oyvl", grad_logits, key_rows, preferred_element_type=jnp.float32
    )
    grad_keys = logit_factor * jnp.einsum(
        "hij,rihe->rjhe", grad_logits, queries, preferred_element_type=jnp.float32
    )
    grad_row_proj = jnp.concatenate(
        [
            grad_queries.reshape(row_count, columns, model_width),
            grad_keys.reshape(row_count, columns, model_width),
            grad_values.reshape(row_count, columns, model_width),
        ],
        axis=-1,
    ).astype(jnp.bfloat16)
    grad_normal_a = product_back(grad_row_proj, horizontal_coefficients)
    from_norm, gain_first, bias_first = jax.vjp(
        normed, source_rows.astype(jnp.float32), gain_rows[0], bias_rows[0]
    )[1](grad_normal_a)
    grad_source = (grad_row + from_norm).astype(jnp.bfloat16)
    operand_pairs = (
        (layernorm_first, grad_row_proj),
        (blended_lines, grad_branch_row),
        (layernorm_second, grad_col_proj),
        (mixed_values, grad_branch_col),
        (normal_c, grad_upward),
        (hidden, grad_branch_ffn),
    )
    norm_grads = (
        jnp.stack([gain_first, gain_middle, gain_last]),
        jnp.stack([bias_first, bias_middle, bias_last]),
    )
    return (grad_source, operand_pairs, norm_grads)


def on_device(
    embedded_families,
    order,
    token_quarter_factor,
    genuine_residue_tally,
    standardizer_scales,
    standardizer_offsets,
    row_qkv,
    row_out,
    col_qkv,
    col_out,
    ffn_up,
    ffn_down,
    upstream_sensitivity,
):
    head_count = HEAD_TALLY
    segment_place = lax.axis_index("pipe")
    gathered = (
        lax.all_gather(row_qkv, "seq", axis=1, tiled=True),
        lax.all_gather(row_out, "seq", axis=1, tiled=True),
        lax.all_gather(col_qkv, "seq", axis=1, tiled=True),
        lax.all_gather(col_out, "seq", axis=1, tiled=True),
        lax.all_gather(ffn_up, "seq", axis=1, tiled=True),
        lax.all_gather(ffn_down, "seq", axis=1, tiled=True),
        lax.all_gather(standardizer_scales.astype(jnp.bfloat16), "seq", axis=2, tiled=True).astype(
            standardizer_scales.dtype
        ),
        lax.all_gather(standardizer_offsets.astype(jnp.bfloat16), "seq", axis=2, tiled=True).astype(
            standardizer_offsets.dtype
        ),
    )
    projection_tables = tuple((gathered_piece[0] for gathered_piece in gathered))
    small_batch_number = embedded_families.shape[0]
    sequence = order[0]
    received = jnp.zeros(embedded_families.shape[1:], jnp.bfloat16)
    results = []
    focus_spread_levies = []
    kept_list = []
    for period in range(small_batch_number + 1):
        slot_here = jnp.clip(period - segment_place, 0, small_batch_number - 1)
        align_here = sequence[slot_here]
        source_rows = jnp.where(segment_place == 0, embedded_families[align_here], received)
        result, disorder_cost, kept_state = layer_forward(
            source_rows, genuine_residue_tally[align_here], projection_tables, head_count
        )
        results.append(result)
        focus_spread_levies.append(disorder_cost)
        kept_list.append(kept_state)
        if period < small_batch_number:
            received = shifted(result, "pipe", 1)
    activations = lax.dynamic_slice_in_dim(jnp.stack(results), segment_place, small_batch_number, 0)
    penalty_output = lax.dynamic_slice_in_dim(
        jnp.stack(focus_spread_levies), segment_place, small_batch_number, 0
    )
    grad_received = jnp.zeros(embedded_families.shape[1:], jnp.bfloat16)
    left_lists = [[] for index in range(6)]
    right_lists = [[] for index in range(6)]
    gain_total = None
    bias_total = None
    grad_sources = []
    for period in range(small_batch_number + 1):
        slot_raw = period - 1 + segment_place
        in_range = jnp.logical_and(slot_raw >= 0, slot_raw < small_batch_number)
        slot_here = jnp.clip(slot_raw, 0, small_batch_number - 1)
        align_here = sequence[slot_here]
        kept_state = choose(
            segment_place == 0,
            kept_list[max(period - 1, 0)],
            kept_list[min(period + 1, small_batch_number)],
        )
        outgrad = (
            upstream_sensitivity[slot_here].astype(jnp.float32)
            * token_quarter_factor[align_here].astype(jnp.float32)[..., None]
            * 0.25
        )
        incoming_grad = jnp.where(segment_place == 1, outgrad, grad_received.astype(jnp.float32))
        grad_source, operand_pairs, norm_grads = layer_backward(
            kept_state,
            genuine_residue_tally[align_here],
            incoming_grad,
            projection_tables,
            head_count,
        )
        for index in range(6):
            left_lists[index].append(operand_pairs[index][0])
            right_lists[index].append(
                jnp.where(
                    in_range, operand_pairs[index][1], jnp.zeros_like(operand_pairs[index][1])
                )
            )
        gain_term = jnp.where(in_range, norm_grads[0], jnp.zeros_like(norm_grads[0]))
        bias_term = jnp.where(in_range, norm_grads[1], jnp.zeros_like(norm_grads[1]))
        gain_total = gain_term if gain_total is None else gain_total + gain_term
        bias_total = bias_term if bias_total is None else bias_total + bias_term
        grad_sources.append(grad_source)
        if period < small_batch_number:
            grad_received = shifted(grad_source, "pipe", -1)
    block_entry_derivs = lax.dynamic_slice_in_dim(
        jnp.stack(grad_sources), 1 - segment_place, small_batch_number, 0
    )
    weight_totals = [
        weight_term(
            jnp.concatenate(left_lists[index], axis=0), jnp.concatenate(right_lists[index], axis=0)
        )
        for index in range(6)
    ]
    shared = (
        lax.psum_scatter(
            weight_totals[0].astype(jnp.bfloat16), "seq", scatter_dimension=0, tiled=True
        ).astype(jnp.float32),
        lax.psum_scatter(
            weight_totals[1].astype(jnp.bfloat16), "seq", scatter_dimension=0, tiled=True
        ).astype(jnp.float32),
        lax.psum_scatter(
            weight_totals[2].astype(jnp.bfloat16), "seq", scatter_dimension=0, tiled=True
        ).astype(jnp.float32),
        lax.psum_scatter(
            weight_totals[3].astype(jnp.bfloat16), "seq", scatter_dimension=0, tiled=True
        ).astype(jnp.float32),
        lax.psum_scatter(
            weight_totals[4].astype(jnp.bfloat16), "seq", scatter_dimension=0, tiled=True
        ).astype(jnp.float32),
        lax.psum_scatter(
            weight_totals[5].astype(jnp.bfloat16), "seq", scatter_dimension=0, tiled=True
        ).astype(jnp.float32),
        lax.psum_scatter(
            gain_total.astype(jnp.bfloat16), "seq", scatter_dimension=1, tiled=True
        ).astype(jnp.float32),
        lax.psum_scatter(
            bias_total.astype(jnp.bfloat16), "seq", scatter_dimension=1, tiled=True
        ).astype(jnp.float32),
    )
    (
        shared_row_qkv,
        shared_row_out,
        shared_col_qkv,
        shared_col_out,
        shared_up,
        shared_down,
        shared_gain,
        shared_bias,
    ) = shared
    summed = (
        lax.psum(shared_row_qkv.astype(jnp.bfloat16), "dp").astype(jnp.float32),
        lax.psum(shared_row_out.astype(jnp.bfloat16), "dp").astype(jnp.float32),
        lax.psum(shared_col_qkv.astype(jnp.bfloat16), "dp").astype(jnp.float32),
        lax.psum(shared_col_out.astype(jnp.bfloat16), "dp").astype(jnp.float32),
        lax.psum(shared_up.astype(jnp.bfloat16), "dp").astype(jnp.float32),
        lax.psum(shared_down.astype(jnp.bfloat16), "dp").astype(jnp.float32),
        lax.psum(shared_gain.astype(jnp.bfloat16), "dp").astype(jnp.float32),
        lax.psum(shared_bias.astype(jnp.bfloat16), "dp").astype(jnp.float32),
    )
    return (
        activations[None],
        block_entry_derivs[None],
        penalty_output[None],
        summed[0][None],
        summed[1][None],
        summed[2][None],
        summed[3][None],
        summed[4][None],
        summed[5][None],
        summed[6][None],
        summed[7][None],
    )


def place():
    pipe, seq, dp = (lax.axis_index("pipe"), lax.axis_index("seq"), lax.axis_index("dp"))
    core = lax.rem(dp, 2)
    pair = lax.div(dp, 2)
    return (pipe, seq, dp, core, pair)


def neighbours(pipe, seq, dp, core, pair):
    other_core = (pipe, seq, dp + 1 - 2 * core)
    other_pair = (pipe, seq, dp + 2 - 4 * pair)
    return (other_core, other_pair)


def greet(pipe, seq, dp, core, pair, across_pipe=False):
    barrier = pltpu.get_barrier_semaphore()
    other_core, other_pair = neighbours(pipe, seq, dp, core, pair)
    count = 0
    for step in range(LINE):
        for flip in range(2):
            if step == 0 and flip == 0:
                continue
            where = dp if flip == 0 else dp + 1 - 2 * core
            pl.semaphore_signal(
                barrier,
                inc=1,
                device_id=(pipe, lax.rem(seq + step, LINE), where),
                device_id_type=MESH,
            )
            count += 1
    more = [other_pair] + ([(1 - pipe, seq, dp)] if across_pipe else [])
    for device in more:
        pl.semaphore_signal(barrier, inc=1, device_id=device, device_id_type=MESH)

    def hear():
        pl.semaphore_wait(barrier, count + len(more))

    return hear


def remote(source, target, send, recv, device):
    return pltpu.make_async_remote_copy(
        src_ref=source,
        dst_ref=target,
        send_sem=send,
        recv_sem=recv,
        device_id=device,
        device_id_type=MESH,
    )


def swap_rows(source, target, send, recv, local, where):
    pipe, seq, dp, core, pair = where
    half, rest = (lax.div(seq, 2), lax.rem(seq, 2))

    def each(action):
        for index in range(2):
            line = 2 * core + index
            here = jnp.logical_and(line == seq, half == core)
            copy = remote(
                source.at[index],
                target.at[rest],
                send.at[index],
                recv.at[rest],
                (pipe, line, dp - core + half),
            )
            arriving = remote(
                source.at[index],
                target.at[index],
                send.at[index],
                recv.at[index],
                (pipe, line, dp - core + half),
            )
            inside = pltpu.make_async_copy(source.at[index], target.at[rest], local)
            action(here, copy, arriving, inside)

    def start(here, copy, arriving, inside):
        pl.when(here)(inside.start)
        pl.when(jnp.logical_not(here))(copy.start)

    def finish(here, copy, arriving, inside):
        pl.when(here)(inside.wait)
        pl.when(jnp.logical_not(here))(copy.wait_send)
        pl.when(jnp.logical_not(here))(arriving.wait_recv)

    return (lambda: each(start), lambda: each(finish))


def dot(left, right, left_axis, right_axis):
    return lax.dot_general(
        left,
        right,
        (((left_axis,), (right_axis,)), ((), ())),
        preferred_element_type=jnp.float32,
    )


def unit_rows(values):
    average = jnp.mean(values, axis=-1, keepdims=True)
    centered = values - average
    variance = jnp.mean(centered * centered, axis=-1, keepdims=True)
    root = lax.rsqrt(variance + norm_epsilon)
    return (centered * root, root)


def unit_rows_back(grad, values, gain_row):
    unit, root = unit_rows(values)
    scaled = grad * gain_row
    inner = jnp.mean(scaled * unit, axis=-1, keepdims=True)
    term = root * (scaled - jnp.mean(scaled, axis=-1, keepdims=True) - unit * inner)
    gain = jnp.sum(grad * unit, axis=0, keepdims=True)
    bias = jnp.sum(grad, axis=0, keepdims=True)
    return (term, gain, bias)


def layers_kernel(
    shard_row,
    shard_row_out,
    shard_col,
    shard_col_out,
    shard_up,
    shard_down,
    families,
    upstream,
    order,
    quarters,
    tally,
    norms,
    act_out,
    der_out,
    cost_out,
    vector_out,
    grads,
    out,
    tiles,
    source,
    normal_a,
    normal_b,
    normal_c,
    mixer,
    mixer_col,
    blended,
    mixed,
    after_row,
    after_col,
    log_share,
    col_share,
    hidden,
    slope,
    total_grad,
    grad_in,
    branch_ffn,
    branch_col,
    branch_row,
    grad_up,
    grad_mixer_col,
    grad_mixer,
    logit_send,
    logit_recv,
    keys_recv,
    keys_send,
    keys_back,
    probs_send,
    probs_recv,
    halves,
    segment,
    spread,
    stage,
    stage_down,
    act,
    der,
    cost,
    piece,
    piece_in,
    sensitivity,
    factor,
    factor_in,
    counts,
    counts_in,
    norms_in,
    rows,
    own_sem,
    line_send,
    line_recv,
    pair_send,
    pair_recv,
    core_send,
    core_recv,
    entry_sems,
    entry_local,
    norm_send,
    norm_recv,
    landing,
    from_pair,
    late_pair,
    der_back,
    clear_sem,
    vector,
    vec_core,
    vec_pair,
    vec_line,
    load_sem,
    near_send,
    near_recv,
    far_send,
    far_recv,
    hop_send,
    left_recv,
    right_recv,
    late_send,
    late_recv,
    share_send,
    share_recv,
    out_sem,
    vec_send,
    vec_recv,
    logit_sems,
    keys_sems,
    back_sems,
    probs_sems,
    pipe_sems,
    stage_sems,
    home_sems,
    home_local,
    cost_send,
    cost_recv,
):
    where = place()
    pipe, seq, dp, core, pair = where
    other_core = (pipe, seq, dp + 1 - 2 * core)
    other_pipe = (1 - pipe, seq, dp)
    columns, width = families.shape[2:]
    tokens = 2 * columns
    heads = HEAD_TALLY
    size = width // heads
    twin = 2 * size
    couples = heads // 2
    total_rows = LINE
    bf16, f32 = (jnp.bfloat16, jnp.float32)
    part_width = width // LINE
    shards = [
        ref.at[0]
        for ref in (shard_row, shard_row_out, shard_col, shard_col_out, shard_up, shard_down)
    ]
    first_tile = (0, 3, 4, 7, 8, 12)
    last_matrix = 5
    pieces = PIECES
    other_pair = (pipe, seq, dp + 2 - 4 * pair)
    right, left = ((pipe, seq + 1, dp), (pipe, seq - 1, dp))
    later = pipe == 1

    hear = greet(*where, across_pipe=True)
    straight = order[0, 0] == 0
    for index in range(2):
        piece[index] = jnp.where(straight, families[index, 0], families[1 - index, 0])
        chosen = jnp.where(straight, quarters[index], quarters[1 - index])
        factor[index] = jnp.broadcast_to(chosen.astype(f32) * 0.25, (columns, columns)).T
        number = jnp.where(straight, tally[index], tally[1 - index])
        counts[index] = jnp.broadcast_to(number, (8, 128)).astype(f32)
    hear()

    def entering(number, source_ref, target_ref):
        return swap_rows(
            source_ref,
            target_ref,
            entry_sems.at[2 * number],
            entry_sems.at[2 * number + 1],
            entry_local.at[number],
            where,
        )

    start_counts, finish_counts = entering(0, counts, counts_in)
    start_piece, finish_piece = entering(1, piece, piece_in)
    start_sensitivity, finish_sensitivity = entering(2, upstream.at[:, 0], sensitivity)
    start_factor, finish_factor = entering(3, factor, factor_in)
    pl.when(later)(start_piece)

    def norm_copy(step, source):
        return remote(
            norms,
            norms_in.at[source],
            norm_send.at[step - 1],
            norm_recv.at[source],
            (pipe, lax.rem(seq + step, LINE), dp),
        )


    def block_of(index, source, start, length):
        depth, wide = shards[index].shape
        if wide == width and depth == width:
            return tiles.at[first_tile[index] + source, pl.ds(start, length)]
        start = pl.multiple_of(source * depth + start, 16)
        return tiles.at[pl.ds(first_tile[index], wide // width), pl.ds(start, length)]

    def piece_of(index):
        matrix = min(index, last_matrix)
        share = shards[matrix].shape[0] // 4
        length = share // 2 if matrix == last_matrix else share
        return (matrix, share, (index - matrix) * length, length)

    def region(index, source, part):
        matrix, share, skip, length = piece_of(index)
        start = pl.multiple_of(part * share + skip, 16)
        return block_of(matrix, source, start, length)

    def cut(index, start, length):
        depth, wide = shards[index].shape
        if wide == width and depth == width:
            yield (
                shards[index].at[pl.ds(start, length)],
                tiles.at[first_tile[index] + seq, pl.ds(start, length)],
            )
            return
        target = pl.multiple_of(seq * depth + start, 16)
        for part in range(wide // width):
            yield (
                shards[index].at[pl.ds(start, length), pl.ds(part * width, width)],
                tiles.at[first_tile[index] + part, pl.ds(target, length)],
            )

    def start_own(index):
        for near, far in cut(index, 0, shards[index].shape[0]):
            pltpu.make_async_copy(near, far, own_sem.at[index]).start()

    def wait_own(index):
        block = block_of(index, seq, 0, shards[index].shape[0])
        pltpu.make_async_copy(block, block, own_sem.at[index]).wait()

    def start_line(index, direction):
        matrix, share, skip, length = piece_of(index)
        for near, far in cut(matrix, pl.multiple_of(dp * share + skip, 16), length):
            remote(
                near,
                far,
                line_send.at[direction, seq, index],
                line_recv.at[seq, index],
                right if direction == 0 else left,
            ).start()

    def along(source, index, direction):
        block = region(index, source, dp)
        return remote(
            block,
            block,
            line_send.at[direction, source, index],
            line_recv.at[source, index],
            right if direction == 0 else left,
        )

    across = dp + 2 - 4 * pair
    opposite = dp + 1 - 2 * core
    opposite_across = across + 1 - 2 * core

    def over_pair(source, index, part):
        block = region(index, source, part)
        return remote(
            block, block, pair_send.at[source, index], pair_recv.at[source, index], other_pair
        )

    def over_core(lane_of, source, index, part):
        block = region(index, source, part)
        return remote(
            block,
            block,
            core_send.at[lane_of, source, index],
            core_recv.at[lane_of, source, index],
            other_core,
        )

    has = (seq < LINE - 1, seq > 0)

    def sources(step):
        for direction in range(2):
            source = seq - step if direction == 0 else seq + step
            yield (direction, source, source >= 0 if direction == 0 else source < LINE)

    def begin(index):
        for direction in range(2):
            pl.when(has[direction])(functools.partial(start_line, index, direction))
        if index <= last_matrix:
            start_own(index)

    def arrive(index, step):
        for direction, source, present in sources(step):

            @pl.when(present)
            def _():
                along(source, index, direction).wait_recv()

                @pl.when(has[direction])
                def _():
                    along(source, index, direction).start()

                over_pair(source, index, dp).start()
                over_core(0, source, index, dp).start()

    def relay(index, step):
        for direction, source, present in sources(step):

            @pl.when(present)
            def _():
                over_pair(source, index, across).wait_recv()
                over_core(1, source, index, across).start()

    def settle(index):
        if index <= last_matrix:
            wait_own(index)
        for step in range(1, LINE):
            for direction, source, present in sources(step):

                @pl.when(present)
                def _():
                    over_core(0, source, index, opposite).wait_recv()
                    over_core(1, source, index, opposite_across).wait_recv()

    def drain(index):
        for direction in range(2):
            pl.when(has[direction])(along(seq, index, direction).wait_send)
        for step in range(1, LINE):
            for direction, source, present in sources(step):

                @pl.when(present)
                def _():
                    pl.when(has[direction])(along(source, index, direction).wait_send)
                    over_pair(source, index, dp).wait_send()
                    over_core(0, source, index, dp).wait_send()
                    over_core(1, source, index, across).wait_send()

    def wave(number):
        if number + 1 < pieces:
            begin(number + 1)
        for step in range(1, LINE):
            if 0 <= number + 1 - step < pieces:
                arrive(number + 1 - step, step)
        for step in range(1, LINE):
            if 0 <= number - step < pieces:
                relay(number - step, step)

    def gather(*waves):
        @pl.when(jnp.logical_not(later))
        def _():
            for number in waves:
                wave(number)

    def ready(index):
        pl.when(jnp.logical_not(later))(lambda: settle(index))

    begin(0)
    start_counts()
    for step in range(1, LINE):
        norm_copy(step, seq).start()
    norms_in[seq] = norms[...]
    hop = remote(piece_in, source, pipe_sems.at[4], pipe_sems.at[5], other_pipe)

    @pl.when(later)
    def _():
        finish_piece()
        hop.start()
        for number in range(pieces + LINE - 1):
            wave(number)
        start_sensitivity()
        start_factor()
        for index in range(pieces):
            settle(index)
            drain(index)
        hop.wait_send()

    lane = lax.broadcasted_iota(jnp.int32, (columns, 2 * twin), 1)
    early = (lax.rem(lane, twin) < size).astype(f32)
    halves[0] = early.astype(bf16)
    halves[1] = (1.0 - early).astype(bf16)
    feature = lax.broadcasted_iota(jnp.int32, (width, 128), 0)
    head = lax.broadcasted_iota(jnp.int32, (width, 128), 1)
    belongs = jnp.logical_and(feature >= head * size, feature < head * size + size)
    segment[...] = belongs.astype(f32).astype(bf16)
    head = lax.broadcasted_iota(jnp.int32, (128, width), 0)
    feature = lax.broadcasted_iota(jnp.int32, (128, width), 1)
    belongs = jnp.logical_and(feature >= head * size, feature < head * size + size)
    spread[...] = belongs.astype(f32).astype(bf16)
    for step in range(1, LINE):
        norm_copy(step, lax.rem(seq + LINE - step, LINE)).wait()
    for part in range(LINE):
        rows[:, part * part_width : (part + 1) * part_width] = norms_in[part, :, 0:part_width]
    finish_counts()

    def gain_of(index):
        return rows[index : index + 1, :]

    def bias_of(index):
        return rows[3 + index : 4 + index, :]

    def keep_vector(index, gain, bias):
        part = width // LINE
        for target in range(LINE):
            window = slice(target * part, (target + 1) * part)
            vector[target, index : index + 1, 0:part] = gain[:, window]
            vector[target, 3 + index : 4 + index, 0:part] = bias[:, window]

    vector[...] = jnp.zeros(vector.shape, f32)

    def both(ref, start):
        return jnp.concatenate(
            [ref[0:columns, start : start + twin], ref[columns:tokens, start : start + twin]],
            axis=1,
        )

    def stacked(ref, start):
        wide = both(ref, start)
        return jnp.concatenate([wide * halves[0], wide * halves[1]], axis=0)

    def unstack(wide):
        early_lane = lax.rem(lax.broadcasted_iota(jnp.int32, (columns, 2 * twin), 1), twin) < size
        return jnp.where(early_lane, wide[0:columns], wide[columns:])

    def put(ref, start, wide):
        ref[0:columns, start : start + twin] = wide[:, 0:twin].astype(bf16)
        ref[columns:tokens, start : start + twin] = wide[:, twin:].astype(bf16)

    def to_core(source_ref, target_ref, sems, index):
        return remote(
            source_ref, target_ref, sems.at[0, index], sems.at[1, index], other_core
        )

    start_act, finish_act = swap_rows(
        act, act_out, home_sems.at[0], home_sems.at[1], home_local.at[0], where
    )
    start_der, finish_der = swap_rows(
        der, der_out, home_sems.at[2], home_sems.at[3], home_local.at[1], where
    )
    sender = core == lax.div(seq, 2)
    spot = lax.rem(seq, 2)
    cost_own = pltpu.make_async_copy(cost, cost_out.at[spot], home_local.at[2])
    cost_copies = [
        remote(
            cost,
            cost_out.at[spot],
            cost_send.at[step - 1],
            cost_recv.at[spot],
            (pipe, lax.rem(seq + step, LINE), dp),
        )
        for step in range(1, LINE)
    ]

    der_over = remote(der, piece, pipe_sems.at[6], pipe_sems.at[7], other_pipe)
    der_home = remote(der_back, der_out, pipe_sems.at[8], pipe_sems.at[9], other_pipe)
    start_back, finish_back = swap_rows(
        piece, der_back, home_sems.at[4], home_sems.at[5], home_local.at[3], where
    )
    send_on = remote(act, source, pipe_sems.at[0], pipe_sems.at[1], other_pipe)
    send_back = remote(der, grad_in, pipe_sems.at[2], pipe_sems.at[3], other_pipe)

    @pl.when(later)
    def _():
        send_on.wait_recv()

    gather(0, 1)

    @pl.when(jnp.logical_not(later))
    def _():
        hop.wait_recv()

    chunks, cycle = (6, 3)
    whole_turns = chunks // cycle
    paired = chunks - whole_turns
    depth = width // chunks
    units = LINE * chunks
    mid = units // 2
    always = lambda target: target >= 0
    far = jnp.maximum(seq, LINE - 1 - seq)
    pair_lag, hop_lag, share_lag = (3, 4, 4)

    def unit_of(number):
        turn = lax.div(number, LINE)
        rank = number - turn * LINE
        halfway = lax.div(rank, 2)
        target = jnp.where(lax.rem(rank, 2) == 0, LINE - 1 - halfway, halfway)
        return (target, chunks - 1 - turn)

    def rank_of(chunk):
        turn = chunks - 1 - chunk
        early_turns = lax.div(turn, cycle)
        return (early_turns, turn - early_turns - 1)

    def is_single(chunk):
        turn = chunks - 1 - chunk
        return lax.rem(turn, cycle) != 0

    def window_of(chunk):
        return pl.ds(pl.multiple_of(chunk * depth, depth), depth)

    def spot_of(number, side, shift, count=1):
        block = jnp.where(
            number < mid, 2 * units + 2 * number + side, 2 * (number - mid) + side
        )
        block = block + shift
        tile = lax.div(block, chunks)
        row = pl.multiple_of((block - tile * chunks) * depth, depth)
        return (tile, pl.ds(row, count * depth))

    def mine_at(number, side, count=1):
        return tiles.at[spot_of(number, side, 0, count)]

    def near_at(number, side):
        return tiles.at[spot_of(number, side, units)]

    def add_into(number, side, ref, start=None):
        spot = spot_of(number, side, 0)
        value = ref[...] if start is None else ref[pl.ds(start, depth), :]
        tiles[spot] = (tiles[spot].astype(f32) + value.astype(f32)).astype(bf16)

    def load(number, side):
        target, chunk = unit_of(number)
        return pltpu.make_async_copy(
            grads.at[target, 2 * side + core, window_of(chunk)],
            mine_at(number, side),
            load_sem.at[number, side],
        )

    def to_near(number, side):
        target, chunk = unit_of(number)
        return remote(
            grads.at[target, 2 * side + 1 - core, window_of(chunk)],
            near_at(number, side),
            near_send.at[number, side],
            near_recv.at[number, side],
            other_core,
        )

    def issue(number, carry):
        for side in range(2):
            to_near(number, side).start()
            load(number, side).start()
        return carry

    def issue_all(start, stop):
        lax.fori_loop(start, stop, issue, 0)

    def pair_start(number):
        turn = lax.div(number, LINE)
        _, rank = rank_of(chunks - 1 - turn)
        return pl.multiple_of((LINE * rank + number - LINE * turn) * depth, depth)

    def to_pair(number):
        return remote(
            mine_at(number, 1 - pair),
            from_pair.at[pl.ds(pair_start(number), depth)],
            far_send.at[number],
            far_recv.at[number],
            other_pair,
        )

    def arrive_near(number, side):
        load(number, side).wait()
        to_near(number, side).wait_recv()
        add_into(number, side, near_at(number, side))

    def land_slot(number, chunk, single, second):
        whole_rank, single_rank = rank_of(chunk)
        turn = chunks - 1 - chunk
        rank = number - LINE * turn
        base = 2 * LINE * whole_turns
        extra = base + LINE * paired
        if single:
            slot = base + LINE * single_rank + rank
            slot = jnp.where(second, extra + 2 * whole_turns + single_rank, slot)
        else:
            slot = 2 * (LINE * whole_rank + rank)
            slot = jnp.where(second, extra + 2 * whole_rank, slot)
        return pl.multiple_of(slot * depth, depth)

    def hop_copy(number, chunk, single, direction):
        target, _ = unit_of(number)
        second = jnp.logical_and(direction == 1, target == seq - 1)
        count = 1 if single else 2
        sems = left_recv if direction == 0 else right_recv
        return remote(
            mine_at(number, pair if single else 0, count),
            landing.at[pl.ds(land_slot(number, chunk, single, second), count * depth)],
            hop_send.at[number],
            sems.at[number],
            right if direction == 0 else left,
        )

    def take(number, chunk, single, direction):
        target, _ = unit_of(number)
        second = jnp.logical_and(direction == 1, target == seq)
        count = 1 if single else 2
        start = land_slot(number, chunk, single, second)
        sems = left_recv if direction == 0 else right_recv
        remote(
            mine_at(number, pair if single else 0, count),
            landing.at[pl.ds(start, count * depth)],
            hop_send.at[number],
            sems.at[number],
            right if direction == 0 else left,
        ).wait_recv()
        if single:
            add_into(number, pair, landing, start)
        else:
            for side in range(2):
                add_into(number, side, landing, start + side * depth)

    def late_start(chunk):
        return pl.multiple_of(2 * rank_of(chunk)[0] * depth, depth)

    def late_copy(number, chunk, single):
        if single:
            return remote(
                mine_at(number, pair),
                out.at[dp, window_of(chunk)],
                late_send.at[chunk],
                late_recv.at[chunk],
                other_pair,
            )
        return remote(
            mine_at(number, 0, 2),
            late_pair.at[pl.ds(late_start(chunk), 2 * depth)],
            late_send.at[chunk],
            late_recv.at[chunk],
            other_pair,
        )

    def share_copy(number, chunk, side, relayed):
        spot_out = out.at[2 * side + core, window_of(chunk)]
        return remote(
            spot_out if relayed else mine_at(number, side),
            spot_out,
            share_send.at[side, chunk],
            share_recv.at[side, chunk],
            other_core,
        )

    def out_copy(number, chunk, side):
        return pltpu.make_async_copy(
            mine_at(number, side), out.at[2 * side + core, window_of(chunk)], out_sem.at[side, chunk]
        )

    def at(number, condition, body):
        clipped = jnp.clip(number, 0, units - 1)
        target, chunk = unit_of(clipped)
        valid = jnp.logical_and(number >= 0, number < units)
        valid = jnp.logical_and(valid, condition(target))

        @pl.when(jnp.logical_and(valid, is_single(chunk)))
        def _():
            body(clipped, chunk, True)

        @pl.when(jnp.logical_and(valid, jnp.logical_not(is_single(chunk))))
        def _():
            body(clipped, chunk, False)

    def first_stage(number, chunk, single):
        if single:
            arrive_near(number, 1 - pair)
            to_pair(number).start()
            arrive_near(number, pair)
        else:
            for side in range(2):
                arrive_near(number, side)

    def first_body(number, carry):
        at(number, always, first_stage)
        return carry

    def second_stage(number, chunk, single):
        if single:
            to_pair(number).wait_recv()
            add_into(number, pair, from_pair, pair_start(number))

    def hop_stage(direction):
        def body(number, chunk, single):
            @pl.when(has[1 - direction])
            def _():
                take(number, chunk, single, direction)

            hop_copy(number, chunk, single, direction).start()

        return body

    def last_stage(number, chunk, single):
        for direction in range(2):

            @pl.when(has[1 - direction])
            def _():
                take(number, chunk, single, direction)

        late_copy(number, chunk, single).start()
        if single:
            out_copy(number, chunk, pair).start()
            share_copy(number, chunk, pair, False).start()

    def share_stage(number, chunk, single):
        if single:
            remote(
                mine_at(number, pair),
                out.at[dp + 2 - 4 * pair, window_of(chunk)],
                late_send.at[chunk],
                late_recv.at[chunk],
                other_pair,
            ).wait_recv()
            share_copy(number, chunk, 1 - pair, True).start()
        else:
            late_copy(number, chunk, False).wait()
            for side in range(2):
                add_into(number, side, late_pair, late_start(chunk) + side * depth)
                out_copy(number, chunk, side).start()
                share_copy(number, chunk, side, False).start()

    def hop_stages(base):
        at(base, always, second_stage)
        at(base - hop_lag * seq, lambda target: target > seq, hop_stage(0))
        at(base - hop_lag * (LINE - 1 - seq), lambda target: target < seq, hop_stage(1))
        at(base - hop_lag * far, lambda target: target == seq, last_stage)
        at(base - hop_lag * far - share_lag, lambda target: target == seq, share_stage)

    def hops(start, stop):
        def body(number, carry):
            hop_stages(number)
            return carry

        lax.fori_loop(start, stop, body, 0)

    def finish_unit(number, carry):
        for side in range(2):
            to_near(number, side).wait_send()

        def sends(number, chunk, single):
            if single:
                to_pair(number).wait_send()

        at(number, always, sends)
        at(
            number,
            lambda target: target > seq,
            lambda number, chunk, single: hop_copy(number, chunk, single, 0).wait_send(),
        )
        at(
            number,
            lambda target: target < seq,
            lambda number, chunk, single: hop_copy(number, chunk, single, 1).wait_send(),
        )

        def shared(number, chunk, single):
            if single:
                late_copy(number, chunk, True).wait_send()
                out_copy(number, chunk, pair).wait()
                share_copy(number, chunk, pair, False).wait_send()
                share_copy(number, chunk, 1 - pair, True).wait_send()
            else:
                for side in range(2):
                    out_copy(number, chunk, side).wait()
                    share_copy(number, chunk, side, False).wait_send()
            for side in range(2):
                spot_out = out.at[2 * side + 1 - core, window_of(chunk)]
                remote(
                    spot_out,
                    spot_out,
                    share_send.at[side, chunk],
                    share_recv.at[side, chunk],
                    other_core,
                ).wait_recv()

        at(number, lambda target: target == seq, shared)
        return carry

    vec_first = remote(vector, vec_core, vec_send.at[0], vec_recv.at[0], other_core)
    vec_second = remote(vec_core, vec_pair, vec_send.at[1], vec_recv.at[1], other_pair)

    def move_copy(step, source):
        goal = lax.rem(seq + step, LINE)
        return remote(
            vec_pair.at[goal],
            vec_line.at[source],
            vec_send.at[1 + step],
            vec_recv.at[2 + source],
            (pipe, goal, dp),
        )

    def vector_to_pair():
        vec_first.wait()
        vec_core[...] = vector[...] + vec_core[...]
        vec_second.start()

    def vector_to_line():
        vec_second.wait()
        vec_pair[...] = vec_core[...] + vec_pair[...]
        for step in range(1, LINE):
            move_copy(step, seq).start()
        vec_line[seq] = vec_pair[seq]

    def vector_end():
        for step in range(1, LINE):
            move_copy(step, lax.rem(seq + LINE - step, LINE)).wait()
        total_vector = vec_line[0]
        for source_of in range(1, LINE):
            total_vector = total_vector + vec_line[source_of]
        vector_out[...] = total_vector

    packed_share = width // (4 * LINE)

    def outer_terms():
        for part in range(4):
            slot = part % 2
            window = slice(part * width, (part + 1) * width)
            if part >= 2:
                down_copy(part - 2).wait()
            term = dot(hidden[:, window], branch_ffn[...], 0, 0).astype(bf16)
            stage_down[slot] = term.reshape(4, width // 4, width)
            down_copy(part).start()
        packed_terms(((normal_c, grad_up, 8 * packed_share),))
        for part in range(2, 4):
            down_copy(part).wait()

    def down_copy(part):
        return pltpu.make_async_copy(
            stage_down.at[part % 2],
            grads.at[part, :, pl.ds(12 * packed_share, width // 4)],
            stage_sems.at[2 + part % 2, 0],
        )

    def inner_terms():
        packed_terms(
            (
                (normal_b, grad_mixer_col, 4 * packed_share),
                (mixed, branch_col, 7 * packed_share),
                (normal_a, grad_mixer, 0),
                (blended, branch_row, 3 * packed_share),
            )
        )

    def packed_terms(pairs):
        waiting = [None, None]
        number = 0
        for first, second, base in pairs:
            for part in range(second.shape[1] // width):
                slot = number % 2
                if waiting[slot] is not None:
                    for copy in waiting[slot]:
                        copy.wait()
                window = slice(part * width, (part + 1) * width)
                term = dot(first[...], second[:, window], 0, 0).astype(bf16)
                stage[slot] = term.reshape(LINE, 4, packed_share, width)
                waiting[slot] = [
                    pltpu.make_async_copy(
                        stage.at[slot, target],
                        grads.at[target, :, pl.ds(base + part * packed_share, packed_share)],
                        stage_sems.at[slot, target],
                    )
                    for target in range(LINE)
                ]
                for copy in waiting[slot]:
                    copy.start()
                number += 1
        for copies in waiting:
            for copy in copies or ():
                copy.wait()

    unit, _ = unit_rows(source[...].reshape(tokens, width).astype(f32))
    normal_a[...] = (unit * gain_of(0) + bias_of(0)).astype(bf16)
    gather(2, 3)
    ready(0)
    for part in range(3):
        window = slice(part * width, (part + 1) * width)
        mixer[:, window] = dot(normal_a[...], tiles[part], 1, 0).astype(bf16)
    logit_factor = 1.0 / (math.sqrt(size) * math.sqrt(total_rows))
    logit_copies = []
    for couple in range(couples):
        partial_value = logit_factor * dot(
            both(mixer, couple * twin), stacked(mixer, width + couple * twin), 1, 1
        )
        logit_send[couple] = partial_value.astype(bf16)
        copy = to_core(logit_send.at[couple], logit_recv.at[couple], logit_sems, couple)
        copy.start()
        logit_copies.append(copy)
    gather(4)
    valid = (
        lax.broadcasted_iota(jnp.int32, (columns, 1), 0).astype(f32) < counts_in[0, 0:1, 0:1]
    ).astype(f32)
    disorder = jnp.zeros((columns, 1), f32)
    for couple in range(couples):
        logit_copies[couple].wait_recv()
        wide = logit_send[couple].astype(f32) + logit_recv[couple].astype(f32)
        shares = []
        for half in range(2):
            logits = wide[:, half * columns : (half + 1) * columns]
            shifted_logits = logits - jnp.max(logits, axis=-1, keepdims=True)
            powers = jnp.exp(shifted_logits)
            total = jnp.sum(powers, axis=-1, keepdims=True)
            logs = shifted_logits - jnp.log(total)
            share = powers / total
            log_share[couple, :, half * columns : (half + 1) * columns] = logs
            disorder = disorder - jnp.sum(share * logs, axis=-1, keepdims=True) * valid
            shares.append(share.astype(bf16))
        put(
            blended,
            couple * twin,
            dot(
                jnp.concatenate(shares, axis=1), stacked(mixer, 2 * width + couple * twin), 1, 0
            ),
        )
    cost[...] = jnp.broadcast_to(
        jnp.sum(disorder, axis=0, keepdims=True) / float(heads * columns), cost.shape
    )
    ready(1)
    after_row[...] = source[...].reshape(tokens, width).astype(f32) + dot(blended[...], tiles[3], 1, 0)
    unit, _ = unit_rows(after_row[...])
    normal_b[...] = (unit * gain_of(1) + bias_of(1)).astype(bf16)
    gather(5)
    ready(2)
    keys_copies = []
    for part in (1, 2, 0):
        window = slice(part * width, (part + 1) * width)
        mixer_col[:, window] = dot(normal_b[...], tiles[4 + part], 1, 0).astype(bf16)
        if part > 0:
            copy = to_core(
                mixer_col.at[:, window], keys_recv.at[part - 1], keys_sems, part - 1
            )
            copy.start()
            keys_copies.append(copy)

    def line_of(part, place_of):
        if place_of < 2:
            rows_of = slice(place_of * columns, (place_of + 1) * columns)
            return mixer_col[rows_of, (1 + part) * width : (2 + part) * width]
        rows_of = slice((place_of - 2) * columns, (place_of - 1) * columns)
        return keys_recv[part, rows_of, :]

    def sums_by_head(wide_ref, start, line):
        products = [
            wide_ref[index * columns : (index + 1) * columns, start : start + width] * line
            for index in range(2)
        ]
        return dot(jnp.concatenate(products, axis=0), segment[...], 1, 0)

    def spread_heads(narrow):
        return dot(narrow, spread[...], 1, 0)

    gather(6)
    scores = []
    for place_of in range(4):
        if place_of == 2:
            keys_copies[0].wait_recv()
        scores.append(sums_by_head(mixer_col, 0, line_of(0, place_of)) / math.sqrt(size))
    highest = functools.reduce(jnp.maximum, scores)
    powers = [jnp.exp(score - highest) for score in scores]
    total = functools.reduce(jnp.add, powers)
    keys_copies[1].wait_recv()
    gathered_mix = None
    for place_of in range(4):
        share = powers[place_of] / total
        col_share[place_of] = share
        wide = spread_heads(share.astype(bf16))
        line = line_of(1, place_of).astype(f32)
        term = jnp.concatenate([wide[0:columns] * line, wide[columns:] * line], axis=0)
        gathered_mix = term if gathered_mix is None else gathered_mix + term
    mixed[...] = gathered_mix.astype(bf16)
    ready(3)
    after_col[...] = after_row[...] + dot(mixed[...], tiles[7], 1, 0)
    unit, _ = unit_rows(after_col[...])
    normal_c[...] = (unit * gain_of(2) + bias_of(2)).astype(bf16)
    gather(7)
    ready(4)
    parts = hidden.shape[1] // width
    result = after_col[...]
    for part in range(parts):
        if part == 2:
            gather(8)
        window = slice(part * width, (part + 1) * width)
        upward = dot(normal_c[...], tiles[8 + part], 1, 0)
        inner = 0.5 + 0.5 * lax.erf(upward * math.sqrt(0.5))
        density = jnp.exp(-0.5 * upward * upward) * (1.0 / math.sqrt(2.0 * math.pi))
        hidden[:, window] = (upward * inner).astype(bf16)
        slope[:, window] = (inner + upward * density).astype(bf16)
    gather(9)
    ready(5)
    ready(6)
    for part in range(parts):
        window = slice(part * width, (part + 1) * width)
        result = result + dot(hidden[:, window], tiles[12 + part], 1, 0)
    act[...] = result.astype(bf16).reshape(2, columns, width)

    @pl.when(pipe == 0)
    def _():
        send_on.start()

    start_act()

    @pl.when(sender)
    def _():
        cost_own.start()
        for copy in cost_copies:
            copy.start()

    @pl.when(pipe == 1)
    def _():
        finish_sensitivity()
        finish_factor()
        for index in range(2):
            total_grad[index * columns : (index + 1) * columns, :] = (
                sensitivity[index].astype(f32) * factor_in[index, :, 0:1]
            )

    @pl.when(pipe == 0)
    def _():
        for index in range(pieces):
            drain(index)
        send_back.wait_recv()
        total_grad[...] = grad_in[...].reshape(tokens, width).astype(f32)

    branch_ffn[...] = total_grad[...].astype(bf16)
    grad_normal = None
    for part in range(parts):
        window = slice(part * width, (part + 1) * width)
        grad_hidden = dot(branch_ffn[...], tiles[12 + part], 1, 1)
        grad_up[:, window] = (grad_hidden * slope[:, window].astype(f32)).astype(bf16)
        term = dot(grad_up[:, window], tiles[8 + part], 1, 1)
        grad_normal = term if grad_normal is None else grad_normal + term
    pl.semaphore_signal(clear_sem, inc=1, device_id=other_core, device_id_type=MESH)

    @pl.when(jnp.logical_not(later))
    def _():
        outer_terms()
        pl.semaphore_wait(clear_sem, 1)
        issue_all(0, mid)

    term, gain, bias = unit_rows_back(grad_normal, after_col[...], gain_of(2))
    keep_vector(2, gain, bias)
    total_grad[...] = total_grad[...] + term
    branch_col[...] = total_grad[...].astype(bf16)
    grad_mixed = dot(branch_col[...], tiles[7], 1, 1).astype(bf16)
    grad_probs = []
    for place_of in range(4):
        line = line_of(1, place_of)
        products = [grad_mixed[0:columns] * line, grad_mixed[columns:] * line]
        grad_probs.append(dot(jnp.concatenate(products, axis=0), segment[...], 1, 0))
    inner = functools.reduce(
        jnp.add, [col_share[place_of] * grad_probs[place_of] for place_of in range(4)]
    )
    root_size = math.sqrt(size)
    grad_query = None
    local_terms = []
    back_copies = []
    grad_lines = grad_mixed.astype(f32)
    query_lines = mixer_col[:, 0:width].astype(f32)
    for place_of in (2, 3, 0, 1):
        share = col_share[place_of]
        narrow = (share * (grad_probs[place_of] - inner)).astype(bf16)
        wide = spread_heads(narrow)
        line = line_of(0, place_of).astype(f32)
        term = jnp.concatenate([wide[0:columns] * line, wide[columns:] * line], axis=0)
        grad_query = term if grad_query is None else grad_query + term
        key_term = wide[0:columns] * query_lines[0:columns] + wide[columns:] * query_lines[columns:]
        key_term = key_term / root_size
        wide = spread_heads(share.astype(bf16))
        value_term = wide[0:columns] * grad_lines[0:columns] + wide[columns:] * grad_lines[columns:]
        if place_of >= 2:
            index = place_of - 2
            rows_of = slice(index * columns, (index + 1) * columns)
            keys_send[rows_of, 0:width] = key_term.astype(bf16)
            keys_send[rows_of, width:] = value_term.astype(bf16)
            copy = to_core(keys_send.at[rows_of, :], keys_back.at[rows_of, :], back_sems, index)
            copy.start()
            back_copies.append(copy)
        else:
            local_terms.append((key_term, value_term))
    grad_mixer_col[:, 0:width] = (grad_query / root_size).astype(bf16)
    for place_of in range(2):
        back_copies[place_of].wait()
        rows_of = slice(place_of * columns, (place_of + 1) * columns)
        for part in range(2):
            window = slice(part * width, (part + 1) * width)
            grad_mixer_col[rows_of, (1 + part) * width : (2 + part) * width] = (
                local_terms[place_of][part] + keys_back[rows_of, window].astype(f32)
            ).astype(bf16)

    @pl.when(jnp.logical_not(later))
    def _():
        lax.fori_loop(0, mid, first_body, 0)
        hops(0, EARLY)

    grad_normal = None
    for part in range(3):
        window = slice(part * width, (part + 1) * width)
        term = dot(grad_mixer_col[:, window], tiles[4 + part], 1, 1)
        grad_normal = term if grad_normal is None else grad_normal + term
    term, gain, bias = unit_rows_back(grad_normal, after_row[...], gain_of(1))
    keep_vector(1, gain, bias)
    total_grad[...] = total_grad[...] + term
    branch_row[...] = total_grad[...].astype(bf16)
    keys_send[:, 0:width] = dot(branch_row[...], tiles[3], 1, 1).astype(bf16)
    probs_copies = []
    for couple in range(couples):
        partial_value = dot(
            both(keys_send, couple * twin), stacked(mixer, 2 * width + couple * twin), 1, 1
        )
        probs_send[couple] = partial_value.astype(bf16)
        copy = to_core(probs_send.at[couple], probs_recv.at[couple], probs_sems, couple)
        copy.start()
        probs_copies.append(copy)

    pl.when(jnp.logical_not(later))(lambda: hops(EARLY, EARLY + MIDDLE))
    column_weight = (float(total_rows * columns) / float(heads * columns)) * valid
    for couple in range(couples):
        start = couple * twin
        logs = log_share[couple]
        share = jnp.exp(logs)
        grad_wide = both(keys_send, start)
        put(
            grad_mixer,
            2 * width + start,
            unstack(dot(share.astype(bf16), grad_wide, 0, 0)),
        )
        probs_copies[couple].wait_recv()
        wide = probs_send[couple].astype(f32) + probs_recv[couple].astype(f32)
        pieces = []
        for half in range(2):
            window = slice(half * columns, (half + 1) * columns)
            part_share, part_logs, part_grad = (share[:, window], logs[:, window], wide[:, window])
            entropy = -jnp.sum(part_share * part_logs, axis=-1, keepdims=True)
            inner = jnp.sum(part_share * part_grad, axis=-1, keepdims=True)
            piece = part_share * (part_grad - inner)
            piece = piece - column_weight * part_share * (part_logs + entropy)
            pieces.append(piece.astype(bf16))
        grad_logits = jnp.concatenate(pieces, axis=1)
        put(
            grad_mixer,
            start,
            logit_factor * dot(grad_logits, stacked(mixer, width + start), 1, 0),
        )
        put(
            grad_mixer,
            width + start,
            logit_factor * unstack(dot(grad_logits, both(mixer, start), 0, 0)),
        )
    grad_normal = None
    for part in range(3):
        window = slice(part * width, (part + 1) * width)
        term = dot(grad_mixer[:, window], tiles[part], 1, 1)
        grad_normal = term if grad_normal is None else grad_normal + term
    term, gain, bias = unit_rows_back(grad_normal, source[...].reshape(tokens, width).astype(f32), gain_of(0))
    keep_vector(0, gain, bias)
    der[...] = (total_grad[...] + term).astype(bf16).reshape(2, columns, width)

    @pl.when(pipe == 1)
    def _():
        send_back.start()

    vec_first.start()

    @pl.when(later)
    def _():
        start_der()

    @pl.when(jnp.logical_not(later))
    def _():
        der_over.start()

    @pl.when(later)
    def _():
        outer_terms()
        pl.semaphore_wait(clear_sem, 1)
        issue_all(0, mid)
        lax.fori_loop(0, mid, first_body, 0)
        hops(0, EARLY + MIDDLE)

    hops(EARLY + MIDDLE, EARLY + MORE)
    inner_terms()
    issue_all(mid, units)
    vector_to_pair()

    def mix(number, carry):
        for index in range(AT_ONCE):
            at(mid + AT_ONCE * number + index, always, first_stage)
        hop_stages(EARLY + MORE + number)
        return carry

    lax.fori_loop(0, mid // AT_ONCE, mix, 0)

    @pl.when(later)
    def _():
        der_over.wait_recv()
        start_back()

    hops(EARLY + MORE + mid // AT_ONCE, units)
    vector_to_line()
    hops(units, units + hop_lag * (LINE - 1) + share_lag)
    vector_end()
    lax.fori_loop(0, units, finish_unit, 0)
    for copy in logit_copies + keys_copies + probs_copies:
        copy.wait_send()

    @pl.when(pipe == 0)
    def _():
        send_on.wait_send()

    @pl.when(pipe == 1)
    def _():
        send_back.wait_send()

    finish_act()

    @pl.when(later)
    def _():
        finish_back()
        der_home.start()
        finish_der()
        der_home.wait_send()

    @pl.when(jnp.logical_not(later))
    def _():
        der_over.wait_send()
        der_home.wait_recv()

    @pl.when(sender)
    def _():
        cost_own.wait()
        for copy in cost_copies:
            copy.wait_send()

    for index in range(2):

        @pl.when(2 * core + index != seq)
        def _():
            remote(
                cost, cost_out.at[index], cost_send.at[0], cost_recv.at[index], other_core
            ).wait_recv()


def run_layers(shards, families, upstream, order, quarters, tally, norms):
    columns, width = families.shape[2:]
    tokens = 2 * columns
    couples = HEAD_TALLY // 2
    wide = shards[4].shape[2]
    entry = jax.ShapeDtypeStruct((2, columns, width), families.dtype)
    sizes = sum(shard.size for shard in shards) * LINE // (width * width)
    depth = width // 6
    block = lambda count: pltpu.VMEM((count * depth, width), bf16)
    anywhere = pl.BlockSpec(memory_space=pl.ANY)
    inside = pl.BlockSpec(memory_space=pltpu.VMEM)
    scalars = pl.BlockSpec(memory_space=pltpu.SMEM)
    dma = pltpu.SemaphoreType.DMA
    bf16, f32 = (jnp.bfloat16, jnp.float32)
    rows_of = lambda columns_of, kind=bf16: pltpu.VMEM((tokens, columns_of), kind)
    scores = pltpu.VMEM((couples, columns, 2 * columns), bf16)
    return pl.pallas_call(
        layers_kernel,
        out_shape=[
            jax.ShapeDtypeStruct(entry.shape, bf16),
            jax.ShapeDtypeStruct(entry.shape, bf16),
            jax.ShapeDtypeStruct((2, 8, 128), f32),
            jax.ShapeDtypeStruct((8, 256), f32),
            jax.ShapeDtypeStruct((LINE, 4, width, width), bf16),
            jax.ShapeDtypeStruct((4, width, width), bf16),
        ],
        in_specs=[anywhere] * 6 + [inside, inside, scalars, inside, scalars, inside],
        out_specs=[anywhere, anywhere, inside, inside, anywhere, anywhere],
        scratch_shapes=[
            pltpu.VMEM((sizes, width, width), bf16),
            pltpu.VMEM(entry.shape, bf16),
            rows_of(width),
            rows_of(width),
            rows_of(width),
            rows_of(3 * width),
            rows_of(3 * width),
            rows_of(width),
            rows_of(width),
            rows_of(width, f32),
            rows_of(width, f32),
            pltpu.VMEM((couples, columns, 2 * columns), f32),
            pltpu.VMEM((4, tokens, 128), f32),
            rows_of(wide),
            rows_of(wide),
            rows_of(width, f32),
            pltpu.VMEM(entry.shape, bf16),
            rows_of(width),
            rows_of(width),
            rows_of(width),
            rows_of(wide),
            rows_of(3 * width),
            rows_of(3 * width),
            scores,
            scores,
            pltpu.VMEM((2, tokens, width), bf16),
            rows_of(2 * width),
            rows_of(2 * width),
            scores,
            scores,
            pltpu.VMEM((2, columns, 2 * columns), bf16),
            pltpu.VMEM((width, 128), bf16),
            pltpu.VMEM((128, width), bf16),
            pltpu.VMEM((2, LINE, 4, width // (4 * LINE), width), bf16),
            pltpu.VMEM((2, 4, width // 4, width), bf16),
            pltpu.VMEM(entry.shape, bf16),
            pltpu.VMEM(entry.shape, bf16),
            pltpu.VMEM((8, 128), f32),
            pltpu.VMEM(entry.shape, bf16),
            pltpu.VMEM(entry.shape, bf16),
            pltpu.VMEM(entry.shape, bf16),
            pltpu.VMEM((2, columns, columns), f32),
            pltpu.VMEM((2, columns, columns), f32),
            pltpu.VMEM((2, 8, 128), f32),
            pltpu.VMEM((2, 8, 128), f32),
            pltpu.VMEM((LINE, 8, 256), f32),
            pltpu.VMEM((8, width), f32),
            dma((6,)),
            dma((2, LINE, PIECES)),
            dma((LINE, PIECES)),
            dma((LINE, PIECES)),
            dma((LINE, PIECES)),
            dma((2, LINE, PIECES)),
            dma((2, LINE, PIECES)),
            dma((8, 2)),
            dma((4,)),
            dma((LINE - 1,)),
            dma((LINE,)),
            block(40),
            block(16),
            block(4),
            pltpu.VMEM(entry.shape, bf16),
            pltpu.SemaphoreType.REGULAR,
            pltpu.VMEM((LINE, 8, 256), f32),
            pltpu.VMEM((LINE, 8, 256), f32),
            pltpu.VMEM((LINE, 8, 256), f32),
            pltpu.VMEM((LINE, 8, 256), f32),
            dma((24, 2)),
            dma((24, 2)),
            dma((24, 2)),
            dma((24,)),
            dma((24,)),
            dma((24,)),
            dma((24,)),
            dma((24,)),
            dma((6,)),
            dma((6,)),
            dma((2, 6)),
            dma((2, 6)),
            dma((2, 6)),
            dma((2 + LINE,)),
            dma((2 + LINE,)),
            dma((2, couples)),
            dma((2, 2)),
            dma((2, 2)),
            dma((2, couples)),
            dma((10,)),
            dma((4, LINE)),
            dma((6, 2)),
            dma((4,)),
            dma((LINE - 1,)),
            dma((2,)),
        ],
        compiler_params=pltpu.CompilerParams(
            collective_id=2, has_side_effects=True, vmem_limit_bytes=63 * 2**20
        ),
        name="two_layers",
    )(*shards, families, upstream, order, quarters, tally, norms)


def unpack_kernel(blocks, act, der, costs, *refs):
    results, act_out, der_out, cost_out = (refs[:6], *refs[6:])
    width = blocks.shape[2]
    base = 0
    for result in results:
        depth, wide = result.shape[1:]
        for part in range(wide // width):
            result[0, :, part * width : (part + 1) * width] = blocks[
                0, base : base + depth, :
            ].astype(jnp.float32)
            base += depth
    act_out[0, :, 0] = act[...]
    der_out[0, :, 0] = der[...]
    cost_out[...] = jnp.concatenate([costs[0, 0:1, 0:1], costs[1, 0:1, 0:1]], axis=1)


def unpack_all(blocks, act, der, costs, shapes):
    columns, width = act.shape[1:]
    large = jax.ShapeDtypeStruct((1, 2, 1, columns, width), act.dtype)
    part = pl.BlockSpec((2, columns // 4, width), lambda step: (0, step, 0))
    wide = pl.BlockSpec((1, 2, 1, columns // 4, width), lambda step: (0, 0, 0, step, 0))
    return pl.pallas_call(
        unpack_kernel,
        grid=(4,),
        out_shape=[jax.ShapeDtypeStruct((1,) + shape, jnp.float32) for shape in shapes]
        + [large, large, jax.ShapeDtypeStruct((1, 2), jnp.float32)],
        in_specs=[
            pl.BlockSpec((1,) + blocks.shape[1:], lambda step: (step, 0, 0)),
            part,
            part,
            pl.BlockSpec(costs.shape, lambda step: (0, 0, 0)),
        ],
        out_specs=[
            pl.BlockSpec((1, shape[0] // 4, shape[1]), lambda step: (0, step, 0))
            for shape in shapes
        ]
        + [wide, wide, pl.BlockSpec((1, 2), lambda step: (0, 0))],
        compiler_params=pltpu.CompilerParams(vmem_limit_bytes=60 * 2**20),
        cost_estimate=pl.CostEstimate(
            flops=blocks.size, bytes_accessed=6 * blocks.size, transcendentals=0
        ),
        name="unpack_grads",
    )(blocks, act, der, costs)


def on_device_lined(
    embedded_families,
    order,
    token_quarter_factor,
    genuine_residue_tally,
    standardizer_scales,
    standardizer_offsets,
    row_qkv,
    row_out,
    col_qkv,
    col_out,
    ffn_up,
    ffn_down,
    upstream_sensitivity,
):
    model_width = embedded_families.shape[-1]
    share = standardizer_scales.shape[-1]
    shards = (row_qkv, row_out, col_qkv, col_out, ffn_up, ffn_down)
    norms = jnp.pad(
        jnp.concatenate([standardizer_scales[0], standardizer_offsets[0]], axis=0),
        ((0, 2), (0, 256 - share)),
    )
    activations, derivs, costs, vector, _, out = run_layers(
        shards,
        embedded_families,
        upstream_sensitivity,
        order,
        token_quarter_factor,
        genuine_residue_tally,
        norms,
    )
    *results, activations, derivs, costs = unpack_all(
        out, activations, derivs, costs, [shard.shape[1:] for shard in shards]
    )
    return (
        activations,
        derivs,
        costs,
        *results,
        vector[None, 0:3, :share],
        vector[None, 3:6, :share],
    )


def solution(mesh):
    in_specs = (
        P("dp", "seq", None, None),
        P("dp", None),
        P("dp", "seq", None),
        P("dp"),
        P("pipe", None, "seq"),
        P("pipe", None, "seq"),
        P("pipe", "seq", None),
        P("pipe", "seq", None),
        P("pipe", "seq", None),
        P("pipe", "seq", None),
        P("pipe", "seq", None),
        P("pipe", "seq", None),
        P("dp", "seq", None, None),
    )
    out_specs = (
        P("pipe", "dp", "seq", None, None),
        P("pipe", "dp", "seq", None, None),
        P("pipe", "dp"),
        P("pipe", "seq", None),
        P("pipe", "seq", None),
        P("pipe", "seq", None),
        P("pipe", "seq", None),
        P("pipe", "seq", None),
        P("pipe", "seq", None),
        P("pipe", None, "seq"),
        P("pipe", None, "seq"),
    )
    lined = mesh.shape["seq"] == LINE and mesh.shape["dp"] == 4 and mesh.shape["pipe"] == 2
    return jax.shard_map(
        on_device_lined if lined else on_device, mesh=mesh, in_specs=in_specs, out_specs=out_specs, check_vma=False
    )
```

```python
import functools
import math

import jax
import jax.numpy as jnp
from jax import lax
from jax.experimental import pallas as pl
from jax.experimental.pallas import tpu as pltpu
from jax.sharding import PartitionSpec as P

HEAD_TALLY = 12
LINE = 4
MESH = pl.DeviceIdType.MESH
EARLY = 4
AT_ONCE = 2
MIDDLE = 0
MORE = 2
PIECES = 7


norm_epsilon = 1e-05


def shifted(value, axis, steps):
    count = lax.axis_size(axis)
    initial, last = (max(0, -steps), min(count, count - steps))
    return lax.ppermute(value, axis, [(source, source + steps) for source in range(initial, last)])


def normed(values, gain_row, bias_row):
    average = jnp.mean(values, axis=-1, keepdims=True)
    centered = values - average
    variance = jnp.mean(centered * centered, axis=-1, keepdims=True)
    return centered * lax.rsqrt(variance + norm_epsilon) * gain_row + bias_row


def gelu_exact(values):
    return jax.nn.gelu(values, approximate=False)


def product(left, weight):
    return lax.dot_general(
        left, weight, (((left.ndim - 1,), (0,)), ((), ())), preferred_element_type=jnp.float32
    )


def product_back(left, weight):
    return lax.dot_general(
        left, weight, (((left.ndim - 1,), (1,)), ((), ())), preferred_element_type=jnp.float32
    )


def weight_term(left, right):
    return lax.dot_general(
        left, right, (((0, 1), (0, 1)), ((), ())), preferred_element_type=jnp.float32
    )


def split_heads(values, head_count):
    return values.reshape(values.shape[:-1] + (head_count, values.shape[-1] // head_count))


def choose(flag, first_tree, second_tree):
    return jax.tree.map(lambda early, later: jnp.where(flag, early, later), first_tree, second_tree)


def column_scores(queries, key_rows, head_count):
    query_heads = split_heads(queries, head_count)
    raw = jnp.einsum(
        "rche,sche->chrs",
        query_heads,
        split_heads(key_rows, head_count),
        preferred_element_type=jnp.float32,
    )
    return raw / math.sqrt(query_heads.shape[-1])


def column_forward(queries, key_rows, content_lines, head_count):
    scores = column_scores(queries, key_rows, head_count)
    log_total = jax.nn.logsumexp(scores, axis=-1)
    vertical_factors = jnp.exp(scores - log_total[..., None]).astype(jnp.bfloat16)
    mixed_cols = jnp.einsum(
        "gmqi,igmu->qgmu",
        vertical_factors,
        split_heads(content_lines, head_count),
        preferred_element_type=jnp.float32,
    )
    return (mixed_cols.reshape(queries.shape).astype(jnp.bfloat16), log_total)


def column_backward(queries, key_rows, content_lines, log_total, grad_mixed, head_count):
    scores = column_scores(queries, key_rows, head_count)
    softmax_share = jnp.exp(scores - log_total[..., None])
    grad_heads = split_heads(grad_mixed, head_count)
    grad_probs = jnp.einsum(
        "rche,sche->chrs",
        grad_heads,
        split_heads(content_lines, head_count),
        preferred_element_type=jnp.float32,
    )
    grad_values = jnp.einsum(
        "chrs,rche->sche",
        softmax_share.astype(jnp.bfloat16),
        grad_heads,
        preferred_element_type=jnp.float32,
    )
    grad_scores = (
        softmax_share * (grad_probs - jnp.sum(softmax_share * grad_probs, axis=-1, keepdims=True))
    ).astype(jnp.bfloat16)
    root_size = math.sqrt(queries.shape[-1] // head_count)
    grad_queries = (
        jnp.einsum(
            "gmqi,igmu->qgmu",
            grad_scores,
            split_heads(key_rows, head_count),
            preferred_element_type=jnp.float32,
        )
        / root_size
    )
    grad_keys = (
        jnp.einsum(
            "chrs,rche->sche",
            grad_scores,
            split_heads(queries, head_count),
            preferred_element_type=jnp.float32,
        )
        / root_size
    )
    return (
        grad_queries.reshape(queries.shape),
        grad_keys.reshape(key_rows.shape),
        grad_values.reshape(content_lines.shape),
    )


def row_split(horizontal_mixer, model_width, head_count):
    queries = split_heads(horizontal_mixer[..., :model_width], head_count)
    key_rows = split_heads(horizontal_mixer[..., model_width : 2 * model_width], head_count)
    content_lines = split_heads(horizontal_mixer[..., 2 * model_width :], head_count)
    return (queries, key_rows, content_lines)


def layer_forward(source_rows, family_residues, projection_tables, head_count):
    (
        horizontal_coefficients,
        w_row_out,
        vertical_coefficients,
        w_col_out,
        w_up,
        w_down,
        gain_rows,
        bias_rows,
    ) = projection_tables
    row_count, columns, model_width = source_rows.shape
    total_rows = row_count * lax.axis_size("seq")
    start = source_rows.astype(jnp.float32)
    layernorm_first = normed(start, gain_rows[0], bias_rows[0]).astype(jnp.bfloat16)
    horizontal_mixer = product(layernorm_first, horizontal_coefficients).astype(jnp.bfloat16)
    queries, key_rows, content_lines = row_split(horizontal_mixer, model_width, head_count)
    logit_factor = 1.0 / (math.sqrt(model_width // head_count) * math.sqrt(total_rows))
    partial_value = logit_factor * jnp.einsum(
        "rihe,rjhe->hij", queries, key_rows, preferred_element_type=jnp.float32
    )
    logits = lax.psum(partial_value.astype(jnp.bfloat16), "seq").astype(jnp.float32)
    softmax_share = jax.nn.softmax(logits, axis=-1)
    log_probs = jax.nn.log_softmax(logits, axis=-1)
    entropy = -jnp.sum(softmax_share * log_probs, axis=-1)
    valid_residues = (jnp.arange(columns, dtype=jnp.int32) < family_residues).astype(jnp.float32)
    disorder_cost = jnp.sum(entropy * valid_residues[None, :]) / float(head_count * columns)
    blended_lines = jnp.einsum(
        "vyp,opvl->oyvl",
        softmax_share.astype(jnp.bfloat16),
        content_lines,
        preferred_element_type=jnp.float32,
    )
    blended_lines = blended_lines.reshape(row_count, columns, model_width).astype(jnp.bfloat16)
    after_row = start + product(blended_lines, w_row_out)
    layernorm_second = normed(after_row, gain_rows[1], bias_rows[1]).astype(jnp.bfloat16)
    vertical_mixer = product(layernorm_second, vertical_coefficients).astype(jnp.bfloat16)
    everyone = lax.all_gather(vertical_mixer[..., model_width:], "seq", axis=0, tiled=True)
    mixed_values, log_total = column_forward(
        vertical_mixer[..., :model_width],
        everyone[..., :model_width],
        everyone[..., model_width:],
        head_count,
    )
    column_state = (everyone, log_total)
    after_col = after_row + product(mixed_values, w_col_out)
    normal_c = normed(after_col, gain_rows[2], bias_rows[2]).astype(jnp.bfloat16)
    upward = product(normal_c, w_up)
    hidden = gelu_exact(upward).astype(jnp.bfloat16)
    result = after_col + product(hidden, w_down)
    kept_state = (
        source_rows,
        layernorm_first,
        horizontal_mixer,
        logits,
        blended_lines,
        after_row,
        layernorm_second,
        vertical_mixer,
        column_state,
        mixed_values,
        after_col,
        normal_c,
        upward,
        hidden,
    )
    return (result.astype(jnp.bfloat16), disorder_cost, kept_state)


def layer_backward(kept_state, family_residues, grad_result, projection_tables, head_count):
    (
        horizontal_coefficients,
        w_row_out,
        vertical_coefficients,
        w_col_out,
        w_up,
        w_down,
        gain_rows,
        bias_rows,
    ) = projection_tables
    (
        source_rows,
        layernorm_first,
        horizontal_mixer,
        logits,
        blended_lines,
        after_row,
        layernorm_second,
        vertical_mixer,
        column_state,
        mixed_values,
        after_col,
        normal_c,
        upward,
        hidden,
    ) = kept_state
    row_count, columns, model_width = source_rows.shape
    total_rows = row_count * lax.axis_size("seq")
    grad_branch_ffn = grad_result.astype(jnp.bfloat16)
    grad_hidden = product_back(grad_branch_ffn, w_down)
    grad_upward = jax.vjp(gelu_exact, upward)[1](grad_hidden)[0].astype(jnp.bfloat16)
    grad_normal_c = product_back(grad_upward, w_up)
    from_norm, gain_last, bias_last = jax.vjp(normed, after_col, gain_rows[2], bias_rows[2])[1](
        grad_normal_c
    )
    grad_col = grad_result + from_norm
    grad_branch_col = grad_col.astype(jnp.bfloat16)
    grad_attended = product_back(grad_branch_col, w_col_out).astype(jnp.bfloat16)
    everyone, log_total = column_state
    grad_query_col, grad_key_col, grad_value_col = column_backward(
        vertical_mixer[..., :model_width],
        everyone[..., :model_width],
        everyone[..., model_width:],
        log_total,
        grad_attended,
        head_count,
    )
    grad_kv_rows = lax.psum_scatter(
        jnp.concatenate([grad_key_col, grad_value_col], axis=-1).astype(jnp.bfloat16),
        "seq",
        scatter_dimension=0,
        tiled=True,
    ).astype(jnp.float32)
    grad_col_proj = jnp.concatenate([grad_query_col, grad_kv_rows], axis=-1).astype(jnp.bfloat16)
    grad_normal_b = product_back(grad_col_proj, vertical_coefficients)
    from_norm, gain_middle, bias_middle = jax.vjp(normed, after_row, gain_rows[1], bias_rows[1])[1](
        grad_normal_b
    )
    grad_row = grad_col + from_norm
    grad_branch_row = grad_row.astype(jnp.bfloat16)
    grad_mixed = split_heads(
        product_back(grad_branch_row, w_row_out).astype(jnp.bfloat16), head_count
    )
    queries, key_rows, content_lines = row_split(horizontal_mixer, model_width, head_count)
    softmax_share = jax.nn.softmax(logits, axis=-1)
    log_probs = jax.nn.log_softmax(logits, axis=-1)
    entropy = -jnp.sum(softmax_share * log_probs, axis=-1)
    partial_value = jnp.einsum(
        "rihe,rjhe->hij", grad_mixed, content_lines, preferred_element_type=jnp.float32
    )
    grad_probs = lax.psum(partial_value.astype(jnp.bfloat16), "seq").astype(jnp.float32)
    grad_values = jnp.einsum(
        "hij,rihe->rjhe",
        softmax_share.astype(jnp.bfloat16),
        grad_mixed,
        preferred_element_type=jnp.float32,
    )
    valid_residues = (jnp.arange(columns, dtype=jnp.int32) < family_residues).astype(jnp.float32)
    column_weight = float(total_rows * columns) * valid_residues / float(head_count * columns)
    grad_logits = softmax_share * (
        grad_probs - jnp.sum(softmax_share * grad_probs, axis=-1, keepdims=True)
    )
    grad_logits = grad_logits - column_weight[None, :, None] * softmax_share * (
        log_probs + entropy[..., None]
    )
    grad_logits = grad_logits.astype(jnp.bfloat16)
    logit_factor = 1.0 / (math.sqrt(model_width // head_count) * math.sqrt(total_rows))
    grad_queries = logit_factor * jnp.einsum(
        "vyp,opvl->oyvl", grad_logits, key_rows, preferred_element_type=jnp.float32
    )
    grad_keys = logit_factor * jnp.einsum(
        "hij,rihe->rjhe", grad_logits, queries, preferred_element_type=jnp.float32
    )
    grad_row_proj = jnp.concatenate(
        [
            grad_queries.reshape(row_count, columns, model_width),
            grad_keys.reshape(row_count, columns, model_width),
            grad_values.reshape(row_count, columns, model_width),
        ],
        axis=-1,
    ).astype(jnp.bfloat16)
    grad_normal_a = product_back(grad_row_proj, horizontal_coefficients)
    from_norm, gain_first, bias_first = jax.vjp(
        normed, source_rows.astype(jnp.float32), gain_rows[0], bias_rows[0]
    )[1](grad_normal_a)
    grad_source = (grad_row + from_norm).astype(jnp.bfloat16)
    operand_pairs = (
        (layernorm_first, grad_row_proj),
        (blended_lines, grad_branch_row),
        (layernorm_second, grad_col_proj),
        (mixed_values, grad_branch_col),
        (normal_c, grad_upward),
        (hidden, grad_branch_ffn),
    )
    norm_grads = (
        jnp.stack([gain_first, gain_middle, gain_last]),
        jnp.stack([bias_first, bias_middle, bias_last]),
    )
    return (grad_source, operand_pairs, norm_grads)


def on_device(
    embedded_families,
    order,
    token_quarter_factor,
    genuine_residue_tally,
    standardizer_scales,
    standardizer_offsets,
    row_qkv,
    row_out,
    col_qkv,
    col_out,
    ffn_up,
    ffn_down,
    upstream_sensitivity,
):
    head_count = HEAD_TALLY
    segment_place = lax.axis_index("pipe")
    gathered = (
        lax.all_gather(row_qkv, "seq", axis=1, tiled=True),
        lax.all_gather(row_out, "seq", axis=1, tiled=True),
        lax.all_gather(col_qkv, "seq", axis=1, tiled=True),
        lax.all_gather(col_out, "seq", axis=1, tiled=True),
        lax.all_gather(ffn_up, "seq", axis=1, tiled=True),
        lax.all_gather(ffn_down, "seq", axis=1, tiled=True),
        lax.all_gather(standardizer_scales.astype(jnp.bfloat16), "seq", axis=2, tiled=True).astype(
            standardizer_scales.dtype
        ),
        lax.all_gather(standardizer_offsets.astype(jnp.bfloat16), "seq", axis=2, tiled=True).astype(
            standardizer_offsets.dtype
        ),
    )
    projection_tables = tuple((gathered_piece[0] for gathered_piece in gathered))
    small_batch_number = embedded_families.shape[0]
    sequence = order[0]
    received = jnp.zeros(embedded_families.shape[1:], jnp.bfloat16)
    results = []
    focus_spread_levies = []
    kept_list = []
    for period in range(small_batch_number + 1):
        slot_here = jnp.clip(period - segment_place, 0, small_batch_number - 1)
        align_here = sequence[slot_here]
        source_rows = jnp.where(segment_place == 0, embedded_families[align_here], received)
        result, disorder_cost, kept_state = layer_forward(
            source_rows, genuine_residue_tally[align_here], projection_tables, head_count
        )
        results.append(result)
        focus_spread_levies.append(disorder_cost)
        kept_list.append(kept_state)
        if period < small_batch_number:
            received = shifted(result, "pipe", 1)
    activations = lax.dynamic_slice_in_dim(jnp.stack(results), segment_place, small_batch_number, 0)
    penalty_output = lax.dynamic_slice_in_dim(
        jnp.stack(focus_spread_levies), segment_place, small_batch_number, 0
    )
    grad_received = jnp.zeros(embedded_families.shape[1:], jnp.bfloat16)
    left_lists = [[] for index in range(6)]
    right_lists = [[] for index in range(6)]
    gain_total = None
    bias_total = None
    grad_sources = []
    for period in range(small_batch_number + 1):
        slot_raw = period - 1 + segment_place
        in_range = jnp.logical_and(slot_raw >= 0, slot_raw < small_batch_number)
        slot_here = jnp.clip(slot_raw, 0, small_batch_number - 1)
        align_here = sequence[slot_here]
        kept_state = choose(
            segment_place == 0,
            kept_list[max(period - 1, 0)],
            kept_list[min(period + 1, small_batch_number)],
        )
        outgrad = (
            upstream_sensitivity[slot_here].astype(jnp.float32)
            * token_quarter_factor[align_here].astype(jnp.float32)[..., None]
            * 0.25
        )
        incoming_grad = jnp.where(segment_place == 1, outgrad, grad_received.astype(jnp.float32))
        grad_source, operand_pairs, norm_grads = layer_backward(
            kept_state,
            genuine_residue_tally[align_here],
            incoming_grad,
            projection_tables,
            head_count,
        )
        for index in range(6):
            left_lists[index].append(operand_pairs[index][0])
            right_lists[index].append(
                jnp.where(
                    in_range, operand_pairs[index][1], jnp.zeros_like(operand_pairs[index][1])
                )
            )
        gain_term = jnp.where(in_range, norm_grads[0], jnp.zeros_like(norm_grads[0]))
        bias_term = jnp.where(in_range, norm_grads[1], jnp.zeros_like(norm_grads[1]))
        gain_total = gain_term if gain_total is None else gain_total + gain_term
        bias_total = bias_term if bias_total is None else bias_total + bias_term
        grad_sources.append(grad_source)
        if period < small_batch_number:
            grad_received = shifted(grad_source, "pipe", -1)
    block_entry_derivs = lax.dynamic_slice_in_dim(
        jnp.stack(grad_sources), 1 - segment_place, small_batch_number, 0
    )
    weight_totals = [
        weight_term(
            jnp.concatenate(left_lists[index], axis=0), jnp.concatenate(right_lists[index], axis=0)
        )
        for index in range(6)
    ]
    shared = (
        lax.psum_scatter(
            weight_totals[0].astype(jnp.bfloat16), "seq", scatter_dimension=0, tiled=True
        ).astype(jnp.float32),
        lax.psum_scatter(
            weight_totals[1].astype(jnp.bfloat16), "seq", scatter_dimension=0, tiled=True
        ).astype(jnp.float32),
        lax.psum_scatter(
            weight_totals[2].astype(jnp.bfloat16), "seq", scatter_dimension=0, tiled=True
        ).astype(jnp.float32),
        lax.psum_scatter(
            weight_totals[3].astype(jnp.bfloat16), "seq", scatter_dimension=0, tiled=True
        ).astype(jnp.float32),
        lax.psum_scatter(
            weight_totals[4].astype(jnp.bfloat16), "seq", scatter_dimension=0, tiled=True
        ).astype(jnp.float32),
        lax.psum_scatter(
            weight_totals[5].astype(jnp.bfloat16), "seq", scatter_dimension=0, tiled=True
        ).astype(jnp.float32),
        lax.psum_scatter(
            gain_total.astype(jnp.bfloat16), "seq", scatter_dimension=1, tiled=True
        ).astype(jnp.float32),
        lax.psum_scatter(
            bias_total.astype(jnp.bfloat16), "seq", scatter_dimension=1, tiled=True
        ).astype(jnp.float32),
    )
    (
        shared_row_qkv,
        shared_row_out,
        shared_col_qkv,
        shared_col_out,
        shared_up,
        shared_down,
        shared_gain,
        shared_bias,
    ) = shared
    summed = (
        lax.psum(shared_row_qkv.astype(jnp.bfloat16), "dp").astype(jnp.float32),
        lax.psum(shared_row_out.astype(jnp.bfloat16), "dp").astype(jnp.float32),
        lax.psum(shared_col_qkv.astype(jnp.bfloat16), "dp").astype(jnp.float32),
        lax.psum(shared_col_out.astype(jnp.bfloat16), "dp").astype(jnp.float32),
        lax.psum(shared_up.astype(jnp.bfloat16), "dp").astype(jnp.float32),
        lax.psum(shared_down.astype(jnp.bfloat16), "dp").astype(jnp.float32),
        lax.psum(shared_gain.astype(jnp.bfloat16), "dp").astype(jnp.float32),
        lax.psum(shared_bias.astype(jnp.bfloat16), "dp").astype(jnp.float32),
    )
    return (
        activations[None],
        block_entry_derivs[None],
        penalty_output[None],
        summed[0][None],
        summed[1][None],
        summed[2][None],
        summed[3][None],
        summed[4][None],
        summed[5][None],
        summed[6][None],
        summed[7][None],
    )


def place():
    pipe, seq, dp = (lax.axis_index("pipe"), lax.axis_index("seq"), lax.axis_index("dp"))
    core = lax.rem(dp, 2)
    pair = lax.div(dp, 2)
    return (pipe, seq, dp, core, pair)


def neighbours(pipe, seq, dp, core, pair):
    other_core = (pipe, seq, dp + 1 - 2 * core)
    other_pair = (pipe, seq, dp + 2 - 4 * pair)
    return (other_core, other_pair)


def greet(pipe, seq, dp, core, pair, across_pipe=False):
    barrier = pltpu.get_barrier_semaphore()
    other_core, other_pair = neighbours(pipe, seq, dp, core, pair)
    count = 0
    for step in range(LINE):
        for flip in range(2):
            if step == 0 and flip == 0:
                continue
            where = dp if flip == 0 else dp + 1 - 2 * core
            pl.semaphore_signal(
                barrier,
                inc=1,
                device_id=(pipe, lax.rem(seq + step, LINE), where),
                device_id_type=MESH,
            )
            count += 1
    more = [other_pair] + ([(1 - pipe, seq, dp)] if across_pipe else [])
    for device in more:
        pl.semaphore_signal(barrier, inc=1, device_id=device, device_id_type=MESH)

    def hear():
        pl.semaphore_wait(barrier, count + len(more))

    return hear


def remote(source, target, send, recv, device):
    return pltpu.make_async_remote_copy(
        src_ref=source,
        dst_ref=target,
        send_sem=send,
        recv_sem=recv,
        device_id=device,
        device_id_type=MESH,
    )


def swap_rows(source, target, send, recv, local, where):
    pipe, seq, dp, core, pair = where
    half, rest = (lax.div(seq, 2), lax.rem(seq, 2))

    def each(action):
        for index in range(2):
            line = 2 * core + index
            here = jnp.logical_and(line == seq, half == core)
            copy = remote(
                source.at[index],
                target.at[rest],
                send.at[index],
                recv.at[rest],
                (pipe, line, dp - core + half),
            )
            arriving = remote(
                source.at[index],
                target.at[index],
                send.at[index],
                recv.at[index],
                (pipe, line, dp - core + half),
            )
            inside = pltpu.make_async_copy(source.at[index], target.at[rest], local)
            action(here, copy, arriving, inside)

    def start(here, copy, arriving, inside):
        pl.when(here)(inside.start)
        pl.when(jnp.logical_not(here))(copy.start)

    def finish(here, copy, arriving, inside):
        pl.when(here)(inside.wait)
        pl.when(jnp.logical_not(here))(copy.wait_send)
        pl.when(jnp.logical_not(here))(arriving.wait_recv)

    return (lambda: each(start), lambda: each(finish))


def dot(left, right, left_axis, right_axis):
    return lax.dot_general(
        left,
        right,
        (((left_axis,), (right_axis,)), ((), ())),
        preferred_element_type=jnp.float32,
    )


def unit_rows(values):
    average = jnp.mean(values, axis=-1, keepdims=True)
    centered = values - average
    variance = jnp.mean(centered * centered, axis=-1, keepdims=True)
    root = lax.rsqrt(variance + norm_epsilon)
    return (centered * root, root)


def unit_rows_back(grad, values, gain_row):
    unit, root = unit_rows(values)
    scaled = grad * gain_row
    inner = jnp.mean(scaled * unit, axis=-1, keepdims=True)
    term = root * (scaled - jnp.mean(scaled, axis=-1, keepdims=True) - unit * inner)
    gain = jnp.sum(grad * unit, axis=0, keepdims=True)
    bias = jnp.sum(grad, axis=0, keepdims=True)
    return (term, gain, bias)


def layers_kernel(
    shard_row,
    shard_row_out,
    shard_col,
    shard_col_out,
    shard_up,
    shard_down,
    families,
    upstream,
    order,
    quarters,
    tally,
    norms,
    act_out,
    der_out,
    cost_out,
    vector_out,
    grads,
    out,
    tiles,
    source,
    normal_a,
    normal_b,
    normal_c,
    mixer,
    mixer_col,
    blended,
    mixed,
    after_row,
    after_col,
    log_share,
    col_share,
    hidden,
    slope,
    total_grad,
    grad_in,
    branch_ffn,
    branch_col,
    branch_row,
    grad_up,
    grad_mixer_col,
    grad_mixer,
    logit_send,
    logit_recv,
    keys_recv,
    keys_send,
    keys_back,
    probs_send,
    probs_recv,
    halves,
    segment,
    spread,
    stage,
    stage_down,
    act,
    der,
    cost,
    piece,
    piece_in,
    sensitivity,
    factor,
    factor_in,
    counts,
    counts_in,
    norms_in,
    rows,
    own_sem,
    line_send,
    line_recv,
    pair_send,
    pair_recv,
    core_send,
    core_recv,
    entry_sems,
    entry_local,
    norm_send,
    norm_recv,
    landing,
    from_pair,
    late_pair,
    der_back,
    clear_sem,
    vector,
    vec_core,
    vec_pair,
    vec_line,
    load_sem,
    near_send,
    near_recv,
    far_send,
    far_recv,
    hop_send,
    left_recv,
    right_recv,
    late_send,
    late_recv,
    share_send,
    share_recv,
    out_sem,
    vec_send,
    vec_recv,
    logit_sems,
    keys_sems,
    back_sems,
    probs_sems,
    pipe_sems,
    stage_sems,
    home_sems,
    home_local,
    cost_send,
    cost_recv,
):
    where = place()
    pipe, seq, dp, core, pair = where
    other_core = (pipe, seq, dp + 1 - 2 * core)
    other_pipe = (1 - pipe, seq, dp)
    columns, width = families.shape[2:]
    tokens = 2 * columns
    heads = HEAD_TALLY
    size = width // heads
    twin = 2 * size
    couples = heads // 2
    total_rows = LINE
    bf16, f32 = (jnp.bfloat16, jnp.float32)
    part_width = width // LINE
    shards = [
        ref.at[0]
        for ref in (shard_row, shard_row_out, shard_col, shard_col_out, shard_up, shard_down)
    ]
    first_tile = (0, 3, 4, 7, 8, 12)
    last_matrix = 5
    pieces = PIECES
    other_pair = (pipe, seq, dp + 2 - 4 * pair)
    right, left = ((pipe, seq + 1, dp), (pipe, seq - 1, dp))
    later = pipe == 1

    hear = greet(*where, across_pipe=True)
    straight = order[0, 0] == 0
    for index in range(2):
        piece[index] = jnp.where(straight, families[index, 0], families[1 - index, 0])
        chosen = jnp.where(straight, quarters[index], quarters[1 - index])
        factor[index] = jnp.broadcast_to(chosen.astype(f32) * 0.25, (columns, columns)).T
        number = jnp.where(straight, tally[index], tally[1 - index])
        counts[index] = jnp.broadcast_to(number, (8, 128)).astype(f32)
    hear()

    def entering(number, source_ref, target_ref):
        return swap_rows(
            source_ref,
            target_ref,
            entry_sems.at[2 * number],
            entry_sems.at[2 * number + 1],
            entry_local.at[number],
            where,
        )

    start_counts, finish_counts = entering(0, counts, counts_in)
    start_piece, finish_piece = entering(1, piece, piece_in)
    start_sensitivity, finish_sensitivity = entering(2, upstream.at[:, 0], sensitivity)
    start_factor, finish_factor = entering(3, factor, factor_in)
    pl.when(later)(start_piece)

    def norm_copy(step, source):
        return remote(
            norms,
            norms_in.at[source],
            norm_send.at[step - 1],
            norm_recv.at[source],
            (pipe, lax.rem(seq + step, LINE), dp),
        )


    def block_of(index, source, start, length):
        depth, wide = shards[index].shape
        if wide == width and depth == width:
            return tiles.at[first_tile[index] + source, pl.ds(start, length)]
        start = pl.multiple_of(source * depth + start, 16)
        return tiles.at[pl.ds(first_tile[index], wide // width), pl.ds(start, length)]

    def piece_of(index):
        matrix = min(index, last_matrix)
        share = shards[matrix].shape[0] // 4
        length = share // 2 if matrix == last_matrix else share
        return (matrix, share, (index - matrix) * length, length)

    def region(index, source, part):
        matrix, share, skip, length = piece_of(index)
        start = pl.multiple_of(part * share + skip, 16)
        return block_of(matrix, source, start, length)

    def cut(index, start, length):
        depth, wide = shards[index].shape
        if wide == width and depth == width:
            yield (
                shards[index].at[pl.ds(start, length)],
                tiles.at[first_tile[index] + seq, pl.ds(start, length)],
            )
            return
        target = pl.multiple_of(seq * depth + start, 16)
        for part in range(wide // width):
            yield (
                shards[index].at[pl.ds(start, length), pl.ds(part * width, width)],
                tiles.at[first_tile[index] + part, pl.ds(target, length)],
            )

    def start_own(index):
        for near, far in cut(index, 0, shards[index].shape[0]):
            pltpu.make_async_copy(near, far, own_sem.at[index]).start()

    def wait_own(index):
        block = block_of(index, seq, 0, shards[index].shape[0])
        pltpu.make_async_copy(block, block, own_sem.at[index]).wait()

    def start_line(index, direction):
        matrix, share, skip, length = piece_of(index)
        for near, far in cut(matrix, pl.multiple_of(dp * share + skip, 16), length):
            remote(
                near,
                far,
                line_send.at[direction, seq, index],
                line_recv.at[seq, index],
                right if direction == 0 else left,
            ).start()

    def along(source, index, direction):
        block = region(index, source, dp)
        return remote(
            block,
            block,
            line_send.at[direction, source, index],
            line_recv.at[source, index],
            right if direction == 0 else left,
        )

    across = dp + 2 - 4 * pair
    opposite = dp + 1 - 2 * core
    opposite_across = across + 1 - 2 * core

    def over_pair(source, index, part):
        block = region(index, source, part)
        return remote(
            block, block, pair_send.at[source, index], pair_recv.at[source, index], other_pair
        )

    def over_core(lane_of, source, index, part):
        block = region(index, source, part)
        return remote(
            block,
            block,
            core_send.at[lane_of, source, index],
            core_recv.at[lane_of, source, index],
            other_core,
        )

    has = (seq < LINE - 1, seq > 0)

    def sources(step):
        for direction in range(2):
            source = seq - step if direction == 0 else seq + step
            yield (direction, source, source >= 0 if direction == 0 else source < LINE)

    def begin(index):
        for direction in range(2):
            pl.when(has[direction])(functools.partial(start_line, index, direction))
        if index <= last_matrix:
            start_own(index)

    def arrive(index, step):
        for direction, source, present in sources(step):

            @pl.when(present)
            def _():
                along(source, index, direction).wait_recv()

                @pl.when(has[direction])
                def _():
                    along(source, index, direction).start()

                over_pair(source, index, dp).start()
                over_core(0, source, index, dp).start()

    def relay(index, step):
        for direction, source, present in sources(step):

            @pl.when(present)
            def _():
                over_pair(source, index, across).wait_recv()
                over_core(1, source, index, across).start()

    def settle(index):
        if index <= last_matrix:
            wait_own(index)
        for step in range(1, LINE):
            for direction, source, present in sources(step):

                @pl.when(present)
                def _():
                    over_core(0, source, index, opposite).wait_recv()
                    over_core(1, source, index, opposite_across).wait_recv()

    def drain(index):
        for direction in range(2):
            pl.when(has[direction])(along(seq, index, direction).wait_send)
        for step in range(1, LINE):
            for direction, source, present in sources(step):

                @pl.when(present)
                def _():
                    pl.when(has[direction])(along(source, index, direction).wait_send)
                    over_pair(source, index, dp).wait_send()
                    over_core(0, source, index, dp).wait_send()
                    over_core(1, source, index, across).wait_send()

    def wave(number):
        if number + 1 < pieces:
            begin(number + 1)
        for step in range(1, LINE):
            if 0 <= number + 1 - step < pieces:
                arrive(number + 1 - step, step)
        for step in range(1, LINE):
            if 0 <= number - step < pieces:
                relay(number - step, step)

    def gather(*waves):
        @pl.when(jnp.logical_not(later))
        def _():
            for number in waves:
                wave(number)

    def ready(index):
        pl.when(jnp.logical_not(later))(lambda: settle(index))

    begin(0)
    start_counts()
    for step in range(1, LINE):
        norm_copy(step, seq).start()
    norms_in[seq] = norms[...]
    hop = remote(piece_in, source, pipe_sems.at[4], pipe_sems.at[5], other_pipe)

    @pl.when(later)
    def _():
        finish_piece()
        hop.start()
        for number in range(pieces + LINE - 1):
            wave(number)
        start_sensitivity()
        start_factor()
        for index in range(pieces):
            settle(index)
            drain(index)
        hop.wait_send()

    lane = lax.broadcasted_iota(jnp.int32, (columns, 2 * twin), 1)
    early = (lax.rem(lane, twin) < size).astype(f32)
    halves[0] = early.astype(bf16)
    halves[1] = (1.0 - early).astype(bf16)
    feature = lax.broadcasted_iota(jnp.int32, (width, 128), 0)
    head = lax.broadcasted_iota(jnp.int32, (width, 128), 1)
    belongs = jnp.logical_and(feature >= head * size, feature < head * size + size)
    segment[...] = belongs.astype(f32).astype(bf16)
    head = lax.broadcasted_iota(jnp.int32, (128, width), 0)
    feature = lax.broadcasted_iota(jnp.int32, (128, width), 1)
    belongs = jnp.logical_and(feature >= head * size, feature < head * size + size)
    spread[...] = belongs.astype(f32).astype(bf16)
    for step in range(1, LINE):
        norm_copy(step, lax.rem(seq + LINE - step, LINE)).wait()
    for part in range(LINE):
        rows[:, part * part_width : (part + 1) * part_width] = norms_in[part, :, 0:part_width]
    finish_counts()

    def gain_of(index):
        return rows[index : index + 1, :]

    def bias_of(index):
        return rows[3 + index : 4 + index, :]

    def keep_vector(index, gain, bias):
        part = width // LINE
        for target in range(LINE):
            window = slice(target * part, (target + 1) * part)
            vector[target, index : index + 1, 0:part] = gain[:, window]
            vector[target, 3 + index : 4 + index, 0:part] = bias[:, window]

    vector[...] = jnp.zeros(vector.shape, f32)

    def both(ref, start):
        return jnp.concatenate(
            [ref[0:columns, start : start + twin], ref[columns:tokens, start : start + twin]],
            axis=1,
        )

    def stacked(ref, start):
        wide = both(ref, start)
        return jnp.concatenate([wide * halves[0], wide * halves[1]], axis=0)

    def unstack(wide):
        early_lane = lax.rem(lax.broadcasted_iota(jnp.int32, (columns, 2 * twin), 1), twin) < size
        return jnp.where(early_lane, wide[0:columns], wide[columns:])

    def put(ref, start, wide):
        ref[0:columns, start : start + twin] = wide[:, 0:twin].astype(bf16)
        ref[columns:tokens, start : start + twin] = wide[:, twin:].astype(bf16)

    def to_core(source_ref, target_ref, sems, index):
        return remote(
            source_ref, target_ref, sems.at[0, index], sems.at[1, index], other_core
        )

    start_act, finish_act = swap_rows(
        act, act_out, home_sems.at[0], home_sems.at[1], home_local.at[0], where
    )
    start_der, finish_der = swap_rows(
        der, der_out, home_sems.at[2], home_sems.at[3], home_local.at[1], where
    )
    sender = core == lax.div(seq, 2)
    spot = lax.rem(seq, 2)
    cost_own = pltpu.make_async_copy(cost, cost_out.at[spot], home_local.at[2])
    cost_copies = [
        remote(
            cost,
            cost_out.at[spot],
            cost_send.at[step - 1],
            cost_recv.at[spot],
            (pipe, lax.rem(seq + step, LINE), dp),
        )
        for step in range(1, LINE)
    ]

    der_over = remote(der, piece, pipe_sems.at[6], pipe_sems.at[7], other_pipe)
    der_home = remote(der_back, der_out, pipe_sems.at[8], pipe_sems.at[9], other_pipe)
    start_back, finish_back = swap_rows(
        piece, der_back, home_sems.at[4], home_sems.at[5], home_local.at[3], where
    )
    send_on = remote(act, source, pipe_sems.at[0], pipe_sems.at[1], other_pipe)
    send_back = remote(der, grad_in, pipe_sems.at[2], pipe_sems.at[3], other_pipe)

    @pl.when(later)
    def _():
        send_on.wait_recv()

    gather(0, 1)

    @pl.when(jnp.logical_not(later))
    def _():
        hop.wait_recv()

    chunks, cycle = (6, 3)
    whole_turns = chunks // cycle
    paired = chunks - whole_turns
    depth = width // chunks
    units = LINE * chunks
    mid = units // 2
    always = lambda target: target >= 0
    far = jnp.maximum(seq, LINE - 1 - seq)
    pair_lag, hop_lag, share_lag = (3, 4, 4)

    def unit_of(number):
        turn = lax.div(number, LINE)
        rank = number - turn * LINE
        halfway = lax.div(rank, 2)
        target = jnp.where(lax.rem(rank, 2) == 0, LINE - 1 - halfway, halfway)
        return (target, chunks - 1 - turn)

    def rank_of(chunk):
        turn = chunks - 1 - chunk
        early_turns = lax.div(turn, cycle)
        return (early_turns, turn - early_turns - 1)

    def is_single(chunk):
        turn = chunks - 1 - chunk
        return lax.rem(turn, cycle) != 0

    def window_of(chunk):
        return pl.ds(pl.multiple_of(chunk * depth, depth), depth)

    def spot_of(number, side, shift, count=1):
        block = jnp.where(
            number < mid, 2 * units + 2 * number + side, 2 * (number - mid) + side
        )
        block = block + shift
        tile = lax.div(block, chunks)
        row = pl.multiple_of((block - tile * chunks) * depth, depth)
        return (tile, pl.ds(row, count * depth))

    def mine_at(number, side, count=1):
        return tiles.at[spot_of(number, side, 0, count)]

    def near_at(number, side):
        return tiles.at[spot_of(number, side, units)]

    def add_into(number, side, ref, start=None):
        spot = spot_of(number, side, 0)
        value = ref[...] if start is None else ref[pl.ds(start, depth), :]
        tiles[spot] = (tiles[spot].astype(f32) + value.astype(f32)).astype(bf16)

    def load(number, side):
        target, chunk = unit_of(number)
        return pltpu.make_async_copy(
            grads.at[target, 2 * side + core, window_of(chunk)],
            mine_at(number, side),
            load_sem.at[number, side],
        )

    def to_near(number, side):
        target, chunk = unit_of(number)
        return remote(
            grads.at[target, 2 * side + 1 - core, window_of(chunk)],
            near_at(number, side),
            near_send.at[number, side],
            near_recv.at[number, side],
            other_core,
        )

    def issue(number, carry):
        for side in range(2):
            to_near(number, side).start()
            load(number, side).start()
        return carry

    def issue_all(start, stop):
        lax.fori_loop(start, stop, issue, 0)

    def pair_start(number):
        turn = lax.div(number, LINE)
        _, rank = rank_of(chunks - 1 - turn)
        return pl.multiple_of((LINE * rank + number - LINE * turn) * depth, depth)

    def to_pair(number):
        return remote(
            mine_at(number, 1 - pair),
            from_pair.at[pl.ds(pair_start(number), depth)],
            far_send.at[number],
            far_recv.at[number],
            other_pair,
        )

    def arrive_near(number, side):
        load(number, side).wait()
        to_near(number, side).wait_recv()
        add_into(number, side, near_at(number, side))

    def land_slot(number, chunk, single, second):
        whole_rank, single_rank = rank_of(chunk)
        turn = chunks - 1 - chunk
        rank = number - LINE * turn
        base = 2 * LINE * whole_turns
        extra = base + LINE * paired
        if single:
            slot = base + LINE * single_rank + rank
            slot = jnp.where(second, extra + 2 * whole_turns + single_rank, slot)
        else:
            slot = 2 * (LINE * whole_rank + rank)
            slot = jnp.where(second, extra + 2 * whole_rank, slot)
        return pl.multiple_of(slot * depth, depth)

    def hop_copy(number, chunk, single, direction):
        target, _ = unit_of(number)
        second = jnp.logical_and(direction == 1, target == seq - 1)
        count = 1 if single else 2
        sems = left_recv if direction == 0 else right_recv
        return remote(
            mine_at(number, pair if single else 0, count),
            landing.at[pl.ds(land_slot(number, chunk, single, second), count * depth)],
            hop_send.at[number],
            sems.at[number],
            right if direction == 0 else left,
        )

    def take(number, chunk, single, direction):
        target, _ = unit_of(number)
        second = jnp.logical_and(direction == 1, target == seq)
        count = 1 if single else 2
        start = land_slot(number, chunk, single, second)
        sems = left_recv if direction == 0 else right_recv
        remote(
            mine_at(number, pair if single else 0, count),
            landing.at[pl.ds(start, count * depth)],
            hop_send.at[number],
            sems.at[number],
            right if direction == 0 else left,
        ).wait_recv()
        if single:
            add_into(number, pair, landing, start)
        else:
            for side in range(2):
                add_into(number, side, landing, start + side * depth)

    def late_start(chunk):
        return pl.multiple_of(2 * rank_of(chunk)[0] * depth, depth)

    def late_copy(number, chunk, single):
        if single:
            return remote(
                mine_at(number, pair),
                out.at[dp, window_of(chunk)],
                late_send.at[chunk],
                late_recv.at[chunk],
                other_pair,
            )
        return remote(
            mine_at(number, 0, 2),
            late_pair.at[pl.ds(late_start(chunk), 2 * depth)],
            late_send.at[chunk],
            late_recv.at[chunk],
            other_pair,
        )

    def share_copy(number, chunk, side, relayed):
        spot_out = out.at[2 * side + core, window_of(chunk)]
        return remote(
            spot_out if relayed else mine_at(number, side),
            spot_out,
            share_send.at[side, chunk],
            share_recv.at[side, chunk],
            other_core,
        )

    def out_copy(number, chunk, side):
        return pltpu.make_async_copy(
            mine_at(number, side), out.at[2 * side + core, window_of(chunk)], out_sem.at[side, chunk]
        )

    def at(number, condition, body):
        clipped = jnp.clip(number, 0, units - 1)
        target, chunk = unit_of(clipped)
        valid = jnp.logical_and(number >= 0, number < units)
        valid = jnp.logical_and(valid, condition(target))

        @pl.when(jnp.logical_and(valid, is_single(chunk)))
        def _():
            body(clipped, chunk, True)

        @pl.when(jnp.logical_and(valid, jnp.logical_not(is_single(chunk))))
        def _():
            body(clipped, chunk, False)

    def first_stage(number, chunk, single):
        if single:
            arrive_near(number, 1 - pair)
            to_pair(number).start()
            arrive_near(number, pair)
        else:
            for side in range(2):
                arrive_near(number, side)

    def first_body(number, carry):
        at(number, always, first_stage)
        return carry

    def second_stage(number, chunk, single):
        if single:
            to_pair(number).wait_recv()
            add_into(number, pair, from_pair, pair_start(number))

    def hop_stage(direction):
        def body(number, chunk, single):
            @pl.when(has[1 - direction])
            def _():
                take(number, chunk, single, direction)

            hop_copy(number, chunk, single, direction).start()

        return body

    def last_stage(number, chunk, single):
        for direction in range(2):

            @pl.when(has[1 - direction])
            def _():
                take(number, chunk, single, direction)

        late_copy(number, chunk, single).start()
        if single:
            out_copy(number, chunk, pair).start()
            share_copy(number, chunk, pair, False).start()

    def share_stage(number, chunk, single):
        if single:
            remote(
                mine_at(number, pair),
                out.at[dp + 2 - 4 * pair, window_of(chunk)],
                late_send.at[chunk],
                late_recv.at[chunk],
                other_pair,
            ).wait_recv()
            share_copy(number, chunk, 1 - pair, True).start()
        else:
            late_copy(number, chunk, False).wait()
            for side in range(2):
                add_into(number, side, late_pair, late_start(chunk) + side * depth)
                out_copy(number, chunk, side).start()
                share_copy(number, chunk, side, False).start()

    def hop_stages(base):
        at(base, always, second_stage)
        at(base - hop_lag * seq, lambda target: target > seq, hop_stage(0))
        at(base - hop_lag * (LINE - 1 - seq), lambda target: target < seq, hop_stage(1))
        at(base - hop_lag * far, lambda target: target == seq, last_stage)
        at(base - hop_lag * far - share_lag, lambda target: target == seq, share_stage)

    def hops(start, stop):
        def body(number, carry):
            hop_stages(number)
            return carry

        lax.fori_loop(start, stop, body, 0)

    def finish_sends(number, carry):
        for side in range(2):
            to_near(number, side).wait_send()

        def sends(number, chunk, single):
            if single:
                to_pair(number).wait_send()

        at(number, always, sends)
        return carry

    def finish_unit(number, carry):
        at(
            number,
            lambda target: target > seq,
            lambda number, chunk, single: hop_copy(number, chunk, single, 0).wait_send(),
        )
        at(
            number,
            lambda target: target < seq,
            lambda number, chunk, single: hop_copy(number, chunk, single, 1).wait_send(),
        )

        def shared(number, chunk, single):
            if single:
                late_copy(number, chunk, True).wait_send()
                out_copy(number, chunk, pair).wait()
                share_copy(number, chunk, pair, False).wait_send()
                share_copy(number, chunk, 1 - pair, True).wait_send()
            else:
                for side in range(2):
                    out_copy(number, chunk, side).wait()
                    share_copy(number, chunk, side, False).wait_send()
            for side in range(2):
                spot_out = out.at[2 * side + 1 - core, window_of(chunk)]
                remote(
                    spot_out,
                    spot_out,
                    share_send.at[side, chunk],
                    share_recv.at[side, chunk],
                    other_core,
                ).wait_recv()

        at(number, lambda target: target == seq, shared)
        return carry

    vec_first = remote(vector, vec_core, vec_send.at[0], vec_recv.at[0], other_core)
    vec_second = remote(vec_core, vec_pair, vec_send.at[1], vec_recv.at[1], other_pair)

    def move_copy(step, source):
        goal = lax.rem(seq + step, LINE)
        return remote(
            vec_pair.at[goal],
            vec_line.at[source],
            vec_send.at[1 + step],
            vec_recv.at[2 + source],
            (pipe, goal, dp),
        )

    def vector_to_pair():
        vec_first.wait()
        vec_core[...] = vector[...] + vec_core[...]
        vec_second.start()

    def vector_to_line():
        vec_second.wait()
        vec_pair[...] = vec_core[...] + vec_pair[...]
        for step in range(1, LINE):
            move_copy(step, seq).start()
        vec_line[seq] = vec_pair[seq]

    def vector_end():
        for step in range(1, LINE):
            move_copy(step, lax.rem(seq + LINE - step, LINE)).wait()
        total_vector = vec_line[0]
        for source_of in range(1, LINE):
            total_vector = total_vector + vec_line[source_of]
        vector_out[...] = total_vector

    packed_share = width // (4 * LINE)

    def outer_terms():
        for part in range(4):
            slot = part % 2
            window = slice(part * width, (part + 1) * width)
            if part >= 2:
                down_copy(part - 2).wait()
            term = dot(hidden[:, window], branch_ffn[...], 0, 0).astype(bf16)
            stage_down[slot] = term.reshape(4, width // 4, width)
            down_copy(part).start()
        packed_terms(((normal_c, grad_up, 8 * packed_share),))
        for part in range(2, 4):
            down_copy(part).wait()

    def down_copy(part):
        return pltpu.make_async_copy(
            stage_down.at[part % 2],
            grads.at[part, :, pl.ds(12 * packed_share, width // 4)],
            stage_sems.at[2 + part % 2, 0],
        )

    def inner_terms():
        packed_terms(
            (
                (normal_b, grad_mixer_col, 4 * packed_share),
                (mixed, branch_col, 7 * packed_share),
                (normal_a, grad_mixer, 0),
                (blended, branch_row, 3 * packed_share),
            )
        )

    def packed_terms(pairs):
        waiting = [None, None]
        number = 0
        for first, second, base in pairs:
            for part in range(second.shape[1] // width):
                slot = number % 2
                if waiting[slot] is not None:
                    for copy in waiting[slot]:
                        copy.wait()
                window = slice(part * width, (part + 1) * width)
                term = dot(first[...], second[:, window], 0, 0).astype(bf16)
                stage[slot] = term.reshape(LINE, 4, packed_share, width)
                waiting[slot] = [
                    pltpu.make_async_copy(
                        stage.at[slot, target],
                        grads.at[target, :, pl.ds(base + part * packed_share, packed_share)],
                        stage_sems.at[slot, target],
                    )
                    for target in range(LINE)
                ]
                for copy in waiting[slot]:
                    copy.start()
                number += 1
        for copies in waiting:
            for copy in copies or ():
                copy.wait()

    unit, _ = unit_rows(source[...].reshape(tokens, width).astype(f32))
    normal_a[...] = (unit * gain_of(0) + bias_of(0)).astype(bf16)
    gather(2, 3)
    ready(0)
    for part in range(3):
        window = slice(part * width, (part + 1) * width)
        mixer[:, window] = dot(normal_a[...], tiles[part], 1, 0).astype(bf16)
    logit_factor = 1.0 / (math.sqrt(size) * math.sqrt(total_rows))
    logit_copies = []
    for couple in range(couples):
        partial_value = logit_factor * dot(
            both(mixer, couple * twin), stacked(mixer, width + couple * twin), 1, 1
        )
        logit_send[couple] = partial_value.astype(bf16)
        copy = to_core(logit_send.at[couple], logit_recv.at[couple], logit_sems, couple)
        copy.start()
        logit_copies.append(copy)
    gather(4)
    valid = (
        lax.broadcasted_iota(jnp.int32, (columns, 1), 0).astype(f32) < counts_in[0, 0:1, 0:1]
    ).astype(f32)
    disorder = jnp.zeros((columns, 1), f32)
    for couple in range(couples):
        logit_copies[couple].wait_recv()
        wide = logit_send[couple].astype(f32) + logit_recv[couple].astype(f32)
        shares = []
        for half in range(2):
            logits = wide[:, half * columns : (half + 1) * columns]
            shifted_logits = logits - jnp.max(logits, axis=-1, keepdims=True)
            powers = jnp.exp(shifted_logits)
            total = jnp.sum(powers, axis=-1, keepdims=True)
            logs = shifted_logits - jnp.log(total)
            share = powers / total
            log_share[couple, :, half * columns : (half + 1) * columns] = logs
            disorder = disorder - jnp.sum(share * logs, axis=-1, keepdims=True) * valid
            shares.append(share.astype(bf16))
        put(
            blended,
            couple * twin,
            dot(
                jnp.concatenate(shares, axis=1), stacked(mixer, 2 * width + couple * twin), 1, 0
            ),
        )
    cost[...] = jnp.broadcast_to(
        jnp.sum(disorder, axis=0, keepdims=True) / float(heads * columns), cost.shape
    )
    ready(1)
    after_row[...] = source[...].reshape(tokens, width).astype(f32) + dot(blended[...], tiles[3], 1, 0)
    unit, _ = unit_rows(after_row[...])
    normal_b[...] = (unit * gain_of(1) + bias_of(1)).astype(bf16)
    gather(5)
    ready(2)
    keys_copies = []
    for part in (1, 2, 0):
        window = slice(part * width, (part + 1) * width)
        mixer_col[:, window] = dot(normal_b[...], tiles[4 + part], 1, 0).astype(bf16)
        if part > 0:
            copy = to_core(
                mixer_col.at[:, window], keys_recv.at[part - 1], keys_sems, part - 1
            )
            copy.start()
            keys_copies.append(copy)

    def line_of(part, place_of):
        if place_of < 2:
            rows_of = slice(place_of * columns, (place_of + 1) * columns)
            return mixer_col[rows_of, (1 + part) * width : (2 + part) * width]
        rows_of = slice((place_of - 2) * columns, (place_of - 1) * columns)
        return keys_recv[part, rows_of, :]

    def sums_by_head(wide_ref, start, line):
        products = [
            wide_ref[index * columns : (index + 1) * columns, start : start + width] * line
            for index in range(2)
        ]
        return dot(jnp.concatenate(products, axis=0), segment[...], 1, 0)

    def spread_heads(narrow):
        return dot(narrow, spread[...], 1, 0)

    gather(6)
    scores = []
    for place_of in range(4):
        if place_of == 2:
            keys_copies[0].wait_recv()
        scores.append(sums_by_head(mixer_col, 0, line_of(0, place_of)) / math.sqrt(size))
    highest = functools.reduce(jnp.maximum, scores)
    powers = [jnp.exp(score - highest) for score in scores]
    total = functools.reduce(jnp.add, powers)
    keys_copies[1].wait_recv()
    gathered_mix = None
    for place_of in range(4):
        share = powers[place_of] / total
        col_share[place_of] = share
        wide = spread_heads(share.astype(bf16))
        line = line_of(1, place_of).astype(f32)
        term = jnp.concatenate([wide[0:columns] * line, wide[columns:] * line], axis=0)
        gathered_mix = term if gathered_mix is None else gathered_mix + term
    mixed[...] = gathered_mix.astype(bf16)
    ready(3)
    after_col[...] = after_row[...] + dot(mixed[...], tiles[7], 1, 0)
    unit, _ = unit_rows(after_col[...])
    normal_c[...] = (unit * gain_of(2) + bias_of(2)).astype(bf16)
    gather(7)
    ready(4)
    parts = hidden.shape[1] // width
    result = after_col[...]
    for part in range(parts):
        if part == 2:
            gather(8)
        window = slice(part * width, (part + 1) * width)
        upward = dot(normal_c[...], tiles[8 + part], 1, 0)
        inner = 0.5 + 0.5 * lax.erf(upward * math.sqrt(0.5))
        density = jnp.exp(-0.5 * upward * upward) * (1.0 / math.sqrt(2.0 * math.pi))
        hidden[:, window] = (upward * inner).astype(bf16)
        slope[:, window] = (inner + upward * density).astype(bf16)
    gather(9)
    ready(5)
    ready(6)
    for part in range(parts):
        window = slice(part * width, (part + 1) * width)
        result = result + dot(hidden[:, window], tiles[12 + part], 1, 0)
    act[...] = result.astype(bf16).reshape(2, columns, width)

    @pl.when(pipe == 0)
    def _():
        send_on.start()

    start_act()

    @pl.when(sender)
    def _():
        cost_own.start()
        for copy in cost_copies:
            copy.start()

    @pl.when(pipe == 1)
    def _():
        finish_sensitivity()
        finish_factor()
        for index in range(2):
            total_grad[index * columns : (index + 1) * columns, :] = (
                sensitivity[index].astype(f32) * factor_in[index, :, 0:1]
            )

    @pl.when(pipe == 0)
    def _():
        for index in range(pieces):
            drain(index)
        send_back.wait_recv()
        total_grad[...] = grad_in[...].reshape(tokens, width).astype(f32)

    branch_ffn[...] = total_grad[...].astype(bf16)
    grad_normal = None
    for part in range(parts):
        window = slice(part * width, (part + 1) * width)
        grad_hidden = dot(branch_ffn[...], tiles[12 + part], 1, 1)
        grad_up[:, window] = (grad_hidden * slope[:, window].astype(f32)).astype(bf16)
        term = dot(grad_up[:, window], tiles[8 + part], 1, 1)
        grad_normal = term if grad_normal is None else grad_normal + term
    pl.semaphore_signal(clear_sem, inc=1, device_id=other_core, device_id_type=MESH)

    @pl.when(jnp.logical_not(later))
    def _():
        outer_terms()
        pl.semaphore_wait(clear_sem, 1)
        issue_all(0, mid)

    term, gain, bias = unit_rows_back(grad_normal, after_col[...], gain_of(2))
    keep_vector(2, gain, bias)
    total_grad[...] = total_grad[...] + term
    branch_col[...] = total_grad[...].astype(bf16)
    grad_mixed = dot(branch_col[...], tiles[7], 1, 1).astype(bf16)
    grad_probs = []
    for place_of in range(4):
        line = line_of(1, place_of)
        products = [grad_mixed[0:columns] * line, grad_mixed[columns:] * line]
        grad_probs.append(dot(jnp.concatenate(products, axis=0), segment[...], 1, 0))
    inner = functools.reduce(
        jnp.add, [col_share[place_of] * grad_probs[place_of] for place_of in range(4)]
    )
    root_size = math.sqrt(size)
    grad_query = None
    local_terms = []
    back_copies = []
    grad_lines = grad_mixed.astype(f32)
    query_lines = mixer_col[:, 0:width].astype(f32)
    for place_of in (2, 3, 0, 1):
        share = col_share[place_of]
        narrow = (share * (grad_probs[place_of] - inner)).astype(bf16)
        wide = spread_heads(narrow)
        line = line_of(0, place_of).astype(f32)
        term = jnp.concatenate([wide[0:columns] * line, wide[columns:] * line], axis=0)
        grad_query = term if grad_query is None else grad_query + term
        key_term = wide[0:columns] * query_lines[0:columns] + wide[columns:] * query_lines[columns:]
        key_term = key_term / root_size
        wide = spread_heads(share.astype(bf16))
        value_term = wide[0:columns] * grad_lines[0:columns] + wide[columns:] * grad_lines[columns:]
        if place_of >= 2:
            index = place_of - 2
            rows_of = slice(index * columns, (index + 1) * columns)
            keys_send[rows_of, 0:width] = key_term.astype(bf16)
            keys_send[rows_of, width:] = value_term.astype(bf16)
            copy = to_core(keys_send.at[rows_of, :], keys_back.at[rows_of, :], back_sems, index)
            copy.start()
            back_copies.append(copy)
        else:
            local_terms.append((key_term, value_term))
    grad_mixer_col[:, 0:width] = (grad_query / root_size).astype(bf16)
    for place_of in range(2):
        back_copies[place_of].wait()
        rows_of = slice(place_of * columns, (place_of + 1) * columns)
        for part in range(2):
            window = slice(part * width, (part + 1) * width)
            grad_mixer_col[rows_of, (1 + part) * width : (2 + part) * width] = (
                local_terms[place_of][part] + keys_back[rows_of, window].astype(f32)
            ).astype(bf16)

    @pl.when(jnp.logical_not(later))
    def _():
        lax.fori_loop(0, mid, first_body, 0)
        hops(0, EARLY)

    grad_normal = None
    for part in range(3):
        window = slice(part * width, (part + 1) * width)
        term = dot(grad_mixer_col[:, window], tiles[4 + part], 1, 1)
        grad_normal = term if grad_normal is None else grad_normal + term
    term, gain, bias = unit_rows_back(grad_normal, after_row[...], gain_of(1))
    keep_vector(1, gain, bias)
    total_grad[...] = total_grad[...] + term
    branch_row[...] = total_grad[...].astype(bf16)
    keys_send[:, 0:width] = dot(branch_row[...], tiles[3], 1, 1).astype(bf16)
    probs_copies = []
    for couple in range(couples):
        partial_value = dot(
            both(keys_send, couple * twin), stacked(mixer, 2 * width + couple * twin), 1, 1
        )
        probs_send[couple] = partial_value.astype(bf16)
        copy = to_core(probs_send.at[couple], probs_recv.at[couple], probs_sems, couple)
        copy.start()
        probs_copies.append(copy)

    pl.when(jnp.logical_not(later))(lambda: hops(EARLY, EARLY + MIDDLE))
    column_weight = (float(total_rows * columns) / float(heads * columns)) * valid
    for couple in range(couples):
        start = couple * twin
        logs = log_share[couple]
        share = jnp.exp(logs)
        grad_wide = both(keys_send, start)
        put(
            grad_mixer,
            2 * width + start,
            unstack(dot(share.astype(bf16), grad_wide, 0, 0)),
        )
        probs_copies[couple].wait_recv()
        wide = probs_send[couple].astype(f32) + probs_recv[couple].astype(f32)
        pieces = []
        for half in range(2):
            window = slice(half * columns, (half + 1) * columns)
            part_share, part_logs, part_grad = (share[:, window], logs[:, window], wide[:, window])
            entropy = -jnp.sum(part_share * part_logs, axis=-1, keepdims=True)
            inner = jnp.sum(part_share * part_grad, axis=-1, keepdims=True)
            piece = part_share * (part_grad - inner)
            piece = piece - column_weight * part_share * (part_logs + entropy)
            pieces.append(piece.astype(bf16))
        grad_logits = jnp.concatenate(pieces, axis=1)
        put(
            grad_mixer,
            start,
            logit_factor * dot(grad_logits, stacked(mixer, width + start), 1, 0),
        )
        put(
            grad_mixer,
            width + start,
            logit_factor * unstack(dot(grad_logits, both(mixer, start), 0, 0)),
        )
    grad_normal = None
    for part in range(3):
        window = slice(part * width, (part + 1) * width)
        term = dot(grad_mixer[:, window], tiles[part], 1, 1)
        grad_normal = term if grad_normal is None else grad_normal + term
    term, gain, bias = unit_rows_back(grad_normal, source[...].reshape(tokens, width).astype(f32), gain_of(0))
    keep_vector(0, gain, bias)
    der[...] = (total_grad[...] + term).astype(bf16).reshape(2, columns, width)

    @pl.when(pipe == 1)
    def _():
        send_back.start()

    vec_first.start()

    @pl.when(later)
    def _():
        start_der()

    @pl.when(jnp.logical_not(later))
    def _():
        der_over.start()

    @pl.when(later)
    def _():
        outer_terms()
        pl.semaphore_wait(clear_sem, 1)
        issue_all(0, mid)
        lax.fori_loop(0, mid, first_body, 0)
        hops(0, EARLY + MIDDLE)

    hops(EARLY + MIDDLE, EARLY + MORE)
    inner_terms()
    issue_all(mid, units)
    vector_to_pair()

    def mix(number, carry):
        for index in range(AT_ONCE):
            at(mid + AT_ONCE * number + index, always, first_stage)
        hop_stages(EARLY + MORE + number)
        return carry

    lax.fori_loop(0, mid // AT_ONCE, mix, 0)

    @pl.when(later)
    def _():
        der_over.wait_recv()
        start_back()

    hops(EARLY + MORE + mid // AT_ONCE, units)
    vector_to_line()
    lax.fori_loop(0, units, finish_sends, 0)
    hops(units, units + hop_lag * (LINE - 1) + share_lag)
    vector_end()
    lax.fori_loop(0, units, finish_unit, 0)
    for copy in logit_copies + keys_copies + probs_copies:
        copy.wait_send()

    @pl.when(pipe == 0)
    def _():
        send_on.wait_send()

    @pl.when(pipe == 1)
    def _():
        send_back.wait_send()

    finish_act()

    @pl.when(later)
    def _():
        finish_back()
        der_home.start()
        finish_der()
        der_home.wait_send()

    @pl.when(jnp.logical_not(later))
    def _():
        der_over.wait_send()
        der_home.wait_recv()

    @pl.when(sender)
    def _():
        cost_own.wait()
        for copy in cost_copies:
            copy.wait_send()

    for index in range(2):

        @pl.when(2 * core + index != seq)
        def _():
            remote(
                cost, cost_out.at[index], cost_send.at[0], cost_recv.at[index], other_core
            ).wait_recv()


def run_layers(shards, families, upstream, order, quarters, tally, norms):
    columns, width = families.shape[2:]
    tokens = 2 * columns
    couples = HEAD_TALLY // 2
    wide = shards[4].shape[2]
    entry = jax.ShapeDtypeStruct((2, columns, width), families.dtype)
    sizes = sum(shard.size for shard in shards) * LINE // (width * width)
    depth = width // 6
    block = lambda count: pltpu.VMEM((count * depth, width), bf16)
    anywhere = pl.BlockSpec(memory_space=pl.ANY)
    inside = pl.BlockSpec(memory_space=pltpu.VMEM)
    scalars = pl.BlockSpec(memory_space=pltpu.SMEM)
    dma = pltpu.SemaphoreType.DMA
    bf16, f32 = (jnp.bfloat16, jnp.float32)
    rows_of = lambda columns_of, kind=bf16: pltpu.VMEM((tokens, columns_of), kind)
    scores = pltpu.VMEM((couples, columns, 2 * columns), bf16)
    return pl.pallas_call(
        layers_kernel,
        out_shape=[
            jax.ShapeDtypeStruct(entry.shape, bf16),
            jax.ShapeDtypeStruct(entry.shape, bf16),
            jax.ShapeDtypeStruct((2, 8, 128), f32),
            jax.ShapeDtypeStruct((8, 256), f32),
            jax.ShapeDtypeStruct((LINE, 4, width, width), bf16),
            jax.ShapeDtypeStruct((4, width, width), bf16),
        ],
        in_specs=[anywhere] * 6 + [inside, inside, scalars, inside, scalars, inside],
        out_specs=[anywhere, anywhere, inside, inside, anywhere, anywhere],
        scratch_shapes=[
            pltpu.VMEM((sizes, width, width), bf16),
            pltpu.VMEM(entry.shape, bf16),
            rows_of(width),
            rows_of(width),
            rows_of(width),
            rows_of(3 * width),
            rows_of(3 * width),
            rows_of(width),
            rows_of(width),
            rows_of(width, f32),
            rows_of(width, f32),
            pltpu.VMEM((couples, columns, 2 * columns), f32),
            pltpu.VMEM((4, tokens, 128), f32),
            rows_of(wide),
            rows_of(wide),
            rows_of(width, f32),
            pltpu.VMEM(entry.shape, bf16),
            rows_of(width),
            rows_of(width),
            rows_of(width),
            rows_of(wide),
            rows_of(3 * width),
            rows_of(3 * width),
            scores,
            scores,
            pltpu.VMEM((2, tokens, width), bf16),
            rows_of(2 * width),
            rows_of(2 * width),
            scores,
            scores,
            pltpu.VMEM((2, columns, 2 * columns), bf16),
            pltpu.VMEM((width, 128), bf16),
            pltpu.VMEM((128, width), bf16),
            pltpu.VMEM((2, LINE, 4, width // (4 * LINE), width), bf16),
            pltpu.VMEM((2, 4, width // 4, width), bf16),
            pltpu.VMEM(entry.shape, bf16),
            pltpu.VMEM(entry.shape, bf16),
            pltpu.VMEM((8, 128), f32),
            pltpu.VMEM(entry.shape, bf16),
            pltpu.VMEM(entry.shape, bf16),
            pltpu.VMEM(entry.shape, bf16),
            pltpu.VMEM((2, columns, columns), f32),
            pltpu.VMEM((2, columns, columns), f32),
            pltpu.VMEM((2, 8, 128), f32),
            pltpu.VMEM((2, 8, 128), f32),
            pltpu.VMEM((LINE, 8, 256), f32),
            pltpu.VMEM((8, width), f32),
            dma((6,)),
            dma((2, LINE, PIECES)),
            dma((LINE, PIECES)),
            dma((LINE, PIECES)),
            dma((LINE, PIECES)),
            dma((2, LINE, PIECES)),
            dma((2, LINE, PIECES)),
            dma((8, 2)),
            dma((4,)),
            dma((LINE - 1,)),
            dma((LINE,)),
            block(40),
            block(16),
            block(4),
            pltpu.VMEM(entry.shape, bf16),
            pltpu.SemaphoreType.REGULAR,
            pltpu.VMEM((LINE, 8, 256), f32),
            pltpu.VMEM((LINE, 8, 256), f32),
            pltpu.VMEM((LINE, 8, 256), f32),
            pltpu.VMEM((LINE, 8, 256), f32),
            dma((24, 2)),
            dma((24, 2)),
            dma((24, 2)),
            dma((24,)),
            dma((24,)),
            dma((24,)),
            dma((24,)),
            dma((24,)),
            dma((6,)),
            dma((6,)),
            dma((2, 6)),
            dma((2, 6)),
            dma((2, 6)),
            dma((2 + LINE,)),
            dma((2 + LINE,)),
            dma((2, couples)),
            dma((2, 2)),
            dma((2, 2)),
            dma((2, couples)),
            dma((10,)),
            dma((4, LINE)),
            dma((6, 2)),
            dma((4,)),
            dma((LINE - 1,)),
            dma((2,)),
        ],
        compiler_params=pltpu.CompilerParams(
            collective_id=2, has_side_effects=True, vmem_limit_bytes=63 * 2**20
        ),
        name="two_layers",
    )(*shards, families, upstream, order, quarters, tally, norms)


def unpack_kernel(blocks, act, der, costs, *refs):
    results, act_out, der_out, cost_out = (refs[:6], *refs[6:])
    width = blocks.shape[2]
    base = 0
    for result in results:
        depth, wide = result.shape[1:]
        for part in range(wide // width):
            result[0, :, part * width : (part + 1) * width] = blocks[
                0, base : base + depth, :
            ].astype(jnp.float32)
            base += depth
    act_out[0, :, 0] = act[...]
    der_out[0, :, 0] = der[...]
    cost_out[...] = jnp.concatenate([costs[0, 0:1, 0:1], costs[1, 0:1, 0:1]], axis=1)


def unpack_all(blocks, act, der, costs, shapes):
    columns, width = act.shape[1:]
    large = jax.ShapeDtypeStruct((1, 2, 1, columns, width), act.dtype)
    part = pl.BlockSpec((2, columns // 4, width), lambda step: (0, step, 0))
    wide = pl.BlockSpec((1, 2, 1, columns // 4, width), lambda step: (0, 0, 0, step, 0))
    return pl.pallas_call(
        unpack_kernel,
        grid=(4,),
        out_shape=[jax.ShapeDtypeStruct((1,) + shape, jnp.float32) for shape in shapes]
        + [large, large, jax.ShapeDtypeStruct((1, 2), jnp.float32)],
        in_specs=[
            pl.BlockSpec((1,) + blocks.shape[1:], lambda step: (step, 0, 0)),
            part,
            part,
            pl.BlockSpec(costs.shape, lambda step: (0, 0, 0)),
        ],
        out_specs=[
            pl.BlockSpec((1, shape[0] // 4, shape[1]), lambda step: (0, step, 0))
            for shape in shapes
        ]
        + [wide, wide, pl.BlockSpec((1, 2), lambda step: (0, 0))],
        compiler_params=pltpu.CompilerParams(vmem_limit_bytes=60 * 2**20),
        cost_estimate=pl.CostEstimate(
            flops=blocks.size, bytes_accessed=6 * blocks.size, transcendentals=0
        ),
        name="unpack_grads",
    )(blocks, act, der, costs)


def on_device_lined(
    embedded_families,
    order,
    token_quarter_factor,
    genuine_residue_tally,
    standardizer_scales,
    standardizer_offsets,
    row_qkv,
    row_out,
    col_qkv,
    col_out,
    ffn_up,
    ffn_down,
    upstream_sensitivity,
):
    model_width = embedded_families.shape[-1]
    share = standardizer_scales.shape[-1]
    shards = (row_qkv, row_out, col_qkv, col_out, ffn_up, ffn_down)
    norms = jnp.pad(
        jnp.concatenate([standardizer_scales[0], standardizer_offsets[0]], axis=0),
        ((0, 2), (0, 256 - share)),
    )
    activations, derivs, costs, vector, _, out = run_layers(
        shards,
        embedded_families,
        upstream_sensitivity,
        order,
        token_quarter_factor,
        genuine_residue_tally,
        norms,
    )
    *results, activations, derivs, costs = unpack_all(
        out, activations, derivs, costs, [shard.shape[1:] for shard in shards]
    )
    return (
        activations,
        derivs,
        costs,
        *results,
        vector[None, 0:3, :share],
        vector[None, 3:6, :share],
    )


def solution(mesh):
    in_specs = (
        P("dp", "seq", None, None),
        P("dp", None),
        P("dp", "seq", None),
        P("dp"),
        P("pipe", None, "seq"),
        P("pipe", None, "seq"),
        P("pipe", "seq", None),
        P("pipe", "seq", None),
        P("pipe", "seq", None),
        P("pipe", "seq", None),
        P("pipe", "seq", None),
        P("pipe", "seq", None),
        P("dp", "seq", None, None),
    )
    out_specs = (
        P("pipe", "dp", "seq", None, None),
        P("pipe", "dp", "seq", None, None),
        P("pipe", "dp"),
        P("pipe", "seq", None),
        P("pipe", "seq", None),
        P("pipe", "seq", None),
        P("pipe", "seq", None),
        P("pipe", "seq", None),
        P("pipe", "seq", None),
        P("pipe", None, "seq"),
        P("pipe", None, "seq"),
    )
    lined = mesh.shape["seq"] == LINE and mesh.shape["dp"] == 4 and mesh.shape["pipe"] == 2
    return jax.shard_map(
        on_device_lined if lined else on_device, mesh=mesh, in_specs=in_specs, out_specs=out_specs, check_vma=False
    )
```
